32 devices in a mesh: gx: 4 (over z), gy: 2 (over x), gz: 4 (over y, core).
Axes of the slice: x: 2, y: 2, z: 4, core: 2. Of those that a mesh axis runs over, the one named last changes fastest.
Arguments:
- magnetization: float32 [3, 64, 256, 256], P(None, 'gz', 'gx', 'gy'), may hold values from -6 to 6
- stiffness: float32 [64, 256, 256], P('gz', 'gx', 'gy'), may hold values from 0.02 to 0.2
- residual_top: float32 [256, 256], P('gx', ('gy', 'gz')), may hold values from -6 to 6
- residual_side: float32 [256, 64], P('gy', 'gz'), may hold values from -6 to 6
- top_kernel: float32 [2, 2, 2048, 2048], P(None, None, ('gx', 'gy', 'gz')), may hold values from -6 to 6
- side_kernel: float32 [2, 2, 128, 2048], P(None, None, ('gy', 'gz')), may hold values from -6 to 6
Outputs:
- gradient: float32 [3, 64, 256, 256], P(None, 'gz', 'gx', 'gy')
The draws below stay inside these ranges and needn't reach their ends.
All inputs are finite; a program needn't handle non-finite values.
Results may differ from the reference program's by a relative error of at most 0.0001.
Values sent between devices are 32-bit elements; how exact they have to be, the bound alone decides.
No kernel may reach another device: no remote copies, remote signals or barrier semaphores. Data moves between devices by JAX's collectives and lax.ppermute only.
A program may use at most 64 MiB of HBM per device.

```python
import math
import jax
import jax.numpy as jnp
from jax import lax

NK = 2048
NKZ = 128
NX = 256
NY = 256
NZ = 64


def draw_residual_top(key, part):
    noise = jnp.clip(jax.random.normal(key, (NX, NY), jnp.float32), -6.0, 6.0)
    return noise


def level_of(stream_key, shape, shards, low, high):
    def one(axis_at, parts):
        draws = jax.random.uniform(jax.random.fold_in(jax.random.fold_in(stream_key, 6), axis_at), (parts,), jnp.float32, low / len(shards), high / len(shards))
        return jnp.repeat(jnp.exp(draws), shape[axis_at] // parts).reshape((-1,) + (1,) * (len(shape) - axis_at - 1))

    level = one(*shards[0])
    for cut in shards[1:]:
        level = level * one(*cut)
    return level


def scatter_about(rng, dims, width, bound, cuts=(), kind=jnp.bfloat16):
    loudness = level_of(rng, dims, cuts, -0.22, 0.18) if cuts else 1.0
    array = jax.random.normal(rng, dims, jnp.float32) * width * loudness
    return jnp.minimum(jnp.maximum(array, -bound), bound).astype(kind)


def setup_inputs(seed: int = 0) -> dict:
    key_list = jax.random.split(jax.random.key(seed), 7)
    return {
        "magnetization": scatter_about(key_list[0], (3, NZ, NX, NY), 1.0, 6.0, ((1, 4), (2, 4), (3, 2)), jnp.float32),
        "stiffness": jnp.clip(jnp.exp(math.log(0.2) - 2.3025851 * jax.random.uniform(key_list[1], (NZ, NX, NY), jnp.float32) ** level_of(key_list[1], (NZ, NX, NY), ((0, 4), (1, 4), (2, 2)), -0.2, 0.2)), 0.02, 0.2),
        "residual_top": draw_residual_top(jax.random.fold_in(key_list[6], 71), 0),
        "residual_side": scatter_about(key_list[3], (NY, NZ), 1.0, 6.0, ((0, 2), (1, 4)), jnp.float32),
        "top_kernel": scatter_about(key_list[4], (2, 2, NK, NK), 1.0, 6.0, ((2, 32),), jnp.float32),
        "side_kernel": scatter_about(key_list[5], (2, 2, NKZ, NK), 1.0, 6.0, ((2, 8),), jnp.float32),
    }


def harmonic(first, second):
    return 2.0 * first * second / (first + second)


def face_term(component_field, stiffness, dimension):
    extent = component_field.shape[dimension]
    upper_pad = [(0, 0), (0, 0), (0, 0)]
    upper_pad[dimension] = (0, 1)
    lower_pad = [(0, 0), (0, 0), (0, 0)]
    lower_pad[dimension] = (1, 0)
    upper_field = lax.slice_in_dim(jnp.pad(component_field, upper_pad), 1, extent + 1, axis=dimension)
    upper_stiff = lax.slice_in_dim(jnp.pad(stiffness, upper_pad), 1, extent + 1, axis=dimension)
    flux_up = harmonic(stiffness, upper_stiff) * (component_field - upper_field)
    flux_down = lax.slice_in_dim(jnp.pad(flux_up, lower_pad), 0, extent, axis=dimension)
    return flux_up - flux_down


def padded_adjoint(residual, kernel, first_size, second_size):
    first_extent, second_extent = residual.shape
    padded = jnp.pad(residual, ((0, first_size - first_extent), (0, second_size - second_extent)))
    spectrum = jnp.fft.fft2(padded)
    images = []
    for component in range(2):
        kernel_entry = lax.complex(kernel[component, 0], kernel[component, 1]).T
        inverse = jnp.fft.ifft2(jnp.conj(kernel_entry) * spectrum)
        images.append(jnp.real(inverse)[:first_extent, :second_extent])
    return images


def reference(magnetization, stiffness, residual_top, residual_side, top_kernel, side_kernel):
    top_grad = padded_adjoint(residual_top, top_kernel, NK, NK)
    side_grad = padded_adjoint(residual_side, side_kernel, NK, NKZ)
    outputs = []
    for component in range(3):
        component_field = magnetization[component]
        summed = face_term(component_field, stiffness, 0) + face_term(component_field, stiffness, 1)
        summed = summed + face_term(component_field, stiffness, 2)
        exchange = 2.0 * summed
        if component < 2:
            exchange = exchange + top_grad[component][None, :, :]
        if component > 0:
            exchange = exchange + side_grad[component - 1].T[:, None, :]
        outputs.append(exchange)
    return jnp.stack(outputs)
```

```python
import functools
import math

import jax
import jax.numpy as jnp
import ml_dtypes
import numpy as np
from jax import lax
from jax.experimental import pallas as pl
from jax.experimental.pallas import tpu as pltpu
from jax.sharding import PartitionSpec as P

LANES = 128
TILE = 8
INNER = 256
ALL = ("gx", "gy", "gz")
f32 = jnp.float32
bf16 = jnp.bfloat16


def split(values):
    high = values.astype(bf16)
    return high, (values - high.astype(f32)).astype(bf16)


def dot3(left, right):
    high, low = split(left)
    def one(a, b):
        return lax.dot_general(a, b, (((1,), (0,)), ((), ())), preferred_element_type=f32)
    return one(high, right[0]) + one(low, right[0]) + one(high, right[1])


def transform_tables(extent, size):
    x = np.arange(extent)
    angle = (np.outer(x, np.arange(INNER)) % size) * (2.0 * math.pi / size)
    forward = np.concatenate([np.cos(angle), np.sin(angle)], 0).astype(np.float32)
    backward = np.concatenate([np.cos(angle).T, np.sin(angle).T], 0).astype(np.float32)

    def parts(table):
        high = table.astype(ml_dtypes.bfloat16)
        return high, (table - high.astype(np.float32)).astype(ml_dtypes.bfloat16)

    outer = size // INNER
    turn = (np.outer(np.arange(outer), x) % outer) * (2.0 * math.pi / outer)
    turns = np.stack([np.cos(turn), np.sin(turn)]).astype(np.float32)
    return parts(forward), parts(backward), turns


def phases(first, second, size):
    angle = (first * second % size).astype(f32) * (2.0 * math.pi / size)
    return jnp.cos(angle), jnp.sin(angle)


def image_kernel(
    counts, gathered, y_table, z_table, fh, fl, bh, bl, turns, top, side, y_back, z_back, out
):
    count_x, count_y, count_z, top_rows = counts
    group = count_y * count_z
    half = LANES // 2
    kys = top.shape[2]
    kzs = side.shape[2]
    forward = (fh[...], fl[...])
    backward = (bh[...], bl[...])

    blocks = [
        gathered[g * group : (g + 1) * group, 0:top_rows, :].reshape(group * top_rows, LANES)
        for g in range(count_x)
    ]
    mixed = dot3(y_table[...], split(jnp.concatenate(blocks, axis=1)))
    low_half, high_half = mixed[: 2 * kys], mixed[2 * kys :]
    lane = lax.broadcasted_iota(jnp.int32, (2 * kys, LANES), 1)
    pieces = []
    for g in range(0, count_x, 2):
        a = slice(g * LANES, (g + 1) * LANES)
        b = slice((g + 1) * LANES, (g + 2) * LANES)
        pieces.append(
            jnp.where(
                lane < half,
                low_half[:, a] + pltpu.roll(high_half[:, a], half, 1),
                pltpu.roll(low_half[:, b], half, 1) + high_half[:, b],
            )
        )
    top_lines = jnp.concatenate(pieces, axis=1)

    side_blocks = []
    for y in range(count_y):
        rows = [
            gathered[(x * count_y + y) * count_z + z, top_rows : top_rows + TILE, :]
            for x in range(count_x)
            for z in range(count_z)
        ]
        side_blocks.append(jnp.concatenate(rows, axis=0))
    side_lines = dot3(z_table[...], split(jnp.concatenate(side_blocks, axis=1)))

    real = jnp.concatenate([top_lines[:kys], side_lines[:kzs]], axis=0)
    imag = jnp.concatenate([top_lines[kys:], side_lines[kzs:]], axis=0)
    rows = kys + kzs
    total_real = total_imag = None
    for b in range(turns.shape[1]):
        cosine, sine = turns[0, b : b + 1, :], turns[1, b : b + 1, :]
        turned_real = real * cosine + imag * sine
        turned_imag = imag * cosine - real * sine
        waves = dot3(
            jnp.concatenate(
                [
                    jnp.concatenate([turned_real, turned_imag], axis=1),
                    jnp.concatenate([turned_imag, -turned_real], axis=1),
                ],
                axis=0,
            ),
            forward,
        )
        wave_real, wave_imag = waves[:rows], waves[rows:]
        columns = slice(b * INNER, (b + 1) * INNER)
        weighted_real, weighted_imag = [], []
        for c in range(2):
            for kernel, part in ((top, slice(0, kys)), (side, slice(kys, rows))):
                kernel_real, kernel_imag = kernel[c, 0, :, columns], kernel[c, 1, :, columns]
                weighted_real.append(
                    kernel_real * wave_real[part] + kernel_imag * wave_imag[part]
                )
                weighted_imag.append(
                    kernel_real * wave_imag[part] - kernel_imag * wave_real[part]
                )
        weighted_real = jnp.concatenate(weighted_real, axis=0)
        weighted_imag = jnp.concatenate(weighted_imag, axis=0)
        back = dot3(
            jnp.concatenate(
                [
                    jnp.concatenate([weighted_real, -weighted_imag], axis=1),
                    jnp.concatenate([weighted_imag, weighted_real], axis=1),
                ],
                axis=0,
            ),
            backward,
        )
        back_real, back_imag = back[: 2 * rows], back[2 * rows :]
        if b == 0:
            total_real, total_imag = back_real, back_imag
        else:
            total_real = total_real + (back_real * cosine - back_imag * sine)
            total_imag = total_imag + (back_real * sine + back_imag * cosine)

    y_parts = split(y_back[...])
    depth_rows = []
    quarter = (out.shape[1] - TILE) // 2
    block_x = quarter * count_z
    for c in range(2):
        start = c * rows
        lines = jnp.concatenate(
            [total_real[start : start + kys], total_imag[start : start + kys]], axis=0
        )
        image = dot3(lines.T, y_parts)
        for x in range(count_x):
            for y in range(count_y):
                for z in range(count_z):
                    first = x * block_x + z * quarter
                    out[
                        (x * count_y + y) * count_z + z, c * quarter : (c + 1) * quarter, :
                    ] = image[first : first + quarter, y * LANES : (y + 1) * LANES]
        depth_rows.append(total_real[start + kys : start + rows])
        depth_rows.append(total_imag[start + kys : start + rows])
    side_image = dot3(z_back[...], split(jnp.concatenate(depth_rows, axis=0)))
    for y in range(count_y):
        for z in range(count_z):
            block = side_image[z * TILE : (z + 1) * TILE, y * LANES : (y + 1) * LANES]
            for x in range(count_x):
                out[(x * count_y + y) * count_z + z, 2 * quarter :, :] = block


def image_parts(gathered, top_kernel, side_kernel, counts, block_x, top_rows, depth_block):
    count_x, count_y, count_z = counts
    group = count_y * count_z
    here = [lax.axis_index(axis) for axis in ALL]
    kys, size = top_kernel.shape[2:]
    kzs = side_kernel.shape[2]
    depth_size = kzs * group
    extent = count_y * LANES
    share = depth_block // count_x
    block_y = top_rows * 2

    ky = ((here[0] * count_y + here[1]) * count_z + here[2]) * kys + lax.iota(jnp.int32, kys)
    kz = (here[1] * count_z + here[2]) * kzs + lax.iota(jnp.int32, kzs)

    row = lax.iota(jnp.int32, group * top_rows)
    y_tables = []
    for h in range(2):
        y = row // top_rows * block_y + h * top_rows + row % top_rows
        cosine, sine = phases(ky[:, None], y[None, :], size)
        y_tables += [cosine, -sine]
    y_table = jnp.concatenate(y_tables, axis=0)

    row = lax.iota(jnp.int32, count_x * count_z * TILE)
    inside = row % TILE
    z = row // TILE % count_z * depth_block + row // (TILE * count_z) * share + inside
    cosine, sine = phases(kz[:, None], z[None, :], depth_size)
    z_table = jnp.where((inside < share)[None, :], jnp.concatenate([cosine, -sine], axis=0), 0.0)

    cosine, sine = phases(ky[:, None], lax.iota(jnp.int32, extent)[None, :], size)
    y_back = jnp.concatenate([cosine, -sine], axis=0) * (1.0 / (size * size))

    row = lax.iota(jnp.int32, count_z * TILE)
    z = row // TILE * depth_block + here[0] * share + row % TILE % share
    cosine, sine = phases(z[:, None], kz[None, :], depth_size)
    both = jnp.concatenate([cosine, -sine], axis=1) * (1.0 / (size * depth_size))
    component = (row % TILE // share)[:, None]
    z_back = jnp.concatenate(
        [jnp.where(component == 0, both, 0.0), jnp.where(component == 1, both, 0.0)], axis=1
    )

    forward, backward, turns = transform_tables(extent, size)
    out_rows = 2 * (block_x // count_z) + TILE
    return pl.pallas_call(
        functools.partial(image_kernel, counts + (top_rows,)),
        out_shape=jax.ShapeDtypeStruct((count_x * group, out_rows, LANES), f32),
        compiler_params=pltpu.CompilerParams(vmem_limit_bytes=56 * 1024 * 1024),
        name="images",
    )(
        gathered,
        y_table,
        z_table,
        *(jnp.asarray(t) for t in forward + backward),
        jnp.asarray(turns),
        top_kernel,
        side_kernel,
        y_back,
        z_back,
    )


def faces_kernel(magnetization, stiffness, z_first, z_last, x_first, x_last, y_faces):
    depth, across = stiffness.shape[:2]
    lane = lax.broadcasted_iota(jnp.int32, (across, LANES), 1)
    sides = jnp.zeros((across, LANES), f32)
    for field in range(4):
        ref = stiffness if field == 3 else magnetization.at[field]
        z_first[field] = ref[0]
        z_last[field] = ref[depth - 1]
        x_first[field] = ref[:, 0, :]
        x_last[field] = ref[:, across - 1, :]
        for z in range(depth):
            column = field * depth + z
            values = ref[z]
            sides = jnp.where(lane == column, values[:, 0:1], sides)
            sides = jnp.where(lane == column + 4 * depth, values[:, LANES - 1 : LANES], sides)
    y_faces[...] = sides


def exchange_kernel(
    magnetization,
    stiffness,
    z_next,
    z_before,
    x_next,
    x_before,
    y_next,
    y_before,
    out,
):
    depth, across = stiffness.shape[:2]
    lane = lax.broadcasted_iota(jnp.int32, (across, LANES), 1)
    sublane = lax.broadcasted_iota(jnp.int32, (across, LANES), 0)
    last_lane, first_lane = lane == LANES - 1, lane == 0
    last_row, first_row = sublane == across - 1, sublane == 0

    def weight(a, b):
        return 2.0 * a * b / (a + b)

    def one(z, field):
        ref = stiffness if field == 3 else magnetization.at[field]
        centre = ref[z]
        column = field * depth + z
        along = jnp.where(
            last_lane, y_next[:, column : column + 1], pltpu.roll(centre, LANES - 1, 1)
        )
        across_next = jnp.where(
            last_row, x_next[field, z : z + 1, :], pltpu.roll(centre, across - 1, 0)
        )
        along_before = y_before[:, 4 * depth + column : 4 * depth + column + 1]
        across_before = x_before[field, z : z + 1, :]
        return centre, along, across_next, along_before, across_before

    below_weight = weight(z_before[3], stiffness[0])
    below = [below_weight * (z_before[c] - magnetization[c, 0]) for c in range(3)]
    for z in range(depth):
        s, s_along, s_across, s_along_before, s_across_before = one(z, 3)
        s_above = stiffness[z + 1] if z + 1 < depth else z_next[3]
        w_along, w_across, w_above = weight(s, s_along), weight(s, s_across), weight(s, s_above)
        w_along_before = weight(s_along_before, s[:, 0:1])
        w_across_before = weight(s_across_before, s[0:1, :])
        for c in range(3):
            m, m_along, m_across, m_along_before, m_across_before = one(z, c)
            m_above = magnetization[c, z + 1] if z + 1 < depth else z_next[c]
            up = w_above * (m - m_above)
            flux_along = w_along * (m - m_along)
            flux_across = w_across * (m - m_across)
            edge_along = w_along_before * (m_along_before - m[:, 0:1])
            edge_across = w_across_before * (m_across_before - m[0:1, :])
            lower_along = jnp.where(first_lane, edge_along, pltpu.roll(flux_along, 1, 1))
            lower_across = jnp.where(first_row, edge_across, pltpu.roll(flux_across, 1, 0))
            total = (up - below[c]) + (flux_across - lower_across) + (flux_along - lower_along)
            out[c, z] = 2.0 * total
            below[c] = up


def shifted(block, axis, distance):
    count = lax.axis_size(axis)
    route = [(i, i + distance) for i in range(count) if 0 <= i + distance < count]
    return lax.ppermute(block, axis, route)


def exchange(magnetization, stiffness):
    depth, across, along = stiffness.shape
    shape = jax.ShapeDtypeStruct
    z_first, z_last, x_first, x_last, y_faces = pl.pallas_call(
        faces_kernel,
        out_shape=[
            shape((4, across, along), f32),
            shape((4, across, along), f32),
            shape((4, depth, along), f32),
            shape((4, depth, along), f32),
            shape((across, LANES), f32),
        ],
        name="faces",
    )(magnetization, stiffness)
    z_next, z_before = shifted(z_first, "gz", -1), shifted(z_last, "gz", 1)
    x_next, x_before = shifted(x_first, "gx", -1), shifted(x_last, "gx", 1)
    if lax.axis_size("gy") == 2:
        other = lax.ppermute(y_faces, "gy", [(0, 1), (1, 0)])
        at = lax.axis_index("gy")
        y_next, y_before = jnp.where(at == 0, other, 0.0), jnp.where(at == 1, other, 0.0)
    else:
        y_next, y_before = shifted(y_faces, "gy", -1), shifted(y_faces, "gy", 1)
    return pl.pallas_call(
        exchange_kernel,
        out_shape=shape(magnetization.shape, f32),
        compiler_params=pltpu.CompilerParams(vmem_limit_bytes=32 * 1024 * 1024),
        name="exchange",
    )(magnetization, stiffness, z_next, z_before, x_next, x_before, y_next, y_before)


def on_device(magnetization, stiffness, residual_top, residual_side, top_kernel, side_kernel):
    counts = tuple(lax.axis_size(axis) for axis in ALL)
    count_x, count_y, count_z = counts
    devices = count_x * count_y * count_z
    depth_block = stiffness.shape[0]
    block_x, block_y = residual_top.shape
    top_rows = block_y // 2
    share = depth_block // count_x

    top_piece = residual_top.T.reshape(2, top_rows, block_x)
    top_piece = jnp.concatenate([top_piece[0], top_piece[1]], axis=1)
    side_piece = lax.dynamic_slice_in_dim(
        residual_side.T, lax.axis_index("gx") * share, share, axis=0
    )
    piece = jnp.concatenate(
        [top_piece, side_piece, jnp.zeros((TILE - share, LANES), f32)], axis=0
    )
    rows = piece.shape[0]
    sent = jnp.broadcast_to(piece[None], (devices, rows, LANES)).reshape(devices * rows, LANES)
    gathered = lax.all_to_all(sent, ALL, 0, 0, tiled=True).reshape(devices, rows, LANES)

    exchange_grad = exchange(magnetization, stiffness)

    parts = image_parts(
        gathered, top_kernel, side_kernel, counts, block_x, top_rows, depth_block
    )
    rows = parts.shape[1]
    arrived = lax.all_to_all(parts.reshape(devices * rows, LANES), ALL, 0, 0, tiled=True)
    arrived = arrived.reshape(devices, rows, LANES)
    top_sum = jnp.sum(arrived[:, : rows - TILE], axis=0)
    side_sum = jnp.sum(
        arrived[:, rows - TILE :].reshape(count_x, count_y * count_z, TILE, LANES), axis=1
    )
    side = side_sum[:, : 2 * share].reshape(count_x, 2, share, LANES)
    side = jnp.swapaxes(side, 0, 1).reshape(2, depth_block, 1, LANES)
    top = lax.all_gather(top_sum, "gz", axis=0)
    top = jnp.swapaxes(top.reshape(count_z, 2, block_x // count_z, LANES), 0, 1)
    top = top.reshape(2, 1, block_x, LANES)
    return jnp.stack(
        [
            exchange_grad[0] + top[0],
            exchange_grad[1] + top[1] + side[0],
            exchange_grad[2] + side[1],
        ]
    )


def solution(mesh):
    placed = (
        P(None, "gz", "gx", "gy"),
        P("gz", "gx", "gy"),
        P("gx", ("gy", "gz")),
        P("gy", "gz"),
        P(None, None, ("gx", "gy", "gz"), None),
        P(None, None, ("gy", "gz"), None),
    )
    return jax.shard_map(
        on_device, mesh=mesh, in_specs=placed, out_specs=P(None, "gz", "gx", "gy"), check_vma=False
    )
```

```python
import functools
import math

import jax
import jax.numpy as jnp
import ml_dtypes
import numpy as np
from jax import lax
from jax.experimental import pallas as pl
from jax.experimental.pallas import tpu as pltpu
from jax.sharding import PartitionSpec as P

LANES = 128
TILE = 8
INNER = 256
ALL = ("gx", "gy", "gz")
f32 = jnp.float32
bf16 = jnp.bfloat16


def split(values):
    high = values.astype(bf16)
    return high, (values - high.astype(f32)).astype(bf16)


def dot3(left, right):
    high, low = split(left)
    def one(a, b):
        return lax.dot_general(a, b, (((1,), (0,)), ((), ())), preferred_element_type=f32)
    return one(high, right[0]) + one(low, right[0]) + one(high, right[1])


def transform_tables(extent, size):
    x = np.arange(extent)
    angle = (np.outer(x, np.arange(INNER)) % size) * (2.0 * math.pi / size)
    forward = np.concatenate([np.cos(angle), np.sin(angle)], 0).astype(np.float32)
    backward = np.concatenate([np.cos(angle).T, np.sin(angle).T], 0).astype(np.float32)

    def parts(table):
        high = table.astype(ml_dtypes.bfloat16)
        return high, (table - high.astype(np.float32)).astype(ml_dtypes.bfloat16)

    outer = size // INNER
    turn = (np.outer(np.arange(outer), x) % outer) * (2.0 * math.pi / outer)
    turns = np.stack([np.cos(turn), np.sin(turn)]).astype(np.float32)
    return parts(forward), parts(backward), turns


def phases(first, second, size):
    angle = (first * second % size).astype(f32) * (2.0 * math.pi / size)
    return jnp.cos(angle), jnp.sin(angle)


def image_kernel(
    counts, gathered, y_table, z_table, fh, fl, bh, bl, turns, top, side, y_back, z_back, out
):
    count_x, count_y, count_z, top_rows = counts
    group = count_y * count_z
    half = LANES // 2
    kys = top.shape[2]
    kzs = side.shape[2]
    forward = (fh[...], fl[...])
    backward = (bh[...], bl[...])

    blocks = [
        gathered[g * group : (g + 1) * group, 0:top_rows, :].reshape(group * top_rows, LANES)
        for g in range(count_x)
    ]
    mixed = dot3(y_table[...], split(jnp.concatenate(blocks, axis=1)))
    low_half, high_half = mixed[: 2 * kys], mixed[2 * kys :]
    lane = lax.broadcasted_iota(jnp.int32, (2 * kys, LANES), 1)
    pieces = []
    for g in range(0, count_x, 2):
        a = slice(g * LANES, (g + 1) * LANES)
        b = slice((g + 1) * LANES, (g + 2) * LANES)
        pieces.append(
            jnp.where(
                lane < half,
                low_half[:, a] + pltpu.roll(high_half[:, a], half, 1),
                pltpu.roll(low_half[:, b], half, 1) + high_half[:, b],
            )
        )
    top_lines = jnp.concatenate(pieces, axis=1)

    side_blocks = []
    for y in range(count_y):
        rows = [
            gathered[(x * count_y + y) * count_z + z, top_rows : top_rows + TILE, :]
            for x in range(count_x)
            for z in range(count_z)
        ]
        side_blocks.append(jnp.concatenate(rows, axis=0))
    side_lines = dot3(z_table[...], split(jnp.concatenate(side_blocks, axis=1)))

    real = jnp.concatenate([top_lines[:kys], side_lines[:kzs]], axis=0)
    imag = jnp.concatenate([top_lines[kys:], side_lines[kzs:]], axis=0)
    rows = kys + kzs
    total_real = total_imag = None
    for b in range(turns.shape[1]):
        cosine, sine = turns[0, b : b + 1, :], turns[1, b : b + 1, :]
        turned_real = real * cosine + imag * sine
        turned_imag = imag * cosine - real * sine
        waves = dot3(
            jnp.concatenate(
                [
                    jnp.concatenate([turned_real, turned_imag], axis=1),
                    jnp.concatenate([turned_imag, -turned_real], axis=1),
                ],
                axis=0,
            ),
            forward,
        )
        wave_real, wave_imag = waves[:rows], waves[rows:]
        columns = slice(b * INNER, (b + 1) * INNER)
        weighted_real, weighted_imag = [], []
        for c in range(2):
            for kernel, part in ((top, slice(0, kys)), (side, slice(kys, rows))):
                kernel_real, kernel_imag = kernel[c, 0, :, columns], kernel[c, 1, :, columns]
                weighted_real.append(
                    kernel_real * wave_real[part] + kernel_imag * wave_imag[part]
                )
                weighted_imag.append(
                    kernel_real * wave_imag[part] - kernel_imag * wave_real[part]
                )
        weighted_real = jnp.concatenate(weighted_real, axis=0)
        weighted_imag = jnp.concatenate(weighted_imag, axis=0)
        back = dot3(
            jnp.concatenate(
                [
                    jnp.concatenate([weighted_real, -weighted_imag], axis=1),
                    jnp.concatenate([weighted_imag, weighted_real], axis=1),
                ],
                axis=0,
            ),
            backward,
        )
        back_real, back_imag = back[: 2 * rows], back[2 * rows :]
        if b == 0:
            total_real, total_imag = back_real, back_imag
        else:
            total_real = total_real + (back_real * cosine - back_imag * sine)
            total_imag = total_imag + (back_real * sine + back_imag * cosine)

    y_parts = split(y_back[...])
    depth_rows = []
    quarter = (out.shape[1] - TILE) // 2
    block_x = quarter * count_z
    for c in range(2):
        start = c * rows
        lines = jnp.concatenate(
            [total_real[start : start + kys], total_imag[start : start + kys]], axis=0
        )
        image = dot3(lines.T, y_parts)
        for x in range(count_x):
            for y in range(count_y):
                for z in range(count_z):
                    first = x * block_x + z * quarter
                    out[
                        (x * count_y + y) * count_z + z, c * quarter : (c + 1) * quarter, :
                    ] = image[first : first + quarter, y * LANES : (y + 1) * LANES]
        depth_rows.append(total_real[start + kys : start + rows])
        depth_rows.append(total_imag[start + kys : start + rows])
    side_image = dot3(z_back[...], split(jnp.concatenate(depth_rows, axis=0)))
    for y in range(count_y):
        for z in range(count_z):
            block = side_image[z * TILE : (z + 1) * TILE, y * LANES : (y + 1) * LANES]
            for x in range(count_x):
                out[(x * count_y + y) * count_z + z, 2 * quarter :, :] = block


def image_parts(gathered, top_kernel, side_kernel, counts, block_x, top_rows, depth_block):
    count_x, count_y, count_z = counts
    group = count_y * count_z
    here = [lax.axis_index(axis) for axis in ALL]
    kys, size = top_kernel.shape[2:]
    kzs = side_kernel.shape[2]
    depth_size = kzs * group
    extent = count_y * LANES
    share = depth_block // count_x
    block_y = top_rows * 2

    ky = ((here[0] * count_y + here[1]) * count_z + here[2]) * kys + lax.iota(jnp.int32, kys)
    kz = (here[1] * count_z + here[2]) * kzs + lax.iota(jnp.int32, kzs)

    row = lax.iota(jnp.int32, group * top_rows)
    y_tables = []
    for h in range(2):
        y = row // top_rows * block_y + h * top_rows + row % top_rows
        cosine, sine = phases(ky[:, None], y[None, :], size)
        y_tables += [cosine, -sine]
    y_table = jnp.concatenate(y_tables, axis=0)

    row = lax.iota(jnp.int32, count_x * count_z * TILE)
    inside = row % TILE
    z = row // TILE % count_z * depth_block + row // (TILE * count_z) * share + inside
    cosine, sine = phases(kz[:, None], z[None, :], depth_size)
    z_table = jnp.where((inside < share)[None, :], jnp.concatenate([cosine, -sine], axis=0), 0.0)

    cosine, sine = phases(ky[:, None], lax.iota(jnp.int32, extent)[None, :], size)
    y_back = jnp.concatenate([cosine, -sine], axis=0) * (1.0 / (size * size))

    row = lax.iota(jnp.int32, count_z * TILE)
    z = row // TILE * depth_block + here[0] * share + row % TILE % share
    cosine, sine = phases(z[:, None], kz[None, :], depth_size)
    both = jnp.concatenate([cosine, -sine], axis=1) * (1.0 / (size * depth_size))
    component = (row % TILE // share)[:, None]
    z_back = jnp.concatenate(
        [jnp.where(component == 0, both, 0.0), jnp.where(component == 1, both, 0.0)], axis=1
    )

    forward, backward, turns = transform_tables(extent, size)
    out_rows = 2 * (block_x // count_z) + TILE
    return pl.pallas_call(
        functools.partial(image_kernel, counts + (top_rows,)),
        out_shape=jax.ShapeDtypeStruct((count_x * group, out_rows, LANES), f32),
        compiler_params=pltpu.CompilerParams(vmem_limit_bytes=56 * 1024 * 1024),
        name="images",
    )(
        gathered,
        y_table,
        z_table,
        *(jnp.asarray(t) for t in forward + backward),
        jnp.asarray(turns),
        top_kernel,
        side_kernel,
        y_back,
        z_back,
    )


def faces_kernel(magnetization, stiffness, z_first, z_last, x_first, x_last, y_faces):
    depth, across = stiffness.shape[:2]
    lane = lax.broadcasted_iota(jnp.int32, (across, LANES), 1)
    sides = jnp.zeros((across, LANES), f32)
    for field in range(4):
        ref = stiffness if field == 3 else magnetization.at[field]
        z_first[field] = ref[0]
        z_last[field] = ref[depth - 1]
        x_first[field] = ref[:, 0, :]
        x_last[field] = ref[:, across - 1, :]
        for z in range(depth):
            column = field * depth + z
            values = ref[z]
            sides = jnp.where(lane == column, values[:, 0:1], sides)
            sides = jnp.where(lane == column + 4 * depth, values[:, LANES - 1 : LANES], sides)
    y_faces[...] = sides


def exchange_kernel(
    magnetization,
    stiffness,
    z_next,
    z_before,
    x_next,
    x_before,
    y_next,
    y_before,
    out,
):
    depth, across = stiffness.shape[:2]
    lane = lax.broadcasted_iota(jnp.int32, (across, LANES), 1)
    sublane = lax.broadcasted_iota(jnp.int32, (across, LANES), 0)
    last_lane, first_lane = lane == LANES - 1, lane == 0
    last_row, first_row = sublane == across - 1, sublane == 0

    def weight(a, b):
        return 2.0 * a * b / (a + b)

    def one(z, field):
        ref = stiffness if field == 3 else magnetization.at[field]
        centre = ref[z]
        column = field * depth + z
        along = jnp.where(
            last_lane, y_next[:, column : column + 1], pltpu.roll(centre, LANES - 1, 1)
        )
        across_next = jnp.where(
            last_row, x_next[field, z : z + 1, :], pltpu.roll(centre, across - 1, 0)
        )
        along_before = y_before[:, 4 * depth + column : 4 * depth + column + 1]
        across_before = x_before[field, z : z + 1, :]
        return centre, along, across_next, along_before, across_before

    below_weight = weight(z_before[3], stiffness[0])
    below = [below_weight * (z_before[c] - magnetization[c, 0]) for c in range(3)]
    for z in range(depth):
        s, s_along, s_across, s_along_before, s_across_before = one(z, 3)
        s_above = stiffness[z + 1] if z + 1 < depth else z_next[3]
        w_along, w_across, w_above = weight(s, s_along), weight(s, s_across), weight(s, s_above)
        w_along_before = weight(s_along_before, s[:, 0:1])
        w_across_before = weight(s_across_before, s[0:1, :])
        for c in range(3):
            m, m_along, m_across, m_along_before, m_across_before = one(z, c)
            m_above = magnetization[c, z + 1] if z + 1 < depth else z_next[c]
            up = w_above * (m - m_above)
            flux_along = w_along * (m - m_along)
            flux_across = w_across * (m - m_across)
            edge_along = w_along_before * (m_along_before - m[:, 0:1])
            edge_across = w_across_before * (m_across_before - m[0:1, :])
            lower_along = jnp.where(first_lane, edge_along, pltpu.roll(flux_along, 1, 1))
            lower_across = jnp.where(first_row, edge_across, pltpu.roll(flux_across, 1, 0))
            total = (up - below[c]) + (flux_across - lower_across) + (flux_along - lower_along)
            out[c, z] = 2.0 * total
            below[c] = up


def shifted(block, axis, distance):
    count = lax.axis_size(axis)
    route = [(i, i + distance) for i in range(count) if 0 <= i + distance < count]
    return lax.ppermute(block, axis, route)


def exchange_halos(magnetization, stiffness):
    depth, across, along = stiffness.shape
    shape = jax.ShapeDtypeStruct
    z_first, z_last, x_first, x_last, y_faces = pl.pallas_call(
        faces_kernel,
        out_shape=[
            shape((4, across, along), f32),
            shape((4, across, along), f32),
            shape((4, depth, along), f32),
            shape((4, depth, along), f32),
            shape((across, LANES), f32),
        ],
        name="faces",
    )(magnetization, stiffness)
    z_next, z_before = shifted(z_first, "gz", -1), shifted(z_last, "gz", 1)
    x_next, x_before = shifted(x_first, "gx", -1), shifted(x_last, "gx", 1)
    if lax.axis_size("gy") == 2:
        other = lax.ppermute(y_faces, "gy", [(0, 1), (1, 0)])
        at = lax.axis_index("gy")
        y_next, y_before = jnp.where(at == 0, other, 0.0), jnp.where(at == 1, other, 0.0)
    else:
        y_next, y_before = shifted(y_faces, "gy", -1), shifted(y_faces, "gy", 1)
    return z_next, z_before, x_next, x_before, y_next, y_before


def exchange_of(magnetization, stiffness, halos):
    return pl.pallas_call(
        exchange_kernel,
        out_shape=jax.ShapeDtypeStruct(magnetization.shape, f32),
        compiler_params=pltpu.CompilerParams(vmem_limit_bytes=32 * 1024 * 1024),
        name="exchange",
    )(magnetization, stiffness, *halos)


def line_tables(counts, top_rows, kys, size):
    group = counts[1] * counts[2]
    row = np.arange(group * top_rows)
    j = np.arange(kys)
    start = np.arange(counts[0] * group) * kys
    steps, offsets = [], []
    for h in range(2):
        y = row // top_rows * top_rows * 2 + h * top_rows + row % top_rows
        for values, into in ((j, steps), (start, offsets)):
            angle = (np.outer(values, y) % size) * (2.0 * math.pi / size)
            into += [np.cos(angle), np.sin(angle)]
    steps = np.stack(steps).astype(np.float32)
    offsets = np.stack(offsets, axis=1).astype(np.float32)
    return steps, np.pad(offsets, ((0, 0), (0, TILE - 4), (0, 0)))


def depth_tables(group, kzs, depth):
    size = group * kzs
    kz = np.arange(size).reshape(group, kzs, 1)
    angle = (kz * np.arange(depth) % size) * (2.0 * math.pi / size)
    there = np.concatenate([np.cos(angle), -np.sin(angle)], axis=1).astype(np.float32)
    back = np.swapaxes(there, 1, 2)
    return there, back


def stacked_product(real, imag, tables, sign):
    if sign < 0:
        upper = jnp.concatenate([real, imag], axis=1)
        lower = jnp.concatenate([imag, -real], axis=1)
    else:
        upper = jnp.concatenate([real, -imag], axis=1)
        lower = jnp.concatenate([imag, real], axis=1)
    return dot3(jnp.concatenate([upper, lower], axis=0), tables)


def back_and_forth(real, imag, kernel, high, low, turns):
    tables = (high[...], low[...])
    rows = real.shape[0]
    total_real = total_imag = None
    for b in range(turns.shape[1]):
        cosine, sine = turns[0, b : b + 1, :], turns[1, b : b + 1, :]
        waves = stacked_product(
            real * cosine + imag * sine, imag * cosine - real * sine, tables, -1
        )
        wave_real, wave_imag = waves[:rows], waves[rows:]
        columns = slice(b * INNER, (b + 1) * INNER)
        weighted_real, weighted_imag = [], []
        for c in range(2):
            kernel_real, kernel_imag = kernel[c, 0, :, columns], kernel[c, 1, :, columns]
            weighted_real.append(kernel_real * wave_real + kernel_imag * wave_imag)
            weighted_imag.append(kernel_real * wave_imag - kernel_imag * wave_real)
        back = stacked_product(
            jnp.concatenate(weighted_real, axis=0),
            jnp.concatenate(weighted_imag, axis=0),
            tables,
            1,
        )
        back_real, back_imag = back[: 2 * rows], back[2 * rows :]
        if b == 0:
            total_real, total_imag = back_real, back_imag
        else:
            total_real = total_real + (back_real * cosine - back_imag * sine)
            total_imag = total_imag + (back_real * sine + back_imag * cosine)
    return [
        (total_real[c * rows : (c + 1) * rows], total_imag[c * rows : (c + 1) * rows])
        for c in range(2)
    ]


def lines_kernel(counts, here, gathered, steps, offsets, high, low, turns, kernel, out):
    count_x, count_y, count_z = counts
    group = count_y * count_z
    top_rows = gathered.shape[1]
    half = LANES // 2
    kys = kernel.shape[2]
    offset = offsets[here[0]]
    table = []
    for h in range(2):
        step_cos, step_sin = steps[2 * h], steps[2 * h + 1]
        offset_cos, offset_sin = offset[2 * h : 2 * h + 1], offset[2 * h + 1 : 2 * h + 2]
        table.append(step_cos * offset_cos - step_sin * offset_sin)
        table.append(-(step_sin * offset_cos + step_cos * offset_sin))
    blocks = [
        gathered[g * group : (g + 1) * group].reshape(group * top_rows, LANES)
        for g in range(count_x)
    ]
    mixed = dot3(jnp.concatenate(table, axis=0), split(jnp.concatenate(blocks, axis=1)))
    low_half, high_half = mixed[: 2 * kys], mixed[2 * kys :]
    lane = lax.broadcasted_iota(jnp.int32, (2 * kys, LANES), 1)
    pieces = []
    for g in range(0, count_x, 2):
        a = slice(g * LANES, (g + 1) * LANES)
        b = slice((g + 1) * LANES, (g + 2) * LANES)
        pieces.append(
            jnp.where(
                lane < half,
                low_half[:, a] + pltpu.roll(high_half[:, a], half, 1),
                pltpu.roll(low_half[:, b], half, 1) + high_half[:, b],
            )
        )
    lines = jnp.concatenate(pieces, axis=1)
    images = back_and_forth(lines[:kys], lines[kys:], kernel, high, low, turns)
    for c in range(2):
        block = jnp.concatenate(images[c], axis=0).T
        out[:, c * TILE : (c + 1) * TILE, :] = block.reshape(count_x * group, TILE, LANES)


def side_kernel_body(counts, here, gathered, there, back, high, low, turns, kernel, out):
    count_y, count_z = counts[1:]
    depth_block = gathered.shape[1]
    kzs = kernel.shape[2]
    blocks = [
        gathered[y * count_z : (y + 1) * count_z].reshape(count_z * depth_block, LANES)
        for y in range(count_y)
    ]
    lines = dot3(there[here[0]], split(jnp.concatenate(blocks, axis=1)))
    images = back_and_forth(lines[:kzs], lines[kzs:], kernel, high, low, turns)
    scale = 1.0 / (count_y * count_z * kzs * kernel.shape[3])
    for c in range(2):
        image = dot3(back[here[0]] * scale, split(jnp.concatenate(images[c], axis=0)))
        for y in range(count_y):
            for z in range(count_z):
                out[y * count_z + z, c * depth_block : (c + 1) * depth_block, :] = image[
                    z * depth_block : (z + 1) * depth_block, y * LANES : (y + 1) * LANES
                ]


def rows_kernel(counts, arrived, side, high, low, turns, out):
    count_y, count_z = counts[1:]
    per_turn = arrived.shape[0] // turns.shape[1]
    half = LANES // 2
    lane = lax.broadcasted_iota(jnp.int32, (2 * TILE, LANES), 1)
    real, imag = [], []
    for b in range(turns.shape[1]):
        real_pieces, imag_pieces = [], []
        for g in range(b * per_turn, (b + 1) * per_turn, 2):
            first, second = arrived[g], arrived[g + 1]
            real_pieces.append(jnp.where(lane < half, first, pltpu.roll(second, half, 1)))
            imag_pieces.append(jnp.where(lane < half, pltpu.roll(first, half, 1), second))
        real.append(jnp.concatenate(real_pieces, axis=1))
        imag.append(jnp.concatenate(imag_pieces, axis=1))
    back = stacked_product(
        jnp.concatenate(real, axis=0), jnp.concatenate(imag, axis=0), (high[...], low[...]), 1
    )
    middle = back.shape[0] // 2
    size = turns.shape[1] * INNER
    total = None
    for b in range(turns.shape[1]):
        part = slice(b * 2 * TILE, (b + 1) * 2 * TILE)
        term = back[:middle][part] * turns[0, b : b + 1, :]
        term = term - back[middle:][part] * turns[1, b : b + 1, :]
        total = term if b == 0 else total + term
    total = total * (1.0 / (size * size))
    for y in range(count_y):
        for z in range(count_z):
            out[y * count_z + z, 0 : 2 * TILE, :] = total[:, y * LANES : (y + 1) * LANES]
    out[:, 2 * TILE :, :] = side[...]


def sum_kernel(exchange_grad, arrived, out):
    depth = exchange_grad.shape[1]
    group = arrived.shape[0]
    side = [None, None]
    top = [None, None]
    for c in range(2):
        rows = slice(2 * TILE + c * depth, 2 * TILE + (c + 1) * depth)
        total = arrived[0, rows, :]
        for p in range(1, group):
            total = total + arrived[p, rows, :]
        side[c] = total
        top[c] = arrived[:, c * TILE : (c + 1) * TILE, :].reshape(group * TILE, LANES)
    for z in range(depth):
        out[0, z] = exchange_grad[0, z] + top[0]
        out[1, z] = exchange_grad[1, z] + top[1] + side[0][z : z + 1]
        out[2, z] = exchange_grad[2, z] + side[1][z : z + 1]


MIB = 1024 * 1024
SMEM = pl.BlockSpec(memory_space=pltpu.SMEM)
VMEM = pl.BlockSpec(memory_space=pltpu.VMEM)


def call(body, name, shape, limit, *operands, scalars=0):
    return pl.pallas_call(
        body,
        out_shape=jax.ShapeDtypeStruct(shape, f32),
        in_specs=[SMEM] * scalars + [VMEM] * (len(operands) - scalars),
        out_specs=VMEM,
        compiler_params=pltpu.CompilerParams(vmem_limit_bytes=limit * MIB),
        name=name,
    )(*operands)


def fast_on_device(magnetization, stiffness, residual_top, residual_side, top_kernel, side_kernel):
    counts = tuple(lax.axis_size(axis) for axis in ALL)
    count_x, count_y, count_z = counts
    group = count_y * count_z
    devices = count_x * group
    block_x, block_y = residual_top.shape
    depth_block = stiffness.shape[0]
    top_rows = block_y // 2
    kys, size = top_kernel.shape[2:]
    kzs = side_kernel.shape[2]
    extent = count_x * block_x
    here = [lax.axis_index(axis) for axis in ALL]
    plane_index = here[1] * count_z + here[2]
    index = (here[0] * group + plane_index).reshape(1)
    plane_index = plane_index.reshape(1)
    (high, low), _, turns = transform_tables(extent, size)
    high, low, turns = jnp.asarray(high), jnp.asarray(low), jnp.asarray(turns)
    steps, offsets = line_tables(counts, top_rows, kys, size)
    there, back = depth_tables(group, kzs, depth_block * count_z)

    piece = residual_top.T.reshape(2, top_rows, block_x)
    piece = jnp.concatenate([piece[0], piece[1]], axis=1)
    sent = jnp.broadcast_to(piece[None], (devices, top_rows, LANES))
    gathered = lax.all_to_all(sent, ALL, 0, 0, tiled=True)

    sent = jnp.broadcast_to(residual_side.T[None], (group, depth_block, LANES))
    side_gathered = lax.all_to_all(sent, ("gy", "gz"), 0, 0, tiled=True)

    halos = exchange_halos(magnetization, stiffness)
    gathered, side_gathered, halos = lax.optimization_barrier((gathered, side_gathered, halos))

    lines = call(
        functools.partial(lines_kernel, counts),
        "lines",
        (devices, 2 * TILE, LANES),
        24,
        index,
        gathered,
        jnp.asarray(steps),
        jnp.asarray(offsets),
        high,
        low,
        turns,
        top_kernel,
        scalars=1,
    )
    arrived = lax.all_to_all(lines, ALL, 0, 0, tiled=True)
    side = call(
        functools.partial(side_kernel_body, counts),
        "side",
        (group, 2 * depth_block, LANES),
        16,
        plane_index,
        side_gathered,
        jnp.asarray(there),
        jnp.asarray(back),
        high,
        low,
        turns,
        side_kernel,
        scalars=1,
    )
    exchange_grad = exchange_of(magnetization, stiffness, halos)
    arrived, side, exchange_grad = lax.optimization_barrier((arrived, side, exchange_grad))
    rows = call(
        functools.partial(rows_kernel, counts),
        "rows",
        (group, 2 * TILE + 2 * depth_block, LANES),
        16,
        arrived,
        side,
        high,
        low,
        turns,
    )
    arrived = lax.all_to_all(rows, ("gy", "gz"), 0, 0, tiled=True)
    return call(sum_kernel, "gradient", magnetization.shape, 16, exchange_grad, arrived)


def fits(counts, stiffness, residual_top, residual_side, top_kernel, side_kernel):
    count_x, count_y, count_z = counts
    block_x, block_y = residual_top.shape
    group = count_y * count_z
    return (
        2 * block_x == LANES
        and 2 * top_kernel.shape[2] == LANES
        and stiffness.shape[2] == LANES
        and block_x == group * TILE
        and block_y * group == count_x * block_x == INNER
        and count_y * LANES == INNER
        and block_y % 16 == 0
        and count_x % 2 == 0
        and (count_x * group) % (2 * top_kernel.shape[3] // INNER) == 0
        and INNER == top_kernel.shape[2] * count_z
        and stiffness.shape[0] % 16 == 0
        and side_kernel.shape[2] % 16 == 0
    )


def on_device(magnetization, stiffness, residual_top, residual_side, top_kernel, side_kernel):
    counts = tuple(lax.axis_size(axis) for axis in ALL)
    count_x, count_y, count_z = counts
    if fits(counts, stiffness, residual_top, residual_side, top_kernel, side_kernel):
        return fast_on_device(
            magnetization, stiffness, residual_top, residual_side, top_kernel, side_kernel
        )
    devices = count_x * count_y * count_z
    depth_block = stiffness.shape[0]
    block_x, block_y = residual_top.shape
    top_rows = block_y // 2
    share = depth_block // count_x

    top_piece = residual_top.T.reshape(2, top_rows, block_x)
    top_piece = jnp.concatenate([top_piece[0], top_piece[1]], axis=1)
    side_piece = lax.dynamic_slice_in_dim(
        residual_side.T, lax.axis_index("gx") * share, share, axis=0
    )
    piece = jnp.concatenate(
        [top_piece, side_piece, jnp.zeros((TILE - share, LANES), f32)], axis=0
    )
    rows = piece.shape[0]
    sent = jnp.broadcast_to(piece[None], (devices, rows, LANES)).reshape(devices * rows, LANES)
    gathered = lax.all_to_all(sent, ALL, 0, 0, tiled=True).reshape(devices, rows, LANES)

    exchange_grad = exchange_of(
        magnetization, stiffness, exchange_halos(magnetization, stiffness)
    )

    parts = image_parts(
        gathered, top_kernel, side_kernel, counts, block_x, top_rows, depth_block
    )
    rows = parts.shape[1]
    arrived = lax.all_to_all(parts.reshape(devices * rows, LANES), ALL, 0, 0, tiled=True)
    arrived = arrived.reshape(devices, rows, LANES)
    top_sum = jnp.sum(arrived[:, : rows - TILE], axis=0)
    side_sum = jnp.sum(
        arrived[:, rows - TILE :].reshape(count_x, count_y * count_z, TILE, LANES), axis=1
    )
    side = side_sum[:, : 2 * share].reshape(count_x, 2, share, LANES)
    side = jnp.swapaxes(side, 0, 1).reshape(2, depth_block, 1, LANES)
    top = lax.all_gather(top_sum, "gz", axis=0)
    top = jnp.swapaxes(top.reshape(count_z, 2, block_x // count_z, LANES), 0, 1)
    top = top.reshape(2, 1, block_x, LANES)
    return jnp.stack(
        [
            exchange_grad[0] + top[0],
            exchange_grad[1] + top[1] + side[0],
            exchange_grad[2] + side[1],
        ]
    )


def solution(mesh):
    placed = (
        P(None, "gz", "gx", "gy"),
        P("gz", "gx", "gy"),
        P("gx", ("gy", "gz")),
        P("gy", "gz"),
        P(None, None, ("gx", "gy", "gz"), None),
        P(None, None, ("gy", "gz"), None),
    )
    return jax.shard_map(
        on_device, mesh=mesh, in_specs=placed, out_specs=P(None, "gz", "gx", "gy"), check_vma=False
    )
```

```python
import functools
import math

import jax
import jax.numpy as jnp
import ml_dtypes
import numpy as np
from jax import lax
from jax.experimental import pallas as pl
from jax.experimental.pallas import tpu as pltpu
from jax.sharding import PartitionSpec as P

LANES = 128
TILE = 8
INNER = 256
ALL = ("gx", "gy", "gz")
f32 = jnp.float32
bf16 = jnp.bfloat16
MIB = 1024 * 1024
SMEM = pl.BlockSpec(memory_space=pltpu.SMEM)
VMEM = pl.BlockSpec(memory_space=pltpu.VMEM)
HBM = pl.BlockSpec(memory_space=pltpu.HBM)


def split(values):
    high = values.astype(bf16)
    return high, (values - high.astype(f32)).astype(bf16)


def dot3(left, right):
    high, low = split(left)
    def one(a, b):
        return lax.dot_general(a, b, (((1,), (0,)), ((), ())), preferred_element_type=f32)
    return one(high, right[0]) + one(low, right[0]) + one(high, right[1])


def transform_tables(extent, size):
    x = np.arange(extent)
    angle = (np.outer(x, np.arange(INNER)) % size) * (2.0 * math.pi / size)
    forward = np.concatenate([np.cos(angle), np.sin(angle)], 0).astype(np.float32)
    backward = np.concatenate([np.cos(angle).T, np.sin(angle).T], 0).astype(np.float32)

    def parts(table):
        high = table.astype(ml_dtypes.bfloat16)
        return high, (table - high.astype(np.float32)).astype(ml_dtypes.bfloat16)

    outer = size // INNER
    turn = (np.outer(np.arange(outer), x) % outer) * (2.0 * math.pi / outer)
    turns = np.stack([np.cos(turn), np.sin(turn)]).astype(np.float32)
    return parts(forward), parts(backward), turns


def phases(first, second, size):
    angle = (first * second % size).astype(f32) * (2.0 * math.pi / size)
    return jnp.cos(angle), jnp.sin(angle)


def image_kernel(
    counts, gathered, y_table, z_table, fh, fl, bh, bl, turns, top, side, y_back, z_back, out
):
    count_x, count_y, count_z, top_rows = counts
    group = count_y * count_z
    half = LANES // 2
    kys = top.shape[2]
    kzs = side.shape[2]
    forward = (fh[...], fl[...])
    backward = (bh[...], bl[...])

    blocks = [
        gathered[g * group : (g + 1) * group, 0:top_rows, :].reshape(group * top_rows, LANES)
        for g in range(count_x)
    ]
    mixed = dot3(y_table[...], split(jnp.concatenate(blocks, axis=1)))
    low_half, high_half = mixed[: 2 * kys], mixed[2 * kys :]
    lane = lax.broadcasted_iota(jnp.int32, (2 * kys, LANES), 1)
    pieces = []
    for g in range(0, count_x, 2):
        a = slice(g * LANES, (g + 1) * LANES)
        b = slice((g + 1) * LANES, (g + 2) * LANES)
        pieces.append(
            jnp.where(
                lane < half,
                low_half[:, a] + pltpu.roll(high_half[:, a], half, 1),
                pltpu.roll(low_half[:, b], half, 1) + high_half[:, b],
            )
        )
    top_lines = jnp.concatenate(pieces, axis=1)

    side_blocks = []
    for y in range(count_y):
        rows = [
            gathered[(x * count_y + y) * count_z + z, top_rows : top_rows + TILE, :]
            for x in range(count_x)
            for z in range(count_z)
        ]
        side_blocks.append(jnp.concatenate(rows, axis=0))
    side_lines = dot3(z_table[...], split(jnp.concatenate(side_blocks, axis=1)))

    real = jnp.concatenate([top_lines[:kys], side_lines[:kzs]], axis=0)
    imag = jnp.concatenate([top_lines[kys:], side_lines[kzs:]], axis=0)
    rows = kys + kzs
    total_real = total_imag = None
    for b in range(turns.shape[1]):
        cosine, sine = turns[0, b : b + 1, :], turns[1, b : b + 1, :]
        turned_real = real * cosine + imag * sine
        turned_imag = imag * cosine - real * sine
        waves = dot3(
            jnp.concatenate(
                [
                    jnp.concatenate([turned_real, turned_imag], axis=1),
                    jnp.concatenate([turned_imag, -turned_real], axis=1),
                ],
                axis=0,
            ),
            forward,
        )
        wave_real, wave_imag = waves[:rows], waves[rows:]
        columns = slice(b * INNER, (b + 1) * INNER)
        weighted_real, weighted_imag = [], []
        for c in range(2):
            for kernel, part in ((top, slice(0, kys)), (side, slice(kys, rows))):
                kernel_real, kernel_imag = kernel[c, 0, :, columns], kernel[c, 1, :, columns]
                weighted_real.append(
                    kernel_real * wave_real[part] + kernel_imag * wave_imag[part]
                )
                weighted_imag.append(
                    kernel_real * wave_imag[part] - kernel_imag * wave_real[part]
                )
        weighted_real = jnp.concatenate(weighted_real, axis=0)
        weighted_imag = jnp.concatenate(weighted_imag, axis=0)
        back = dot3(
            jnp.concatenate(
                [
                    jnp.concatenate([weighted_real, -weighted_imag], axis=1),
                    jnp.concatenate([weighted_imag, weighted_real], axis=1),
                ],
                axis=0,
            ),
            backward,
        )
        back_real, back_imag = back[: 2 * rows], back[2 * rows :]
        if b == 0:
            total_real, total_imag = back_real, back_imag
        else:
            total_real = total_real + (back_real * cosine - back_imag * sine)
            total_imag = total_imag + (back_real * sine + back_imag * cosine)

    y_parts = split(y_back[...])
    depth_rows = []
    quarter = (out.shape[1] - TILE) // 2
    block_x = quarter * count_z
    for c in range(2):
        start = c * rows
        lines = jnp.concatenate(
            [total_real[start : start + kys], total_imag[start : start + kys]], axis=0
        )
        image = dot3(lines.T, y_parts)
        for x in range(count_x):
            for y in range(count_y):
                for z in range(count_z):
                    first = x * block_x + z * quarter
                    out[
                        (x * count_y + y) * count_z + z, c * quarter : (c + 1) * quarter, :
                    ] = image[first : first + quarter, y * LANES : (y + 1) * LANES]
        depth_rows.append(total_real[start + kys : start + rows])
        depth_rows.append(total_imag[start + kys : start + rows])
    side_image = dot3(z_back[...], split(jnp.concatenate(depth_rows, axis=0)))
    for y in range(count_y):
        for z in range(count_z):
            block = side_image[z * TILE : (z + 1) * TILE, y * LANES : (y + 1) * LANES]
            for x in range(count_x):
                out[(x * count_y + y) * count_z + z, 2 * quarter :, :] = block


def image_parts(gathered, top_kernel, side_kernel, counts, block_x, top_rows, depth_block):
    count_x, count_y, count_z = counts
    group = count_y * count_z
    here = [lax.axis_index(axis) for axis in ALL]
    kys, size = top_kernel.shape[2:]
    kzs = side_kernel.shape[2]
    depth_size = kzs * group
    extent = count_y * LANES
    share = depth_block // count_x
    block_y = top_rows * 2

    ky = ((here[0] * count_y + here[1]) * count_z + here[2]) * kys + lax.iota(jnp.int32, kys)
    kz = (here[1] * count_z + here[2]) * kzs + lax.iota(jnp.int32, kzs)

    row = lax.iota(jnp.int32, group * top_rows)
    y_tables = []
    for h in range(2):
        y = row // top_rows * block_y + h * top_rows + row % top_rows
        cosine, sine = phases(ky[:, None], y[None, :], size)
        y_tables += [cosine, -sine]
    y_table = jnp.concatenate(y_tables, axis=0)

    row = lax.iota(jnp.int32, count_x * count_z * TILE)
    inside = row % TILE
    z = row // TILE % count_z * depth_block + row // (TILE * count_z) * share + inside
    cosine, sine = phases(kz[:, None], z[None, :], depth_size)
    z_table = jnp.where((inside < share)[None, :], jnp.concatenate([cosine, -sine], axis=0), 0.0)

    cosine, sine = phases(ky[:, None], lax.iota(jnp.int32, extent)[None, :], size)
    y_back = jnp.concatenate([cosine, -sine], axis=0) * (1.0 / (size * size))

    row = lax.iota(jnp.int32, count_z * TILE)
    z = row // TILE * depth_block + here[0] * share + row % TILE % share
    cosine, sine = phases(z[:, None], kz[None, :], depth_size)
    both = jnp.concatenate([cosine, -sine], axis=1) * (1.0 / (size * depth_size))
    component = (row % TILE // share)[:, None]
    z_back = jnp.concatenate(
        [jnp.where(component == 0, both, 0.0), jnp.where(component == 1, both, 0.0)], axis=1
    )

    forward, backward, turns = transform_tables(extent, size)
    out_rows = 2 * (block_x // count_z) + TILE
    return pl.pallas_call(
        functools.partial(image_kernel, counts + (top_rows,)),
        out_shape=jax.ShapeDtypeStruct((count_x * group, out_rows, LANES), f32),
        compiler_params=pltpu.CompilerParams(vmem_limit_bytes=56 * 1024 * 1024),
        name="images",
    )(
        gathered,
        y_table,
        z_table,
        *(jnp.asarray(t) for t in forward + backward),
        jnp.asarray(turns),
        top_kernel,
        side_kernel,
        y_back,
        z_back,
    )


def copies_of(pairs, semaphores):
    started = [
        pltpu.make_async_copy(source, target, semaphores.at[i])
        for i, (source, target) in enumerate(pairs)
    ]
    for copy in started:
        copy.start()
    return started


def faces_kernel(
    magnetization, stiffness, z_first, z_last, x_first, x_last, y_faces, m, s, semaphores, sent
):
    depth, across = stiffness.shape[:2]
    loads = copies_of(
        [(stiffness, s)] + [(magnetization.at[c], m.at[c]) for c in range(3)], semaphores
    )
    lane = lax.broadcasted_iota(jnp.int32, (across, LANES), 1)
    first = jnp.zeros((across, LANES), f32)
    last = jnp.zeros((across, LANES), f32)
    stores = []
    for field, load in ((3, loads[0]), (0, loads[1]), (1, loads[2]), (2, loads[3])):
        load.wait()
        ref = s if field == 3 else m.at[field]
        for k, (target, z) in enumerate(((z_first, 0), (z_last, depth - 1))):
            store = pltpu.make_async_copy(ref.at[z], target.at[field], sent.at[2 * field + k])
            store.start()
            stores.append(store)
        x_first[field] = ref[:, 0, :]
        x_last[field] = ref[:, across - 1, :]
        for z in range(depth):
            column = field * depth + z
            turned = pltpu.roll(ref[z], column, 1) if column else ref[z]
            first = jnp.where(lane == column, turned, first)
            last = jnp.where(lane == (column - 1) % LANES, turned, last)
    y_faces[...] = jnp.where(
        lane < LANES // 2, first, pltpu.roll(last, LANES // 2 + 1, 1)
    )
    for store in stores:
        store.wait()


def twice_weight(a, b):
    return 4.0 * a * b / (a + b)


def exchange_kernel(
    counts,
    here,
    magnetization,
    stiffness,
    z_next,
    z_before,
    x_next,
    x_before,
    y_next,
    y_before,
    y_faces,
    out,
    m,
    s,
    semaphores,
):
    depth, across = stiffness.shape[:2]
    chunk = depth // 4
    pairs = []
    for k in range(4):
        layers = slice(k * chunk, (k + 1) * chunk)
        pairs.append((stiffness.at[layers], s.at[layers]))
        pairs.append((magnetization.at[:, layers], m.at[:, layers]))
    loads = copies_of(pairs, semaphores)

    count_x, count_y, count_z = counts
    at_z = here[0] % count_z
    at_y = here[0] // count_z % count_y
    at_x = here[0] // (count_z * count_y)

    def inside(condition, values):
        return jnp.where(condition, values, 0.0)

    lane = lax.broadcasted_iota(jnp.int32, (across, LANES), 1)
    row = lax.broadcasted_iota(jnp.int32, (across, LANES), 0)
    first_lane, last_lane, last_row = lane == 0, lane == LANES - 1, row == across - 1
    half = LANES // 2

    stiff = (lane >= 3 * depth) & (lane < 4 * depth)

    def y_edge(own, halo, present):
        halo_stiffness = inside(present, halo)
        weight = twice_weight(jnp.where(stiff, own, 1.0), jnp.where(stiff, halo_stiffness, 1.0))
        spread = pltpu.roll(weight, LANES - 3 * depth, 1)
        for c in (1, 2):
            spread = jnp.where(
                lane >= c * depth, pltpu.roll(weight, LANES - (3 - c) * depth, 1), spread
            )
        return spread * (own - halo)

    own = y_faces[...]
    after = y_edge(pltpu.roll(own, half, 1), y_next[...], at_y < count_y - 1)
    before = y_edge(own, pltpu.roll(y_before[...], half, 1), at_y > 0)

    loads[0].wait()
    loads[1].wait()
    below_weight = twice_weight(inside(at_z > 0, z_before[3]), s[0])
    below = [below_weight * (z_before[c] - m[c, 0]) for c in range(3)]
    for z in range(depth):
        if z % chunk == 0 and z + chunk < depth:
            for load in loads[2 * (z // chunk + 1) : 2 * (z // chunk + 2)]:
                load.wait()
        centre = s[z]
        above = s[z + 1] if z + 1 < depth else inside(at_z < count_z - 1, z_next[3])
        weight_z = twice_weight(centre, above)
        weight_x = jnp.where(
            last_row, 0.0, twice_weight(centre, pltpu.roll(centre, across - 1, 0))
        )
        weight_y = jnp.where(
            last_lane, 0.0, twice_weight(centre, pltpu.roll(centre, LANES - 1, 1))
        )
        for c in range(3):
            column = c * depth + z
            values = m[c, z]
            upper = m[c, z + 1] if z + 1 < depth else z_next[c]
            up = weight_z * (values - upper)
            flux_x = weight_x * (values - pltpu.roll(values, across - 1, 0))
            flux_y = weight_y * (values - pltpu.roll(values, LANES - 1, 1))
            total = (up - below[c]) + (flux_x - pltpu.roll(flux_x, 1, 0))
            total = total + (flux_y - pltpu.roll(flux_y, 1, 1))
            edge = jnp.where(
                first_lane,
                before[:, column : column + 1],
                jnp.where(last_lane, after[:, column : column + 1], 0.0),
            )
            out[c, z] = total + edge
            below[c] = up

    for edge_row, halo, present in (
        (across - 1, x_next, at_x < count_x - 1),
        (0, x_before, at_x > 0),
    ):
        weight = twice_weight(s[:, edge_row, :], inside(present, halo[3]))
        for c in range(3):
            out[c, :, edge_row, :] += weight * (m[c, :, edge_row, :] - halo[c])


def ring(block, axis, distance):
    count = lax.axis_size(axis)
    return lax.ppermute(block, axis, [(i, (i + distance) % count) for i in range(count)])


def exchange_halos(magnetization, stiffness):
    depth, across, along = stiffness.shape
    shape = jax.ShapeDtypeStruct
    z_first, z_last, x_first, x_last, y_faces = pl.pallas_call(
        faces_kernel,
        in_specs=[HBM, HBM],
        out_specs=[HBM, HBM, VMEM, VMEM, VMEM],
        out_shape=[
            shape((4, across, along), f32),
            shape((4, across, along), f32),
            shape((4, depth, along), f32),
            shape((4, depth, along), f32),
            shape((across, LANES), f32),
        ],
        scratch_shapes=[
            pltpu.VMEM(magnetization.shape, f32),
            pltpu.VMEM(stiffness.shape, f32),
            pltpu.SemaphoreType.DMA((4,)),
            pltpu.SemaphoreType.DMA((8,)),
        ],
        compiler_params=pltpu.CompilerParams(vmem_limit_bytes=8 * MIB),
        name="faces",
    )(magnetization, stiffness)
    z_next, z_before = ring(z_first, "gz", -1), ring(z_last, "gz", 1)
    x_next, x_before = ring(x_first, "gx", -1), ring(x_last, "gx", 1)
    y_next = ring(y_faces, "gy", -1)
    y_before = y_next if lax.axis_size("gy") == 2 else ring(y_faces, "gy", 1)
    return z_next, z_before, x_next, x_before, y_next, y_before, y_faces


def exchange_of(counts, index, magnetization, stiffness, halos):
    return pl.pallas_call(
        functools.partial(exchange_kernel, counts),
        in_specs=[SMEM, HBM, HBM] + [VMEM] * len(halos),
        out_specs=VMEM,
        out_shape=jax.ShapeDtypeStruct(magnetization.shape, f32),
        scratch_shapes=[
            pltpu.VMEM(magnetization.shape, f32),
            pltpu.VMEM(stiffness.shape, f32),
            pltpu.SemaphoreType.DMA((8,)),
        ],
        compiler_params=pltpu.CompilerParams(vmem_limit_bytes=16 * MIB),
        name="exchange",
    )(index, magnetization, stiffness, *halos)


def line_tables(counts, top_rows, kys, size):
    group = counts[1] * counts[2]
    row = np.arange(group * top_rows)
    j = np.arange(kys)
    start = np.arange(counts[0] * group) * kys
    steps, offsets = [], []
    for h in range(2):
        y = row // top_rows * top_rows * 2 + h * top_rows + row % top_rows
        for values, into in ((j, steps), (start, offsets)):
            angle = (np.outer(values, y) % size) * (2.0 * math.pi / size)
            into += [np.cos(angle), np.sin(angle)]
    steps = np.stack(steps).astype(np.float32)
    offsets = np.stack(offsets, axis=1).astype(np.float32)
    return steps, np.pad(offsets, ((0, 0), (0, TILE - 4), (0, 0)))


def depth_tables(counts, kzs, depth_block):
    count_x, count_y, count_z = counts
    size = count_y * count_z * kzs
    share = depth_block // count_x
    kz = np.arange(size).reshape(count_y * count_z, kzs, 1)

    def table(z):
        angle = (kz * z % size) * (2.0 * math.pi / size)
        return np.concatenate([np.cos(angle), -np.sin(angle)], axis=1).astype(np.float32)

    row = np.arange(count_x * count_z * TILE)
    within = row % TILE
    z = row // TILE % count_z * depth_block + row // (TILE * count_z) * share + within
    there = np.where(within < share, table(z), np.float32(0.0))
    return there, np.swapaxes(table(np.arange(depth_block * count_z)), 1, 2)


def stacked_product(real, imag, tables, sign):
    if sign < 0:
        upper = jnp.concatenate([real, imag], axis=1)
        lower = jnp.concatenate([imag, -real], axis=1)
    else:
        upper = jnp.concatenate([real, -imag], axis=1)
        lower = jnp.concatenate([imag, real], axis=1)
    return dot3(jnp.concatenate([upper, lower], axis=0), tables)


def back_and_forth(real, imag, columns_of, tables, turns):
    rows = real.shape[0]
    total_real = total_imag = None
    for b in range(turns.shape[1]):
        cosine, sine = turns[0, b : b + 1, :], turns[1, b : b + 1, :]
        waves = stacked_product(
            real * cosine + imag * sine, imag * cosine - real * sine, tables, -1
        )
        wave_real, wave_imag = waves[:rows], waves[rows:]
        kernel = columns_of(b)
        weighted_real, weighted_imag = [], []
        for c in range(2):
            kernel_real, kernel_imag = kernel[c, 0], kernel[c, 1]
            weighted_real.append(kernel_real * wave_real + kernel_imag * wave_imag)
            weighted_imag.append(kernel_real * wave_imag - kernel_imag * wave_real)
        back = stacked_product(
            jnp.concatenate(weighted_real, axis=0),
            jnp.concatenate(weighted_imag, axis=0),
            tables,
            1,
        )
        back_real, back_imag = back[: 2 * rows], back[2 * rows :]
        if b == 0:
            total_real, total_imag = back_real, back_imag
        else:
            total_real = total_real + (back_real * cosine - back_imag * sine)
            total_imag = total_imag + (back_real * sine + back_imag * cosine)
    return [
        (total_real[c * rows : (c + 1) * rows], total_imag[c * rows : (c + 1) * rows])
        for c in range(2)
    ]


def lines_kernel(
    counts,
    here,
    gathered,
    steps_from,
    offsets_from,
    high_from,
    low_from,
    turns_from,
    kernel_from,
    out,
    steps,
    offset,
    high,
    low,
    turns,
    kernel,
    semaphores,
):
    count_x, count_y, count_z = counts
    group = count_y * count_z
    top_rows = LANES // group
    half = LANES // 2
    kys = kernel_from.shape[2]
    pairs = [
        (steps_from, steps),
        (offsets_from.at[here[0]], offset),
        (turns_from, turns),
        (high_from, high),
        (low_from, low),
    ]
    for b in range(kernel.shape[0]):
        pairs.append((kernel_from.at[:, :, :, pl.ds(b * INNER, INNER)], kernel.at[b]))
    loads = copies_of(pairs, semaphores)
    loads[0].wait()
    loads[1].wait()
    table = []
    for h in range(2):
        step_cos, step_sin = steps[2 * h], steps[2 * h + 1]
        offset_cos, offset_sin = offset[2 * h : 2 * h + 1], offset[2 * h + 1 : 2 * h + 2]
        table.append(step_cos * offset_cos - step_sin * offset_sin)
        table.append(-(step_sin * offset_cos + step_cos * offset_sin))
    blocks = [
        gathered[g * group : (g + 1) * group, 0:top_rows, :].reshape(group * top_rows, LANES)
        for g in range(count_x)
    ]
    mixed = dot3(jnp.concatenate(table, axis=0), split(jnp.concatenate(blocks, axis=1)))
    low_half, high_half = mixed[: 2 * kys], mixed[2 * kys :]
    lane = lax.broadcasted_iota(jnp.int32, (2 * kys, LANES), 1)
    pieces = []
    for g in range(0, count_x, 2):
        a = slice(g * LANES, (g + 1) * LANES)
        b = slice((g + 1) * LANES, (g + 2) * LANES)
        pieces.append(
            jnp.where(
                lane < half,
                low_half[:, a] + pltpu.roll(high_half[:, a], half, 1),
                pltpu.roll(low_half[:, b], half, 1) + high_half[:, b],
            )
        )
    lines = jnp.concatenate(pieces, axis=1)
    for load in loads[2:5]:
        load.wait()

    def columns_of(b):
        loads[5 + b].wait()
        return kernel.at[b]

    images = back_and_forth(
        lines[:kys], lines[kys:], columns_of, (high[...], low[...]), turns
    )
    for c in range(2):
        block = jnp.concatenate(images[c], axis=0).T
        out[:, c * TILE : (c + 1) * TILE, :] = block.reshape(count_x * group, TILE, LANES)


def side_kernel_body(counts, here, gathered, there, back, high, low, turns, kernel, out):
    count_x, count_y, count_z = counts
    depth_block = out.shape[1] // 2
    top_rows = gathered.shape[1] - TILE
    kzs = kernel.shape[2]
    blocks = []
    for y in range(count_y):
        rows = [
            gathered[(x * count_y + y) * count_z + z, top_rows:, :]
            for x in range(count_x)
            for z in range(count_z)
        ]
        blocks.append(jnp.concatenate(rows, axis=0))
    lines = dot3(there[here[0]], split(jnp.concatenate(blocks, axis=1)))

    def columns_of(b):
        return kernel.at[:, :, :, b * INNER : (b + 1) * INNER]

    images = back_and_forth(
        lines[:kzs], lines[kzs:], columns_of, (high[...], low[...]), turns
    )
    scale = 1.0 / (count_y * count_z * kzs * kernel.shape[3])
    for c in range(2):
        image = dot3(back[here[0]] * scale, split(jnp.concatenate(images[c], axis=0)))
        for y in range(count_y):
            for z in range(count_z):
                out[y * count_z + z, c * depth_block : (c + 1) * depth_block, :] = image[
                    z * depth_block : (z + 1) * depth_block, y * LANES : (y + 1) * LANES
                ]


def rows_kernel(counts, arrived, side, high, low, turns, out):
    count_y, count_z = counts[1:]
    per_turn = arrived.shape[0] // turns.shape[1]
    half = LANES // 2
    lane = lax.broadcasted_iota(jnp.int32, (2 * TILE, LANES), 1)
    real, imag = [], []
    for b in range(turns.shape[1]):
        real_pieces, imag_pieces = [], []
        for g in range(b * per_turn, (b + 1) * per_turn, 2):
            first, second = arrived[g], arrived[g + 1]
            real_pieces.append(jnp.where(lane < half, first, pltpu.roll(second, half, 1)))
            imag_pieces.append(jnp.where(lane < half, pltpu.roll(first, half, 1), second))
        real.append(jnp.concatenate(real_pieces, axis=1))
        imag.append(jnp.concatenate(imag_pieces, axis=1))
    back = stacked_product(
        jnp.concatenate(real, axis=0), jnp.concatenate(imag, axis=0), (high[...], low[...]), 1
    )
    middle = back.shape[0] // 2
    size = turns.shape[1] * INNER
    total = None
    for b in range(turns.shape[1]):
        part = slice(b * 2 * TILE, (b + 1) * 2 * TILE)
        term = back[:middle][part] * turns[0, b : b + 1, :]
        term = term - back[middle:][part] * turns[1, b : b + 1, :]
        total = term if b == 0 else total + term
    total = total * (1.0 / (size * size))
    for y in range(count_y):
        for z in range(count_z):
            out[y * count_z + z, 0 : 2 * TILE, :] = total[:, y * LANES : (y + 1) * LANES]
    out[:, 2 * TILE :, :] = side[...]


def sum_kernel(exchange_grad, arrived, out):
    depth = exchange_grad.shape[1]
    group = arrived.shape[0]
    side = [None, None]
    top = [None, None]
    for c in range(2):
        rows = slice(2 * TILE + c * depth, 2 * TILE + (c + 1) * depth)
        total = arrived[0, rows, :]
        for p in range(1, group):
            total = total + arrived[p, rows, :]
        side[c] = total
        top[c] = arrived[:, c * TILE : (c + 1) * TILE, :].reshape(group * TILE, LANES)
    for z in range(depth):
        out[0, z] = exchange_grad[0, z] + top[0]
        out[1, z] = exchange_grad[1, z] + top[1] + side[0][z : z + 1]
        out[2, z] = exchange_grad[2, z] + side[1][z : z + 1]


def call(body, name, shape, limit, kinds, operands, scratch=()):
    return pl.pallas_call(
        body,
        out_shape=jax.ShapeDtypeStruct(shape, f32),
        in_specs=[{"s": SMEM, "v": VMEM, "h": HBM}[kind] for kind in kinds],
        out_specs=VMEM,
        scratch_shapes=list(scratch),
        compiler_params=pltpu.CompilerParams(vmem_limit_bytes=limit * MIB),
        name=name,
    )(*operands)


def residual_blocks(residual_top, residual_side, devices, share):
    block_x, block_y = residual_top.shape
    top_rows = block_y // 2
    top_piece = residual_top.T.reshape(2, top_rows, block_x)
    top_piece = jnp.concatenate([top_piece[0], top_piece[1]], axis=1)
    side_piece = lax.dynamic_slice_in_dim(
        residual_side.T, lax.axis_index("gx") * share, share, axis=0
    )
    piece = jnp.concatenate(
        [top_piece, side_piece, jnp.zeros((TILE - share, LANES), f32)], axis=0
    )
    return jnp.broadcast_to(piece[None], (devices,) + piece.shape)


def fast_on_device(magnetization, stiffness, residual_top, residual_side, top_kernel, side_kernel):
    counts = tuple(lax.axis_size(axis) for axis in ALL)
    count_x, count_y, count_z = counts
    group = count_y * count_z
    devices = count_x * group
    block_x, block_y = residual_top.shape
    depth_block = stiffness.shape[0]
    top_rows = block_y // 2
    kys, size = top_kernel.shape[2:]
    kzs = side_kernel.shape[2]
    extent = count_x * block_x
    here = [lax.axis_index(axis) for axis in ALL]
    plane_index = here[1] * count_z + here[2]
    index = (here[0] * group + plane_index).reshape(1)
    plane_index = plane_index.reshape(1)
    (high, low), _, turns = transform_tables(extent, size)
    high, low, turns = jnp.asarray(high), jnp.asarray(low), jnp.asarray(turns)
    steps, offsets = line_tables(counts, top_rows, kys, size)
    there, back = depth_tables(counts, kzs, depth_block)

    sent = residual_blocks(residual_top, residual_side, devices, depth_block // count_x)
    gathered = lax.all_to_all(sent, ALL, 0, 0, tiled=True)
    halos = exchange_halos(magnetization, stiffness)
    gathered, halos = lax.optimization_barrier((gathered, halos))

    lines = call(
        functools.partial(lines_kernel, counts),
        "lines",
        (devices, 2 * TILE, LANES),
        24,
        "svhhhhhh",
        (index, gathered, jnp.asarray(steps), jnp.asarray(offsets), high, low, turns, top_kernel),
        [
            pltpu.VMEM(steps.shape, f32),
            pltpu.VMEM(offsets.shape[1:], f32),
            pltpu.VMEM(high.shape, bf16),
            pltpu.VMEM(low.shape, bf16),
            pltpu.VMEM(turns.shape, f32),
            pltpu.VMEM((size // INNER, 2, 2, kys, INNER), f32),
            pltpu.SemaphoreType.DMA((5 + size // INNER,)),
        ],
    )
    arrived = lax.all_to_all(lines, ALL, 0, 0, tiled=True)
    side = call(
        functools.partial(side_kernel_body, counts),
        "side",
        (group, 2 * depth_block, LANES),
        16,
        "svvvvvvv",
        (
            plane_index,
            gathered,
            jnp.asarray(there),
            jnp.asarray(back),
            high,
            low,
            turns,
            side_kernel,
        ),
    )
    exchange_grad = exchange_of(counts, index, magnetization, stiffness, halos)
    arrived, side, exchange_grad = lax.optimization_barrier((arrived, side, exchange_grad))
    rows = call(
        functools.partial(rows_kernel, counts),
        "rows",
        (group, 2 * TILE + 2 * depth_block, LANES),
        16,
        "vvvvv",
        (arrived, side, high, low, turns),
    )
    arrived = lax.all_to_all(rows, ("gy", "gz"), 0, 0, tiled=True)
    return call(sum_kernel, "gradient", magnetization.shape, 16, "vv", (exchange_grad, arrived))


def fits(counts, stiffness, residual_top, residual_side, top_kernel, side_kernel):
    count_x, count_y, count_z = counts
    block_x, block_y = residual_top.shape
    group = count_y * count_z
    return (
        2 * block_x == LANES
        and 2 * top_kernel.shape[2] == LANES
        and stiffness.shape[2] == LANES
        and block_x == group * TILE
        and block_y * group == count_x * block_x == INNER
        and count_y * LANES == INNER
        and block_y % 16 == 0
        and count_x % 2 == 0
        and (count_x * group) % (2 * top_kernel.shape[3] // INNER) == 0
        and INNER == top_kernel.shape[2] * count_z
        and stiffness.shape[0] % 16 == 0
        and side_kernel.shape[2] % 16 == 0
    )


def on_device(magnetization, stiffness, residual_top, residual_side, top_kernel, side_kernel):
    counts = tuple(lax.axis_size(axis) for axis in ALL)
    count_x, count_y, count_z = counts
    if fits(counts, stiffness, residual_top, residual_side, top_kernel, side_kernel):
        return fast_on_device(
            magnetization, stiffness, residual_top, residual_side, top_kernel, side_kernel
        )
    devices = count_x * count_y * count_z
    depth_block = stiffness.shape[0]
    block_x, block_y = residual_top.shape
    top_rows = block_y // 2
    share = depth_block // count_x

    sent = residual_blocks(residual_top, residual_side, devices, share)
    rows = sent.shape[1]
    gathered = lax.all_to_all(sent, ALL, 0, 0, tiled=True)
    index = (
        (lax.axis_index("gx") * count_y + lax.axis_index("gy")) * count_z + lax.axis_index("gz")
    ).reshape(1)
    exchange_grad = exchange_of(
        counts, index, magnetization, stiffness, exchange_halos(magnetization, stiffness)
    )

    parts = image_parts(
        gathered, top_kernel, side_kernel, counts, block_x, top_rows, depth_block
    )
    rows = parts.shape[1]
    arrived = lax.all_to_all(parts.reshape(devices * rows, LANES), ALL, 0, 0, tiled=True)
    arrived = arrived.reshape(devices, rows, LANES)
    top_sum = jnp.sum(arrived[:, : rows - TILE], axis=0)
    side_sum = jnp.sum(
        arrived[:, rows - TILE :].reshape(count_x, count_y * count_z, TILE, LANES), axis=1
    )
    side = side_sum[:, : 2 * share].reshape(count_x, 2, share, LANES)
    side = jnp.swapaxes(side, 0, 1).reshape(2, depth_block, 1, LANES)
    top = lax.all_gather(top_sum, "gz", axis=0)
    top = jnp.swapaxes(top.reshape(count_z, 2, block_x // count_z, LANES), 0, 1)
    top = top.reshape(2, 1, block_x, LANES)
    return jnp.stack(
        [
            exchange_grad[0] + top[0],
            exchange_grad[1] + top[1] + side[0],
            exchange_grad[2] + side[1],
        ]
    )


def solution(mesh):
    placed = (
        P(None, "gz", "gx", "gy"),
        P("gz", "gx", "gy"),
        P("gx", ("gy", "gz")),
        P("gy", "gz"),
        P(None, None, ("gx", "gy", "gz"), None),
        P(None, None, ("gy", "gz"), None),
    )
    return jax.shard_map(
        on_device, mesh=mesh, in_specs=placed, out_specs=P(None, "gz", "gx", "gy"), check_vma=False
    )
```

```python
import functools
import math

import jax
import jax.numpy as jnp
import ml_dtypes
import numpy as np
from jax import lax
from jax.experimental import pallas as pl
from jax.experimental.pallas import tpu as pltpu
from jax.sharding import PartitionSpec as P

LANES = 128
TILE = 8
INNER = 256
ALL = ("gx", "gy", "gz")
f32 = jnp.float32
bf16 = jnp.bfloat16
MIB = 1024 * 1024
SMEM = pl.BlockSpec(memory_space=pltpu.SMEM)
VMEM = pl.BlockSpec(memory_space=pltpu.VMEM)
HBM = pl.BlockSpec(memory_space=pltpu.HBM)


def split(values):
    high = values.astype(bf16)
    return high, (values - high.astype(f32)).astype(bf16)


def dot3(left, right):
    high, low = split(left)
    def one(a, b):
        return lax.dot_general(a, b, (((1,), (0,)), ((), ())), preferred_element_type=f32)
    return one(high, right[0]) + one(low, right[0]) + one(high, right[1])


def call(body, name, shape, limit, kinds, operands, scratch=()):
    return pl.pallas_call(
        body,
        out_shape=jax.ShapeDtypeStruct(shape, f32),
        in_specs=[{"s": SMEM, "v": VMEM, "h": HBM}[kind] for kind in kinds],
        out_specs=VMEM,
        scratch_shapes=list(scratch),
        compiler_params=pltpu.CompilerParams(vmem_limit_bytes=limit * MIB),
        name=name,
    )(*operands)


def transform_tables(extent, size):
    x = np.arange(extent)
    angle = (np.outer(x, np.arange(INNER)) % size) * (2.0 * math.pi / size)
    forward = np.concatenate([np.cos(angle), np.sin(angle)], 0).astype(np.float32)
    backward = np.concatenate([np.cos(angle).T, np.sin(angle).T], 0).astype(np.float32)

    def parts(table):
        high = table.astype(ml_dtypes.bfloat16)
        return high, (table - high.astype(np.float32)).astype(ml_dtypes.bfloat16)

    outer = size // INNER
    turn = (np.outer(np.arange(outer), x) % outer) * (2.0 * math.pi / outer)
    turns = np.stack([np.cos(turn), np.sin(turn)]).astype(np.float32)
    return parts(forward), parts(backward), turns


def phases(first, second, size):
    angle = (first * second % size).astype(f32) * (2.0 * math.pi / size)
    return jnp.cos(angle), jnp.sin(angle)


def image_kernel(
    counts, gathered, y_table, z_table, fh, fl, bh, bl, turns, top, side, y_back, z_back, out
):
    count_x, count_y, count_z, top_rows = counts
    group = count_y * count_z
    half = LANES // 2
    kys = top.shape[2]
    kzs = side.shape[2]
    forward = (fh[...], fl[...])
    backward = (bh[...], bl[...])

    blocks = [
        gathered[g * group : (g + 1) * group, 0:top_rows, :].reshape(group * top_rows, LANES)
        for g in range(count_x)
    ]
    mixed = dot3(y_table[...], split(jnp.concatenate(blocks, axis=1)))
    low_half, high_half = mixed[: 2 * kys], mixed[2 * kys :]
    lane = lax.broadcasted_iota(jnp.int32, (2 * kys, LANES), 1)
    pieces = []
    for g in range(0, count_x, 2):
        a = slice(g * LANES, (g + 1) * LANES)
        b = slice((g + 1) * LANES, (g + 2) * LANES)
        pieces.append(
            jnp.where(
                lane < half,
                low_half[:, a] + pltpu.roll(high_half[:, a], half, 1),
                pltpu.roll(low_half[:, b], half, 1) + high_half[:, b],
            )
        )
    top_lines = jnp.concatenate(pieces, axis=1)

    side_blocks = []
    for y in range(count_y):
        rows = [
            gathered[(x * count_y + y) * count_z + z, top_rows : top_rows + TILE, :]
            for x in range(count_x)
            for z in range(count_z)
        ]
        side_blocks.append(jnp.concatenate(rows, axis=0))
    side_lines = dot3(z_table[...], split(jnp.concatenate(side_blocks, axis=1)))

    real = jnp.concatenate([top_lines[:kys], side_lines[:kzs]], axis=0)
    imag = jnp.concatenate([top_lines[kys:], side_lines[kzs:]], axis=0)
    rows = kys + kzs
    total_real = total_imag = None
    for b in range(turns.shape[1]):
        cosine, sine = turns[0, b : b + 1, :], turns[1, b : b + 1, :]
        turned_real = real * cosine + imag * sine
        turned_imag = imag * cosine - real * sine
        waves = dot3(
            jnp.concatenate(
                [
                    jnp.concatenate([turned_real, turned_imag], axis=1),
                    jnp.concatenate([turned_imag, -turned_real], axis=1),
                ],
                axis=0,
            ),
            forward,
        )
        wave_real, wave_imag = waves[:rows], waves[rows:]
        columns = slice(b * INNER, (b + 1) * INNER)
        weighted_real, weighted_imag = [], []
        for c in range(2):
            for kernel, part in ((top, slice(0, kys)), (side, slice(kys, rows))):
                kernel_real, kernel_imag = kernel[c, 0, :, columns], kernel[c, 1, :, columns]
                weighted_real.append(
                    kernel_real * wave_real[part] + kernel_imag * wave_imag[part]
                )
                weighted_imag.append(
                    kernel_real * wave_imag[part] - kernel_imag * wave_real[part]
                )
        weighted_real = jnp.concatenate(weighted_real, axis=0)
        weighted_imag = jnp.concatenate(weighted_imag, axis=0)
        back = dot3(
            jnp.concatenate(
                [
                    jnp.concatenate([weighted_real, -weighted_imag], axis=1),
                    jnp.concatenate([weighted_imag, weighted_real], axis=1),
                ],
                axis=0,
            ),
            backward,
        )
        back_real, back_imag = back[: 2 * rows], back[2 * rows :]
        if b == 0:
            total_real, total_imag = back_real, back_imag
        else:
            total_real = total_real + (back_real * cosine - back_imag * sine)
            total_imag = total_imag + (back_real * sine + back_imag * cosine)

    y_parts = split(y_back[...])
    depth_rows = []
    quarter = (out.shape[1] - TILE) // 2
    block_x = quarter * count_z
    for c in range(2):
        start = c * rows
        lines = jnp.concatenate(
            [total_real[start : start + kys], total_imag[start : start + kys]], axis=0
        )
        image = dot3(lines.T, y_parts)
        for x in range(count_x):
            for y in range(count_y):
                for z in range(count_z):
                    first = x * block_x + z * quarter
                    out[
                        (x * count_y + y) * count_z + z, c * quarter : (c + 1) * quarter, :
                    ] = image[first : first + quarter, y * LANES : (y + 1) * LANES]
        depth_rows.append(total_real[start + kys : start + rows])
        depth_rows.append(total_imag[start + kys : start + rows])
    side_image = dot3(z_back[...], split(jnp.concatenate(depth_rows, axis=0)))
    for y in range(count_y):
        for z in range(count_z):
            block = side_image[z * TILE : (z + 1) * TILE, y * LANES : (y + 1) * LANES]
            for x in range(count_x):
                out[(x * count_y + y) * count_z + z, 2 * quarter :, :] = block


def image_parts(gathered, top_kernel, side_kernel, counts, block_x, top_rows, depth_block):
    count_x, count_y, count_z = counts
    group = count_y * count_z
    here = [lax.axis_index(axis) for axis in ALL]
    kys, size = top_kernel.shape[2:]
    kzs = side_kernel.shape[2]
    depth_size = kzs * group
    extent = count_y * LANES
    share = depth_block // count_x
    block_y = top_rows * 2

    ky = ((here[0] * count_y + here[1]) * count_z + here[2]) * kys + lax.iota(jnp.int32, kys)
    kz = (here[1] * count_z + here[2]) * kzs + lax.iota(jnp.int32, kzs)

    row = lax.iota(jnp.int32, group * top_rows)
    y_tables = []
    for h in range(2):
        y = row // top_rows * block_y + h * top_rows + row % top_rows
        cosine, sine = phases(ky[:, None], y[None, :], size)
        y_tables += [cosine, -sine]
    y_table = jnp.concatenate(y_tables, axis=0)

    row = lax.iota(jnp.int32, count_x * count_z * TILE)
    inside = row % TILE
    z = row // TILE % count_z * depth_block + row // (TILE * count_z) * share + inside
    cosine, sine = phases(kz[:, None], z[None, :], depth_size)
    z_table = jnp.where((inside < share)[None, :], jnp.concatenate([cosine, -sine], axis=0), 0.0)

    cosine, sine = phases(ky[:, None], lax.iota(jnp.int32, extent)[None, :], size)
    y_back = jnp.concatenate([cosine, -sine], axis=0) * (1.0 / (size * size))

    row = lax.iota(jnp.int32, count_z * TILE)
    z = row // TILE * depth_block + here[0] * share + row % TILE % share
    cosine, sine = phases(z[:, None], kz[None, :], depth_size)
    both = jnp.concatenate([cosine, -sine], axis=1) * (1.0 / (size * depth_size))
    component = (row % TILE // share)[:, None]
    z_back = jnp.concatenate(
        [jnp.where(component == 0, both, 0.0), jnp.where(component == 1, both, 0.0)], axis=1
    )

    forward, backward, turns = transform_tables(extent, size)
    out_rows = 2 * (block_x // count_z) + TILE
    return pl.pallas_call(
        functools.partial(image_kernel, counts + (top_rows,)),
        out_shape=jax.ShapeDtypeStruct((count_x * group, out_rows, LANES), f32),
        compiler_params=pltpu.CompilerParams(vmem_limit_bytes=56 * 1024 * 1024),
        name="images",
    )(
        gathered,
        y_table,
        z_table,
        *(jnp.asarray(t) for t in forward + backward),
        jnp.asarray(turns),
        top_kernel,
        side_kernel,
        y_back,
        z_back,
    )


def copies_of(pairs, semaphores):
    started = [
        pltpu.make_async_copy(source, target, semaphores.at[i])
        for i, (source, target) in enumerate(pairs)
    ]
    for copy in started:
        copy.start()
    return started


def faces_kernel(
    magnetization, stiffness, z_first, z_last, x_first, x_last, y_faces, m, s, semaphores, sent
):
    depth, across = stiffness.shape[:2]
    loads = copies_of(
        [(stiffness, s)] + [(magnetization.at[c], m.at[c]) for c in range(3)], semaphores
    )
    lane = lax.broadcasted_iota(jnp.int32, (across, LANES), 1)
    first = jnp.zeros((across, LANES), f32)
    last = jnp.zeros((across, LANES), f32)
    stores = []
    for field, load in ((3, loads[0]), (0, loads[1]), (1, loads[2]), (2, loads[3])):
        load.wait()
        ref = s if field == 3 else m.at[field]
        for k, (target, z) in enumerate(((z_first, 0), (z_last, depth - 1))):
            store = pltpu.make_async_copy(ref.at[z], target.at[field], sent.at[2 * field + k])
            store.start()
            stores.append(store)
        x_first[field] = ref[:, 0, :]
        x_last[field] = ref[:, across - 1, :]
        for z in range(depth):
            column = field * depth + z
            turned = pltpu.roll(ref[z], column, 1) if column else ref[z]
            first = jnp.where(lane == column, turned, first)
            last = jnp.where(lane == (column - 1) % LANES, turned, last)
    y_faces[...] = jnp.where(
        lane < LANES // 2, first, pltpu.roll(last, LANES // 2 + 1, 1)
    )
    for store in stores:
        store.wait()


def twice_weight(a, b):
    return 4.0 * a * b / (a + b)


def edges_kernel(
    counts,
    here,
    z_first,
    z_last,
    x_first,
    x_last,
    y_faces,
    z_next,
    z_before,
    x_next,
    x_before,
    y_next,
    y_before,
    out,
):
    across = y_faces.shape[0]
    depth = x_first.shape[1]
    half = LANES // 2
    count_x, count_y, count_z = counts
    at_z = here[0] % count_z
    at_y = here[0] // count_z % count_y
    at_x = here[0] // (count_z * count_y)

    def inside(condition, values):
        return jnp.where(condition, values, 0.0)

    row = 0
    for own, halo, present in (
        (z_last, z_next, at_z < count_z - 1),
        (z_first, z_before, at_z > 0),
        (x_last, x_next, at_x < count_x - 1),
        (x_first, x_before, at_x > 0),
    ):
        rows = own.shape[1]
        weight = twice_weight(own[3], inside(present, halo[3]))
        for c in range(3):
            out[row : row + rows, :] = weight * (own[c] - halo[c])
            row += rows

    lane = lax.broadcasted_iota(jnp.int32, (across, LANES), 1)
    stiff = (lane >= 3 * depth) & (lane < 4 * depth)

    def y_edge(own, halo, present):
        weight = twice_weight(
            jnp.where(stiff, own, 1.0), jnp.where(stiff, inside(present, halo), 1.0)
        )
        spread = pltpu.roll(weight, LANES - 3 * depth, 1)
        for c in (1, 2):
            spread = jnp.where(
                lane >= c * depth, pltpu.roll(weight, LANES - (3 - c) * depth, 1), spread
            )
        return spread * (own - halo)

    own = y_faces[...]
    after = y_edge(pltpu.roll(own, half, 1), y_next[...], at_y < count_y - 1)
    before = y_edge(own, pltpu.roll(y_before[...], half, 1), at_y > 0)
    out[row : row + across, :] = jnp.where(lane < half, after, pltpu.roll(before, half, 1))


def exchange_kernel(magnetization, stiffness, edges, out):
    depth, across = stiffness.shape[:2]
    half = LANES // 2
    lane = lax.broadcasted_iota(jnp.int32, (across, LANES), 1)
    row = lax.broadcasted_iota(jnp.int32, (across, LANES), 0)
    first_lane, last_lane, last_row = lane == 0, lane == LANES - 1, row == across - 1
    z_rows, x_rows = 3 * across, 3 * depth
    y_row = 2 * (z_rows + x_rows)
    sides = edges[y_row : y_row + across, :]
    below = [-edges[z_rows + c * across : z_rows + (c + 1) * across, :] for c in range(3)]
    for z in range(depth):
        centre = stiffness[z]
        if z + 1 < depth:
            weight_z = twice_weight(centre, stiffness[z + 1])
        weight_x = jnp.where(
            last_row, 0.0, twice_weight(centre, pltpu.roll(centre, across - 1, 0))
        )
        weight_y = jnp.where(
            last_lane, 0.0, twice_weight(centre, pltpu.roll(centre, LANES - 1, 1))
        )
        for c in range(3):
            column = c * depth + z
            values = magnetization[c, z]
            if z + 1 < depth:
                up = weight_z * (values - magnetization[c, z + 1])
            else:
                up = edges[c * across : (c + 1) * across, :]
            flux_x = weight_x * (values - pltpu.roll(values, across - 1, 0))
            flux_y = weight_y * (values - pltpu.roll(values, LANES - 1, 1))
            total = (up - below[c]) + (flux_x - pltpu.roll(flux_x, 1, 0))
            total = total + (flux_y - pltpu.roll(flux_y, 1, 1))
            side = jnp.where(
                first_lane,
                sides[:, half + column : half + column + 1],
                jnp.where(last_lane, sides[:, column : column + 1], 0.0),
            )
            out[c, z] = total + side
            below[c] = up
    for start, edge_row in ((2 * z_rows, across - 1), (2 * z_rows + x_rows, 0)):
        for c in range(3):
            out[c, :, edge_row, :] += edges[start + c * depth : start + (c + 1) * depth, :]


def ring(block, axis, distance):
    count = lax.axis_size(axis)
    return lax.ppermute(block, axis, [(i, (i + distance) % count) for i in range(count)])


def edge_terms(counts, index, magnetization, stiffness):
    depth, across, along = stiffness.shape
    shape = jax.ShapeDtypeStruct
    faces = pl.pallas_call(
        faces_kernel,
        in_specs=[HBM, HBM],
        out_specs=[HBM, HBM, VMEM, VMEM, VMEM],
        out_shape=[
            shape((4, across, along), f32),
            shape((4, across, along), f32),
            shape((4, depth, along), f32),
            shape((4, depth, along), f32),
            shape((across, LANES), f32),
        ],
        scratch_shapes=[
            pltpu.VMEM(magnetization.shape, f32),
            pltpu.VMEM(stiffness.shape, f32),
            pltpu.SemaphoreType.DMA((4,)),
            pltpu.SemaphoreType.DMA((8,)),
        ],
        compiler_params=pltpu.CompilerParams(vmem_limit_bytes=60 * MIB),
        name="faces",
    )(magnetization, stiffness)
    z_first, z_last, x_first, x_last, y_faces = faces
    z_next, z_before = ring(z_first, "gz", -1), ring(z_last, "gz", 1)
    x_next, x_before = ring(x_first, "gx", -1), ring(x_last, "gx", 1)
    y_next = ring(y_faces, "gy", -1)
    y_before = y_next if lax.axis_size("gy") == 2 else ring(y_faces, "gy", 1)
    return call(
        functools.partial(edges_kernel, counts),
        "edges",
        (7 * across + 6 * depth, LANES),
        16,
        "s" + "v" * 11,
        (index, *faces, z_next, z_before, x_next, x_before, y_next, y_before),
    )


def exchange_of(magnetization, stiffness, edges):
    return call(
        exchange_kernel,
        "exchange",
        magnetization.shape,
        16,
        "vvv",
        (magnetization, stiffness, edges),
    )


def line_tables(counts, top_rows, kys, size):
    group = counts[1] * counts[2]
    row = np.arange(group * top_rows)
    j = np.arange(kys)
    start = np.arange(counts[0] * group) * kys
    steps, offsets = [], []
    for h in range(2):
        y = row // top_rows * top_rows * 2 + h * top_rows + row % top_rows
        for values, into in ((j, steps), (start, offsets)):
            angle = (np.outer(values, y) % size) * (2.0 * math.pi / size)
            into += [np.cos(angle), np.sin(angle)]
    steps = np.stack(steps).astype(np.float32)
    offsets = np.stack(offsets, axis=1).astype(np.float32)
    return steps, np.pad(offsets, ((0, 0), (0, TILE - 4), (0, 0)))


def depth_tables(counts, kzs, depth_block):
    count_x, count_y, count_z = counts
    size = count_y * count_z * kzs
    share = depth_block // count_x
    kz = np.arange(size).reshape(count_y * count_z, kzs, 1)

    def table(z):
        angle = (kz * z % size) * (2.0 * math.pi / size)
        return np.concatenate([np.cos(angle), -np.sin(angle)], axis=1).astype(np.float32)

    row = np.arange(count_x * count_z * TILE)
    within = row % TILE
    z = row // TILE % count_z * depth_block + row // (TILE * count_z) * share + within
    there = np.where(within < share, table(z), np.float32(0.0))
    return there, np.swapaxes(table(np.arange(depth_block * count_z)), 1, 2)


def stacked_product(real, imag, tables, sign):
    if sign < 0:
        upper = jnp.concatenate([real, imag], axis=1)
        lower = jnp.concatenate([imag, -real], axis=1)
    else:
        upper = jnp.concatenate([real, -imag], axis=1)
        lower = jnp.concatenate([imag, real], axis=1)
    return dot3(jnp.concatenate([upper, lower], axis=0), tables)


def back_and_forth(real, imag, columns_of, tables, turns):
    rows = real.shape[0]
    total_real = total_imag = None
    for b in range(turns.shape[1]):
        cosine, sine = turns[0, b : b + 1, :], turns[1, b : b + 1, :]
        waves = stacked_product(
            real * cosine + imag * sine, imag * cosine - real * sine, tables, -1
        )
        wave_real, wave_imag = waves[:rows], waves[rows:]
        kernel = columns_of(b)
        weighted_real, weighted_imag = [], []
        for c in range(2):
            kernel_real, kernel_imag = kernel[c, 0], kernel[c, 1]
            weighted_real.append(kernel_real * wave_real + kernel_imag * wave_imag)
            weighted_imag.append(kernel_real * wave_imag - kernel_imag * wave_real)
        back = stacked_product(
            jnp.concatenate(weighted_real, axis=0),
            jnp.concatenate(weighted_imag, axis=0),
            tables,
            1,
        )
        back_real, back_imag = back[: 2 * rows], back[2 * rows :]
        if b == 0:
            total_real, total_imag = back_real, back_imag
        else:
            total_real = total_real + (back_real * cosine - back_imag * sine)
            total_imag = total_imag + (back_real * sine + back_imag * cosine)
    return [
        (total_real[c * rows : (c + 1) * rows], total_imag[c * rows : (c + 1) * rows])
        for c in range(2)
    ]


def lines_kernel(counts, here, gathered, steps, offsets, high, low, turns, kernel, out):
    count_x, count_y, count_z = counts
    group = count_y * count_z
    top_rows = LANES // group
    half = LANES // 2
    kys = kernel.shape[2]
    offset = offsets[here[0]]
    table = []
    for h in range(2):
        step_cos, step_sin = steps[2 * h], steps[2 * h + 1]
        offset_cos, offset_sin = offset[2 * h : 2 * h + 1], offset[2 * h + 1 : 2 * h + 2]
        table.append(step_cos * offset_cos - step_sin * offset_sin)
        table.append(-(step_sin * offset_cos + step_cos * offset_sin))
    blocks = [
        gathered[g * group : (g + 1) * group, 0:top_rows, :].reshape(group * top_rows, LANES)
        for g in range(count_x)
    ]
    mixed = dot3(jnp.concatenate(table, axis=0), split(jnp.concatenate(blocks, axis=1)))
    low_half, high_half = mixed[: 2 * kys], mixed[2 * kys :]
    lane = lax.broadcasted_iota(jnp.int32, (2 * kys, LANES), 1)
    pieces = []
    for g in range(0, count_x, 2):
        a = slice(g * LANES, (g + 1) * LANES)
        b = slice((g + 1) * LANES, (g + 2) * LANES)
        pieces.append(
            jnp.where(
                lane < half,
                low_half[:, a] + pltpu.roll(high_half[:, a], half, 1),
                pltpu.roll(low_half[:, b], half, 1) + high_half[:, b],
            )
        )
    lines = jnp.concatenate(pieces, axis=1)

    def columns_of(b):
        return kernel.at[:, :, :, b * INNER : (b + 1) * INNER]

    images = back_and_forth(
        lines[:kys], lines[kys:], columns_of, (high[...], low[...]), turns
    )
    for c in range(2):
        block = jnp.concatenate(images[c], axis=0).T
        out[:, c * TILE : (c + 1) * TILE, :] = block.reshape(count_x * group, TILE, LANES)


def side_kernel_body(counts, here, gathered, there, back, high, low, turns, kernel, out):
    count_x, count_y, count_z = counts
    depth_block = out.shape[1] // 2
    top_rows = gathered.shape[1] - TILE
    kzs = kernel.shape[2]
    blocks = []
    for y in range(count_y):
        rows = [
            gathered[(x * count_y + y) * count_z + z, top_rows:, :]
            for x in range(count_x)
            for z in range(count_z)
        ]
        blocks.append(jnp.concatenate(rows, axis=0))
    lines = dot3(there[here[0]], split(jnp.concatenate(blocks, axis=1)))

    def columns_of(b):
        return kernel.at[:, :, :, b * INNER : (b + 1) * INNER]

    images = back_and_forth(
        lines[:kzs], lines[kzs:], columns_of, (high[...], low[...]), turns
    )
    scale = 1.0 / (count_y * count_z * kzs * kernel.shape[3])
    for c in range(2):
        image = dot3(back[here[0]] * scale, split(jnp.concatenate(images[c], axis=0)))
        for y in range(count_y):
            for z in range(count_z):
                out[y * count_z + z, c * depth_block : (c + 1) * depth_block, :] = image[
                    z * depth_block : (z + 1) * depth_block, y * LANES : (y + 1) * LANES
                ]


def rows_kernel(counts, arrived, side, high, low, turns, out):
    count_y, count_z = counts[1:]
    per_turn = arrived.shape[0] // turns.shape[1]
    half = LANES // 2
    lane = lax.broadcasted_iota(jnp.int32, (2 * TILE, LANES), 1)
    real, imag = [], []
    for b in range(turns.shape[1]):
        real_pieces, imag_pieces = [], []
        for g in range(b * per_turn, (b + 1) * per_turn, 2):
            first, second = arrived[g], arrived[g + 1]
            real_pieces.append(jnp.where(lane < half, first, pltpu.roll(second, half, 1)))
            imag_pieces.append(jnp.where(lane < half, pltpu.roll(first, half, 1), second))
        real.append(jnp.concatenate(real_pieces, axis=1))
        imag.append(jnp.concatenate(imag_pieces, axis=1))
    back = stacked_product(
        jnp.concatenate(real, axis=0), jnp.concatenate(imag, axis=0), (high[...], low[...]), 1
    )
    middle = back.shape[0] // 2
    size = turns.shape[1] * INNER
    total = None
    for b in range(turns.shape[1]):
        part = slice(b * 2 * TILE, (b + 1) * 2 * TILE)
        term = back[:middle][part] * turns[0, b : b + 1, :]
        term = term - back[middle:][part] * turns[1, b : b + 1, :]
        total = term if b == 0 else total + term
    total = total * (1.0 / (size * size))
    for y in range(count_y):
        for z in range(count_z):
            out[y * count_z + z, 0 : 2 * TILE, :] = total[:, y * LANES : (y + 1) * LANES]
    out[:, 2 * TILE :, :] = side[...]


def sum_kernel(exchange_grad, arrived, out):
    depth = exchange_grad.shape[1]
    group = arrived.shape[0]
    side = [None, None]
    top = [None, None]
    for c in range(2):
        rows = slice(2 * TILE + c * depth, 2 * TILE + (c + 1) * depth)
        total = arrived[0, rows, :]
        for p in range(1, group):
            total = total + arrived[p, rows, :]
        side[c] = total
        top[c] = arrived[:, c * TILE : (c + 1) * TILE, :].reshape(group * TILE, LANES)
    for z in range(depth):
        out[0, z] = exchange_grad[0, z] + top[0]
        out[1, z] = exchange_grad[1, z] + top[1] + side[0][z : z + 1]
        out[2, z] = exchange_grad[2, z] + side[1][z : z + 1]


def residual_blocks(residual_top, residual_side, devices, share):
    block_x, block_y = residual_top.shape
    top_rows = block_y // 2

    def body(at_x, top, side, out):
        piece = jnp.concatenate([top[0:top_rows, :], top[top_rows:, :]], axis=1)
        part = side[pl.ds(at_x[0] * share, share), :]
        part = jnp.concatenate([part, jnp.zeros((TILE - share, LANES), f32)], axis=0)
        for device in range(devices):
            out[device, 0:top_rows, :] = piece
            out[device, top_rows:, :] = part

    return call(
        body,
        "pack",
        (devices, top_rows + TILE, LANES),
        8,
        "svv",
        (lax.axis_index("gx").reshape(1), residual_top.T, residual_side.T),
    )


def fast_on_device(magnetization, stiffness, residual_top, residual_side, top_kernel, side_kernel):
    counts = tuple(lax.axis_size(axis) for axis in ALL)
    count_x, count_y, count_z = counts
    group = count_y * count_z
    devices = count_x * group
    block_x, block_y = residual_top.shape
    depth_block = stiffness.shape[0]
    top_rows = block_y // 2
    kys, size = top_kernel.shape[2:]
    kzs = side_kernel.shape[2]
    extent = count_x * block_x
    here = [lax.axis_index(axis) for axis in ALL]
    plane_index = here[1] * count_z + here[2]
    index = (here[0] * group + plane_index).reshape(1)
    plane_index = plane_index.reshape(1)
    (high, low), _, turns = transform_tables(extent, size)
    high, low, turns = jnp.asarray(high), jnp.asarray(low), jnp.asarray(turns)
    steps, offsets = line_tables(counts, top_rows, kys, size)
    there, back = depth_tables(counts, kzs, depth_block)

    sent = residual_blocks(residual_top, residual_side, devices, depth_block // count_x)
    gathered = lax.all_to_all(sent, ALL, 0, 0, tiled=True)
    edges = edge_terms(counts, index, magnetization, stiffness)
    gathered, edges = lax.optimization_barrier((gathered, edges))

    lines = call(
        functools.partial(lines_kernel, counts),
        "lines",
        (devices, 2 * TILE, LANES),
        24,
        "svvvvvvv",
        (index, gathered, jnp.asarray(steps), jnp.asarray(offsets), high, low, turns, top_kernel),
    )
    arrived = lax.all_to_all(lines, ALL, 0, 0, tiled=True)
    side = call(
        functools.partial(side_kernel_body, counts),
        "side",
        (group, 2 * depth_block, LANES),
        16,
        "svvvvvvv",
        (
            plane_index,
            gathered,
            jnp.asarray(there),
            jnp.asarray(back),
            high,
            low,
            turns,
            side_kernel,
        ),
    )
    exchange_grad = exchange_of(magnetization, stiffness, edges)
    arrived, side, exchange_grad = lax.optimization_barrier((arrived, side, exchange_grad))
    rows = call(
        functools.partial(rows_kernel, counts),
        "rows",
        (group, 2 * TILE + 2 * depth_block, LANES),
        60,
        "vvvvv",
        (arrived, side, high, low, turns),
    )
    arrived = lax.all_to_all(rows, ("gy", "gz"), 0, 0, tiled=True)
    return call(sum_kernel, "gradient", magnetization.shape, 16, "vv", (exchange_grad, arrived))


def fits(counts, stiffness, residual_top, residual_side, top_kernel, side_kernel):
    count_x, count_y, count_z = counts
    block_x, block_y = residual_top.shape
    group = count_y * count_z
    return (
        2 * block_x == LANES
        and 2 * top_kernel.shape[2] == LANES
        and stiffness.shape[2] == LANES
        and block_x == group * TILE
        and block_y * group == count_x * block_x == INNER
        and count_y * LANES == INNER
        and block_y % 16 == 0
        and count_x % 2 == 0
        and (count_x * group) % (2 * top_kernel.shape[3] // INNER) == 0
        and INNER == top_kernel.shape[2] * count_z
        and stiffness.shape[0] % 16 == 0
        and side_kernel.shape[2] % 16 == 0
    )


def on_device(magnetization, stiffness, residual_top, residual_side, top_kernel, side_kernel):
    counts = tuple(lax.axis_size(axis) for axis in ALL)
    count_x, count_y, count_z = counts
    if fits(counts, stiffness, residual_top, residual_side, top_kernel, side_kernel):
        return fast_on_device(
            magnetization, stiffness, residual_top, residual_side, top_kernel, side_kernel
        )
    devices = count_x * count_y * count_z
    depth_block = stiffness.shape[0]
    block_x, block_y = residual_top.shape
    top_rows = block_y // 2
    share = depth_block // count_x

    sent = residual_blocks(residual_top, residual_side, devices, share)
    rows = sent.shape[1]
    gathered = lax.all_to_all(sent, ALL, 0, 0, tiled=True)
    index = (
        (lax.axis_index("gx") * count_y + lax.axis_index("gy")) * count_z + lax.axis_index("gz")
    ).reshape(1)
    exchange_grad = exchange_of(
        magnetization, stiffness, edge_terms(counts, index, magnetization, stiffness)
    )

    parts = image_parts(
        gathered, top_kernel, side_kernel, counts, block_x, top_rows, depth_block
    )
    rows = parts.shape[1]
    arrived = lax.all_to_all(parts.reshape(devices * rows, LANES), ALL, 0, 0, tiled=True)
    arrived = arrived.reshape(devices, rows, LANES)
    top_sum = jnp.sum(arrived[:, : rows - TILE], axis=0)
    side_sum = jnp.sum(
        arrived[:, rows - TILE :].reshape(count_x, count_y * count_z, TILE, LANES), axis=1
    )
    side = side_sum[:, : 2 * share].reshape(count_x, 2, share, LANES)
    side = jnp.swapaxes(side, 0, 1).reshape(2, depth_block, 1, LANES)
    top = lax.all_gather(top_sum, "gz", axis=0)
    top = jnp.swapaxes(top.reshape(count_z, 2, block_x // count_z, LANES), 0, 1)
    top = top.reshape(2, 1, block_x, LANES)
    return jnp.stack(
        [
            exchange_grad[0] + top[0],
            exchange_grad[1] + top[1] + side[0],
            exchange_grad[2] + side[1],
        ]
    )


def solution(mesh):
    placed = (
        P(None, "gz", "gx", "gy"),
        P("gz", "gx", "gy"),
        P("gx", ("gy", "gz")),
        P("gy", "gz"),
        P(None, None, ("gx", "gy", "gz"), None),
        P(None, None, ("gy", "gz"), None),
    )
    return jax.shard_map(
        on_device, mesh=mesh, in_specs=placed, out_specs=P(None, "gz", "gx", "gy"), check_vma=False
    )
```

```python
import functools
import math

import jax
import jax.numpy as jnp
import ml_dtypes
import numpy as np
from jax import lax
from jax.experimental import pallas as pl
from jax.experimental.pallas import tpu as pltpu
from jax.sharding import PartitionSpec as P

LANES = 128
TILE = 8
INNER = 256
ALL = ("gx", "gy", "gz")
f32 = jnp.float32
bf16 = jnp.bfloat16
MIB = 1024 * 1024
SMEM = pl.BlockSpec(memory_space=pltpu.SMEM)
VMEM = pl.BlockSpec(memory_space=pltpu.VMEM)
HBM = pl.BlockSpec(memory_space=pltpu.HBM)


def split(values):
    high = values.astype(bf16)
    return high, (values - high.astype(f32)).astype(bf16)


def dot3(left, right):
    high, low = split(left)
    def one(a, b):
        return lax.dot_general(a, b, (((1,), (0,)), ((), ())), preferred_element_type=f32)
    return one(high, right[0]) + one(low, right[0]) + one(high, right[1])


def from_hbm(values):
    return pltpu.with_memory_space_constraint(values, pltpu.HBM)


def call(body, name, shape, limit, microseconds, operands, in_hbm=(), scratch=(), refs=()):
    shapes = shape if isinstance(shape, list) else [shape]
    moved = sum(4 * math.prod(each) for each in shapes)
    moved += sum(x.size * x.dtype.itemsize for x in operands)
    results = pl.pallas_call(
        body,
        out_shape=[
            pltpu.HBM(each, f32) if i in in_hbm else jax.ShapeDtypeStruct(each, f32)
            for i, each in enumerate(shapes)
        ],
        in_specs=[
            SMEM if x.shape == (1,) else HBM if i in refs else VMEM
            for i, x in enumerate(operands)
        ],
        out_specs=[VMEM] * len(shapes),
        scratch_shapes=list(scratch),
        compiler_params=pltpu.CompilerParams(vmem_limit_bytes=limit * MIB),
        cost_estimate=pl.CostEstimate(
            flops=int(microseconds * 1e9), bytes_accessed=moved, transcendentals=0
        ),
        name=name,
    )(*operands)
    return results if isinstance(shape, list) else results[0]


def transform_tables(extent, size):
    x = np.arange(extent)
    angle = (np.outer(x, np.arange(INNER)) % size) * (2.0 * math.pi / size)
    forward = np.concatenate([np.cos(angle), np.sin(angle)], 0).astype(np.float32)
    backward = np.concatenate([np.cos(angle).T, np.sin(angle).T], 0).astype(np.float32)

    def parts(table):
        high = table.astype(ml_dtypes.bfloat16)
        return high, (table - high.astype(np.float32)).astype(ml_dtypes.bfloat16)

    outer = size // INNER
    turn = (np.outer(np.arange(outer), x) % outer) * (2.0 * math.pi / outer)
    turns = np.stack([np.cos(turn), np.sin(turn)]).astype(np.float32)
    return parts(forward), parts(backward), turns


def phases(first, second, size):
    angle = (first * second % size).astype(f32) * (2.0 * math.pi / size)
    return jnp.cos(angle), jnp.sin(angle)


def image_kernel(
    counts, gathered, y_table, z_table, fh, fl, bh, bl, turns, top, side, y_back, z_back, out
):
    count_x, count_y, count_z, top_rows = counts
    group = count_y * count_z
    half = LANES // 2
    kys = top.shape[2]
    kzs = side.shape[2]
    forward = (fh[...], fl[...])
    backward = (bh[...], bl[...])

    blocks = [
        gathered[g * group : (g + 1) * group, 0:top_rows, :].reshape(group * top_rows, LANES)
        for g in range(count_x)
    ]
    mixed = dot3(y_table[...], split(jnp.concatenate(blocks, axis=1)))
    low_half, high_half = mixed[: 2 * kys], mixed[2 * kys :]
    lane = lax.broadcasted_iota(jnp.int32, (2 * kys, LANES), 1)
    pieces = []
    for g in range(0, count_x, 2):
        a = slice(g * LANES, (g + 1) * LANES)
        b = slice((g + 1) * LANES, (g + 2) * LANES)
        pieces.append(
            jnp.where(
                lane < half,
                low_half[:, a] + pltpu.roll(high_half[:, a], half, 1),
                pltpu.roll(low_half[:, b], half, 1) + high_half[:, b],
            )
        )
    top_lines = jnp.concatenate(pieces, axis=1)

    side_blocks = []
    for y in range(count_y):
        rows = [
            gathered[(x * count_y + y) * count_z + z, top_rows : top_rows + TILE, :]
            for x in range(count_x)
            for z in range(count_z)
        ]
        side_blocks.append(jnp.concatenate(rows, axis=0))
    side_lines = dot3(z_table[...], split(jnp.concatenate(side_blocks, axis=1)))

    real = jnp.concatenate([top_lines[:kys], side_lines[:kzs]], axis=0)
    imag = jnp.concatenate([top_lines[kys:], side_lines[kzs:]], axis=0)
    rows = kys + kzs
    total_real = total_imag = None
    for b in range(turns.shape[1]):
        cosine, sine = turns[0, b : b + 1, :], turns[1, b : b + 1, :]
        turned_real = real * cosine + imag * sine
        turned_imag = imag * cosine - real * sine
        waves = dot3(
            jnp.concatenate(
                [
                    jnp.concatenate([turned_real, turned_imag], axis=1),
                    jnp.concatenate([turned_imag, -turned_real], axis=1),
                ],
                axis=0,
            ),
            forward,
        )
        wave_real, wave_imag = waves[:rows], waves[rows:]
        columns = slice(b * INNER, (b + 1) * INNER)
        weighted_real, weighted_imag = [], []
        for c in range(2):
            for kernel, part in ((top, slice(0, kys)), (side, slice(kys, rows))):
                kernel_real, kernel_imag = kernel[c, 0, :, columns], kernel[c, 1, :, columns]
                weighted_real.append(
                    kernel_real * wave_real[part] + kernel_imag * wave_imag[part]
                )
                weighted_imag.append(
                    kernel_real * wave_imag[part] - kernel_imag * wave_real[part]
                )
        weighted_real = jnp.concatenate(weighted_real, axis=0)
        weighted_imag = jnp.concatenate(weighted_imag, axis=0)
        back = dot3(
            jnp.concatenate(
                [
                    jnp.concatenate([weighted_real, -weighted_imag], axis=1),
                    jnp.concatenate([weighted_imag, weighted_real], axis=1),
                ],
                axis=0,
            ),
            backward,
        )
        back_real, back_imag = back[: 2 * rows], back[2 * rows :]
        if b == 0:
            total_real, total_imag = back_real, back_imag
        else:
            total_real = total_real + (back_real * cosine - back_imag * sine)
            total_imag = total_imag + (back_real * sine + back_imag * cosine)

    y_parts = split(y_back[...])
    depth_rows = []
    quarter = (out.shape[1] - TILE) // 2
    block_x = quarter * count_z
    for c in range(2):
        start = c * rows
        lines = jnp.concatenate(
            [total_real[start : start + kys], total_imag[start : start + kys]], axis=0
        )
        image = dot3(lines.T, y_parts)
        for x in range(count_x):
            for y in range(count_y):
                for z in range(count_z):
                    first = x * block_x + z * quarter
                    out[
                        (x * count_y + y) * count_z + z, c * quarter : (c + 1) * quarter, :
                    ] = image[first : first + quarter, y * LANES : (y + 1) * LANES]
        depth_rows.append(total_real[start + kys : start + rows])
        depth_rows.append(total_imag[start + kys : start + rows])
    side_image = dot3(z_back[...], split(jnp.concatenate(depth_rows, axis=0)))
    for y in range(count_y):
        for z in range(count_z):
            block = side_image[z * TILE : (z + 1) * TILE, y * LANES : (y + 1) * LANES]
            for x in range(count_x):
                out[(x * count_y + y) * count_z + z, 2 * quarter :, :] = block


def image_parts(gathered, top_kernel, side_kernel, counts, block_x, top_rows, depth_block):
    count_x, count_y, count_z = counts
    group = count_y * count_z
    here = [lax.axis_index(axis) for axis in ALL]
    kys, size = top_kernel.shape[2:]
    kzs = side_kernel.shape[2]
    depth_size = kzs * group
    extent = count_y * LANES
    share = depth_block // count_x
    block_y = top_rows * 2

    ky = ((here[0] * count_y + here[1]) * count_z + here[2]) * kys + lax.iota(jnp.int32, kys)
    kz = (here[1] * count_z + here[2]) * kzs + lax.iota(jnp.int32, kzs)

    row = lax.iota(jnp.int32, group * top_rows)
    y_tables = []
    for h in range(2):
        y = row // top_rows * block_y + h * top_rows + row % top_rows
        cosine, sine = phases(ky[:, None], y[None, :], size)
        y_tables += [cosine, -sine]
    y_table = jnp.concatenate(y_tables, axis=0)

    row = lax.iota(jnp.int32, count_x * count_z * TILE)
    inside = row % TILE
    z = row // TILE % count_z * depth_block + row // (TILE * count_z) * share + inside
    cosine, sine = phases(kz[:, None], z[None, :], depth_size)
    z_table = jnp.where((inside < share)[None, :], jnp.concatenate([cosine, -sine], axis=0), 0.0)

    cosine, sine = phases(ky[:, None], lax.iota(jnp.int32, extent)[None, :], size)
    y_back = jnp.concatenate([cosine, -sine], axis=0) * (1.0 / (size * size))

    row = lax.iota(jnp.int32, count_z * TILE)
    z = row // TILE * depth_block + here[0] * share + row % TILE % share
    cosine, sine = phases(z[:, None], kz[None, :], depth_size)
    both = jnp.concatenate([cosine, -sine], axis=1) * (1.0 / (size * depth_size))
    component = (row % TILE // share)[:, None]
    z_back = jnp.concatenate(
        [jnp.where(component == 0, both, 0.0), jnp.where(component == 1, both, 0.0)], axis=1
    )

    forward, backward, turns = transform_tables(extent, size)
    out_rows = 2 * (block_x // count_z) + TILE
    return pl.pallas_call(
        functools.partial(image_kernel, counts + (top_rows,)),
        out_shape=jax.ShapeDtypeStruct((count_x * group, out_rows, LANES), f32),
        compiler_params=pltpu.CompilerParams(vmem_limit_bytes=56 * 1024 * 1024),
        name="images",
    )(
        gathered,
        y_table,
        z_table,
        *(jnp.asarray(t) for t in forward + backward),
        jnp.asarray(turns),
        top_kernel,
        side_kernel,
        y_back,
        z_back,
    )


def begin(semaphores, pairs):
    started = [
        pltpu.make_async_copy(source, target, semaphores.at[i])
        for i, (source, target) in enumerate(pairs)
    ]
    for copy in started:
        copy.start()
    return started


def faces_kernel(
    magnetization, stiffness, z_first, z_last, x_first, x_last, y_faces, m, s, loading
):
    depth, across = stiffness.shape[:2]
    loads = begin(
        loading, [(stiffness, s)] + [(magnetization.at[c], m.at[c]) for c in range(3)]
    )
    lane = lax.broadcasted_iota(jnp.int32, (across, LANES), 1)
    first = jnp.zeros((across, LANES), f32)
    last = jnp.zeros((across, LANES), f32)
    for field in (3, 0, 1, 2):
        loads[(field + 1) % 4].wait()
        ref = s if field == 3 else m.at[field]
        z_first[field] = ref[0]
        z_last[field] = ref[depth - 1]
        x_first[field] = ref[:, 0, :]
        x_last[field] = ref[:, across - 1, :]
        for z in range(depth):
            column = field * depth + z
            turned = pltpu.roll(ref[z], column, 1) if column else ref[z]
            first = jnp.where(lane == column, turned, first)
            last = jnp.where(lane == (column - 1) % LANES, turned, last)
    y_faces[...] = jnp.where(lane < LANES // 2, first, pltpu.roll(last, LANES // 2 + 1, 1))


def twice_weight(a, b):
    return 4.0 * a * b / (a + b)


def exchange_kernel(
    counts,
    here,
    magnetization_from,
    stiffness_from,
    z_next_from,
    z_before_from,
    x_next_from,
    x_before_from,
    y_next_from,
    y_before_from,
    y_faces_from,
    out,
    m,
    s,
    z_next,
    z_before,
    x_next,
    x_before,
    y_next,
    y_before,
    y_faces,
    loading,
):
    depth, across = s.shape[:2]
    chunk = depth // 4
    pairs = [
        (y_next_from, y_next),
        (y_before_from, y_before),
        (y_faces_from, y_faces),
        (z_before_from, z_before),
    ]
    for k in range(4):
        layers = pl.ds(k * chunk, chunk)
        pairs.append((stiffness_from.at[layers], s.at[layers]))
        pairs.append((magnetization_from.at[:, layers], m.at[:, layers]))
    pairs += [
        (z_next_from, z_next),
        (x_next_from, x_next),
        (x_before_from, x_before),
    ]
    loads = begin(loading, pairs)

    count_x, count_y, count_z = counts
    at_z = here[0] % count_z
    at_y = here[0] // count_z % count_y
    at_x = here[0] // (count_z * count_y)

    def inside(condition, values):
        return jnp.where(condition, values, 0.0)

    half = LANES // 2
    lane = lax.broadcasted_iota(jnp.int32, (across, LANES), 1)
    row = lax.broadcasted_iota(jnp.int32, (across, LANES), 0)
    first_lane, last_lane, last_row = lane == 0, lane == LANES - 1, row == across - 1

    stiff = (lane >= 3 * depth) & (lane < 4 * depth)

    def y_edge(own, halo, present):
        weight = twice_weight(
            jnp.where(stiff, own, 1.0), jnp.where(stiff, inside(present, halo), 1.0)
        )
        spread = pltpu.roll(weight, LANES - 3 * depth, 1)
        for c in (1, 2):
            spread = jnp.where(
                lane >= c * depth, pltpu.roll(weight, LANES - (3 - c) * depth, 1), spread
            )
        return spread * (own - halo)

    for copy in loads[:3]:
        copy.wait()
    own = y_faces[...]
    after = y_edge(pltpu.roll(own, half, 1), y_next[...], at_y < count_y - 1)
    before = y_edge(own, pltpu.roll(y_before[...], half, 1), at_y > 0)

    for copy in loads[3:6]:
        copy.wait()
    below_weight = twice_weight(inside(at_z > 0, z_before[3]), s[0])
    below = [below_weight * (z_before[c] - m[c, 0]) for c in range(3)]
    for z in range(depth):
        if z % chunk == chunk - 1:
            k = 4 + 2 * (z // chunk + 1)
            for copy in loads[k : k + 2] if z + 1 < depth else loads[k:]:
                copy.wait()
        centre = s[z]
        above = s[z + 1] if z + 1 < depth else inside(at_z < count_z - 1, z_next[3])
        weight_z = twice_weight(centre, above)
        weight_x = jnp.where(
            last_row, 0.0, twice_weight(centre, pltpu.roll(centre, across - 1, 0))
        )
        weight_y = jnp.where(
            last_lane, 0.0, twice_weight(centre, pltpu.roll(centre, LANES - 1, 1))
        )
        for c in range(3):
            column = c * depth + z
            values = m[c, z]
            upper = m[c, z + 1] if z + 1 < depth else z_next[c]
            up = weight_z * (values - upper)
            flux_x = weight_x * (values - pltpu.roll(values, across - 1, 0))
            flux_y = weight_y * (values - pltpu.roll(values, LANES - 1, 1))
            total = (up - below[c]) + (flux_x - pltpu.roll(flux_x, 1, 0))
            total = total + (flux_y - pltpu.roll(flux_y, 1, 1))
            side = jnp.where(
                first_lane,
                before[:, column : column + 1],
                jnp.where(last_lane, after[:, column : column + 1], 0.0),
            )
            out[c, z] = total + side
            below[c] = up
    for edge_row, halo, present in (
        (across - 1, x_next, at_x < count_x - 1),
        (0, x_before, at_x > 0),
    ):
        weight = twice_weight(s[:, edge_row, :], inside(present, halo[3]))
        for c in range(3):
            out[c, :, edge_row, :] += weight * (m[c, :, edge_row, :] - halo[c])


def ring(block, axis, distance):
    count = lax.axis_size(axis)
    return lax.ppermute(block, axis, [(i, (i + distance) % count) for i in range(count)])


def faces_of(magnetization, stiffness):
    depth, across, along = stiffness.shape
    return call(
        faces_kernel,
        "faces",
        [
            (4, across, along),
            (4, across, along),
            (4, depth, along),
            (4, depth, along),
            (across, LANES),
        ],
        8,
        2.0,
        (from_hbm(magnetization), from_hbm(stiffness)),
        in_hbm=(4,),
        refs=(0, 1),
        scratch=[
            pltpu.VMEM(magnetization.shape, f32),
            pltpu.VMEM(stiffness.shape, f32),
            pltpu.SemaphoreType.DMA((4,)),
        ],
    )


def halos_zy(z_first, z_last, y_faces):
    y_next = ring(y_faces, "gy", -1)
    y_before = y_next if lax.axis_size("gy") == 2 else ring(y_faces, "gy", 1)
    return ring(z_first, "gz", -1), ring(z_last, "gz", 1), y_next, y_before, y_faces


def halos_x(x_first, x_last):
    return ring(x_first, "gx", -1), ring(x_last, "gx", 1)


def exchange_of(counts, index, magnetization, stiffness, zy, x):
    z_next, z_before, y_next, y_before, y_faces = zy
    arrays = (magnetization, stiffness, z_next, z_before, *x, y_next, y_before, y_faces)
    return call(
        functools.partial(exchange_kernel, counts),
        "exchange",
        magnetization.shape,
        8,
        5.0,
        (index, *(from_hbm(array) for array in arrays)),
        refs=range(1, 10),
        scratch=[pltpu.VMEM(array.shape, f32) for array in arrays]
        + [pltpu.SemaphoreType.DMA((15,))],
    )


def whole_log(count):
    return count.bit_length() - 1


def cos_sin(steps, size):
    quarter = steps >> whole_log(size // 4)
    angle = ((steps & (size // 4 - 1)) - size // 8).astype(f32) * (2.0 * math.pi / size)
    square = angle * angle
    sine = cosine = 0.0
    for k in range(5, -1, -1):
        sine = sine * square + (-1) ** k / math.factorial(2 * k + 1)
        cosine = cosine * square + (-1) ** k / math.factorial(2 * k)
    sine = sine * angle
    first, second = (cosine - sine) * math.sqrt(0.5), (cosine + sine) * math.sqrt(0.5)
    odd = (quarter & 1) == 1
    real = jnp.where(odd, -second, first)
    imag = jnp.where(odd, first, second)
    back = quarter >= 2
    return jnp.where(back, -real, real), jnp.where(back, -imag, imag)


def stacked_product(real, imag, tables, sign):
    if sign < 0:
        upper = jnp.concatenate([real, imag], axis=1)
        lower = jnp.concatenate([imag, -real], axis=1)
    else:
        upper = jnp.concatenate([real, -imag], axis=1)
        lower = jnp.concatenate([imag, real], axis=1)
    return dot3(jnp.concatenate([upper, lower], axis=0), tables)


def back_and_forth(real, imag, columns_of, tables, turns):
    rows = real.shape[0]
    total_real = total_imag = None
    for b in range(turns.shape[1]):
        cosine, sine = turns[0, b : b + 1, :], turns[1, b : b + 1, :]
        waves = stacked_product(
            real * cosine + imag * sine, imag * cosine - real * sine, tables, -1
        )
        wave_real, wave_imag = waves[:rows], waves[rows:]
        kernel = columns_of(b)
        weighted_real, weighted_imag = [], []
        for c in range(2):
            kernel_real, kernel_imag = kernel[c, 0], kernel[c, 1]
            weighted_real.append(kernel_real * wave_real + kernel_imag * wave_imag)
            weighted_imag.append(kernel_real * wave_imag - kernel_imag * wave_real)
        back = stacked_product(
            jnp.concatenate(weighted_real, axis=0),
            jnp.concatenate(weighted_imag, axis=0),
            tables,
            1,
        )
        back_real, back_imag = back[: 2 * rows], back[2 * rows :]
        if b == 0:
            total_real, total_imag = back_real, back_imag
        else:
            total_real = total_real + (back_real * cosine - back_imag * sine)
            total_imag = total_imag + (back_real * sine + back_imag * cosine)
    return [
        (total_real[c * rows : (c + 1) * rows], total_imag[c * rows : (c + 1) * rows])
        for c in range(2)
    ]


def lines_kernel(counts, here, gathered, swapped, high, low, turns, kernel, out):
    count_x, count_y, count_z = counts
    group = count_y * count_z
    top_rows = LANES // group
    half = LANES // 2
    kys, size = kernel.shape[2:]
    ky = here[0] * kys + lax.broadcasted_iota(jnp.int32, (kys, LANES), 0)
    lane = lax.broadcasted_iota(jnp.int32, (kys, LANES), 1)
    odd = (lane >> whole_log(LANES // 2)) ^ (here[0] & 1)
    pair = lane >> whole_log(top_rows) & (group // 2 - 1)
    table = []
    for h in range(2):
        y = (2 * pair + odd) * (2 * top_rows) + h * top_rows + (lane & (top_rows - 1))
        cosine, sine = cos_sin(ky * y & (size - 1), size)
        table += [cosine, -sine]
    blocks = []
    for g in range(count_x):
        members = slice(g * group // 2, (g + 1) * group // 2)
        blocks.append(
            jnp.concatenate(
                [
                    part[members, 0:top_rows, :].reshape(half, LANES)
                    for part in (gathered, swapped)
                ],
                axis=0,
            )
        )
    mixed = dot3(jnp.concatenate(table, axis=0), split(jnp.concatenate(blocks, axis=1)))
    low_half, high_half = mixed[: 2 * kys], mixed[2 * kys :]
    lane = lax.broadcasted_iota(jnp.int32, (2 * kys, LANES), 1)
    pieces = []
    for g in range(0, count_x, 2):
        a = slice(g * LANES, (g + 1) * LANES)
        b = slice((g + 1) * LANES, (g + 2) * LANES)
        pieces.append(
            jnp.where(
                lane < half,
                low_half[:, a] + pltpu.roll(high_half[:, a], half, 1),
                pltpu.roll(low_half[:, b], half, 1) + high_half[:, b],
            )
        )
    lines = jnp.concatenate(pieces, axis=1)

    def columns_of(b):
        return kernel.at[:, :, :, b * INNER : (b + 1) * INNER]

    images = back_and_forth(
        lines[:kys], lines[kys:], columns_of, (high[...], low[...]), turns
    )
    for c in range(2):
        block = jnp.concatenate(images[c], axis=0).T
        out[:, c * TILE : (c + 1) * TILE, :] = block.reshape(count_x * group, TILE, LANES)


def side_kernel_body(
    counts, here, gathered, swapped, high, low, turns, kernel_from, out, kernel, loading
):
    count_x, count_y, count_z = counts
    depth_block = out.shape[1] // 2
    top_rows = gathered.shape[1] - TILE
    kzs, length = kernel_from.shape[2:]
    loads = begin(
        loading,
        [
            (kernel_from.at[:, :, :, pl.ds(b * INNER, INNER)], kernel.at[b])
            for b in range(length // INNER)
        ],
    )
    size = kzs * count_y * count_z
    share = depth_block // count_x

    columns = count_x * count_z * TILE
    kz = here[0] * kzs + lax.broadcasted_iota(jnp.int32, (kzs, columns), 0)
    column = lax.broadcasted_iota(jnp.int32, (kzs, columns), 1)
    within = column & (TILE - 1)
    pair = column >> whole_log(TILE) & (count_z // 2 - 1)
    odd = (column >> whole_log(columns // 2)) ^ (here[0] & 1)
    z = (2 * pair + odd) * depth_block + within
    z = z + (column >> whole_log(TILE * count_z // 2) & (count_x - 1)) * share
    cosine, sine = cos_sin(kz * z & (size - 1), size)
    there = jnp.concatenate([cosine, -sine], axis=0)
    there = jnp.where(jnp.concatenate([within, within], axis=0) < share, there, 0.0)

    blocks = []
    for y in range(count_y):
        rows = [
            part[(x * count_y + y) * count_z // 2 + pair, top_rows:, :]
            for part in (gathered, swapped)
            for x in range(count_x)
            for pair in range(count_z // 2)
        ]
        blocks.append(jnp.concatenate(rows, axis=0))
    lines = dot3(there, split(jnp.concatenate(blocks, axis=1)))

    def columns_of(b):
        loads[b].wait()
        return kernel.at[b]

    images = back_and_forth(
        lines[:kzs], lines[kzs:], columns_of, (high[...], low[...]), turns
    )

    rows = depth_block * count_z
    z = lax.broadcasted_iota(jnp.int32, (rows, 2 * kzs), 0)
    column = lax.broadcasted_iota(jnp.int32, (rows, 2 * kzs), 1)
    cosine, sine = cos_sin((here[0] * kzs + (column & (kzs - 1))) * z & (size - 1), size)
    back = jnp.where(column < kzs, cosine, -sine) * (1.0 / (size * length))
    for c in range(2):
        image = dot3(back, split(jnp.concatenate(images[c], axis=0)))
        for y in range(count_y):
            for z in range(count_z):
                out[y * count_z + z, c * depth_block : (c + 1) * depth_block, :] = image[
                    z * depth_block : (z + 1) * depth_block, y * LANES : (y + 1) * LANES
                ]


def rows_kernel(counts, arrived, side, high, low, turns, out, loading):
    count_y, count_z = counts[1:]
    loads = begin(loading, [(side, out.at[:, 2 * TILE :, :])])
    per_turn = arrived.shape[0] // turns.shape[1]
    half = LANES // 2
    lane = lax.broadcasted_iota(jnp.int32, (2 * TILE, LANES), 1)
    real, imag = [], []
    for b in range(turns.shape[1]):
        real_pieces, imag_pieces = [], []
        for g in range(b * per_turn, (b + 1) * per_turn, 2):
            first, second = arrived[g], arrived[g + 1]
            real_pieces.append(jnp.where(lane < half, first, pltpu.roll(second, half, 1)))
            imag_pieces.append(jnp.where(lane < half, pltpu.roll(first, half, 1), second))
        real.append(jnp.concatenate(real_pieces, axis=1))
        imag.append(jnp.concatenate(imag_pieces, axis=1))
    back = stacked_product(
        jnp.concatenate(real, axis=0), jnp.concatenate(imag, axis=0), (high[...], low[...]), 1
    )
    middle = back.shape[0] // 2
    size = turns.shape[1] * INNER
    total = None
    for b in range(turns.shape[1]):
        part = slice(b * 2 * TILE, (b + 1) * 2 * TILE)
        term = back[:middle][part] * turns[0, b : b + 1, :]
        term = term - back[middle:][part] * turns[1, b : b + 1, :]
        total = term if b == 0 else total + term
    total = total * (1.0 / (size * size))
    for y in range(count_y):
        for z in range(count_z):
            out[y * count_z + z, 0 : 2 * TILE, :] = total[:, y * LANES : (y + 1) * LANES]
    loads[0].wait()


def sum_kernel(exchange_grad, arrived, out):
    depth = exchange_grad.shape[1]
    group = arrived.shape[0]
    side = [None, None]
    top = [None, None]
    for c in range(2):
        rows = slice(2 * TILE + c * depth, 2 * TILE + (c + 1) * depth)
        total = arrived[0, rows, :]
        for p in range(1, group):
            total = total + arrived[p, rows, :]
        side[c] = total
        top[c] = arrived[:, c * TILE : (c + 1) * TILE, :].reshape(group * TILE, LANES)
    for z in range(depth):
        out[0, z] = exchange_grad[0, z] + top[0]
        out[1, z] = exchange_grad[1, z] + top[1] + side[0][z : z + 1]
        out[2, z] = exchange_grad[2, z] + side[1][z : z + 1]


def residual_blocks(residual_top, residual_side, devices, share):
    block_x, block_y = residual_top.shape
    top_rows = block_y // 2

    def body(at_x, top, side, out):
        piece = jnp.concatenate([top[0:top_rows, :], top[top_rows:, :]], axis=1)
        part = side[pl.ds(at_x[0] * share, share), :]
        part = jnp.concatenate([part, jnp.zeros((TILE - share, LANES), f32)], axis=0)
        for device in range(devices):
            out[device, 0:top_rows, :] = piece
            out[device, top_rows:, :] = part

    return call(
        body,
        "pack",
        (devices, top_rows + TILE, LANES),
        60,
        0.8,
        (lax.axis_index("gx").reshape(1), residual_top.T, residual_side.T),
    )


def fast_on_device(magnetization, stiffness, residual_top, residual_side, top_kernel, side_kernel):
    counts = tuple(lax.axis_size(axis) for axis in ALL)
    count_x, count_y, count_z = counts
    group = count_y * count_z
    devices = count_x * group
    block_x, block_y = residual_top.shape
    depth_block = stiffness.shape[0]
    top_rows = block_y // 2
    kys, size = top_kernel.shape[2:]
    kzs = side_kernel.shape[2]
    extent = count_x * block_x
    here = [lax.axis_index(axis) for axis in ALL]
    plane_index = here[1] * count_z + here[2]
    index = (here[0] * group + plane_index).reshape(1)
    plane_index = plane_index.reshape(1)
    (high, low), _, turns = transform_tables(extent, size)
    high, low, turns = jnp.asarray(high), jnp.asarray(low), jnp.asarray(turns)

    parities = [range(parity, devices, 2) for parity in range(2)]
    sent = residual_blocks(residual_top, residual_side, devices // 2, depth_block // count_x)
    gathered = lax.all_to_all(
        sent, ALL, 0, 0, tiled=True, axis_index_groups=[list(each) for each in parities]
    )
    z_first, z_last, x_first, x_last, y_faces = faces_of(magnetization, stiffness)
    gathered, x_first, x_last, y_faces = lax.optimization_barrier(
        (gathered, x_first, x_last, y_faces)
    )
    swapped = lax.ppermute(gathered, "gz", [(i, i ^ 1) for i in range(count_z)])
    zy = halos_zy(z_first, z_last, y_faces)

    lines = call(
        functools.partial(lines_kernel, counts),
        "lines",
        (devices, 2 * TILE, LANES),
        16,
        4.0,
        (index, gathered, swapped, high, low, turns, top_kernel),
    )
    arrived = lax.all_to_all(lines, ALL, 0, 0, tiled=True)
    lines, x_first, x_last = lax.optimization_barrier((lines, x_first, x_last))
    x = halos_x(x_first, x_last)
    side = call(
        functools.partial(side_kernel_body, counts),
        "side",
        (group, 2 * depth_block, LANES),
        8,
        2.8,
        (plane_index, gathered, swapped, high, low, turns, from_hbm(side_kernel)),
        in_hbm=(0,),
        refs=(6,),
        scratch=[
            pltpu.VMEM((size // INNER, 2, 2, kzs, INNER), f32),
            pltpu.SemaphoreType.DMA((size // INNER,)),
        ],
    )
    arrived, side = lax.optimization_barrier((arrived, side))
    rows = call(
        functools.partial(rows_kernel, counts),
        "rows",
        (group, 2 * TILE + 2 * depth_block, LANES),
        8,
        1.4,
        (arrived, from_hbm(side), high, low, turns),
        refs=(1,),
        scratch=[pltpu.SemaphoreType.DMA((1,))],
    )
    rows, zy, x = lax.optimization_barrier((rows, zy, x))
    arrived = lax.all_to_all(rows, ("gy", "gz"), 0, 0, tiled=True)
    exchange_grad = exchange_of(counts, index, magnetization, stiffness, zy, x)
    return call(sum_kernel, "gradient", magnetization.shape, 16, 1.2, (exchange_grad, arrived))


def fits(counts, stiffness, residual_top, residual_side, top_kernel, side_kernel):
    count_x, count_y, count_z = counts
    block_x, block_y = residual_top.shape
    group = count_y * count_z
    return (
        2 * block_x == LANES
        and 2 * top_kernel.shape[2] == LANES
        and stiffness.shape[2] == LANES
        and block_x == group * TILE
        and block_y * group == count_x * block_x == INNER
        and count_y * LANES == INNER
        and block_y % 16 == 0
        and count_x % 2 == 0
        and count_z % 2 == 0
        and (count_x * group) % (2 * top_kernel.shape[3] // INNER) == 0
        and INNER == top_kernel.shape[2] * count_z
        and stiffness.shape[0] % 16 == 0
        and side_kernel.shape[2] % 16 == 0
        and all(
            count & (count - 1) == 0
            for count in (group, count_x, count_z, top_kernel.shape[3], side_kernel.shape[2])
        )
    )


def on_device(magnetization, stiffness, residual_top, residual_side, top_kernel, side_kernel):
    counts = tuple(lax.axis_size(axis) for axis in ALL)
    count_x, count_y, count_z = counts
    if fits(counts, stiffness, residual_top, residual_side, top_kernel, side_kernel):
        return fast_on_device(
            magnetization, stiffness, residual_top, residual_side, top_kernel, side_kernel
        )
    devices = count_x * count_y * count_z
    depth_block = stiffness.shape[0]
    block_x, block_y = residual_top.shape
    top_rows = block_y // 2
    share = depth_block // count_x

    sent = residual_blocks(residual_top, residual_side, devices, share)
    rows = sent.shape[1]
    gathered = lax.all_to_all(sent, ALL, 0, 0, tiled=True)
    index = (
        (lax.axis_index("gx") * count_y + lax.axis_index("gy")) * count_z + lax.axis_index("gz")
    ).reshape(1)
    z_first, z_last, x_first, x_last, y_faces = faces_of(magnetization, stiffness)
    exchange_grad = exchange_of(
        counts,
        index,
        magnetization,
        stiffness,
        halos_zy(z_first, z_last, y_faces),
        halos_x(x_first, x_last),
    )

    parts = image_parts(
        gathered, top_kernel, side_kernel, counts, block_x, top_rows, depth_block
    )
    rows = parts.shape[1]
    arrived = lax.all_to_all(parts.reshape(devices * rows, LANES), ALL, 0, 0, tiled=True)
    arrived = arrived.reshape(devices, rows, LANES)
    top_sum = jnp.sum(arrived[:, : rows - TILE], axis=0)
    side_sum = jnp.sum(
        arrived[:, rows - TILE :].reshape(count_x, count_y * count_z, TILE, LANES), axis=1
    )
    side = side_sum[:, : 2 * share].reshape(count_x, 2, share, LANES)
    side = jnp.swapaxes(side, 0, 1).reshape(2, depth_block, 1, LANES)
    top = lax.all_gather(top_sum, "gz", axis=0)
    top = jnp.swapaxes(top.reshape(count_z, 2, block_x // count_z, LANES), 0, 1)
    top = top.reshape(2, 1, block_x, LANES)
    return jnp.stack(
        [
            exchange_grad[0] + top[0],
            exchange_grad[1] + top[1] + side[0],
            exchange_grad[2] + side[1],
        ]
    )


def solution(mesh):
    placed = (
        P(None, "gz", "gx", "gy"),
        P("gz", "gx", "gy"),
        P("gx", ("gy", "gz")),
        P("gy", "gz"),
        P(None, None, ("gx", "gy", "gz"), None),
        P(None, None, ("gy", "gz"), None),
    )
    return jax.shard_map(
        on_device, mesh=mesh, in_specs=placed, out_specs=P(None, "gz", "gx", "gy"), check_vma=False
    )
```

```python
import functools
import math

import jax
import jax.numpy as jnp
import ml_dtypes
import numpy as np
from jax import lax
from jax.experimental import pallas as pl
from jax.experimental.pallas import tpu as pltpu
from jax.sharding import PartitionSpec as P

LANES = 128
TILE = 8
INNER = 256
ALL = ("gx", "gy", "gz")
f32 = jnp.float32
bf16 = jnp.bfloat16
MIB = 1024 * 1024
SMEM = pl.BlockSpec(memory_space=pltpu.SMEM)
VMEM = pl.BlockSpec(memory_space=pltpu.VMEM)
HBM = pl.BlockSpec(memory_space=pltpu.HBM)


def split(values):
    high = values.astype(bf16)
    return high, (values - high.astype(f32)).astype(bf16)


def dot3(left, right):
    high, low = split(left)
    def one(a, b):
        return lax.dot_general(a, b, (((1,), (0,)), ((), ())), preferred_element_type=f32)
    return one(high, right[0]) + one(low, right[0]) + one(high, right[1])


def from_hbm(values):
    return pltpu.with_memory_space_constraint(values, pltpu.HBM)


def call(body, name, shape, limit, microseconds, operands, in_hbm=(), scratch=(), refs=()):
    shapes = shape if isinstance(shape, list) else [shape]
    moved = sum(4 * math.prod(each) for each in shapes)
    moved += sum(x.size * x.dtype.itemsize for x in operands)
    results = pl.pallas_call(
        body,
        out_shape=[
            pltpu.HBM(each, f32) if i in in_hbm else jax.ShapeDtypeStruct(each, f32)
            for i, each in enumerate(shapes)
        ],
        in_specs=[
            SMEM if x.shape == (1,) else HBM if i in refs else VMEM
            for i, x in enumerate(operands)
        ],
        out_specs=[VMEM] * len(shapes),
        scratch_shapes=list(scratch),
        compiler_params=pltpu.CompilerParams(vmem_limit_bytes=limit * MIB),
        cost_estimate=pl.CostEstimate(
            flops=int(microseconds * 1e9), bytes_accessed=moved, transcendentals=0
        ),
        name=name,
    )(*operands)
    return results if isinstance(shape, list) else results[0]


def transform_tables(extent, size):
    x = np.arange(extent)
    angle = (np.outer(x, np.arange(INNER)) % size) * (2.0 * math.pi / size)
    forward = np.concatenate([np.cos(angle), np.sin(angle)], 0).astype(np.float32)
    backward = np.concatenate([np.cos(angle).T, np.sin(angle).T], 0).astype(np.float32)

    def parts(table):
        high = table.astype(ml_dtypes.bfloat16)
        return high, (table - high.astype(np.float32)).astype(ml_dtypes.bfloat16)

    outer = size // INNER
    turn = (np.outer(np.arange(outer), x) % outer) * (2.0 * math.pi / outer)
    turns = np.stack([np.cos(turn), np.sin(turn)]).astype(np.float32)
    return parts(forward), parts(backward), turns


def phases(first, second, size):
    angle = (first * second % size).astype(f32) * (2.0 * math.pi / size)
    return jnp.cos(angle), jnp.sin(angle)


def image_kernel(
    counts, gathered, y_table, z_table, fh, fl, bh, bl, turns, top, side, y_back, z_back, out
):
    count_x, count_y, count_z, top_rows = counts
    group = count_y * count_z
    half = LANES // 2
    kys = top.shape[2]
    kzs = side.shape[2]
    forward = (fh[...], fl[...])
    backward = (bh[...], bl[...])

    blocks = [
        gathered[g * group : (g + 1) * group, 0:top_rows, :].reshape(group * top_rows, LANES)
        for g in range(count_x)
    ]
    mixed = dot3(y_table[...], split(jnp.concatenate(blocks, axis=1)))
    low_half, high_half = mixed[: 2 * kys], mixed[2 * kys :]
    lane = lax.broadcasted_iota(jnp.int32, (2 * kys, LANES), 1)
    pieces = []
    for g in range(0, count_x, 2):
        a = slice(g * LANES, (g + 1) * LANES)
        b = slice((g + 1) * LANES, (g + 2) * LANES)
        pieces.append(
            jnp.where(
                lane < half,
                low_half[:, a] + pltpu.roll(high_half[:, a], half, 1),
                pltpu.roll(low_half[:, b], half, 1) + high_half[:, b],
            )
        )
    top_lines = jnp.concatenate(pieces, axis=1)

    side_blocks = []
    for y in range(count_y):
        rows = [
            gathered[(x * count_y + y) * count_z + z, top_rows : top_rows + TILE, :]
            for x in range(count_x)
            for z in range(count_z)
        ]
        side_blocks.append(jnp.concatenate(rows, axis=0))
    side_lines = dot3(z_table[...], split(jnp.concatenate(side_blocks, axis=1)))

    real = jnp.concatenate([top_lines[:kys], side_lines[:kzs]], axis=0)
    imag = jnp.concatenate([top_lines[kys:], side_lines[kzs:]], axis=0)
    rows = kys + kzs
    total_real = total_imag = None
    for b in range(turns.shape[1]):
        cosine, sine = turns[0, b : b + 1, :], turns[1, b : b + 1, :]
        turned_real = real * cosine + imag * sine
        turned_imag = imag * cosine - real * sine
        waves = dot3(
            jnp.concatenate(
                [
                    jnp.concatenate([turned_real, turned_imag], axis=1),
                    jnp.concatenate([turned_imag, -turned_real], axis=1),
                ],
                axis=0,
            ),
            forward,
        )
        wave_real, wave_imag = waves[:rows], waves[rows:]
        columns = slice(b * INNER, (b + 1) * INNER)
        weighted_real, weighted_imag = [], []
        for c in range(2):
            for kernel, part in ((top, slice(0, kys)), (side, slice(kys, rows))):
                kernel_real, kernel_imag = kernel[c, 0, :, columns], kernel[c, 1, :, columns]
                weighted_real.append(
                    kernel_real * wave_real[part] + kernel_imag * wave_imag[part]
                )
                weighted_imag.append(
                    kernel_real * wave_imag[part] - kernel_imag * wave_real[part]
                )
        weighted_real = jnp.concatenate(weighted_real, axis=0)
        weighted_imag = jnp.concatenate(weighted_imag, axis=0)
        back = dot3(
            jnp.concatenate(
                [
                    jnp.concatenate([weighted_real, -weighted_imag], axis=1),
                    jnp.concatenate([weighted_imag, weighted_real], axis=1),
                ],
                axis=0,
            ),
            backward,
        )
        back_real, back_imag = back[: 2 * rows], back[2 * rows :]
        if b == 0:
            total_real, total_imag = back_real, back_imag
        else:
            total_real = total_real + (back_real * cosine - back_imag * sine)
            total_imag = total_imag + (back_real * sine + back_imag * cosine)

    y_parts = split(y_back[...])
    depth_rows = []
    quarter = (out.shape[1] - TILE) // 2
    block_x = quarter * count_z
    for c in range(2):
        start = c * rows
        lines = jnp.concatenate(
            [total_real[start : start + kys], total_imag[start : start + kys]], axis=0
        )
        image = dot3(lines.T, y_parts)
        for x in range(count_x):
            for y in range(count_y):
                for z in range(count_z):
                    first = x * block_x + z * quarter
                    out[
                        (x * count_y + y) * count_z + z, c * quarter : (c + 1) * quarter, :
                    ] = image[first : first + quarter, y * LANES : (y + 1) * LANES]
        depth_rows.append(total_real[start + kys : start + rows])
        depth_rows.append(total_imag[start + kys : start + rows])
    side_image = dot3(z_back[...], split(jnp.concatenate(depth_rows, axis=0)))
    for y in range(count_y):
        for z in range(count_z):
            block = side_image[z * TILE : (z + 1) * TILE, y * LANES : (y + 1) * LANES]
            for x in range(count_x):
                out[(x * count_y + y) * count_z + z, 2 * quarter :, :] = block


def image_parts(gathered, top_kernel, side_kernel, counts, block_x, top_rows, depth_block):
    count_x, count_y, count_z = counts
    group = count_y * count_z
    here = [lax.axis_index(axis) for axis in ALL]
    kys, size = top_kernel.shape[2:]
    kzs = side_kernel.shape[2]
    depth_size = kzs * group
    extent = count_y * LANES
    share = depth_block // count_x
    block_y = top_rows * 2

    ky = ((here[0] * count_y + here[1]) * count_z + here[2]) * kys + lax.iota(jnp.int32, kys)
    kz = (here[1] * count_z + here[2]) * kzs + lax.iota(jnp.int32, kzs)

    row = lax.iota(jnp.int32, group * top_rows)
    y_tables = []
    for h in range(2):
        y = row // top_rows * block_y + h * top_rows + row % top_rows
        cosine, sine = phases(ky[:, None], y[None, :], size)
        y_tables += [cosine, -sine]
    y_table = jnp.concatenate(y_tables, axis=0)

    row = lax.iota(jnp.int32, count_x * count_z * TILE)
    inside = row % TILE
    z = row // TILE % count_z * depth_block + row // (TILE * count_z) * share + inside
    cosine, sine = phases(kz[:, None], z[None, :], depth_size)
    z_table = jnp.where((inside < share)[None, :], jnp.concatenate([cosine, -sine], axis=0), 0.0)

    cosine, sine = phases(ky[:, None], lax.iota(jnp.int32, extent)[None, :], size)
    y_back = jnp.concatenate([cosine, -sine], axis=0) * (1.0 / (size * size))

    row = lax.iota(jnp.int32, count_z * TILE)
    z = row // TILE * depth_block + here[0] * share + row % TILE % share
    cosine, sine = phases(z[:, None], kz[None, :], depth_size)
    both = jnp.concatenate([cosine, -sine], axis=1) * (1.0 / (size * depth_size))
    component = (row % TILE // share)[:, None]
    z_back = jnp.concatenate(
        [jnp.where(component == 0, both, 0.0), jnp.where(component == 1, both, 0.0)], axis=1
    )

    forward, backward, turns = transform_tables(extent, size)
    out_rows = 2 * (block_x // count_z) + TILE
    return pl.pallas_call(
        functools.partial(image_kernel, counts + (top_rows,)),
        out_shape=jax.ShapeDtypeStruct((count_x * group, out_rows, LANES), f32),
        compiler_params=pltpu.CompilerParams(vmem_limit_bytes=56 * 1024 * 1024),
        name="images",
    )(
        gathered,
        y_table,
        z_table,
        *(jnp.asarray(t) for t in forward + backward),
        jnp.asarray(turns),
        top_kernel,
        side_kernel,
        y_back,
        z_back,
    )


def begin(semaphores, pairs):
    started = [
        pltpu.make_async_copy(source, target, semaphores.at[i])
        for i, (source, target) in enumerate(pairs)
    ]
    for copy in started:
        copy.start()
    return started


def faces_kernel(
    magnetization, stiffness, z_first, z_last, x_first, x_last, y_faces, m, s, loading
):
    depth, across = stiffness.shape[:2]
    loads = begin(
        loading, [(stiffness, s)] + [(magnetization.at[c], m.at[c]) for c in range(3)]
    )
    lane = lax.broadcasted_iota(jnp.int32, (across, LANES), 1)
    first = jnp.zeros((across, LANES), f32)
    last = jnp.zeros((across, LANES), f32)
    for field in (3, 0, 1, 2):
        loads[(field + 1) % 4].wait()
        ref = s if field == 3 else m.at[field]
        z_first[field] = ref[0]
        z_last[field] = ref[depth - 1]
        x_first[field] = ref[:, 0, :]
        x_last[field] = ref[:, across - 1, :]
        for z in range(depth):
            column = field * depth + z
            turned = pltpu.roll(ref[z], column, 1) if column else ref[z]
            first = jnp.where(lane == column, turned, first)
            last = jnp.where(lane == (column - 1) % LANES, turned, last)
    y_faces[...] = jnp.where(lane < LANES // 2, first, pltpu.roll(last, LANES // 2 + 1, 1))


def twice_weight(a, b):
    return 4.0 * a * b / (a + b)


def exchange_kernel(
    counts,
    here,
    magnetization_from,
    stiffness_from,
    z_next_from,
    z_before_from,
    x_next_from,
    x_before_from,
    y_next_from,
    y_before_from,
    y_faces_from,
    out,
    m,
    s,
    z_next,
    z_before,
    x_next,
    x_before,
    y_next,
    y_before,
    y_faces,
    loading,
):
    depth, across = s.shape[:2]
    chunk = depth // 4
    pairs = [
        (y_next_from, y_next),
        (y_before_from, y_before),
        (y_faces_from, y_faces),
        (z_before_from, z_before),
    ]
    for k in range(4):
        layers = pl.ds(k * chunk, chunk)
        pairs.append((stiffness_from.at[layers], s.at[layers]))
        pairs.append((magnetization_from.at[:, layers], m.at[:, layers]))
    pairs += [
        (z_next_from, z_next),
        (x_next_from, x_next),
        (x_before_from, x_before),
    ]
    loads = begin(loading, pairs)

    count_x, count_y, count_z = counts
    at_z = here[0] % count_z
    at_y = here[0] // count_z % count_y
    at_x = here[0] // (count_z * count_y)

    def inside(condition, values):
        return jnp.where(condition, values, 0.0)

    half = LANES // 2
    lane = lax.broadcasted_iota(jnp.int32, (across, LANES), 1)
    row = lax.broadcasted_iota(jnp.int32, (across, LANES), 0)
    first_lane, last_lane, last_row = lane == 0, lane == LANES - 1, row == across - 1

    stiff = (lane >= 3 * depth) & (lane < 4 * depth)

    def y_edge(own, halo, present):
        weight = twice_weight(
            jnp.where(stiff, own, 1.0), jnp.where(stiff, inside(present, halo), 1.0)
        )
        spread = pltpu.roll(weight, LANES - 3 * depth, 1)
        for c in (1, 2):
            spread = jnp.where(
                lane >= c * depth, pltpu.roll(weight, LANES - (3 - c) * depth, 1), spread
            )
        return spread * (own - halo)

    for copy in loads[:3]:
        copy.wait()
    own = y_faces[...]
    after = y_edge(pltpu.roll(own, half, 1), y_next[...], at_y < count_y - 1)
    before = y_edge(own, pltpu.roll(y_before[...], half, 1), at_y > 0)

    for copy in loads[3:6]:
        copy.wait()
    below_weight = twice_weight(inside(at_z > 0, z_before[3]), s[0])
    below = [below_weight * (z_before[c] - m[c, 0]) for c in range(3)]
    for z in range(depth):
        if z % chunk == chunk - 1:
            k = 4 + 2 * (z // chunk + 1)
            for copy in loads[k : k + 2] if z + 1 < depth else loads[k:]:
                copy.wait()
        centre = s[z]
        above = s[z + 1] if z + 1 < depth else inside(at_z < count_z - 1, z_next[3])
        weight_z = twice_weight(centre, above)
        weight_x = jnp.where(
            last_row, 0.0, twice_weight(centre, pltpu.roll(centre, across - 1, 0))
        )
        weight_y = jnp.where(
            last_lane, 0.0, twice_weight(centre, pltpu.roll(centre, LANES - 1, 1))
        )
        for c in range(3):
            column = c * depth + z
            values = m[c, z]
            upper = m[c, z + 1] if z + 1 < depth else z_next[c]
            up = weight_z * (values - upper)
            flux_x = weight_x * (values - pltpu.roll(values, across - 1, 0))
            flux_y = weight_y * (values - pltpu.roll(values, LANES - 1, 1))
            total = (up - below[c]) + (flux_x - pltpu.roll(flux_x, 1, 0))
            total = total + (flux_y - pltpu.roll(flux_y, 1, 1))
            side = jnp.where(
                first_lane,
                before[:, column : column + 1],
                jnp.where(last_lane, after[:, column : column + 1], 0.0),
            )
            out[c, z] = total + side
            below[c] = up
    for edge_row, halo, present in (
        (across - 1, x_next, at_x < count_x - 1),
        (0, x_before, at_x > 0),
    ):
        weight = twice_weight(s[:, edge_row, :], inside(present, halo[3]))
        for c in range(3):
            out[c, :, edge_row, :] += weight * (m[c, :, edge_row, :] - halo[c])


def ring(block, axis, distance):
    count = lax.axis_size(axis)
    return lax.ppermute(block, axis, [(i, (i + distance) % count) for i in range(count)])


def faces_of(magnetization, stiffness):
    depth, across, along = stiffness.shape
    return call(
        faces_kernel,
        "faces",
        [
            (4, across, along),
            (4, across, along),
            (4, depth, along),
            (4, depth, along),
            (across, LANES),
        ],
        8,
        2.0,
        (from_hbm(magnetization), from_hbm(stiffness)),
        in_hbm=(4,),
        refs=(0, 1),
        scratch=[
            pltpu.VMEM(magnetization.shape, f32),
            pltpu.VMEM(stiffness.shape, f32),
            pltpu.SemaphoreType.DMA((4,)),
        ],
    )


def halos_zy(z_first, z_last, y_faces):
    y_next = ring(y_faces, "gy", -1)
    y_before = y_next if lax.axis_size("gy") == 2 else ring(y_faces, "gy", 1)
    return ring(z_first, "gz", -1), ring(z_last, "gz", 1), y_next, y_before, y_faces


def halos_x(x_first, x_last):
    return ring(x_first, "gx", -1), ring(x_last, "gx", 1)


def exchange_of(counts, index, magnetization, stiffness, zy, x):
    z_next, z_before, y_next, y_before, y_faces = zy
    arrays = (magnetization, stiffness, z_next, z_before, *x, y_next, y_before, y_faces)
    return call(
        functools.partial(exchange_kernel, counts),
        "exchange",
        magnetization.shape,
        8,
        5.0,
        (index, *(from_hbm(array) for array in arrays)),
        refs=range(1, 10),
        scratch=[pltpu.VMEM(array.shape, f32) for array in arrays]
        + [pltpu.SemaphoreType.DMA((15,))],
    )


def whole_log(count):
    return count.bit_length() - 1


def cos_sin(steps, size):
    quarter = steps >> whole_log(size // 4)
    angle = ((steps & (size // 4 - 1)) - size // 8).astype(f32) * (2.0 * math.pi / size)
    square = angle * angle
    sine = cosine = 0.0
    for k in range(5, -1, -1):
        sine = sine * square + (-1) ** k / math.factorial(2 * k + 1)
        cosine = cosine * square + (-1) ** k / math.factorial(2 * k)
    sine = sine * angle
    first, second = (cosine - sine) * math.sqrt(0.5), (cosine + sine) * math.sqrt(0.5)
    odd = (quarter & 1) == 1
    real = jnp.where(odd, -second, first)
    imag = jnp.where(odd, first, second)
    back = quarter >= 2
    return jnp.where(back, -real, real), jnp.where(back, -imag, imag)


def stacked_product(real, imag, tables, sign):
    if sign < 0:
        upper = jnp.concatenate([real, imag], axis=1)
        lower = jnp.concatenate([imag, -real], axis=1)
    else:
        upper = jnp.concatenate([real, -imag], axis=1)
        lower = jnp.concatenate([imag, real], axis=1)
    return dot3(jnp.concatenate([upper, lower], axis=0), tables)


def add(a, b):
    return a[0] + b[0], a[1] + b[1]


def subtract(a, b):
    return a[0] - b[0], a[1] - b[1]


def eight_points(z, sign):
    def quarter_turn(a):
        return (-a[1], a[0]) if sign > 0 else (a[1], -a[0])

    def four_points(p, q, r, s):
        e, f, g, h = add(p, r), subtract(p, r), add(q, s), quarter_turn(subtract(q, s))
        return add(e, g), add(f, h), subtract(e, g), subtract(f, h)

    even = four_points(z[0], z[2], z[4], z[6])
    odd = four_points(z[1], z[3], z[5], z[7])
    root = math.sqrt(0.5)
    first, third = add(odd[1], quarter_turn(odd[1])), subtract(quarter_turn(odd[3]), odd[3])
    odd = (
        odd[0],
        (first[0] * root, first[1] * root),
        quarter_turn(odd[2]),
        (third[0] * root, third[1] * root),
    )
    return [add(a, b) for a, b in zip(even, odd)] + [subtract(a, b) for a, b in zip(even, odd)]


def spread_tables(extent, size):
    step = size // INNER
    count = extent // step
    angle = np.outer(np.arange(count), np.arange(INNER)) * (2.0 * math.pi / INNER)
    cosine, sine = np.cos(angle), np.sin(angle)

    def parts(table):
        table = table.astype(np.float32)
        high = table.astype(ml_dtypes.bfloat16)
        return high, (table - high.astype(np.float32)).astype(ml_dtypes.bfloat16)

    high, low = parts(np.block([[cosine, -sine], [sine, cosine]]))
    there = np.concatenate([high, high, low, np.zeros_like(low)], axis=0)
    high, low = parts(np.block([[cosine.T, sine.T], [-sine.T, cosine.T]]))
    back = np.concatenate([high, low], axis=1)
    angle = np.outer(np.arange(step), np.arange(INNER)) * (2.0 * math.pi / size)
    return there, back, np.stack([np.cos(angle), np.sin(angle)]).astype(np.float32)


def regrouping(extent, step, transposed):
    x = lax.broadcasted_iota(jnp.int32, (extent, extent), int(transposed))
    place = lax.broadcasted_iota(jnp.int32, (extent, extent), 1 - int(transposed))
    count = extent // step
    moved = (x & (step - 1)) * count + (x >> whole_log(step))
    return jnp.where(moved == place, 1.0, 0.0).astype(bf16)


def product(left, right):
    return lax.dot_general(left, right, (((1,), (0,)), ((), ())), preferred_element_type=f32)


def there_and_back(real, imag, columns_of, there, back, turns):
    rows, extent = real.shape
    step = turns.shape[1]
    count = extent // step
    per = LANES // count
    high, low = split(jnp.concatenate([real, imag], axis=0))
    moved = product(jnp.concatenate([high, low], axis=0), regrouping(extent, step, False))
    lane = lax.broadcasted_iota(jnp.int32, (rows, LANES), 1)
    lines = []
    for v in range(step):
        column = v // per * LANES
        first = None
        for k in range(4):
            piece = moved[k * rows : (k + 1) * rows, column : column + LANES]
            shift = (k - v) * count % LANES
            piece = pltpu.roll(piece, shift, 1) if shift else piece
            first = piece if k == 0 else jnp.where(lane < k * count, first, piece)
        second = jnp.where(lane < 2 * count, first, 0.0)
        lines.append(jnp.concatenate([first, second], axis=1))
    waves = product(jnp.concatenate(lines, axis=0).astype(bf16), there)

    results = []
    for start in range(0, rows, 16):
        halves = [[], []]
        for half in range(INNER // LANES):
            lanes = slice(half * LANES, (half + 1) * LANES)
            turn = [(turns[0, v : v + 1, lanes], turns[1, v : v + 1, lanes]) for v in range(step)]
            z = []
            for v in range(step):
                part = waves[v * rows + start : v * rows + start + 16]
                a = part[:, lanes]
                b = part[:, INNER + half * LANES : INNER + (half + 1) * LANES]
                if v:
                    cosine, sine = turn[v]
                    a, b = a * cosine + b * sine, b * cosine - a * sine
                z.append((a, b))
            z = eight_points(z, -1)
            for c in range(2):
                weighted = []
                for k in range(step):
                    kernel = columns_of(k)
                    kernel_real = kernel[c, 0, start : start + 16, lanes]
                    kernel_imag = kernel[c, 1, start : start + 16, lanes]
                    weighted.append(
                        (
                            kernel_real * z[k][0] + kernel_imag * z[k][1],
                            kernel_real * z[k][1] - kernel_imag * z[k][0],
                        )
                    )
                weighted = eight_points(weighted, 1)
                for v in range(1, step):
                    (a, b), (cosine, sine) = weighted[v], turn[v]
                    weighted[v] = (a * cosine - b * sine, a * sine + b * cosine)
                halves[c].append(weighted)
        parts = ([], [])
        for v in range(step):
            for c in range(2):
                pieces = [
                    split(halves[c][half][v][k])
                    for k in range(2)
                    for half in range(INNER // LANES)
                ]
                for k in range(2):
                    parts[k].append(jnp.concatenate([piece[k] for piece in pieces], axis=1))
        both = product(jnp.concatenate(parts[0] + parts[1], axis=0), back)
        middle = both.shape[0] // 2
        results.append(both[:middle] + pltpu.roll(both[:middle], LANES // 2, 1) + both[middle:])
    return results


def lines_kernel(counts, here, gathered, swapped, there, back, turns, kernel, out):
    count_x, count_y, count_z = counts
    group = count_y * count_z
    top_rows = LANES // group
    half = LANES // 2
    kys, size = kernel.shape[2:]
    ky = here[0] * kys + lax.broadcasted_iota(jnp.int32, (kys, LANES), 0)
    lane = lax.broadcasted_iota(jnp.int32, (kys, LANES), 1)
    odd = (lane >> whole_log(LANES // 2)) ^ (here[0] & 1)
    pair = lane >> whole_log(top_rows) & (group // 2 - 1)
    table = []
    for h in range(2):
        y = (2 * pair + odd) * (2 * top_rows) + h * top_rows + (lane & (top_rows - 1))
        cosine, sine = cos_sin(ky * y & (size - 1), size)
        table += [cosine, -sine]
    blocks = []
    for g in range(count_x):
        members = slice(g * group // 2, (g + 1) * group // 2)
        blocks.append(
            jnp.concatenate(
                [
                    part[members, 0:top_rows, :].reshape(half, LANES)
                    for part in (gathered, swapped)
                ],
                axis=0,
            )
        )
    mixed = dot3(jnp.concatenate(table, axis=0), split(jnp.concatenate(blocks, axis=1)))
    low_half, high_half = mixed[: 2 * kys], mixed[2 * kys :]
    lane = lax.broadcasted_iota(jnp.int32, (2 * kys, LANES), 1)
    pieces = []
    for g in range(0, count_x, 2):
        a = slice(g * LANES, (g + 1) * LANES)
        b = slice((g + 1) * LANES, (g + 2) * LANES)
        pieces.append(
            jnp.where(
                lane < half,
                low_half[:, a] + pltpu.roll(high_half[:, a], half, 1),
                pltpu.roll(low_half[:, b], half, 1) + high_half[:, b],
            )
        )
    lines = jnp.concatenate(pieces, axis=1)

    def columns_of(b):
        return kernel.at[:, :, :, b * INNER : (b + 1) * INNER]

    results = there_and_back(
        lines[:kys], lines[kys:], columns_of, there[...], back[...], turns
    )
    count = count_x * group
    for v in range(turns.shape[1]):
        block = jnp.concatenate(
            [result[(2 * v + c) * 16 : (2 * v + c + 1) * 16] for c in range(2) for result in results],
            axis=0,
        ).T
        out[:, v, :] = block[:count]
        out[:, TILE + v, :] = block[count : 2 * count]


def side_kernel_body(
    counts, here, gathered, swapped, there, back, turns, kernel_from, out, kernel, loading
):
    count_x, count_y, count_z = counts
    depth_block = out.shape[1] // 2
    top_rows = gathered.shape[1] - TILE
    kzs, length = kernel_from.shape[2:]
    loads = begin(
        loading,
        [
            (kernel_from.at[:, :, :, pl.ds(b * INNER, INNER)], kernel.at[b])
            for b in range(length // INNER)
        ],
    )
    size = kzs * count_y * count_z
    share = depth_block // count_x

    columns = count_x * count_z * TILE
    kz = here[0] * kzs + lax.broadcasted_iota(jnp.int32, (kzs, columns), 0)
    column = lax.broadcasted_iota(jnp.int32, (kzs, columns), 1)
    within = column & (TILE - 1)
    pair = column >> whole_log(TILE) & (count_z // 2 - 1)
    odd = (column >> whole_log(columns // 2)) ^ (here[0] & 1)
    z = (2 * pair + odd) * depth_block + within
    z = z + (column >> whole_log(TILE * count_z // 2) & (count_x - 1)) * share
    cosine, sine = cos_sin(kz * z & (size - 1), size)
    table = jnp.concatenate([cosine, -sine], axis=0)
    table = jnp.where(jnp.concatenate([within, within], axis=0) < share, table, 0.0)

    blocks = []
    for y in range(count_y):
        rows = [
            part[(x * count_y + y) * count_z // 2 + pair, top_rows:, :]
            for part in (gathered, swapped)
            for x in range(count_x)
            for pair in range(count_z // 2)
        ]
        blocks.append(jnp.concatenate(rows, axis=0))
    lines = dot3(table, split(jnp.concatenate(blocks, axis=1)))

    waiting = dict(enumerate(loads))

    def columns_of(b):
        if b in waiting:
            waiting.pop(b).wait()
        return kernel.at[b]

    result = there_and_back(
        lines[:kzs], lines[kzs:], columns_of, there[...], back[...], turns
    )[0]
    step = turns.shape[1]
    extent = count_y * LANES
    count = extent // step
    per = LANES // count
    lane = lax.broadcasted_iota(jnp.int32, (kzs, LANES), 1)
    images = []
    for c in range(2):
        for k in range(2):
            columns = []
            for first in range(0, step, per):
                column = None
                for v in range(first, first + per):
                    piece = result[(2 * v + c) * 16 : (2 * v + c + 1) * 16]
                    shift = (v - first - k) * count % LANES
                    piece = pltpu.roll(piece, shift, 1) if shift else piece
                    column = (
                        piece
                        if v == first
                        else jnp.where(lane < (v - first) * count, column, piece)
                    )
                columns.append(column)
            images.append(jnp.concatenate(columns, axis=1))
    high, low = split(jnp.concatenate(images, axis=0))
    order = regrouping(extent, step, True)
    images = product(high, order) + product(low, order)

    rows = depth_block * count_z
    z = lax.broadcasted_iota(jnp.int32, (rows, 2 * kzs), 0)
    column = lax.broadcasted_iota(jnp.int32, (rows, 2 * kzs), 1)
    cosine, sine = cos_sin((here[0] * kzs + (column & (kzs - 1))) * z & (size - 1), size)
    table = jnp.where(column < kzs, cosine, -sine) * (1.0 / (size * length))
    for c in range(2):
        image = dot3(table, split(images[2 * kzs * c : 2 * kzs * (c + 1)]))
        for y in range(count_y):
            for z in range(count_z):
                out[y * count_z + z, c * depth_block : (c + 1) * depth_block, :] = image[
                    z * depth_block : (z + 1) * depth_block, y * LANES : (y + 1) * LANES
                ]


def rows_kernel(counts, arrived, side, high, low, turns, out, loading):
    count_y, count_z = counts[1:]
    loads = begin(loading, [(side, out.at[:, 2 * TILE :, :])])
    per_turn = arrived.shape[0] // turns.shape[1]
    half = LANES // 2
    lane = lax.broadcasted_iota(jnp.int32, (2 * TILE, LANES), 1)
    parts = [[], []]
    for b in range(turns.shape[1]):
        spectra = ([], [])
        for g in range(b * per_turn, (b + 1) * per_turn, 2):
            first, second = arrived[g], arrived[g + 1]
            spectra[0].append(jnp.where(lane < half, first, pltpu.roll(second, half, 1)))
            spectra[1].append(jnp.where(lane < half, pltpu.roll(first, half, 1), second))
        spectra = [jnp.concatenate(pieces, axis=1) for pieces in spectra]
        for k in range(2):
            parts[k] += [spectrum[k * TILE : (k + 1) * TILE] for spectrum in spectra]
    real, imag = parts
    back = stacked_product(
        jnp.concatenate(real, axis=0), jnp.concatenate(imag, axis=0), (high[...], low[...]), 1
    )
    middle = back.shape[0] // 2
    size = turns.shape[1] * INNER
    total = None
    for b in range(turns.shape[1]):
        part = slice(b * 2 * TILE, (b + 1) * 2 * TILE)
        term = back[:middle][part] * turns[0, b : b + 1, :]
        term = term - back[middle:][part] * turns[1, b : b + 1, :]
        total = term if b == 0 else total + term
    total = total * (1.0 / (size * size))
    for y in range(count_y):
        for z in range(count_z):
            out[y * count_z + z, 0 : 2 * TILE, :] = total[:, y * LANES : (y + 1) * LANES]
    loads[0].wait()


def sum_kernel(exchange_grad, arrived, out):
    depth = exchange_grad.shape[1]
    group = arrived.shape[0]
    side = [None, None]
    top = [None, None]
    for c in range(2):
        rows = slice(2 * TILE + c * depth, 2 * TILE + (c + 1) * depth)
        total = arrived[0, rows, :]
        for p in range(1, group):
            total = total + arrived[p, rows, :]
        side[c] = total
        top[c] = arrived[:, c * TILE : (c + 1) * TILE, :].reshape(group * TILE, LANES)
    for z in range(depth):
        out[0, z] = exchange_grad[0, z] + top[0]
        out[1, z] = exchange_grad[1, z] + top[1] + side[0][z : z + 1]
        out[2, z] = exchange_grad[2, z] + side[1][z : z + 1]


def residual_blocks(residual_top, residual_side, devices, share):
    block_x, block_y = residual_top.shape
    top_rows = block_y // 2

    def body(at_x, top, side, out):
        piece = jnp.concatenate([top[0:top_rows, :], top[top_rows:, :]], axis=1)
        part = side[pl.ds(at_x[0] * share, share), :]
        part = jnp.concatenate([part, jnp.zeros((TILE - share, LANES), f32)], axis=0)
        for device in range(devices):
            out[device, 0:top_rows, :] = piece
            out[device, top_rows:, :] = part

    return call(
        body,
        "pack",
        (devices, top_rows + TILE, LANES),
        60,
        0.8,
        (lax.axis_index("gx").reshape(1), residual_top.T, residual_side.T),
    )


def fast_on_device(magnetization, stiffness, residual_top, residual_side, top_kernel, side_kernel):
    counts = tuple(lax.axis_size(axis) for axis in ALL)
    count_x, count_y, count_z = counts
    group = count_y * count_z
    devices = count_x * group
    block_x, block_y = residual_top.shape
    depth_block = stiffness.shape[0]
    top_rows = block_y // 2
    kys, size = top_kernel.shape[2:]
    kzs = side_kernel.shape[2]
    extent = count_x * block_x
    here = [lax.axis_index(axis) for axis in ALL]
    plane_index = here[1] * count_z + here[2]
    index = (here[0] * group + plane_index).reshape(1)
    plane_index = plane_index.reshape(1)
    (high, low), _, turns = transform_tables(extent, size)
    high, low, turns = jnp.asarray(high), jnp.asarray(low), jnp.asarray(turns)
    there, back, spread_turns = (jnp.asarray(table) for table in spread_tables(extent, size))

    parities = [range(parity, devices, 2) for parity in range(2)]
    sent = residual_blocks(residual_top, residual_side, devices // 2, depth_block // count_x)
    gathered = lax.all_to_all(
        sent, ALL, 0, 0, tiled=True, axis_index_groups=[list(each) for each in parities]
    )
    z_first, z_last, x_first, x_last, y_faces = faces_of(magnetization, stiffness)
    gathered, x_first, x_last, y_faces = lax.optimization_barrier(
        (gathered, x_first, x_last, y_faces)
    )
    swapped = lax.ppermute(gathered, "gz", [(i, i ^ 1) for i in range(count_z)])
    zy = halos_zy(z_first, z_last, y_faces)

    lines = call(
        functools.partial(lines_kernel, counts),
        "lines",
        (devices, 2 * TILE, LANES),
        16,
        4.0,
        (index, gathered, swapped, there, back, spread_turns, top_kernel),
    )
    arrived = lax.all_to_all(lines, ALL, 0, 0, tiled=True)
    lines, x_first, x_last = lax.optimization_barrier((lines, x_first, x_last))
    x = halos_x(x_first, x_last)
    side = call(
        functools.partial(side_kernel_body, counts),
        "side",
        (group, 2 * depth_block, LANES),
        8,
        2.8,
        (plane_index, gathered, swapped, there, back, spread_turns, from_hbm(side_kernel)),
        in_hbm=(0,),
        refs=(6,),
        scratch=[
            pltpu.VMEM((size // INNER, 2, 2, kzs, INNER), f32),
            pltpu.SemaphoreType.DMA((size // INNER,)),
        ],
    )
    arrived, side = lax.optimization_barrier((arrived, side))
    rows = call(
        functools.partial(rows_kernel, counts),
        "rows",
        (group, 2 * TILE + 2 * depth_block, LANES),
        8,
        1.4,
        (arrived, from_hbm(side), high, low, turns),
        refs=(1,),
        scratch=[pltpu.SemaphoreType.DMA((1,))],
    )
    rows, zy, x = lax.optimization_barrier((rows, zy, x))
    arrived = lax.all_to_all(rows, ("gy", "gz"), 0, 0, tiled=True)
    exchange_grad = exchange_of(counts, index, magnetization, stiffness, zy, x)
    return call(sum_kernel, "gradient", magnetization.shape, 16, 1.2, (exchange_grad, arrived))


def fits(counts, stiffness, residual_top, residual_side, top_kernel, side_kernel):
    count_x, count_y, count_z = counts
    block_x, block_y = residual_top.shape
    group = count_y * count_z
    return (
        2 * block_x == LANES
        and 2 * top_kernel.shape[2] == LANES
        and stiffness.shape[2] == LANES
        and block_x == group * TILE
        and block_y * group == count_x * block_x == INNER
        and count_y * LANES == INNER
        and block_y % 16 == 0
        and count_x % 2 == 0
        and count_z % 2 == 0
        and (count_x * group) % (2 * top_kernel.shape[3] // INNER) == 0
        and INNER == top_kernel.shape[2] * count_z
        and top_kernel.shape[3] == TILE * INNER == side_kernel.shape[3]
        and INNER == 2 * LANES
        and stiffness.shape[0] % 16 == 0
        and side_kernel.shape[2] % 16 == 0
        and all(
            count & (count - 1) == 0
            for count in (group, count_x, count_z, top_kernel.shape[3], side_kernel.shape[2])
        )
    )


def on_device(magnetization, stiffness, residual_top, residual_side, top_kernel, side_kernel):
    counts = tuple(lax.axis_size(axis) for axis in ALL)
    count_x, count_y, count_z = counts
    if fits(counts, stiffness, residual_top, residual_side, top_kernel, side_kernel):
        return fast_on_device(
            magnetization, stiffness, residual_top, residual_side, top_kernel, side_kernel
        )
    devices = count_x * count_y * count_z
    depth_block = stiffness.shape[0]
    block_x, block_y = residual_top.shape
    top_rows = block_y // 2
    share = depth_block // count_x

    sent = residual_blocks(residual_top, residual_side, devices, share)
    rows = sent.shape[1]
    gathered = lax.all_to_all(sent, ALL, 0, 0, tiled=True)
    index = (
        (lax.axis_index("gx") * count_y + lax.axis_index("gy")) * count_z + lax.axis_index("gz")
    ).reshape(1)
    z_first, z_last, x_first, x_last, y_faces = faces_of(magnetization, stiffness)
    exchange_grad = exchange_of(
        counts,
        index,
        magnetization,
        stiffness,
        halos_zy(z_first, z_last, y_faces),
        halos_x(x_first, x_last),
    )

    parts = image_parts(
        gathered, top_kernel, side_kernel, counts, block_x, top_rows, depth_block
    )
    rows = parts.shape[1]
    arrived = lax.all_to_all(parts.reshape(devices * rows, LANES), ALL, 0, 0, tiled=True)
    arrived = arrived.reshape(devices, rows, LANES)
    top_sum = jnp.sum(arrived[:, : rows - TILE], axis=0)
    side_sum = jnp.sum(
        arrived[:, rows - TILE :].reshape(count_x, count_y * count_z, TILE, LANES), axis=1
    )
    side = side_sum[:, : 2 * share].reshape(count_x, 2, share, LANES)
    side = jnp.swapaxes(side, 0, 1).reshape(2, depth_block, 1, LANES)
    top = lax.all_gather(top_sum, "gz", axis=0)
    top = jnp.swapaxes(top.reshape(count_z, 2, block_x // count_z, LANES), 0, 1)
    top = top.reshape(2, 1, block_x, LANES)
    return jnp.stack(
        [
            exchange_grad[0] + top[0],
            exchange_grad[1] + top[1] + side[0],
            exchange_grad[2] + side[1],
        ]
    )


def solution(mesh):
    placed = (
        P(None, "gz", "gx", "gy"),
        P("gz", "gx", "gy"),
        P("gx", ("gy", "gz")),
        P("gy", "gz"),
        P(None, None, ("gx", "gy", "gz"), None),
        P(None, None, ("gy", "gz"), None),
    )
    return jax.shard_map(
        on_device, mesh=mesh, in_specs=placed, out_specs=P(None, "gz", "gx", "gy"), check_vma=False
    )
```

```python
import functools
import math

import jax
import jax.numpy as jnp
import ml_dtypes
import numpy as np
from jax import lax
from jax.experimental import pallas as pl
from jax.experimental.pallas import tpu as pltpu
from jax.sharding import PartitionSpec as P

LANES = 128
TILE = 8
INNER = 256
ALL = ("gx", "gy", "gz")
f32 = jnp.float32
bf16 = jnp.bfloat16
MIB = 1024 * 1024
SMEM = pl.BlockSpec(memory_space=pltpu.SMEM)
VMEM = pl.BlockSpec(memory_space=pltpu.VMEM)
HBM = pl.BlockSpec(memory_space=pltpu.HBM)


def whole_log(count):
    return count.bit_length() - 1


def split(values):
    high = values.astype(bf16)
    return high, (values - high.astype(f32)).astype(bf16)


def dot3(left, right):
    high, low = split(left)
    def one(a, b):
        return lax.dot_general(a, b, (((1,), (0,)), ((), ())), preferred_element_type=f32)
    return one(high, right[0]) + one(low, right[0]) + one(high, right[1])


def from_hbm(values):
    return pltpu.with_memory_space_constraint(values, pltpu.HBM)


def call(body, name, shape, limit, microseconds, operands, in_hbm=(), scratch=(), refs=(), out_refs=(), aliases=()):
    shapes = shape if isinstance(shape, list) else [shape]
    moved = sum(4 * math.prod(each) for each in shapes)
    moved += sum(x.size * x.dtype.itemsize for x in operands)
    results = pl.pallas_call(
        body,
        out_shape=[
            pltpu.HBM(each, f32) if i in in_hbm else jax.ShapeDtypeStruct(each, f32)
            for i, each in enumerate(shapes)
        ],
        in_specs=[
            SMEM if x.shape == (1,) else HBM if i in refs else VMEM
            for i, x in enumerate(operands)
        ],
        out_specs=[HBM if i in out_refs else VMEM for i in range(len(shapes))],
        input_output_aliases=dict(aliases),
        scratch_shapes=list(scratch),
        compiler_params=pltpu.CompilerParams(vmem_limit_bytes=limit * MIB),
        cost_estimate=pl.CostEstimate(
            flops=int(microseconds * 1e9), bytes_accessed=moved, transcendentals=0
        ),
        name=name,
    )(*operands)
    return results if isinstance(shape, list) else results[0]


def transform_tables(extent, size):
    x = np.arange(extent)
    angle = (np.outer(x, np.arange(INNER)) % size) * (2.0 * math.pi / size)
    forward = np.concatenate([np.cos(angle), np.sin(angle)], 0).astype(np.float32)
    backward = np.concatenate([np.cos(angle).T, np.sin(angle).T], 0).astype(np.float32)

    def parts(table):
        high = table.astype(ml_dtypes.bfloat16)
        return high, (table - high.astype(np.float32)).astype(ml_dtypes.bfloat16)

    outer = size // INNER
    turn = (np.outer(np.arange(outer), x) % outer) * (2.0 * math.pi / outer)
    turns = np.stack([np.cos(turn), np.sin(turn)]).astype(np.float32)
    return parts(forward), parts(backward), turns


def phases(first, second, size):
    angle = (first * second % size).astype(f32) * (2.0 * math.pi / size)
    return jnp.cos(angle), jnp.sin(angle)


def image_kernel(
    counts, gathered, y_table, z_table, fh, fl, bh, bl, turns, top, side, y_back, z_back, out
):
    count_x, count_y, count_z, top_rows = counts
    group = count_y * count_z
    half = LANES // 2
    kys = top.shape[2]
    kzs = side.shape[2]
    forward = (fh[...], fl[...])
    backward = (bh[...], bl[...])

    blocks = [
        gathered[g * group : (g + 1) * group, 0:top_rows, :].reshape(group * top_rows, LANES)
        for g in range(count_x)
    ]
    mixed = dot3(y_table[...], split(jnp.concatenate(blocks, axis=1)))
    low_half, high_half = mixed[: 2 * kys], mixed[2 * kys :]
    lane = lax.broadcasted_iota(jnp.int32, (2 * kys, LANES), 1)
    pieces = []
    for g in range(0, count_x, 2):
        a = slice(g * LANES, (g + 1) * LANES)
        b = slice((g + 1) * LANES, (g + 2) * LANES)
        pieces.append(
            jnp.where(
                lane < half,
                low_half[:, a] + pltpu.roll(high_half[:, a], half, 1),
                pltpu.roll(low_half[:, b], half, 1) + high_half[:, b],
            )
        )
    top_lines = jnp.concatenate(pieces, axis=1)

    side_blocks = []
    for y in range(count_y):
        rows = [
            gathered[(x * count_y + y) * count_z + z, top_rows : top_rows + TILE, :]
            for x in range(count_x)
            for z in range(count_z)
        ]
        side_blocks.append(jnp.concatenate(rows, axis=0))
    side_lines = dot3(z_table[...], split(jnp.concatenate(side_blocks, axis=1)))

    real = jnp.concatenate([top_lines[:kys], side_lines[:kzs]], axis=0)
    imag = jnp.concatenate([top_lines[kys:], side_lines[kzs:]], axis=0)
    rows = kys + kzs
    total_real = total_imag = None
    for b in range(turns.shape[1]):
        cosine, sine = turns[0, b : b + 1, :], turns[1, b : b + 1, :]
        turned_real = real * cosine + imag * sine
        turned_imag = imag * cosine - real * sine
        waves = dot3(
            jnp.concatenate(
                [
                    jnp.concatenate([turned_real, turned_imag], axis=1),
                    jnp.concatenate([turned_imag, -turned_real], axis=1),
                ],
                axis=0,
            ),
            forward,
        )
        wave_real, wave_imag = waves[:rows], waves[rows:]
        columns = slice(b * INNER, (b + 1) * INNER)
        weighted_real, weighted_imag = [], []
        for c in range(2):
            for kernel, part in ((top, slice(0, kys)), (side, slice(kys, rows))):
                kernel_real, kernel_imag = kernel[c, 0, :, columns], kernel[c, 1, :, columns]
                weighted_real.append(
                    kernel_real * wave_real[part] + kernel_imag * wave_imag[part]
                )
                weighted_imag.append(
                    kernel_real * wave_imag[part] - kernel_imag * wave_real[part]
                )
        weighted_real = jnp.concatenate(weighted_real, axis=0)
        weighted_imag = jnp.concatenate(weighted_imag, axis=0)
        back = dot3(
            jnp.concatenate(
                [
                    jnp.concatenate([weighted_real, -weighted_imag], axis=1),
                    jnp.concatenate([weighted_imag, weighted_real], axis=1),
                ],
                axis=0,
            ),
            backward,
        )
        back_real, back_imag = back[: 2 * rows], back[2 * rows :]
        if b == 0:
            total_real, total_imag = back_real, back_imag
        else:
            total_real = total_real + (back_real * cosine - back_imag * sine)
            total_imag = total_imag + (back_real * sine + back_imag * cosine)

    y_parts = split(y_back[...])
    depth_rows = []
    quarter = (out.shape[1] - TILE) // 2
    block_x = quarter * count_z
    for c in range(2):
        start = c * rows
        lines = jnp.concatenate(
            [total_real[start : start + kys], total_imag[start : start + kys]], axis=0
        )
        image = dot3(lines.T, y_parts)
        for x in range(count_x):
            for y in range(count_y):
                for z in range(count_z):
                    first = x * block_x + z * quarter
                    out[
                        (x * count_y + y) * count_z + z, c * quarter : (c + 1) * quarter, :
                    ] = image[first : first + quarter, y * LANES : (y + 1) * LANES]
        depth_rows.append(total_real[start + kys : start + rows])
        depth_rows.append(total_imag[start + kys : start + rows])
    side_image = dot3(z_back[...], split(jnp.concatenate(depth_rows, axis=0)))
    for y in range(count_y):
        for z in range(count_z):
            block = side_image[z * TILE : (z + 1) * TILE, y * LANES : (y + 1) * LANES]
            for x in range(count_x):
                out[(x * count_y + y) * count_z + z, 2 * quarter :, :] = block


def image_parts(gathered, top_kernel, side_kernel, counts, block_x, top_rows, depth_block):
    count_x, count_y, count_z = counts
    group = count_y * count_z
    here = [lax.axis_index(axis) for axis in ALL]
    kys, size = top_kernel.shape[2:]
    kzs = side_kernel.shape[2]
    depth_size = kzs * group
    extent = count_y * LANES
    share = depth_block // count_x
    block_y = top_rows * 2

    ky = ((here[0] * count_y + here[1]) * count_z + here[2]) * kys + lax.iota(jnp.int32, kys)
    kz = (here[1] * count_z + here[2]) * kzs + lax.iota(jnp.int32, kzs)

    row = lax.iota(jnp.int32, group * top_rows)
    y_tables = []
    for h in range(2):
        y = row // top_rows * block_y + h * top_rows + row % top_rows
        cosine, sine = phases(ky[:, None], y[None, :], size)
        y_tables += [cosine, -sine]
    y_table = jnp.concatenate(y_tables, axis=0)

    row = lax.iota(jnp.int32, count_x * count_z * TILE)
    inside = row % TILE
    z = row // TILE % count_z * depth_block + row // (TILE * count_z) * share + inside
    cosine, sine = phases(kz[:, None], z[None, :], depth_size)
    z_table = jnp.where((inside < share)[None, :], jnp.concatenate([cosine, -sine], axis=0), 0.0)

    cosine, sine = phases(ky[:, None], lax.iota(jnp.int32, extent)[None, :], size)
    y_back = jnp.concatenate([cosine, -sine], axis=0) * (1.0 / (size * size))

    row = lax.iota(jnp.int32, count_z * TILE)
    z = row // TILE * depth_block + here[0] * share + row % TILE % share
    cosine, sine = phases(z[:, None], kz[None, :], depth_size)
    both = jnp.concatenate([cosine, -sine], axis=1) * (1.0 / (size * depth_size))
    component = (row % TILE // share)[:, None]
    z_back = jnp.concatenate(
        [jnp.where(component == 0, both, 0.0), jnp.where(component == 1, both, 0.0)], axis=1
    )

    forward, backward, turns = transform_tables(extent, size)
    out_rows = 2 * (block_x // count_z) + TILE
    return pl.pallas_call(
        functools.partial(image_kernel, counts + (top_rows,)),
        out_shape=jax.ShapeDtypeStruct((count_x * group, out_rows, LANES), f32),
        compiler_params=pltpu.CompilerParams(vmem_limit_bytes=56 * 1024 * 1024),
        name="images",
    )(
        gathered,
        y_table,
        z_table,
        *(jnp.asarray(t) for t in forward + backward),
        jnp.asarray(turns),
        top_kernel,
        side_kernel,
        y_back,
        z_back,
    )


def begin(semaphores, pairs):
    started = [
        pltpu.make_async_copy(source, target, semaphores.at[i])
        for i, (source, target) in enumerate(pairs)
    ]
    for copy in started:
        copy.start()
    return started


def faces_kernel(
    magnetization, stiffness, z_first, z_last, x_first, x_last, y_faces, m, s, loading
):
    depth, across = stiffness.shape[:2]
    loads = begin(
        loading, [(stiffness, s)] + [(magnetization.at[c], m.at[c]) for c in range(3)]
    )
    lane = lax.broadcasted_iota(jnp.int32, (across, LANES), 1)
    pair = (lane + 1 & (LANES - 1)) >> 1
    sides = jnp.zeros((across, LANES), f32)
    for field in (3, 0, 1, 2):
        loads[(field + 1) % 4].wait()
        ref = s if field == 3 else m.at[field]
        z_first[field] = ref[0]
        z_last[field] = ref[depth - 1]
        x_first[field] = ref[:, 0, :]
        x_last[field] = ref[:, across - 1, :]
        for z in range(depth):
            column = field * depth + z
            turned = pltpu.roll(ref[z], 2 * column, 1) if column else ref[z]
            sides = jnp.where(pair == column, turned, sides)
    y_faces[...] = sides


def twice_weight(a, b):
    total = a + b
    inverse = pl.reciprocal(total, approx=True)
    return 4.0 * a * b * (inverse * (2.0 - total * inverse))


def exchange_kernel(
    counts,
    here,
    magnetization_from,
    stiffness_from,
    z_next_from,
    z_before_from,
    x_next_from,
    x_before_from,
    y_next_from,
    y_before_from,
    y_faces_from,
    out,
    m,
    s,
    z_next,
    z_before,
    x_next,
    x_before,
    y_next,
    y_before,
    y_faces,
    loading,
):
    depth, across = s.shape[:2]
    chunk = depth // 4
    pairs = [
        (y_next_from, y_next),
        (y_before_from, y_before),
        (y_faces_from, y_faces),
        (z_before_from, z_before),
    ]
    for k in range(4):
        layers = pl.ds(k * chunk, chunk)
        pairs.append((stiffness_from.at[layers], s.at[layers]))
        pairs.append((magnetization_from.at[:, layers], m.at[:, layers]))
    pairs += [
        (z_next_from, z_next),
        (x_next_from, x_next),
        (x_before_from, x_before),
    ]
    loads = begin(loading, pairs)

    count_x, count_y, count_z = counts
    at_z = here[0] % count_z
    at_y = here[0] // count_z % count_y
    at_x = here[0] // (count_z * count_y)

    def inside(condition, values):
        return jnp.where(condition, values, 0.0)

    lane = lax.broadcasted_iota(jnp.int32, (across, LANES), 1)
    row = lax.broadcasted_iota(jnp.int32, (across, LANES), 0)
    first_lane, last_lane, last_row = lane == 0, lane == LANES - 1, row == across - 1

    for copy in loads[:3]:
        copy.wait()
    own = y_faces[...]
    even = (lane & 1) == 0
    field = (lane + 1 & (LANES - 1)) >> whole_log(2 * depth)
    halo = jnp.where(
        even, pltpu.roll(y_before[...], 1, 1), pltpu.roll(y_next[...], LANES - 1, 1)
    )
    present = jnp.where(even, at_y, count_y - 1 - at_y) > 0
    weight = twice_weight(
        jnp.where(field == 3, own, 1.0),
        jnp.where(field == 3, jnp.where(present, halo, 0.0), 1.0),
    )
    spread = pltpu.roll(weight, LANES - 6 * depth, 1)
    for c in (1, 2):
        spread = jnp.where(
            field == c, pltpu.roll(weight, LANES - (3 - c) * 2 * depth, 1), spread
        )
    sides = spread * (own - halo)
    outer = first_lane | last_lane

    for copy in loads[3:6]:
        copy.wait()
    below_weight = twice_weight(inside(at_z > 0, z_before[3]), s[0])
    below = [below_weight * (z_before[c] - m[c, 0]) for c in range(3)]
    for z in range(depth):
        if z % chunk == chunk - 1:
            k = 4 + 2 * (z // chunk + 1)
            for copy in loads[k : k + 2] if z + 1 < depth else loads[k:]:
                copy.wait()
        centre = s[z]
        above = s[z + 1] if z + 1 < depth else inside(at_z < count_z - 1, z_next[3])
        weight_z = twice_weight(centre, above)
        weight_x = jnp.where(
            last_row, 0.0, twice_weight(centre, pltpu.roll(centre, across - 1, 0))
        )
        weight_y = jnp.where(
            last_lane, 0.0, twice_weight(centre, pltpu.roll(centre, LANES - 1, 1))
        )
        for c in range(3):
            column = c * depth + z
            values = m[c, z]
            upper = m[c, z + 1] if z + 1 < depth else z_next[c]
            up = weight_z * (values - upper)
            flux_x = weight_x * (values - pltpu.roll(values, across - 1, 0))
            flux_y = weight_y * (values - pltpu.roll(values, LANES - 1, 1))
            total = (up - below[c]) + (flux_x - pltpu.roll(flux_x, 1, 0))
            total = total + (flux_y - pltpu.roll(flux_y, 1, 1))
            both = pltpu.roll(sides, LANES - 2 * column, 1) if column else sides
            out[c, z] = jnp.where(outer, total + both, total)
            below[c] = up
    for edge_row, halo, present in (
        (across - 1, x_next, at_x < count_x - 1),
        (0, x_before, at_x > 0),
    ):
        weight = twice_weight(s[:, edge_row, :], inside(present, halo[3]))
        for c in range(3):
            out[c, :, edge_row, :] += weight * (m[c, :, edge_row, :] - halo[c])


def ring(block, axis, distance):
    count = lax.axis_size(axis)
    return lax.ppermute(block, axis, [(i, (i + distance) % count) for i in range(count)])


def faces_of(magnetization, stiffness):
    depth, across, along = stiffness.shape
    return call(
        faces_kernel,
        "faces",
        [
            (4, across, along),
            (4, across, along),
            (4, depth, along),
            (4, depth, along),
            (across, LANES),
        ],
        8,
        2.0,
        (from_hbm(magnetization), from_hbm(stiffness)),
        in_hbm=(4,),
        refs=(0, 1),
        scratch=[
            pltpu.VMEM(magnetization.shape, f32),
            pltpu.VMEM(stiffness.shape, f32),
            pltpu.SemaphoreType.DMA((4,)),
        ],
    )


def halos_zy(z_first, z_last, y_faces):
    y_next = ring(y_faces, "gy", -1)
    y_before = y_next if lax.axis_size("gy") == 2 else ring(y_faces, "gy", 1)
    return ring(z_first, "gz", -1), ring(z_last, "gz", 1), y_next, y_before, y_faces


def halos_x(x_first, x_last):
    return ring(x_first, "gx", -1), ring(x_last, "gx", 1)


def exchange_of(counts, index, magnetization, stiffness, zy, x):
    z_next, z_before, y_next, y_before, y_faces = zy
    arrays = (magnetization, stiffness, z_next, z_before, *x, y_next, y_before, y_faces)
    return call(
        functools.partial(exchange_kernel, counts),
        "exchange",
        magnetization.shape,
        8,
        5.0,
        (index, *(from_hbm(array) for array in arrays)),
        refs=range(1, 10),
        scratch=[pltpu.VMEM(array.shape, f32) for array in arrays]
        + [pltpu.SemaphoreType.DMA((15,))],
    )


def cos_sin(steps, size):
    quarter = steps >> whole_log(size // 4)
    angle = ((steps & (size // 4 - 1)) - size // 8).astype(f32) * (2.0 * math.pi / size)
    square = angle * angle
    sine = cosine = 0.0
    for k in range(5, -1, -1):
        sine = sine * square + (-1) ** k / math.factorial(2 * k + 1)
        cosine = cosine * square + (-1) ** k / math.factorial(2 * k)
    sine = sine * angle
    first, second = (cosine - sine) * math.sqrt(0.5), (cosine + sine) * math.sqrt(0.5)
    odd = (quarter & 1) == 1
    real = jnp.where(odd, -second, first)
    imag = jnp.where(odd, first, second)
    back = quarter >= 2
    return jnp.where(back, -real, real), jnp.where(back, -imag, imag)


def add(a, b):
    return a[0] + b[0], a[1] + b[1]


def subtract(a, b):
    return a[0] - b[0], a[1] - b[1]


def eight_points(z, sign):
    def quarter_turn(a):
        return (-a[1], a[0]) if sign > 0 else (a[1], -a[0])

    def four_points(p, q, r, s):
        e, f, g, h = add(p, r), subtract(p, r), add(q, s), quarter_turn(subtract(q, s))
        return add(e, g), add(f, h), subtract(e, g), subtract(f, h)

    even = four_points(z[0], z[2], z[4], z[6])
    odd = four_points(z[1], z[3], z[5], z[7])
    root = math.sqrt(0.5)
    first, third = add(odd[1], quarter_turn(odd[1])), subtract(quarter_turn(odd[3]), odd[3])
    odd = (
        odd[0],
        (first[0] * root, first[1] * root),
        quarter_turn(odd[2]),
        (third[0] * root, third[1] * root),
    )
    return [add(a, b) for a, b in zip(even, odd)] + [subtract(a, b) for a, b in zip(even, odd)]


def spread_tables(extent, size):
    step = size // INNER
    angle = np.outer(np.arange(INNER), np.arange(extent // step)) * (2.0 * math.pi / INNER)
    cosine, sine = np.cos(angle), np.sin(angle)
    table = np.block([[cosine, sine], [-sine, cosine]]).astype(np.float32)
    high = table.astype(ml_dtypes.bfloat16)
    low = (table - high.astype(np.float32)).astype(ml_dtypes.bfloat16)
    angle = np.outer(np.arange(step), np.arange(INNER)) * (2.0 * math.pi / size)
    turns = np.stack([np.cos(angle), np.sin(angle)]).astype(np.float32)
    return np.concatenate([high, low], axis=1), turns


def regrouping(extent, step, transposed):
    x = lax.broadcasted_iota(jnp.int32, (extent, extent), int(transposed))
    place = lax.broadcasted_iota(jnp.int32, (extent, extent), 1 - int(transposed))
    count = extent // step
    moved = (x & (step - 1)) * count + (x >> whole_log(step))
    return jnp.where(moved == place, 1.0, 0.0).astype(bf16)


def product(left, right, contracted=0):
    return lax.dot_general(
        left, right, (((1,), (contracted,)), ((), ())), preferred_element_type=f32
    )


def regrouped(values, step, transposed):
    high, low = split(values)
    rest = (values - high.astype(f32) - low.astype(f32)).astype(bf16)
    order = regrouping(values.shape[1], step, transposed)
    return product(high, order) + product(low, order) + product(rest, order)


def beside(pieces, count):
    per = LANES // count
    lane = lax.broadcasted_iota(jnp.int32, pieces[0].shape, 1)
    columns = []
    for start in range(0, len(pieces), per):
        column = pieces[start]
        for i in range(1, per):
            piece = pltpu.roll(pieces[start + i], i * count, 1)
            column = jnp.where(lane < i * count, column, piece)
        columns.append(column)
    return jnp.concatenate(columns, axis=1)


def back_product(turned, back):
    high, low = split(turned)
    both = product(jnp.concatenate([high, low], axis=0), back)
    middle = both.shape[0] // 2
    return both[:middle] + pltpu.roll(both[:middle], LANES // 2, 1) + both[middle:]


def there_and_back(real, imag, columns_of, back, turns):
    rows, extent = real.shape
    step = turns.shape[1]
    count = extent // step
    per = LANES // count
    high, low = split(jnp.concatenate([real, imag], axis=0))
    moved = product(jnp.concatenate([high, low], axis=0), regrouping(extent, step, False))
    lane = lax.broadcasted_iota(jnp.int32, (rows, LANES), 1)
    lines = []
    for v in range(step):
        column = v // per * LANES

        def piece(k, to):
            block = moved[k * rows : (k + 1) * rows, column : column + LANES]
            shift = (to - v) * count % LANES
            return pltpu.roll(block, shift, 1) if shift else block

        first = jnp.where(lane < count, piece(0, 0), piece(1, 1))
        first = jnp.where(lane < 2 * count, first, pltpu.roll(first, 2 * count, 1))
        second = jnp.where(lane < count, piece(2, 0), piece(3, 1))
        second = jnp.where(lane < 2 * count, second, 0.0)
        lines.append(jnp.concatenate([first, second], axis=1))
    waves = product(
        jnp.concatenate(lines, axis=0).astype(bf16), jnp.concatenate([back, back], axis=1), 1
    )

    results = []
    for start in range(0, rows, 16):
        halves = [[], []]
        for half in range(INNER // LANES):
            lanes = slice(half * LANES, (half + 1) * LANES)
            turn = [(turns[0, v : v + 1, lanes], turns[1, v : v + 1, lanes]) for v in range(step)]
            z = []
            for v in range(step):
                part = waves[v * rows + start : v * rows + start + 16]
                a = part[:, lanes]
                b = part[:, INNER + half * LANES : INNER + (half + 1) * LANES]
                if v:
                    cosine, sine = turn[v]
                    a, b = a * cosine + b * sine, b * cosine - a * sine
                z.append((a, b))
            z = eight_points(z, -1)
            for c in range(2):
                weighted = []
                for k in range(step):
                    kernel = columns_of(k)
                    kernel_real = kernel[c, 0, start : start + 16, lanes]
                    kernel_imag = kernel[c, 1, start : start + 16, lanes]
                    weighted.append(
                        (
                            kernel_real * z[k][0] + kernel_imag * z[k][1],
                            kernel_real * z[k][1] - kernel_imag * z[k][0],
                        )
                    )
                weighted = eight_points(weighted, 1)
                for v in range(1, step):
                    (a, b), (cosine, sine) = weighted[v], turn[v]
                    weighted[v] = (a * cosine - b * sine, a * sine + b * cosine)
                halves[c].append(weighted)
        turned = [
            jnp.concatenate(
                [halves[c][half][v][k] for k in range(2) for half in range(INNER // LANES)],
                axis=1,
            )
            for v in range(step)
            for c in range(2)
        ]
        results.append(back_product(jnp.concatenate(turned, axis=0), back))
    return results


def lines_kernel(counts, here, gathered, swapped, back, turns, kernel, out):
    count_x, count_y, count_z = counts
    group = count_y * count_z
    top_rows = LANES // group
    half = LANES // 2
    kys, size = kernel.shape[2:]
    ky = here[0] * kys + lax.broadcasted_iota(jnp.int32, (kys, LANES), 0)
    lane = lax.broadcasted_iota(jnp.int32, (kys, LANES), 1)
    odd = (lane >> whole_log(LANES // 2)) ^ (here[0] & 1)
    pair = lane >> whole_log(top_rows) & (group // 2 - 1)
    table = []
    for h in range(2):
        y = (2 * pair + odd) * (2 * top_rows) + h * top_rows + (lane & (top_rows - 1))
        cosine, sine = cos_sin(ky * y & (size - 1), size)
        table += [cosine, -sine]
    blocks = []
    for g in range(count_x):
        members = slice(g * group // 2, (g + 1) * group // 2)
        blocks.append(
            jnp.concatenate(
                [
                    part[members, 0:top_rows, :].reshape(half, LANES)
                    for part in (gathered, swapped)
                ],
                axis=0,
            )
        )
    mixed = dot3(jnp.concatenate(table, axis=0), split(jnp.concatenate(blocks, axis=1)))
    low_half, high_half = mixed[: 2 * kys], mixed[2 * kys :]
    lane = lax.broadcasted_iota(jnp.int32, (2 * kys, LANES), 1)
    pieces = []
    for g in range(0, count_x, 2):
        a = slice(g * LANES, (g + 1) * LANES)
        b = slice((g + 1) * LANES, (g + 2) * LANES)
        pieces.append(
            jnp.where(
                lane < half,
                low_half[:, a] + pltpu.roll(high_half[:, a], half, 1),
                pltpu.roll(low_half[:, b], half, 1) + high_half[:, b],
            )
        )
    lines = jnp.concatenate(pieces, axis=1)

    def columns_of(b):
        return kernel.at[:, :, :, b * INNER : (b + 1) * INNER]

    results = there_and_back(lines[:kys], lines[kys:], columns_of, back[...], turns)
    count = count_x * group
    for v in range(turns.shape[1]):
        block = jnp.concatenate(
            [result[(2 * v + c) * 16 : (2 * v + c + 1) * 16] for c in range(2) for result in results],
            axis=0,
        ).T
        out[:, v, :] = block[:count]
        out[:, TILE + v, :] = block[count : 2 * count]


def side_kernel_body(
    counts, here, gathered, swapped, back, turns, kernel_from, out, kernel, loading
):
    count_x, count_y, count_z = counts
    depth_block = (out.shape[1] - 2 * TILE) // 2
    top_rows = gathered.shape[1] - TILE
    kzs, length = kernel_from.shape[2:]
    loads = begin(
        loading,
        [
            (kernel_from.at[:, :, :, pl.ds(b * INNER, INNER)], kernel.at[b])
            for b in range(length // INNER)
        ],
    )
    size = kzs * count_y * count_z
    share = depth_block // count_x

    columns = count_x * count_z * TILE
    kz = here[0] * kzs + lax.broadcasted_iota(jnp.int32, (kzs, columns), 0)
    column = lax.broadcasted_iota(jnp.int32, (kzs, columns), 1)
    within = column & (TILE - 1)
    pair = column >> whole_log(TILE) & (count_z // 2 - 1)
    odd = (column >> whole_log(columns // 2)) ^ (here[0] & 1)
    z = (2 * pair + odd) * depth_block + within
    z = z + (column >> whole_log(TILE * count_z // 2) & (count_x - 1)) * share
    cosine, sine = cos_sin(kz * z & (size - 1), size)
    table = jnp.concatenate([cosine, -sine], axis=0)
    table = jnp.where(jnp.concatenate([within, within], axis=0) < share, table, 0.0)

    blocks = []
    for y in range(count_y):
        rows = [
            part[(x * count_y + y) * count_z // 2 + pair, top_rows:, :]
            for part in (gathered, swapped)
            for x in range(count_x)
            for pair in range(count_z // 2)
        ]
        blocks.append(jnp.concatenate(rows, axis=0))
    lines = dot3(table, split(jnp.concatenate(blocks, axis=1)))

    waiting = dict(enumerate(loads))

    def columns_of(b):
        if b in waiting:
            waiting.pop(b).wait()
        return kernel.at[b]

    result = there_and_back(lines[:kzs], lines[kzs:], columns_of, back[...], turns)[0]
    step = turns.shape[1]
    count = count_y * LANES // step
    images = []
    for c in range(2):
        pieces = [result[(2 * v + c) * 16 : (2 * v + c + 1) * 16] for v in range(step)]
        images.append(beside(pieces, count))
        images.append(beside([pltpu.roll(piece, LANES - count, 1) for piece in pieces], count))
    images = regrouped(jnp.concatenate(images, axis=0), step, True)

    rows = depth_block * count_z
    z = lax.broadcasted_iota(jnp.int32, (rows, 2 * kzs), 0)
    column = lax.broadcasted_iota(jnp.int32, (rows, 2 * kzs), 1)
    cosine, sine = cos_sin((here[0] * kzs + (column & (kzs - 1))) * z & (size - 1), size)
    table = jnp.where(column < kzs, cosine, -sine) * (1.0 / (size * length))
    for c in range(2):
        image = dot3(table, split(images[2 * kzs * c : 2 * kzs * (c + 1)]))
        for y in range(count_y):
            for z in range(count_z):
                start = 2 * TILE + c * depth_block
                out[y * count_z + z, start : start + depth_block, :] = image[
                    z * depth_block : (z + 1) * depth_block, y * LANES : (y + 1) * LANES
                ]
    out[:, 0 : 2 * TILE, :] = jnp.zeros((out.shape[0], 2 * TILE, LANES), f32)


def rows_kernel(counts, arrived, side, back, turns, out, result, sending):
    del side
    count_y, count_z = counts[1:]
    step = turns.shape[1]
    size = step * INNER
    per_turn = arrived.shape[0] // step
    half = LANES // 2
    lane = lax.broadcasted_iota(jnp.int32, (2 * TILE, LANES), 1)
    halves = []
    for pair in range(0, per_turn, 2):
        z = []
        for b in range(step):
            first, second = arrived[b * per_turn + pair], arrived[b * per_turn + pair + 1]
            spectra = (
                jnp.where(lane < half, first, pltpu.roll(second, half, 1)),
                jnp.where(lane < half, pltpu.roll(first, half, 1), second),
            )
            z.append(
                tuple(
                    jnp.concatenate(
                        [spectrum[k * TILE : (k + 1) * TILE] for spectrum in spectra], axis=0
                    )
                    for k in range(2)
                )
            )
        z = eight_points(z, 1)
        lanes = slice(pair // 2 * LANES, (pair // 2 + 1) * LANES)
        for v in range(1, step):
            cosine, sine = turns[0, v : v + 1, lanes], turns[1, v : v + 1, lanes]
            a, b = z[v]
            z[v] = (a * cosine - b * sine, a * sine + b * cosine)
        halves.append(z)
    turned = [
        jnp.concatenate([z[v][k] for k in range(2) for z in halves], axis=1) for v in range(step)
    ]
    lines = back_product(jnp.concatenate(turned, axis=0), back[...])
    pieces = [lines[v * 2 * TILE : (v + 1) * 2 * TILE] for v in range(step)]
    total = regrouped(beside(pieces, count_y * LANES // step), step, True)
    total = total * (1.0 / (size * size))
    for y in range(count_y):
        result[y] = total[:, y * LANES : (y + 1) * LANES]
    sends = begin(
        sending,
        [
            (result.at[y], out.at[y * count_z + z, 0 : 2 * TILE, :])
            for y in range(count_y)
            for z in range(count_z)
        ],
    )
    for copy in sends:
        copy.wait()


def sum_kernel(exchange_grad, arrived, out, result, sending):
    depth = exchange_grad.shape[1]
    group = arrived.shape[0]
    sends = []

    def send(c):
        sends.append(pltpu.make_async_copy(result.at[c], out.at[c], sending.at[c]))
        sends[-1].start()

    def top(c):
        return arrived[:, c * TILE : (c + 1) * TILE, :].reshape(group * TILE, LANES)

    def side(c):
        rows = slice(2 * TILE + c * depth, 2 * TILE + (c + 1) * depth)
        total = arrived[0, rows, :]
        for p in range(1, group):
            total = total + arrived[p, rows, :]
        return total

    image = top(0)
    for z in range(depth):
        result[0, z] = exchange_grad[0, z] + image
    send(0)
    column = side(1)
    for z in range(depth):
        result[2, z] = exchange_grad[2, z] + column[z : z + 1]
    send(2)
    image, column = top(1), side(0)
    for z in range(depth):
        result[1, z] = exchange_grad[1, z] + image + column[z : z + 1]
    send(1)
    for copy in sends:
        copy.wait()


def residual_blocks(residual_top, residual_side, devices, share):
    block_x, block_y = residual_top.shape
    top_rows = block_y // 2

    def body(at_x, top, side, out):
        piece = jnp.concatenate([top[0:top_rows, :], top[top_rows:, :]], axis=1)
        part = side[pl.ds(at_x[0] * share, share), :]
        part = jnp.concatenate([part, jnp.zeros((TILE - share, LANES), f32)], axis=0)
        for device in range(devices):
            out[device, 0:top_rows, :] = piece
            out[device, top_rows:, :] = part

    return call(
        body,
        "pack",
        (devices, top_rows + TILE, LANES),
        60,
        0.8,
        (lax.axis_index("gx").reshape(1), residual_top.T, residual_side.T),
    )


def fast_on_device(magnetization, stiffness, residual_top, residual_side, top_kernel, side_kernel):
    counts = tuple(lax.axis_size(axis) for axis in ALL)
    count_x, count_y, count_z = counts
    group = count_y * count_z
    devices = count_x * group
    block_x, block_y = residual_top.shape
    depth_block = stiffness.shape[0]
    top_rows = block_y // 2
    kys, size = top_kernel.shape[2:]
    kzs = side_kernel.shape[2]
    extent = count_x * block_x
    here = [lax.axis_index(axis) for axis in ALL]
    plane_index = here[1] * count_z + here[2]
    index = (here[0] * group + plane_index).reshape(1)
    plane_index = plane_index.reshape(1)
    back, turns = (jnp.asarray(table) for table in spread_tables(extent, size))

    parities = [range(parity, devices, 2) for parity in range(2)]
    sent = residual_blocks(residual_top, residual_side, devices // 2, depth_block // count_x)
    gathered = lax.all_to_all(
        sent, ALL, 0, 0, tiled=True, axis_index_groups=[list(each) for each in parities]
    )
    z_first, z_last, x_first, x_last, y_faces = faces_of(magnetization, stiffness)
    gathered, x_first, x_last, y_faces = lax.optimization_barrier(
        (gathered, x_first, x_last, y_faces)
    )
    swapped = lax.ppermute(gathered, "gz", [(i, i ^ 1) for i in range(count_z)])
    zy = halos_zy(z_first, z_last, y_faces)

    lines = call(
        functools.partial(lines_kernel, counts),
        "lines",
        (devices, 2 * TILE, LANES),
        16,
        4.0,
        (index, gathered, swapped, back, turns, top_kernel),
    )
    arrived = lax.all_to_all(lines, ALL, 0, 0, tiled=True)
    lines, x_first, x_last = lax.optimization_barrier((lines, x_first, x_last))
    x = halos_x(x_first, x_last)
    side = call(
        functools.partial(side_kernel_body, counts),
        "side",
        (group, 2 * TILE + 2 * depth_block, LANES),
        8,
        2.8,
        (plane_index, gathered, swapped, back, turns, from_hbm(side_kernel)),
        in_hbm=(0,),
        refs=(5,),
        scratch=[
            pltpu.VMEM((size // INNER, 2, 2, kzs, INNER), f32),
            pltpu.SemaphoreType.DMA((size // INNER,)),
        ],
    )
    arrived, side = lax.optimization_barrier((arrived, side))
    rows = call(
        functools.partial(rows_kernel, counts),
        "rows",
        (group, 2 * TILE + 2 * depth_block, LANES),
        8,
        1.4,
        (arrived, from_hbm(side), back, turns),
        in_hbm=(0,),
        refs=(1,),
        scratch=[
            pltpu.VMEM((count_y, 2 * TILE, LANES), f32),
            pltpu.SemaphoreType.DMA((group,)),
        ],
        out_refs=(0,),
        aliases={1: 0},
    )
    rows, zy, x = lax.optimization_barrier((rows, zy, x))
    arrived = lax.all_to_all(rows, ("gy", "gz"), 0, 0, tiled=True)
    exchange_grad = exchange_of(counts, index, magnetization, stiffness, zy, x)
    return call(
        sum_kernel,
        "gradient",
        magnetization.shape,
        16,
        1.2,
        (exchange_grad, arrived),
        out_refs=(0,),
        scratch=[pltpu.VMEM(magnetization.shape, f32), pltpu.SemaphoreType.DMA((3,))],
    )


def fits(counts, stiffness, residual_top, residual_side, top_kernel, side_kernel):
    count_x, count_y, count_z = counts
    block_x, block_y = residual_top.shape
    group = count_y * count_z
    return (
        2 * block_x == LANES
        and 2 * top_kernel.shape[2] == LANES
        and stiffness.shape[2] == LANES
        and block_x == group * TILE
        and block_y * group == count_x * block_x == INNER
        and count_y * LANES == INNER
        and block_y % 16 == 0
        and count_x % 2 == 0
        and count_z % 2 == 0
        and (count_x * group) % (2 * top_kernel.shape[3] // INNER) == 0
        and INNER == top_kernel.shape[2] * count_z
        and top_kernel.shape[3] == TILE * INNER == side_kernel.shape[3]
        and INNER == 2 * LANES
        and stiffness.shape[0] % 16 == 0
        and side_kernel.shape[2] % 16 == 0
        and all(
            count & (count - 1) == 0
            for count in (group, count_x, count_z, top_kernel.shape[3], side_kernel.shape[2])
        )
    )


def on_device(magnetization, stiffness, residual_top, residual_side, top_kernel, side_kernel):
    counts = tuple(lax.axis_size(axis) for axis in ALL)
    count_x, count_y, count_z = counts
    if fits(counts, stiffness, residual_top, residual_side, top_kernel, side_kernel):
        return fast_on_device(
            magnetization, stiffness, residual_top, residual_side, top_kernel, side_kernel
        )
    devices = count_x * count_y * count_z
    depth_block = stiffness.shape[0]
    block_x, block_y = residual_top.shape
    top_rows = block_y // 2
    share = depth_block // count_x

    sent = residual_blocks(residual_top, residual_side, devices, share)
    rows = sent.shape[1]
    gathered = lax.all_to_all(sent, ALL, 0, 0, tiled=True)
    index = (
        (lax.axis_index("gx") * count_y + lax.axis_index("gy")) * count_z + lax.axis_index("gz")
    ).reshape(1)
    z_first, z_last, x_first, x_last, y_faces = faces_of(magnetization, stiffness)
    exchange_grad = exchange_of(
        counts,
        index,
        magnetization,
        stiffness,
        halos_zy(z_first, z_last, y_faces),
        halos_x(x_first, x_last),
    )

    parts = image_parts(
        gathered, top_kernel, side_kernel, counts, block_x, top_rows, depth_block
    )
    rows = parts.shape[1]
    arrived = lax.all_to_all(parts.reshape(devices * rows, LANES), ALL, 0, 0, tiled=True)
    arrived = arrived.reshape(devices, rows, LANES)
    top_sum = jnp.sum(arrived[:, : rows - TILE], axis=0)
    side_sum = jnp.sum(
        arrived[:, rows - TILE :].reshape(count_x, count_y * count_z, TILE, LANES), axis=1
    )
    side = side_sum[:, : 2 * share].reshape(count_x, 2, share, LANES)
    side = jnp.swapaxes(side, 0, 1).reshape(2, depth_block, 1, LANES)
    top = lax.all_gather(top_sum, "gz", axis=0)
    top = jnp.swapaxes(top.reshape(count_z, 2, block_x // count_z, LANES), 0, 1)
    top = top.reshape(2, 1, block_x, LANES)
    return jnp.stack(
        [
            exchange_grad[0] + top[0],
            exchange_grad[1] + top[1] + side[0],
            exchange_grad[2] + side[1],
        ]
    )


def solution(mesh):
    placed = (
        P(None, "gz", "gx", "gy"),
        P("gz", "gx", "gy"),
        P("gx", ("gy", "gz")),
        P("gy", "gz"),
        P(None, None, ("gx", "gy", "gz"), None),
        P(None, None, ("gy", "gz"), None),
    )
    return jax.shard_map(
        on_device, mesh=mesh, in_specs=placed, out_specs=P(None, "gz", "gx", "gy"), check_vma=False
    )
```

```python
import functools
import math

import jax
import jax.numpy as jnp
import ml_dtypes
import numpy as np
from jax import lax
from jax.experimental import pallas as pl
from jax.experimental.pallas import tpu as pltpu
from jax.sharding import PartitionSpec as P

LANES = 128
TILE = 8
INNER = 256
ALL = ("gx", "gy", "gz")
f32 = jnp.float32
bf16 = jnp.bfloat16
MIB = 1024 * 1024
QUAD = 4
SMEM = pl.BlockSpec(memory_space=pltpu.SMEM)
VMEM = pl.BlockSpec(memory_space=pltpu.VMEM)
HBM = pl.BlockSpec(memory_space=pltpu.HBM)


def whole_log(count):
    return count.bit_length() - 1


def split(values):
    high = values.astype(bf16)
    return high, (values - high.astype(f32)).astype(bf16)


def dot3(left, right):
    high, low = split(left)
    def one(a, b):
        return lax.dot_general(a, b, (((1,), (0,)), ((), ())), preferred_element_type=f32)
    return one(high, right[0]) + one(low, right[0]) + one(high, right[1])


def from_hbm(values):
    return pltpu.with_memory_space_constraint(values, pltpu.HBM)


def call(body, name, shape, limit, microseconds, operands, in_hbm=(), scratch=(), refs=(), out_refs=(), aliases=()):
    shapes = shape if isinstance(shape, list) else [shape]
    moved = sum(4 * math.prod(each) for each in shapes)
    moved += sum(x.size * x.dtype.itemsize for x in operands)
    results = pl.pallas_call(
        body,
        out_shape=[
            pltpu.HBM(each, f32) if i in in_hbm else jax.ShapeDtypeStruct(each, f32)
            for i, each in enumerate(shapes)
        ],
        in_specs=[
            SMEM if x.shape == (1,) else HBM if i in refs else VMEM
            for i, x in enumerate(operands)
        ],
        out_specs=[HBM if i in out_refs else VMEM for i in range(len(shapes))],
        input_output_aliases=dict(aliases),
        scratch_shapes=list(scratch),
        compiler_params=pltpu.CompilerParams(vmem_limit_bytes=limit * MIB),
        cost_estimate=pl.CostEstimate(
            flops=int(microseconds * 1e9), bytes_accessed=moved, transcendentals=0
        ),
        name=name,
    )(*operands)
    return results if isinstance(shape, list) else results[0]


def transform_tables(extent, size):
    x = np.arange(extent)
    angle = (np.outer(x, np.arange(INNER)) % size) * (2.0 * math.pi / size)
    forward = np.concatenate([np.cos(angle), np.sin(angle)], 0).astype(np.float32)
    backward = np.concatenate([np.cos(angle).T, np.sin(angle).T], 0).astype(np.float32)

    def parts(table):
        high = table.astype(ml_dtypes.bfloat16)
        return high, (table - high.astype(np.float32)).astype(ml_dtypes.bfloat16)

    outer = size // INNER
    turn = (np.outer(np.arange(outer), x) % outer) * (2.0 * math.pi / outer)
    turns = np.stack([np.cos(turn), np.sin(turn)]).astype(np.float32)
    return parts(forward), parts(backward), turns


def phases(first, second, size):
    angle = (first * second % size).astype(f32) * (2.0 * math.pi / size)
    return jnp.cos(angle), jnp.sin(angle)


def image_kernel(
    counts, gathered, y_table, z_table, fh, fl, bh, bl, turns, top, side, y_back, z_back, out
):
    count_x, count_y, count_z, top_rows = counts
    group = count_y * count_z
    half = LANES // 2
    kys = top.shape[2]
    kzs = side.shape[2]
    forward = (fh[...], fl[...])
    backward = (bh[...], bl[...])

    blocks = [
        gathered[g * group : (g + 1) * group, 0:top_rows, :].reshape(group * top_rows, LANES)
        for g in range(count_x)
    ]
    mixed = dot3(y_table[...], split(jnp.concatenate(blocks, axis=1)))
    low_half, high_half = mixed[: 2 * kys], mixed[2 * kys :]
    lane = lax.broadcasted_iota(jnp.int32, (2 * kys, LANES), 1)
    pieces = []
    for g in range(0, count_x, 2):
        a = slice(g * LANES, (g + 1) * LANES)
        b = slice((g + 1) * LANES, (g + 2) * LANES)
        pieces.append(
            jnp.where(
                lane < half,
                low_half[:, a] + pltpu.roll(high_half[:, a], half, 1),
                pltpu.roll(low_half[:, b], half, 1) + high_half[:, b],
            )
        )
    top_lines = jnp.concatenate(pieces, axis=1)

    side_blocks = []
    for y in range(count_y):
        rows = [
            gathered[(x * count_y + y) * count_z + z, top_rows : top_rows + TILE, :]
            for x in range(count_x)
            for z in range(count_z)
        ]
        side_blocks.append(jnp.concatenate(rows, axis=0))
    side_lines = dot3(z_table[...], split(jnp.concatenate(side_blocks, axis=1)))

    real = jnp.concatenate([top_lines[:kys], side_lines[:kzs]], axis=0)
    imag = jnp.concatenate([top_lines[kys:], side_lines[kzs:]], axis=0)
    rows = kys + kzs
    total_real = total_imag = None
    for b in range(turns.shape[1]):
        cosine, sine = turns[0, b : b + 1, :], turns[1, b : b + 1, :]
        turned_real = real * cosine + imag * sine
        turned_imag = imag * cosine - real * sine
        waves = dot3(
            jnp.concatenate(
                [
                    jnp.concatenate([turned_real, turned_imag], axis=1),
                    jnp.concatenate([turned_imag, -turned_real], axis=1),
                ],
                axis=0,
            ),
            forward,
        )
        wave_real, wave_imag = waves[:rows], waves[rows:]
        columns = slice(b * INNER, (b + 1) * INNER)
        weighted_real, weighted_imag = [], []
        for c in range(2):
            for kernel, part in ((top, slice(0, kys)), (side, slice(kys, rows))):
                kernel_real, kernel_imag = kernel[c, 0, :, columns], kernel[c, 1, :, columns]
                weighted_real.append(
                    kernel_real * wave_real[part] + kernel_imag * wave_imag[part]
                )
                weighted_imag.append(
                    kernel_real * wave_imag[part] - kernel_imag * wave_real[part]
                )
        weighted_real = jnp.concatenate(weighted_real, axis=0)
        weighted_imag = jnp.concatenate(weighted_imag, axis=0)
        back = dot3(
            jnp.concatenate(
                [
                    jnp.concatenate([weighted_real, -weighted_imag], axis=1),
                    jnp.concatenate([weighted_imag, weighted_real], axis=1),
                ],
                axis=0,
            ),
            backward,
        )
        back_real, back_imag = back[: 2 * rows], back[2 * rows :]
        if b == 0:
            total_real, total_imag = back_real, back_imag
        else:
            total_real = total_real + (back_real * cosine - back_imag * sine)
            total_imag = total_imag + (back_real * sine + back_imag * cosine)

    y_parts = split(y_back[...])
    depth_rows = []
    quarter = (out.shape[1] - TILE) // 2
    block_x = quarter * count_z
    for c in range(2):
        start = c * rows
        lines = jnp.concatenate(
            [total_real[start : start + kys], total_imag[start : start + kys]], axis=0
        )
        image = dot3(lines.T, y_parts)
        for x in range(count_x):
            for y in range(count_y):
                for z in range(count_z):
                    first = x * block_x + z * quarter
                    out[
                        (x * count_y + y) * count_z + z, c * quarter : (c + 1) * quarter, :
                    ] = image[first : first + quarter, y * LANES : (y + 1) * LANES]
        depth_rows.append(total_real[start + kys : start + rows])
        depth_rows.append(total_imag[start + kys : start + rows])
    side_image = dot3(z_back[...], split(jnp.concatenate(depth_rows, axis=0)))
    for y in range(count_y):
        for z in range(count_z):
            block = side_image[z * TILE : (z + 1) * TILE, y * LANES : (y + 1) * LANES]
            for x in range(count_x):
                out[(x * count_y + y) * count_z + z, 2 * quarter :, :] = block


def image_parts(gathered, top_kernel, side_kernel, counts, block_x, top_rows, depth_block):
    count_x, count_y, count_z = counts
    group = count_y * count_z
    here = [lax.axis_index(axis) for axis in ALL]
    kys, size = top_kernel.shape[2:]
    kzs = side_kernel.shape[2]
    depth_size = kzs * group
    extent = count_y * LANES
    share = depth_block // count_x
    block_y = top_rows * 2

    ky = ((here[0] * count_y + here[1]) * count_z + here[2]) * kys + lax.iota(jnp.int32, kys)
    kz = (here[1] * count_z + here[2]) * kzs + lax.iota(jnp.int32, kzs)

    row = lax.iota(jnp.int32, group * top_rows)
    y_tables = []
    for h in range(2):
        y = row // top_rows * block_y + h * top_rows + row % top_rows
        cosine, sine = phases(ky[:, None], y[None, :], size)
        y_tables += [cosine, -sine]
    y_table = jnp.concatenate(y_tables, axis=0)

    row = lax.iota(jnp.int32, count_x * count_z * TILE)
    inside = row % TILE
    z = row // TILE % count_z * depth_block + row // (TILE * count_z) * share + inside
    cosine, sine = phases(kz[:, None], z[None, :], depth_size)
    z_table = jnp.where((inside < share)[None, :], jnp.concatenate([cosine, -sine], axis=0), 0.0)

    cosine, sine = phases(ky[:, None], lax.iota(jnp.int32, extent)[None, :], size)
    y_back = jnp.concatenate([cosine, -sine], axis=0) * (1.0 / (size * size))

    row = lax.iota(jnp.int32, count_z * TILE)
    z = row // TILE * depth_block + here[0] * share + row % TILE % share
    cosine, sine = phases(z[:, None], kz[None, :], depth_size)
    both = jnp.concatenate([cosine, -sine], axis=1) * (1.0 / (size * depth_size))
    component = (row % TILE // share)[:, None]
    z_back = jnp.concatenate(
        [jnp.where(component == 0, both, 0.0), jnp.where(component == 1, both, 0.0)], axis=1
    )

    forward, backward, turns = transform_tables(extent, size)
    out_rows = 2 * (block_x // count_z) + TILE
    return pl.pallas_call(
        functools.partial(image_kernel, counts + (top_rows,)),
        out_shape=jax.ShapeDtypeStruct((count_x * group, out_rows, LANES), f32),
        compiler_params=pltpu.CompilerParams(vmem_limit_bytes=56 * 1024 * 1024),
        name="images",
    )(
        gathered,
        y_table,
        z_table,
        *(jnp.asarray(t) for t in forward + backward),
        jnp.asarray(turns),
        top_kernel,
        side_kernel,
        y_back,
        z_back,
    )


def begin(semaphores, pairs):
    started = [
        pltpu.make_async_copy(source, target, semaphores.at[i])
        for i, (source, target) in enumerate(pairs)
    ]
    for copy in started:
        copy.start()
    return started


def faces_kernel(
    magnetization, stiffness, z_first, z_last, x_first, x_last, y_faces, m, s, loading
):
    depth, across = stiffness.shape[:2]
    loads = begin(
        loading, [(stiffness, s)] + [(magnetization.at[c], m.at[c]) for c in range(3)]
    )
    lane = lax.broadcasted_iota(jnp.int32, (across, LANES), 1)
    pair = (lane + 1 & (LANES - 1)) >> 1
    sides = jnp.zeros((across, LANES), f32)
    for field in (3, 0, 1, 2):
        loads[(field + 1) % 4].wait()
        ref = s if field == 3 else m.at[field]
        z_first[field] = ref[0]
        z_last[field] = ref[depth - 1]
        x_first[field] = ref[:, 0, :]
        x_last[field] = ref[:, across - 1, :]
        for z in range(depth):
            column = field * depth + z
            turned = pltpu.roll(ref[z], 2 * column, 1) if column else ref[z]
            sides = jnp.where(pair == column, turned, sides)
    y_faces[...] = sides


def twice_weight(a, b):
    total = a + b
    inverse = pl.reciprocal(total, approx=True)
    return 4.0 * a * b * (inverse * (2.0 - total * inverse))


def exchange_kernel(
    counts,
    here,
    magnetization_from,
    stiffness_from,
    z_next_from,
    z_before_from,
    x_next_from,
    x_before_from,
    y_next_from,
    y_before_from,
    y_faces_from,
    out,
    m,
    s,
    z_next,
    z_before,
    x_next,
    x_before,
    y_next,
    y_before,
    y_faces,
    loading,
):
    depth, across = s.shape[:2]
    chunk = depth // 4
    pairs = [
        (y_next_from, y_next),
        (y_before_from, y_before),
        (y_faces_from, y_faces),
        (z_before_from, z_before),
    ]
    for k in range(4):
        layers = pl.ds(k * chunk, chunk)
        pairs.append((stiffness_from.at[layers], s.at[layers]))
        pairs.append((magnetization_from.at[:, layers], m.at[:, layers]))
    pairs += [
        (z_next_from, z_next),
        (x_next_from, x_next),
        (x_before_from, x_before),
    ]
    loads = begin(loading, pairs)

    count_x, count_y, count_z = counts
    at_z = here[0] % count_z
    at_y = here[0] // count_z % count_y
    at_x = here[0] // (count_z * count_y)

    def inside(condition, values):
        return jnp.where(condition, values, 0.0)

    lane = lax.broadcasted_iota(jnp.int32, (across, LANES), 1)
    row = lax.broadcasted_iota(jnp.int32, (across, LANES), 0)
    first_lane, last_lane, last_row = lane == 0, lane == LANES - 1, row == across - 1

    for copy in loads[:3]:
        copy.wait()
    own = y_faces[...]
    even = (lane & 1) == 0
    field = (lane + 1 & (LANES - 1)) >> whole_log(2 * depth)
    halo = jnp.where(
        even, pltpu.roll(y_before[...], 1, 1), pltpu.roll(y_next[...], LANES - 1, 1)
    )
    present = jnp.where(even, at_y, count_y - 1 - at_y) > 0
    weight = twice_weight(
        jnp.where(field == 3, own, 1.0),
        jnp.where(field == 3, jnp.where(present, halo, 0.0), 1.0),
    )
    spread = pltpu.roll(weight, LANES - 6 * depth, 1)
    for c in (1, 2):
        spread = jnp.where(
            field == c, pltpu.roll(weight, LANES - (3 - c) * 2 * depth, 1), spread
        )
    sides = spread * (own - halo)
    outer = first_lane | last_lane

    for copy in loads[3:6]:
        copy.wait()
    below_weight = twice_weight(inside(at_z > 0, z_before[3]), s[0])
    below = [below_weight * (z_before[c] - m[c, 0]) for c in range(3)]
    for z in range(depth):
        if z % chunk == chunk - 1:
            k = 4 + 2 * (z // chunk + 1)
            for copy in loads[k : k + 2] if z + 1 < depth else loads[k:]:
                copy.wait()
        centre = s[z]
        above = s[z + 1] if z + 1 < depth else inside(at_z < count_z - 1, z_next[3])
        weight_z = twice_weight(centre, above)
        weight_x = jnp.where(
            last_row, 0.0, twice_weight(centre, pltpu.roll(centre, across - 1, 0))
        )
        weight_y = jnp.where(
            last_lane, 0.0, twice_weight(centre, pltpu.roll(centre, LANES - 1, 1))
        )
        for c in range(3):
            column = c * depth + z
            values = m[c, z]
            upper = m[c, z + 1] if z + 1 < depth else z_next[c]
            up = weight_z * (values - upper)
            flux_x = weight_x * (values - pltpu.roll(values, across - 1, 0))
            flux_y = weight_y * (values - pltpu.roll(values, LANES - 1, 1))
            total = (up - below[c]) + (flux_x - pltpu.roll(flux_x, 1, 0))
            total = total + (flux_y - pltpu.roll(flux_y, 1, 1))
            both = pltpu.roll(sides, LANES - 2 * column, 1) if column else sides
            out[c, z] = jnp.where(outer, total + both, total)
            below[c] = up
    for edge_row, halo, present in (
        (across - 1, x_next, at_x < count_x - 1),
        (0, x_before, at_x > 0),
    ):
        weight = twice_weight(s[:, edge_row, :], inside(present, halo[3]))
        for c in range(3):
            out[c, :, edge_row, :] += weight * (m[c, :, edge_row, :] - halo[c])


def ring(block, axis, distance):
    count = lax.axis_size(axis)
    return lax.ppermute(block, axis, [(i, (i + distance) % count) for i in range(count)])


def faces_of(magnetization, stiffness):
    depth, across, along = stiffness.shape
    return call(
        faces_kernel,
        "faces",
        [
            (4, across, along),
            (4, across, along),
            (4, depth, along),
            (4, depth, along),
            (across, LANES),
        ],
        8,
        2.0,
        (from_hbm(magnetization), from_hbm(stiffness)),
        in_hbm=(4,),
        refs=(0, 1),
        scratch=[
            pltpu.VMEM(magnetization.shape, f32),
            pltpu.VMEM(stiffness.shape, f32),
            pltpu.SemaphoreType.DMA((4,)),
        ],
    )


def halos_zy(z_first, z_last, y_faces):
    y_next = ring(y_faces, "gy", -1)
    y_before = y_next if lax.axis_size("gy") == 2 else ring(y_faces, "gy", 1)
    return ring(z_first, "gz", -1), ring(z_last, "gz", 1), y_next, y_before, y_faces


def halos_x(x_first, x_last):
    return ring(x_first, "gx", -1), ring(x_last, "gx", 1)


def exchange_of(counts, index, magnetization, stiffness, zy, x):
    z_next, z_before, y_next, y_before, y_faces = zy
    arrays = (magnetization, stiffness, z_next, z_before, *x, y_next, y_before, y_faces)
    return call(
        functools.partial(exchange_kernel, counts),
        "exchange",
        magnetization.shape,
        8,
        5.0,
        (index, *(from_hbm(array) for array in arrays)),
        refs=range(1, 10),
        scratch=[pltpu.VMEM(array.shape, f32) for array in arrays]
        + [pltpu.SemaphoreType.DMA((15,))],
    )


def cos_sin(steps, size):
    quarter = steps >> whole_log(size // 4)
    angle = ((steps & (size // 4 - 1)) - size // 8).astype(f32) * (2.0 * math.pi / size)
    square = angle * angle
    sine = cosine = 0.0
    for k in range(5, -1, -1):
        sine = sine * square + (-1) ** k / math.factorial(2 * k + 1)
        cosine = cosine * square + (-1) ** k / math.factorial(2 * k)
    sine = sine * angle
    first, second = (cosine - sine) * math.sqrt(0.5), (cosine + sine) * math.sqrt(0.5)
    odd = (quarter & 1) == 1
    real = jnp.where(odd, -second, first)
    imag = jnp.where(odd, first, second)
    back = quarter >= 2
    return jnp.where(back, -real, real), jnp.where(back, -imag, imag)


def add(a, b):
    return a[0] + b[0], a[1] + b[1]


def subtract(a, b):
    return a[0] - b[0], a[1] - b[1]


def eight_points(z, sign):
    def quarter_turn(a):
        return (-a[1], a[0]) if sign > 0 else (a[1], -a[0])

    def four_points(p, q, r, s):
        e, f, g, h = add(p, r), subtract(p, r), add(q, s), quarter_turn(subtract(q, s))
        return add(e, g), add(f, h), subtract(e, g), subtract(f, h)

    even = four_points(z[0], z[2], z[4], z[6])
    odd = four_points(z[1], z[3], z[5], z[7])
    root = math.sqrt(0.5)
    first, third = add(odd[1], quarter_turn(odd[1])), subtract(quarter_turn(odd[3]), odd[3])
    odd = (
        odd[0],
        (first[0] * root, first[1] * root),
        quarter_turn(odd[2]),
        (third[0] * root, third[1] * root),
    )
    return [add(a, b) for a, b in zip(even, odd)] + [subtract(a, b) for a, b in zip(even, odd)]


def spread_tables(extent, size):
    step = size // INNER
    angle = np.outer(np.arange(INNER), np.arange(extent // step)) * (2.0 * math.pi / INNER)
    cosine, sine = np.cos(angle), np.sin(angle)
    table = np.block([[cosine, sine], [-sine, cosine]]).astype(np.float32)
    high = table.astype(ml_dtypes.bfloat16)
    low = (table - high.astype(np.float32)).astype(ml_dtypes.bfloat16)
    angle = np.outer(np.arange(step), np.arange(INNER)) * (2.0 * math.pi / size)
    turns = np.stack([np.cos(angle), np.sin(angle)]).astype(np.float32)
    return np.concatenate([high, low], axis=1), turns


def regrouping(extent, step, transposed):
    x = lax.broadcasted_iota(jnp.int32, (extent, extent), int(transposed))
    place = lax.broadcasted_iota(jnp.int32, (extent, extent), 1 - int(transposed))
    count = extent // step
    moved = (x & (step - 1)) * count + (x >> whole_log(step))
    return jnp.where(moved == place, 1.0, 0.0).astype(bf16)


def product(left, right, contracted=0):
    return lax.dot_general(
        left, right, (((1,), (contracted,)), ((), ())), preferred_element_type=f32
    )


def regrouped(values, step, transposed):
    high, low = split(values)
    rest = (values - high.astype(f32) - low.astype(f32)).astype(bf16)
    order = regrouping(values.shape[1], step, transposed)
    return product(high, order) + product(low, order) + product(rest, order)


def beside(pieces, count):
    per = LANES // count
    lane = lax.broadcasted_iota(jnp.int32, pieces[0].shape, 1)
    columns = []
    for start in range(0, len(pieces), per):
        column = pieces[start]
        for i in range(1, per):
            piece = pltpu.roll(pieces[start + i], i * count, 1)
            column = jnp.where(lane < i * count, column, piece)
        columns.append(column)
    return jnp.concatenate(columns, axis=1)


def back_product(turned, back):
    high, low = split(turned)
    both = product(jnp.concatenate([high, low], axis=0), back)
    middle = both.shape[0] // 2
    return both[:middle] + pltpu.roll(both[:middle], LANES // 2, 1) + both[middle:]


def there_and_back(real, imag, columns_of, back, turns):
    rows, extent = real.shape
    step = turns.shape[1]
    count = extent // step
    per = LANES // count
    high, low = split(jnp.concatenate([real, imag], axis=0))
    moved = product(jnp.concatenate([high, low], axis=0), regrouping(extent, step, False))
    lane = lax.broadcasted_iota(jnp.int32, (rows, LANES), 1)
    lines = []
    for v in range(step):
        column = v // per * LANES

        def piece(k, to):
            block = moved[k * rows : (k + 1) * rows, column : column + LANES]
            shift = (to - v) * count % LANES
            return pltpu.roll(block, shift, 1) if shift else block

        first = jnp.where(lane < count, piece(0, 0), piece(1, 1))
        first = jnp.where(lane < 2 * count, first, pltpu.roll(first, 2 * count, 1))
        second = jnp.where(lane < count, piece(2, 0), piece(3, 1))
        second = jnp.where(lane < 2 * count, second, 0.0)
        lines.append(jnp.concatenate([first, second], axis=1))
    waves = product(
        jnp.concatenate(lines, axis=0).astype(bf16), jnp.concatenate([back, back], axis=1), 1
    )

    results = []
    for start in range(0, rows, 16):
        halves = [[], []]
        for half in range(INNER // LANES):
            lanes = slice(half * LANES, (half + 1) * LANES)
            turn = [(turns[0, v : v + 1, lanes], turns[1, v : v + 1, lanes]) for v in range(step)]
            z = []
            for v in range(step):
                part = waves[v * rows + start : v * rows + start + 16]
                a = part[:, lanes]
                b = part[:, INNER + half * LANES : INNER + (half + 1) * LANES]
                if v:
                    cosine, sine = turn[v]
                    a, b = a * cosine + b * sine, b * cosine - a * sine
                z.append((a, b))
            z = eight_points(z, -1)
            for c in range(2):
                weighted = []
                for k in range(step):
                    kernel = columns_of(k)
                    kernel_real = kernel[c, 0, start : start + 16, lanes]
                    kernel_imag = kernel[c, 1, start : start + 16, lanes]
                    weighted.append(
                        (
                            kernel_real * z[k][0] + kernel_imag * z[k][1],
                            kernel_real * z[k][1] - kernel_imag * z[k][0],
                        )
                    )
                weighted = eight_points(weighted, 1)
                for v in range(1, step):
                    (a, b), (cosine, sine) = weighted[v], turn[v]
                    weighted[v] = (a * cosine - b * sine, a * sine + b * cosine)
                halves[c].append(weighted)
        turned = [
            jnp.concatenate(
                [halves[c][half][v][k] for k in range(2) for half in range(INNER // LANES)],
                axis=1,
            )
            for v in range(step)
            for c in range(2)
        ]
        results.append(back_product(jnp.concatenate(turned, axis=0), back))
    return results


def lines_kernel(counts, here, gathered, swapped, back, turns, kernel, out, received):
    count_x, count_y, count_z = counts
    group = count_y * count_z
    top_rows = LANES // group
    half = LANES // 2
    kys, size = kernel.shape[2:]
    ky = here[0] * kys + lax.broadcasted_iota(jnp.int32, (kys, LANES), 0)
    lane = lax.broadcasted_iota(jnp.int32, (kys, LANES), 1)
    odd = (lane >> whole_log(LANES // 2)) ^ (here[0] & 1)
    pair = lane >> whole_log(top_rows) & (group // 2 - 1)
    table = []
    for h in range(2):
        y = (2 * pair + odd) * (2 * top_rows) + h * top_rows + (lane & (top_rows - 1))
        cosine, sine = cos_sin(ky * y & (size - 1), size)
        table += [cosine, -sine]
    for k, part in enumerate((gathered, swapped)):
        for member in range(part.shape[0]):
            g, place = divmod(member, group // 2)
            for j in range(top_rows // QUAD):
                row = (k * group // 2 + place) * top_rows + j * QUAD
                received[g, row : row + QUAD, :] = part[member, j]
    blocks = [received[g] for g in range(count_x)]
    mixed = dot3(jnp.concatenate(table, axis=0), split(jnp.concatenate(blocks, axis=1)))
    low_half, high_half = mixed[: 2 * kys], mixed[2 * kys :]
    lane = lax.broadcasted_iota(jnp.int32, (2 * kys, LANES), 1)
    pieces = []
    for g in range(0, count_x, 2):
        a = slice(g * LANES, (g + 1) * LANES)
        b = slice((g + 1) * LANES, (g + 2) * LANES)
        pieces.append(
            jnp.where(
                lane < half,
                low_half[:, a] + pltpu.roll(high_half[:, a], half, 1),
                pltpu.roll(low_half[:, b], half, 1) + high_half[:, b],
            )
        )
    lines = jnp.concatenate(pieces, axis=1)

    def columns_of(b):
        return kernel.at[:, :, :, b * INNER : (b + 1) * INNER]

    results = there_and_back(lines[:kys], lines[kys:], columns_of, back[...], turns)
    count = count_x * group
    for v in range(turns.shape[1]):
        block = jnp.concatenate(
            [result[(2 * v + c) * 16 : (2 * v + c + 1) * 16] for c in range(2) for result in results],
            axis=0,
        ).T
        out[:, v, :] = block[:count]
        out[:, TILE + v, :] = block[count : 2 * count]


def side_kernel_body(
    counts, here, gathered, swapped, back, turns, kernel_from, out, kernel, received, loading
):
    count_x, count_y, count_z = counts
    depth_block = (out.shape[1] - 2 * TILE) // 2
    last = gathered.shape[1] - 1
    kzs, length = kernel_from.shape[2:]
    loads = begin(
        loading,
        [
            (kernel_from.at[:, :, :, pl.ds(b * INNER, INNER)], kernel.at[b])
            for b in range(length // INNER)
        ],
    )
    size = kzs * count_y * count_z
    columns = count_x * count_z * QUAD
    kz = here[0] * kzs + lax.broadcasted_iota(jnp.int32, (kzs, columns), 0)
    column = lax.broadcasted_iota(jnp.int32, (kzs, columns), 1)
    pair = column >> whole_log(QUAD) & (count_z // 2 - 1)
    odd = (column >> whole_log(columns // 2)) ^ (here[0] & 1)
    z = (2 * pair + odd) * depth_block + (column & (QUAD - 1))
    z = z + (column >> whole_log(QUAD * count_z // 2) & (count_x - 1)) * QUAD
    cosine, sine = cos_sin(kz * z & (size - 1), size)
    table = jnp.concatenate([cosine, -sine], axis=0)
    for k, part in enumerate((gathered, swapped)):
        for x in range(count_x):
            for y in range(count_y):
                for pair in range(count_z // 2):
                    row = ((k * count_x + x) * count_z // 2 + pair) * QUAD
                    member = (x * count_y + y) * count_z // 2 + pair
                    received[y, row : row + QUAD, :] = part[member, last]
    blocks = [received[y] for y in range(count_y)]
    lines = dot3(table, split(jnp.concatenate(blocks, axis=1)))

    waiting = dict(enumerate(loads))

    def columns_of(b):
        if b in waiting:
            waiting.pop(b).wait()
        return kernel.at[b]

    result = there_and_back(lines[:kzs], lines[kzs:], columns_of, back[...], turns)[0]
    step = turns.shape[1]
    count = count_y * LANES // step
    images = []
    for c in range(2):
        pieces = [result[(2 * v + c) * 16 : (2 * v + c + 1) * 16] for v in range(step)]
        images.append(beside(pieces, count))
        images.append(beside([pltpu.roll(piece, LANES - count, 1) for piece in pieces], count))
    images = regrouped(jnp.concatenate(images, axis=0), step, True)

    rows = depth_block * count_z
    z = lax.broadcasted_iota(jnp.int32, (rows, 2 * kzs), 0)
    column = lax.broadcasted_iota(jnp.int32, (rows, 2 * kzs), 1)
    cosine, sine = cos_sin((here[0] * kzs + (column & (kzs - 1))) * z & (size - 1), size)
    table = jnp.where(column < kzs, cosine, -sine) * (1.0 / (size * length))
    for c in range(2):
        image = dot3(table, split(images[2 * kzs * c : 2 * kzs * (c + 1)]))
        for y in range(count_y):
            for z in range(count_z):
                start = 2 * TILE + c * depth_block
                out[y * count_z + z, start : start + depth_block, :] = image[
                    z * depth_block : (z + 1) * depth_block, y * LANES : (y + 1) * LANES
                ]
    out[:, 0 : 2 * TILE, :] = jnp.zeros((out.shape[0], 2 * TILE, LANES), f32)


def rows_kernel(counts, arrived, side, back, turns, out, result, sending):
    del side
    count_y, count_z = counts[1:]
    step = turns.shape[1]
    size = step * INNER
    per_turn = arrived.shape[0] // step
    half = LANES // 2
    lane = lax.broadcasted_iota(jnp.int32, (2 * TILE, LANES), 1)
    halves = []
    for pair in range(0, per_turn, 2):
        z = []
        for b in range(step):
            first, second = arrived[b * per_turn + pair], arrived[b * per_turn + pair + 1]
            spectra = (
                jnp.where(lane < half, first, pltpu.roll(second, half, 1)),
                jnp.where(lane < half, pltpu.roll(first, half, 1), second),
            )
            z.append(
                tuple(
                    jnp.concatenate(
                        [spectrum[k * TILE : (k + 1) * TILE] for spectrum in spectra], axis=0
                    )
                    for k in range(2)
                )
            )
        z = eight_points(z, 1)
        lanes = slice(pair // 2 * LANES, (pair // 2 + 1) * LANES)
        for v in range(1, step):
            cosine, sine = turns[0, v : v + 1, lanes], turns[1, v : v + 1, lanes]
            a, b = z[v]
            z[v] = (a * cosine - b * sine, a * sine + b * cosine)
        halves.append(z)
    turned = [
        jnp.concatenate([z[v][k] for k in range(2) for z in halves], axis=1) for v in range(step)
    ]
    lines = back_product(jnp.concatenate(turned, axis=0), back[...])
    pieces = [lines[v * 2 * TILE : (v + 1) * 2 * TILE] for v in range(step)]
    total = regrouped(beside(pieces, count_y * LANES // step), step, True)
    total = total * (1.0 / (size * size))
    for y in range(count_y):
        result[y] = total[:, y * LANES : (y + 1) * LANES]
    sends = begin(
        sending,
        [
            (result.at[y], out.at[y * count_z + z, 0 : 2 * TILE, :])
            for y in range(count_y)
            for z in range(count_z)
        ],
    )
    for copy in sends:
        copy.wait()


def sum_kernel(exchange_grad, arrived, out, result, sending):
    depth = exchange_grad.shape[1]
    group = arrived.shape[0]
    sends = []

    def send(c):
        sends.append(pltpu.make_async_copy(result.at[c], out.at[c], sending.at[c]))
        sends[-1].start()

    def top(c):
        return arrived[:, c * TILE : (c + 1) * TILE, :].reshape(group * TILE, LANES)

    def side(c):
        rows = slice(2 * TILE + c * depth, 2 * TILE + (c + 1) * depth)
        total = arrived[0, rows, :]
        for p in range(1, group):
            total = total + arrived[p, rows, :]
        return total

    image = top(0)
    for z in range(depth):
        result[0, z] = exchange_grad[0, z] + image
    send(0)
    column = side(1)
    for z in range(depth):
        result[2, z] = exchange_grad[2, z] + column[z : z + 1]
    send(2)
    image, column = top(1), side(0)
    for z in range(depth):
        result[1, z] = exchange_grad[1, z] + image + column[z : z + 1]
    send(1)
    for copy in sends:
        copy.wait()


def residual_blocks(residual_top, residual_side, copies, share, quads):
    block_x, block_y = residual_top.shape
    top_rows = block_y // 2

    def body(at_x, top, side, out):
        piece = jnp.concatenate([top[0:top_rows, :], top[top_rows:, :]], axis=1)
        part = side[pl.ds(at_x[0] * share, share), :]
        if not quads:
            part = jnp.concatenate([part, jnp.zeros((TILE - share, LANES), f32)], axis=0)
        for copy in range(copies):
            if quads:
                for j in range(top_rows // QUAD):
                    out[copy, j] = piece[j * QUAD : (j + 1) * QUAD]
                out[copy, top_rows // QUAD] = part
            else:
                out[copy, 0:top_rows, :] = piece
                out[copy, top_rows:, :] = part

    shape = (top_rows // QUAD + 1, QUAD) if quads else (top_rows + TILE,)
    return call(
        body,
        "pack",
        (copies, *shape, LANES),
        60,
        0.8,
        (lax.axis_index("gx").reshape(1), residual_top.T, residual_side.T),
    )


def fast_on_device(magnetization, stiffness, residual_top, residual_side, top_kernel, side_kernel):
    counts = tuple(lax.axis_size(axis) for axis in ALL)
    count_x, count_y, count_z = counts
    group = count_y * count_z
    devices = count_x * group
    block_x, block_y = residual_top.shape
    depth_block = stiffness.shape[0]
    top_rows = block_y // 2
    kys, size = top_kernel.shape[2:]
    kzs = side_kernel.shape[2]
    extent = count_x * block_x
    here = [lax.axis_index(axis) for axis in ALL]
    plane_index = here[1] * count_z + here[2]
    index = (here[0] * group + plane_index).reshape(1)
    plane_index = plane_index.reshape(1)
    back, turns = (jnp.asarray(table) for table in spread_tables(extent, size))

    parities = [range(parity, devices, 2) for parity in range(2)]
    sent = residual_blocks(
        residual_top, residual_side, devices // 2, depth_block // count_x, True
    )
    gathered = lax.all_to_all(
        sent, ALL, 0, 0, tiled=True, axis_index_groups=[list(each) for each in parities]
    )
    z_first, z_last, x_first, x_last, y_faces = faces_of(magnetization, stiffness)
    gathered, x_first, x_last, y_faces = lax.optimization_barrier(
        (gathered, x_first, x_last, y_faces)
    )
    swapped = lax.ppermute(gathered, "gz", [(i, i ^ 1) for i in range(count_z)])
    zy = halos_zy(z_first, z_last, y_faces)

    lines = call(
        functools.partial(lines_kernel, counts),
        "lines",
        (devices, 2 * TILE, LANES),
        16,
        4.0,
        (index, gathered, swapped, back, turns, top_kernel),
        scratch=[pltpu.VMEM((count_x, LANES, LANES), f32)],
    )
    arrived = lax.all_to_all(lines, ALL, 0, 0, tiled=True)
    lines, x_first, x_last = lax.optimization_barrier((lines, x_first, x_last))
    x = halos_x(x_first, x_last)
    side = call(
        functools.partial(side_kernel_body, counts),
        "side",
        (group, 2 * TILE + 2 * depth_block, LANES),
        8,
        2.8,
        (plane_index, gathered, swapped, back, turns, from_hbm(side_kernel)),
        in_hbm=(0,),
        refs=(5,),
        scratch=[
            pltpu.VMEM((size // INNER, 2, 2, kzs, INNER), f32),
            pltpu.VMEM((count_y, count_x * count_z * QUAD, LANES), f32),
            pltpu.SemaphoreType.DMA((size // INNER,)),
        ],
    )
    arrived, side = lax.optimization_barrier((arrived, side))
    rows = call(
        functools.partial(rows_kernel, counts),
        "rows",
        (group, 2 * TILE + 2 * depth_block, LANES),
        8,
        1.4,
        (arrived, from_hbm(side), back, turns),
        in_hbm=(0,),
        refs=(1,),
        scratch=[
            pltpu.VMEM((count_y, 2 * TILE, LANES), f32),
            pltpu.SemaphoreType.DMA((group,)),
        ],
        out_refs=(0,),
        aliases={1: 0},
    )
    rows, zy, x = lax.optimization_barrier((rows, zy, x))
    arrived = lax.all_to_all(rows, ("gy", "gz"), 0, 0, tiled=True)
    exchange_grad = exchange_of(counts, index, magnetization, stiffness, zy, x)
    return call(
        sum_kernel,
        "gradient",
        magnetization.shape,
        16,
        1.2,
        (exchange_grad, arrived),
        out_refs=(0,),
        scratch=[pltpu.VMEM(magnetization.shape, f32), pltpu.SemaphoreType.DMA((3,))],
    )


def fits(counts, stiffness, residual_top, residual_side, top_kernel, side_kernel):
    count_x, count_y, count_z = counts
    block_x, block_y = residual_top.shape
    group = count_y * count_z
    return (
        2 * block_x == LANES
        and 2 * top_kernel.shape[2] == LANES
        and stiffness.shape[2] == LANES
        and block_x == group * TILE
        and block_y * group == count_x * block_x == INNER
        and count_y * LANES == INNER
        and block_y % 16 == 0
        and count_x % 2 == 0
        and count_z % 2 == 0
        and (count_x * group) % (2 * top_kernel.shape[3] // INNER) == 0
        and INNER == top_kernel.shape[2] * count_z
        and top_kernel.shape[3] == TILE * INNER == side_kernel.shape[3]
        and INNER == 2 * LANES
        and stiffness.shape[0] % 16 == 0
        and stiffness.shape[0] == count_x * QUAD
        and side_kernel.shape[2] % 16 == 0
        and all(
            count & (count - 1) == 0
            for count in (group, count_x, count_z, top_kernel.shape[3], side_kernel.shape[2])
        )
    )


def on_device(magnetization, stiffness, residual_top, residual_side, top_kernel, side_kernel):
    counts = tuple(lax.axis_size(axis) for axis in ALL)
    count_x, count_y, count_z = counts
    if fits(counts, stiffness, residual_top, residual_side, top_kernel, side_kernel):
        return fast_on_device(
            magnetization, stiffness, residual_top, residual_side, top_kernel, side_kernel
        )
    devices = count_x * count_y * count_z
    depth_block = stiffness.shape[0]
    block_x, block_y = residual_top.shape
    top_rows = block_y // 2
    share = depth_block // count_x

    sent = residual_blocks(residual_top, residual_side, devices, share, False)
    rows = sent.shape[1]
    gathered = lax.all_to_all(sent, ALL, 0, 0, tiled=True)
    index = (
        (lax.axis_index("gx") * count_y + lax.axis_index("gy")) * count_z + lax.axis_index("gz")
    ).reshape(1)
    z_first, z_last, x_first, x_last, y_faces = faces_of(magnetization, stiffness)
    exchange_grad = exchange_of(
        counts,
        index,
        magnetization,
        stiffness,
        halos_zy(z_first, z_last, y_faces),
        halos_x(x_first, x_last),
    )

    parts = image_parts(
        gathered, top_kernel, side_kernel, counts, block_x, top_rows, depth_block
    )
    rows = parts.shape[1]
    arrived = lax.all_to_all(parts.reshape(devices * rows, LANES), ALL, 0, 0, tiled=True)
    arrived = arrived.reshape(devices, rows, LANES)
    top_sum = jnp.sum(arrived[:, : rows - TILE], axis=0)
    side_sum = jnp.sum(
        arrived[:, rows - TILE :].reshape(count_x, count_y * count_z, TILE, LANES), axis=1
    )
    side = side_sum[:, : 2 * share].reshape(count_x, 2, share, LANES)
    side = jnp.swapaxes(side, 0, 1).reshape(2, depth_block, 1, LANES)
    top = lax.all_gather(top_sum, "gz", axis=0)
    top = jnp.swapaxes(top.reshape(count_z, 2, block_x // count_z, LANES), 0, 1)
    top = top.reshape(2, 1, block_x, LANES)
    return jnp.stack(
        [
            exchange_grad[0] + top[0],
            exchange_grad[1] + top[1] + side[0],
            exchange_grad[2] + side[1],
        ]
    )


def solution(mesh):
    placed = (
        P(None, "gz", "gx", "gy"),
        P("gz", "gx", "gy"),
        P("gx", ("gy", "gz")),
        P("gy", "gz"),
        P(None, None, ("gx", "gy", "gz"), None),
        P(None, None, ("gy", "gz"), None),
    )
    return jax.shard_map(
        on_device, mesh=mesh, in_specs=placed, out_specs=P(None, "gz", "gx", "gy"), check_vma=False
    )
```

```python
import functools
import math

import jax
import jax.numpy as jnp
import ml_dtypes
import numpy as np
from jax import lax
from jax.experimental import pallas as pl
from jax.experimental.pallas import tpu as pltpu
from jax.sharding import PartitionSpec as P

LANES = 128
TILE = 8
INNER = 256
ALL = ("gx", "gy", "gz")
f32 = jnp.float32
bf16 = jnp.bfloat16
MIB = 1024 * 1024
QUAD = 4
SMEM = pl.BlockSpec(memory_space=pltpu.SMEM)
VMEM = pl.BlockSpec(memory_space=pltpu.VMEM)
HBM = pl.BlockSpec(memory_space=pltpu.HBM)


def whole_log(count):
    return count.bit_length() - 1


def split(values):
    high = values.astype(bf16)
    return high, (values - high.astype(f32)).astype(bf16)


def dot3(left, right):
    high, low = split(left)
    def one(a, b):
        return lax.dot_general(a, b, (((1,), (0,)), ((), ())), preferred_element_type=f32)
    return one(high, right[0]) + one(low, right[0]) + one(high, right[1])


def from_hbm(values):
    return pltpu.with_memory_space_constraint(values, pltpu.HBM)


def call(body, name, shape, limit, microseconds, operands, in_hbm=(), scratch=(), refs=(), out_refs=(), aliases=()):
    shapes = shape if isinstance(shape, list) else [shape]
    moved = sum(4 * math.prod(each) for each in shapes)
    moved += sum(x.size * x.dtype.itemsize for x in operands)
    results = pl.pallas_call(
        body,
        out_shape=[
            pltpu.HBM(each, f32) if i in in_hbm else jax.ShapeDtypeStruct(each, f32)
            for i, each in enumerate(shapes)
        ],
        in_specs=[
            SMEM if x.shape == (1,) else HBM if i in refs else VMEM
            for i, x in enumerate(operands)
        ],
        out_specs=[HBM if i in out_refs else VMEM for i in range(len(shapes))],
        input_output_aliases=dict(aliases),
        scratch_shapes=list(scratch),
        compiler_params=pltpu.CompilerParams(vmem_limit_bytes=limit * MIB),
        cost_estimate=pl.CostEstimate(
            flops=int(microseconds * 1e9), bytes_accessed=moved, transcendentals=0
        ),
        name=name,
    )(*operands)
    return results if isinstance(shape, list) else results[0]


def transform_tables(extent, size):
    x = np.arange(extent)
    angle = (np.outer(x, np.arange(INNER)) % size) * (2.0 * math.pi / size)
    forward = np.concatenate([np.cos(angle), np.sin(angle)], 0).astype(np.float32)
    backward = np.concatenate([np.cos(angle).T, np.sin(angle).T], 0).astype(np.float32)

    def parts(table):
        high = table.astype(ml_dtypes.bfloat16)
        return high, (table - high.astype(np.float32)).astype(ml_dtypes.bfloat16)

    outer = size // INNER
    turn = (np.outer(np.arange(outer), x) % outer) * (2.0 * math.pi / outer)
    turns = np.stack([np.cos(turn), np.sin(turn)]).astype(np.float32)
    return parts(forward), parts(backward), turns


def phases(first, second, size):
    angle = (first * second % size).astype(f32) * (2.0 * math.pi / size)
    return jnp.cos(angle), jnp.sin(angle)


def image_kernel(
    counts, gathered, y_table, z_table, fh, fl, bh, bl, turns, top, side, y_back, z_back, out
):
    count_x, count_y, count_z, top_rows = counts
    group = count_y * count_z
    half = LANES // 2
    kys = top.shape[2]
    kzs = side.shape[2]
    forward = (fh[...], fl[...])
    backward = (bh[...], bl[...])

    blocks = [
        gathered[g * group : (g + 1) * group, 0:top_rows, :].reshape(group * top_rows, LANES)
        for g in range(count_x)
    ]
    mixed = dot3(y_table[...], split(jnp.concatenate(blocks, axis=1)))
    low_half, high_half = mixed[: 2 * kys], mixed[2 * kys :]
    lane = lax.broadcasted_iota(jnp.int32, (2 * kys, LANES), 1)
    pieces = []
    for g in range(0, count_x, 2):
        a = slice(g * LANES, (g + 1) * LANES)
        b = slice((g + 1) * LANES, (g + 2) * LANES)
        pieces.append(
            jnp.where(
                lane < half,
                low_half[:, a] + pltpu.roll(high_half[:, a], half, 1),
                pltpu.roll(low_half[:, b], half, 1) + high_half[:, b],
            )
        )
    top_lines = jnp.concatenate(pieces, axis=1)

    side_blocks = []
    for y in range(count_y):
        rows = [
            gathered[(x * count_y + y) * count_z + z, top_rows : top_rows + TILE, :]
            for x in range(count_x)
            for z in range(count_z)
        ]
        side_blocks.append(jnp.concatenate(rows, axis=0))
    side_lines = dot3(z_table[...], split(jnp.concatenate(side_blocks, axis=1)))

    real = jnp.concatenate([top_lines[:kys], side_lines[:kzs]], axis=0)
    imag = jnp.concatenate([top_lines[kys:], side_lines[kzs:]], axis=0)
    rows = kys + kzs
    total_real = total_imag = None
    for b in range(turns.shape[1]):
        cosine, sine = turns[0, b : b + 1, :], turns[1, b : b + 1, :]
        turned_real = real * cosine + imag * sine
        turned_imag = imag * cosine - real * sine
        waves = dot3(
            jnp.concatenate(
                [
                    jnp.concatenate([turned_real, turned_imag], axis=1),
                    jnp.concatenate([turned_imag, -turned_real], axis=1),
                ],
                axis=0,
            ),
            forward,
        )
        wave_real, wave_imag = waves[:rows], waves[rows:]
        columns = slice(b * INNER, (b + 1) * INNER)
        weighted_real, weighted_imag = [], []
        for c in range(2):
            for kernel, part in ((top, slice(0, kys)), (side, slice(kys, rows))):
                kernel_real, kernel_imag = kernel[c, 0, :, columns], kernel[c, 1, :, columns]
                weighted_real.append(
                    kernel_real * wave_real[part] + kernel_imag * wave_imag[part]
                )
                weighted_imag.append(
                    kernel_real * wave_imag[part] - kernel_imag * wave_real[part]
                )
        weighted_real = jnp.concatenate(weighted_real, axis=0)
        weighted_imag = jnp.concatenate(weighted_imag, axis=0)
        back = dot3(
            jnp.concatenate(
                [
                    jnp.concatenate([weighted_real, -weighted_imag], axis=1),
                    jnp.concatenate([weighted_imag, weighted_real], axis=1),
                ],
                axis=0,
            ),
            backward,
        )
        back_real, back_imag = back[: 2 * rows], back[2 * rows :]
        if b == 0:
            total_real, total_imag = back_real, back_imag
        else:
            total_real = total_real + (back_real * cosine - back_imag * sine)
            total_imag = total_imag + (back_real * sine + back_imag * cosine)

    y_parts = split(y_back[...])
    depth_rows = []
    quarter = (out.shape[1] - TILE) // 2
    block_x = quarter * count_z
    for c in range(2):
        start = c * rows
        lines = jnp.concatenate(
            [total_real[start : start + kys], total_imag[start : start + kys]], axis=0
        )
        image = dot3(lines.T, y_parts)
        for x in range(count_x):
            for y in range(count_y):
                for z in range(count_z):
                    first = x * block_x + z * quarter
                    out[
                        (x * count_y + y) * count_z + z, c * quarter : (c + 1) * quarter, :
                    ] = image[first : first + quarter, y * LANES : (y + 1) * LANES]
        depth_rows.append(total_real[start + kys : start + rows])
        depth_rows.append(total_imag[start + kys : start + rows])
    side_image = dot3(z_back[...], split(jnp.concatenate(depth_rows, axis=0)))
    for y in range(count_y):
        for z in range(count_z):
            block = side_image[z * TILE : (z + 1) * TILE, y * LANES : (y + 1) * LANES]
            for x in range(count_x):
                out[(x * count_y + y) * count_z + z, 2 * quarter :, :] = block


def image_parts(gathered, top_kernel, side_kernel, counts, block_x, top_rows, depth_block):
    count_x, count_y, count_z = counts
    group = count_y * count_z
    here = [lax.axis_index(axis) for axis in ALL]
    kys, size = top_kernel.shape[2:]
    kzs = side_kernel.shape[2]
    depth_size = kzs * group
    extent = count_y * LANES
    share = depth_block // count_x
    block_y = top_rows * 2

    ky = ((here[0] * count_y + here[1]) * count_z + here[2]) * kys + lax.iota(jnp.int32, kys)
    kz = (here[1] * count_z + here[2]) * kzs + lax.iota(jnp.int32, kzs)

    row = lax.iota(jnp.int32, group * top_rows)
    y_tables = []
    for h in range(2):
        y = row // top_rows * block_y + h * top_rows + row % top_rows
        cosine, sine = phases(ky[:, None], y[None, :], size)
        y_tables += [cosine, -sine]
    y_table = jnp.concatenate(y_tables, axis=0)

    row = lax.iota(jnp.int32, count_x * count_z * TILE)
    inside = row % TILE
    z = row // TILE % count_z * depth_block + row // (TILE * count_z) * share + inside
    cosine, sine = phases(kz[:, None], z[None, :], depth_size)
    z_table = jnp.where((inside < share)[None, :], jnp.concatenate([cosine, -sine], axis=0), 0.0)

    cosine, sine = phases(ky[:, None], lax.iota(jnp.int32, extent)[None, :], size)
    y_back = jnp.concatenate([cosine, -sine], axis=0) * (1.0 / (size * size))

    row = lax.iota(jnp.int32, count_z * TILE)
    z = row // TILE * depth_block + here[0] * share + row % TILE % share
    cosine, sine = phases(z[:, None], kz[None, :], depth_size)
    both = jnp.concatenate([cosine, -sine], axis=1) * (1.0 / (size * depth_size))
    component = (row % TILE // share)[:, None]
    z_back = jnp.concatenate(
        [jnp.where(component == 0, both, 0.0), jnp.where(component == 1, both, 0.0)], axis=1
    )

    forward, backward, turns = transform_tables(extent, size)
    out_rows = 2 * (block_x // count_z) + TILE
    return pl.pallas_call(
        functools.partial(image_kernel, counts + (top_rows,)),
        out_shape=jax.ShapeDtypeStruct((count_x * group, out_rows, LANES), f32),
        compiler_params=pltpu.CompilerParams(vmem_limit_bytes=56 * 1024 * 1024),
        name="images",
    )(
        gathered,
        y_table,
        z_table,
        *(jnp.asarray(t) for t in forward + backward),
        jnp.asarray(turns),
        top_kernel,
        side_kernel,
        y_back,
        z_back,
    )


def begin(semaphores, pairs):
    started = [
        pltpu.make_async_copy(source, target, semaphores.at[i])
        for i, (source, target) in enumerate(pairs)
    ]
    for copy in started:
        copy.start()
    return started


def faces_kernel(
    magnetization, stiffness, z_first, z_last, x_first, x_last, y_faces, m, s, loading
):
    depth, across = stiffness.shape[:2]
    loads = begin(
        loading, [(stiffness, s)] + [(magnetization.at[c], m.at[c]) for c in range(3)]
    )
    lane = lax.broadcasted_iota(jnp.int32, (across, LANES), 1)
    pair = (lane + 1 & (LANES - 1)) >> 1
    sides = jnp.zeros((across, LANES), f32)
    for field in (3, 0, 1, 2):
        loads[(field + 1) % 4].wait()
        ref = s if field == 3 else m.at[field]
        z_first[field] = ref[0]
        z_last[field] = ref[depth - 1]
        x_first[field] = ref[:, 0, :]
        x_last[field] = ref[:, across - 1, :]
        for z in range(depth):
            column = field * depth + z
            turned = pltpu.roll(ref[z], 2 * column, 1) if column else ref[z]
            sides = jnp.where(pair == column, turned, sides)
    y_faces[...] = sides


def twice_weight(a, b):
    total = a + b
    inverse = pl.reciprocal(total, approx=True)
    return 4.0 * a * b * (inverse * (2.0 - total * inverse))


def exchange_kernel(
    counts,
    here,
    magnetization_from,
    stiffness_from,
    z_next_from,
    z_before_from,
    x_next_from,
    x_before_from,
    y_next_from,
    y_before_from,
    y_faces_from,
    out,
    m,
    s,
    z_next,
    z_before,
    x_next,
    x_before,
    y_next,
    y_before,
    y_faces,
    loading,
):
    depth, across = s.shape[:2]
    chunk = depth // 4
    pairs = [
        (y_next_from, y_next),
        (y_before_from, y_before),
        (y_faces_from, y_faces),
        (z_before_from, z_before),
    ]
    for k in range(4):
        layers = pl.ds(k * chunk, chunk)
        pairs.append((stiffness_from.at[layers], s.at[layers]))
        pairs.append((magnetization_from.at[:, layers], m.at[:, layers]))
    pairs += [
        (z_next_from, z_next),
        (x_next_from, x_next),
        (x_before_from, x_before),
    ]
    loads = begin(loading, pairs)

    count_x, count_y, count_z = counts
    at_z = here[0] % count_z
    at_y = here[0] // count_z % count_y
    at_x = here[0] // (count_z * count_y)

    def inside(condition, values):
        return jnp.where(condition, values, 0.0)

    lane = lax.broadcasted_iota(jnp.int32, (across, LANES), 1)
    row = lax.broadcasted_iota(jnp.int32, (across, LANES), 0)
    first_lane, last_lane, last_row = lane == 0, lane == LANES - 1, row == across - 1

    for copy in loads[:3]:
        copy.wait()
    own = y_faces[...]
    even = (lane & 1) == 0
    field = (lane + 1 & (LANES - 1)) >> whole_log(2 * depth)
    halo = jnp.where(
        even, pltpu.roll(y_before[...], 1, 1), pltpu.roll(y_next[...], LANES - 1, 1)
    )
    present = jnp.where(even, at_y, count_y - 1 - at_y) > 0
    weight = twice_weight(
        jnp.where(field == 3, own, 1.0),
        jnp.where(field == 3, jnp.where(present, halo, 0.0), 1.0),
    )
    spread = pltpu.roll(weight, LANES - 6 * depth, 1)
    for c in (1, 2):
        spread = jnp.where(
            field == c, pltpu.roll(weight, LANES - (3 - c) * 2 * depth, 1), spread
        )
    sides = spread * (own - halo)
    outer = first_lane | last_lane

    for copy in loads[3:6]:
        copy.wait()
    below_weight = twice_weight(inside(at_z > 0, z_before[3]), s[0])
    below = [below_weight * (z_before[c] - m[c, 0]) for c in range(3)]
    for z in range(depth):
        if z % chunk == chunk - 1:
            k = 4 + 2 * (z // chunk + 1)
            for copy in loads[k : k + 2] if z + 1 < depth else loads[k:]:
                copy.wait()
        centre = s[z]
        above = s[z + 1] if z + 1 < depth else inside(at_z < count_z - 1, z_next[3])
        weight_z = twice_weight(centre, above)
        weight_x = jnp.where(
            last_row, 0.0, twice_weight(centre, pltpu.roll(centre, across - 1, 0))
        )
        weight_y = jnp.where(
            last_lane, 0.0, twice_weight(centre, pltpu.roll(centre, LANES - 1, 1))
        )
        for c in range(3):
            column = c * depth + z
            values = m[c, z]
            upper = m[c, z + 1] if z + 1 < depth else z_next[c]
            up = weight_z * (values - upper)
            flux_x = weight_x * (values - pltpu.roll(values, across - 1, 0))
            flux_y = weight_y * (values - pltpu.roll(values, LANES - 1, 1))
            total = (up - below[c]) + (flux_x - pltpu.roll(flux_x, 1, 0))
            total = total + (flux_y - pltpu.roll(flux_y, 1, 1))
            both = pltpu.roll(sides, LANES - 2 * column, 1) if column else sides
            out[c, z] = jnp.where(outer, total + both, total)
            below[c] = up
    for edge_row, halo, present in (
        (across - 1, x_next, at_x < count_x - 1),
        (0, x_before, at_x > 0),
    ):
        weight = twice_weight(s[:, edge_row, :], inside(present, halo[3]))
        for c in range(3):
            out[c, :, edge_row, :] += weight * (m[c, :, edge_row, :] - halo[c])


def ring(block, axis, distance):
    count = lax.axis_size(axis)
    return lax.ppermute(block, axis, [(i, (i + distance) % count) for i in range(count)])


def faces_of(magnetization, stiffness):
    depth, across, along = stiffness.shape
    return call(
        faces_kernel,
        "faces",
        [
            (4, across, along),
            (4, across, along),
            (4, depth, along),
            (4, depth, along),
            (across, LANES),
        ],
        8,
        2.0,
        (from_hbm(magnetization), from_hbm(stiffness)),
        in_hbm=(4,),
        refs=(0, 1),
        scratch=[
            pltpu.VMEM(magnetization.shape, f32),
            pltpu.VMEM(stiffness.shape, f32),
            pltpu.SemaphoreType.DMA((4,)),
        ],
    )


def halos_zy(z_first, z_last, y_faces):
    y_next = ring(y_faces, "gy", -1)
    y_before = y_next if lax.axis_size("gy") == 2 else ring(y_faces, "gy", 1)
    return ring(z_first, "gz", -1), ring(z_last, "gz", 1), y_next, y_before, y_faces


def halos_x(x_first, x_last):
    return ring(x_first, "gx", -1), ring(x_last, "gx", 1)


def exchange_of(counts, index, magnetization, stiffness, zy, x):
    z_next, z_before, y_next, y_before, y_faces = zy
    arrays = (magnetization, stiffness, z_next, z_before, *x, y_next, y_before, y_faces)
    return call(
        functools.partial(exchange_kernel, counts),
        "exchange",
        magnetization.shape,
        8,
        5.0,
        (index, *(from_hbm(array) for array in arrays)),
        refs=range(1, 10),
        scratch=[pltpu.VMEM(array.shape, f32) for array in arrays]
        + [pltpu.SemaphoreType.DMA((15,))],
    )


def cos_sin(steps, size):
    quarter = steps >> whole_log(size // 4)
    angle = ((steps & (size // 4 - 1)) - size // 8).astype(f32) * (2.0 * math.pi / size)
    square = angle * angle
    sine = cosine = 0.0
    for k in range(5, -1, -1):
        sine = sine * square + (-1) ** k / math.factorial(2 * k + 1)
        cosine = cosine * square + (-1) ** k / math.factorial(2 * k)
    sine = sine * angle
    first, second = (cosine - sine) * math.sqrt(0.5), (cosine + sine) * math.sqrt(0.5)
    odd = (quarter & 1) == 1
    real = jnp.where(odd, -second, first)
    imag = jnp.where(odd, first, second)
    back = quarter >= 2
    return jnp.where(back, -real, real), jnp.where(back, -imag, imag)


def add(a, b):
    return a[0] + b[0], a[1] + b[1]


def subtract(a, b):
    return a[0] - b[0], a[1] - b[1]


def eight_points(z, sign):
    def quarter_turn(a):
        return (-a[1], a[0]) if sign > 0 else (a[1], -a[0])

    def four_points(p, q, r, s):
        e, f, g, h = add(p, r), subtract(p, r), add(q, s), quarter_turn(subtract(q, s))
        return add(e, g), add(f, h), subtract(e, g), subtract(f, h)

    even = four_points(z[0], z[2], z[4], z[6])
    odd = four_points(z[1], z[3], z[5], z[7])
    root = math.sqrt(0.5)
    first, third = add(odd[1], quarter_turn(odd[1])), subtract(quarter_turn(odd[3]), odd[3])
    odd = (
        odd[0],
        (first[0] * root, first[1] * root),
        quarter_turn(odd[2]),
        (third[0] * root, third[1] * root),
    )
    return [add(a, b) for a, b in zip(even, odd)] + [subtract(a, b) for a, b in zip(even, odd)]


def spread_tables(extent, size):
    step = size // INNER
    angle = np.outer(np.arange(INNER), np.arange(extent // step)) * (2.0 * math.pi / INNER)
    cosine, sine = np.cos(angle), np.sin(angle)
    table = np.block([[cosine, sine], [-sine, cosine]]).astype(np.float32)
    high = table.astype(ml_dtypes.bfloat16)
    low = (table - high.astype(np.float32)).astype(ml_dtypes.bfloat16)
    angle = np.outer(np.arange(step), np.arange(INNER)) * (2.0 * math.pi / size)
    turns = np.stack([np.cos(angle), np.sin(angle)]).astype(np.float32)
    return np.concatenate([high, low], axis=1), turns


def halves_of(table):
    table = table.astype(np.float32)
    high = table.astype(ml_dtypes.bfloat16)
    return high, (table - high.astype(np.float32)).astype(ml_dtypes.bfloat16)


def narrow_tables(extent, size):
    length = 2 * extent
    ratio = size // length
    m = np.arange(size)
    lags = np.arange(1, extent)
    window = 1.0 + 2.0 * np.cos(np.outer(m, lags) % size * (2.0 * math.pi / size)).sum(axis=1)
    i = np.arange(INNER)
    place = np.arange(0, size, INNER)[:, None, None] + i[:, None] - ratio * i[None, :]
    high, low = halves_of(window[place % size] / length)
    tiles = np.stack([high, low], axis=1)
    angle = np.outer(i, i) * (2.0 * math.pi / length)
    table = np.stack(halves_of(np.concatenate([np.cos(angle), np.sin(angle)], axis=0)))
    return tiles, table


def narrow_kernel(top, side, tiles, top_out, side_out):
    count = tiles.shape[0]
    parts = top_out.shape[3] // INNER
    step = count // parts
    top_rows, side_rows = top.shape[2], side.shape[2]
    totals = [None] * parts
    for k in range(count):
        columns = slice(k * INNER, (k + 1) * INNER)
        lines = jnp.concatenate(
            [
                top[:, :, :, columns].reshape(4 * top_rows, INNER),
                side[:, :, :, columns].reshape(4 * side_rows, INNER),
            ],
            axis=0,
        )
        high, low = split(lines)
        lines = jnp.concatenate([high, low, high], axis=1)
        for part in range(parts):
            tile = tiles[(k - part * step) % count]
            term = product(lines, jnp.concatenate([tile[0], tile[0], tile[1]], axis=0))
            totals[part] = term if k == 0 else totals[part] + term
    for part in range(parts):
        columns = slice(part * INNER, (part + 1) * INNER)
        top_out[:, :, :, columns] = totals[part][: 4 * top_rows].reshape(2, 2, top_rows, INNER)
        side_out[:, :, :, columns] = totals[part][4 * top_rows :].reshape(2, 2, side_rows, INNER)


def regrouping(extent, step, transposed):
    x = lax.broadcasted_iota(jnp.int32, (extent, extent), int(transposed))
    place = lax.broadcasted_iota(jnp.int32, (extent, extent), 1 - int(transposed))
    count = extent // step
    moved = (x & (step - 1)) * count + (x >> whole_log(step))
    return jnp.where(moved == place, 1.0, 0.0).astype(bf16)


def product(left, right, contracted=0):
    return lax.dot_general(
        left, right, (((1,), (contracted,)), ((), ())), preferred_element_type=f32
    )


def regrouped(values, step, transposed):
    high, low = split(values)
    rest = (values - high.astype(f32) - low.astype(f32)).astype(bf16)
    order = regrouping(values.shape[1], step, transposed)
    return product(high, order) + product(low, order) + product(rest, order)


def beside(pieces, count):
    per = LANES // count
    lane = lax.broadcasted_iota(jnp.int32, pieces[0].shape, 1)
    columns = []
    for start in range(0, len(pieces), per):
        column = pieces[start]
        for i in range(1, per):
            piece = pltpu.roll(pieces[start + i], i * count, 1)
            column = jnp.where(lane < i * count, column, piece)
        columns.append(column)
    return jnp.concatenate(columns, axis=1)


def back_product(turned, back):
    high, low = split(turned)
    both = product(jnp.concatenate([high, low], axis=0), back)
    middle = both.shape[0] // 2
    return both[:middle] + pltpu.roll(both[:middle], LANES // 2, 1) + both[middle:]


def dot3_with(values, table):
    high, low = split(values)
    lines = jnp.concatenate([high, low, high], axis=1)
    return product(lines, jnp.concatenate([table[0], table[0], table[1]], axis=0))


def there_and_back(real, imag, kernel, table):
    rows, extent = real.shape
    sign = jnp.where(lax.broadcasted_iota(jnp.int32, (1, extent), 1) & 1 == 0, 1.0, -1.0)
    lines = jnp.concatenate(
        [jnp.concatenate([real, imag], axis=1), jnp.concatenate([imag, -real], axis=1)], axis=0
    )
    signs = jnp.concatenate([sign, sign], axis=1)
    waves = dot3_with(jnp.concatenate([lines, lines * signs], axis=0), table)
    totals = []
    for b in range(2):
        wave_real, wave_imag = (
            waves[(2 * b + k) * rows : (2 * b + k + 1) * rows] for k in range(2)
        )
        columns = slice(b * INNER, (b + 1) * INNER)
        weighted = ([], [])
        for c in range(2):
            kernel_real, kernel_imag = kernel[c, 0, :, columns], kernel[c, 1, :, columns]
            weighted[0].append(kernel_real * wave_real + kernel_imag * wave_imag)
            weighted[1].append(kernel_real * wave_imag - kernel_imag * wave_real)
        a, b = (jnp.concatenate(part, axis=0) for part in weighted)
        lines = jnp.concatenate(
            [jnp.concatenate([a, -b], axis=1), jnp.concatenate([b, a], axis=1)], axis=0
        )
        totals.append(dot3_with(lines, table))
    total = totals[0] + totals[1] * sign
    return total[: 2 * rows], total[2 * rows :]


def lines_kernel(counts, here, gathered, swapped, table, kernel, out, received):
    count_x, count_y, count_z = counts
    group = count_y * count_z
    top_rows = LANES // group
    half = LANES // 2
    kys, size = kernel.shape[2], INNER * TILE
    ky = here[0] * kys + lax.broadcasted_iota(jnp.int32, (kys, LANES), 0)
    lane = lax.broadcasted_iota(jnp.int32, (kys, LANES), 1)
    odd = (lane >> whole_log(LANES // 2)) ^ (here[0] & 1)
    pair = lane >> whole_log(top_rows) & (group // 2 - 1)
    phases_of = []
    for h in range(2):
        y = (2 * pair + odd) * (2 * top_rows) + h * top_rows + (lane & (top_rows - 1))
        cosine, sine = cos_sin(ky * y & (size - 1), size)
        phases_of += [cosine, -sine]
    for k, part in enumerate((gathered, swapped)):
        for member in range(part.shape[0]):
            g, place = divmod(member, group // 2)
            for j in range(top_rows // QUAD):
                row = (k * group // 2 + place) * top_rows + j * QUAD
                received[g, row : row + QUAD, :] = part[member, j]
    blocks = [received[g] for g in range(count_x)]
    mixed = dot3(jnp.concatenate(phases_of, axis=0), split(jnp.concatenate(blocks, axis=1)))
    low_half, high_half = mixed[: 2 * kys], mixed[2 * kys :]
    lane = lax.broadcasted_iota(jnp.int32, (2 * kys, LANES), 1)
    pieces = []
    for g in range(0, count_x, 2):
        a = slice(g * LANES, (g + 1) * LANES)
        b = slice((g + 1) * LANES, (g + 2) * LANES)
        pieces.append(
            jnp.where(
                lane < half,
                low_half[:, a] + pltpu.roll(high_half[:, a], half, 1),
                pltpu.roll(low_half[:, b], half, 1) + high_half[:, b],
            )
        )
    lines = jnp.concatenate(pieces, axis=1)
    for k, part in enumerate(there_and_back(lines[:kys], lines[kys:], kernel, table)):
        out[:, k * TILE : (k + 1) * TILE, :] = part.T.reshape(count_x * group, TILE, LANES)


def side_kernel_body(
    counts, here, gathered, swapped, spectrum, kernel, out, received
):
    count_x, count_y, count_z = counts
    depth_block = (out.shape[1] - 2 * TILE) // 2
    last = gathered.shape[1] - 1
    kzs, length = kernel.shape[2], INNER * TILE
    size = kzs * count_y * count_z
    columns = count_x * count_z * QUAD
    kz = here[0] * kzs + lax.broadcasted_iota(jnp.int32, (kzs, columns), 0)
    column = lax.broadcasted_iota(jnp.int32, (kzs, columns), 1)
    pair = column >> whole_log(QUAD) & (count_z // 2 - 1)
    odd = (column >> whole_log(columns // 2)) ^ (here[0] & 1)
    z = (2 * pair + odd) * depth_block + (column & (QUAD - 1))
    z = z + (column >> whole_log(QUAD * count_z // 2) & (count_x - 1)) * QUAD
    cosine, sine = cos_sin(kz * z & (size - 1), size)
    table = jnp.concatenate([cosine, -sine], axis=0)
    for k, part in enumerate((gathered, swapped)):
        for x in range(count_x):
            for y in range(count_y):
                for pair in range(count_z // 2):
                    row = ((k * count_x + x) * count_z // 2 + pair) * QUAD
                    member = (x * count_y + y) * count_z // 2 + pair
                    received[y, row : row + QUAD, :] = part[member, last]
    blocks = [received[y] for y in range(count_y)]
    lines = dot3(table, split(jnp.concatenate(blocks, axis=1)))

    real, imag = there_and_back(lines[:kzs], lines[kzs:], kernel, spectrum)

    rows = depth_block * count_z
    z = lax.broadcasted_iota(jnp.int32, (rows, 2 * kzs), 0)
    column = lax.broadcasted_iota(jnp.int32, (rows, 2 * kzs), 1)
    cosine, sine = cos_sin((here[0] * kzs + (column & (kzs - 1))) * z & (size - 1), size)
    table = jnp.where(column < kzs, cosine, -sine) * (1.0 / (size * length))
    for c in range(2):
        part = slice(c * kzs, (c + 1) * kzs)
        image = dot3(table, split(jnp.concatenate([real[part], imag[part]], axis=0)))
        for y in range(count_y):
            for z in range(count_z):
                start = 2 * TILE + c * depth_block
                out[y * count_z + z, start : start + depth_block, :] = image[
                    z * depth_block : (z + 1) * depth_block, y * LANES : (y + 1) * LANES
                ]
    out[:, 0 : 2 * TILE, :] = jnp.zeros((out.shape[0], 2 * TILE, LANES), f32)


def rows_kernel(counts, arrived, side, back, turns, out, result, sending):
    del side
    count_y, count_z = counts[1:]
    step = turns.shape[1]
    size = step * INNER
    per_turn = arrived.shape[0] // step
    half = LANES // 2
    lane = lax.broadcasted_iota(jnp.int32, (2 * TILE, LANES), 1)
    halves = []
    for pair in range(0, per_turn, 2):
        z = []
        for b in range(step):
            first, second = arrived[b * per_turn + pair], arrived[b * per_turn + pair + 1]
            spectra = (
                jnp.where(lane < half, first, pltpu.roll(second, half, 1)),
                jnp.where(lane < half, pltpu.roll(first, half, 1), second),
            )
            z.append(
                tuple(
                    jnp.concatenate(
                        [spectrum[k * TILE : (k + 1) * TILE] for spectrum in spectra], axis=0
                    )
                    for k in range(2)
                )
            )
        z = eight_points(z, 1)
        lanes = slice(pair // 2 * LANES, (pair // 2 + 1) * LANES)
        for v in range(1, step):
            cosine, sine = turns[0, v : v + 1, lanes], turns[1, v : v + 1, lanes]
            a, b = z[v]
            z[v] = (a * cosine - b * sine, a * sine + b * cosine)
        halves.append(z)
    turned = [
        jnp.concatenate([z[v][k] for k in range(2) for z in halves], axis=1) for v in range(step)
    ]
    lines = back_product(jnp.concatenate(turned, axis=0), back[...])
    pieces = [lines[v * 2 * TILE : (v + 1) * 2 * TILE] for v in range(step)]
    total = regrouped(beside(pieces, count_y * LANES // step), step, True)
    total = total * (1.0 / (size * size))
    for y in range(count_y):
        result[y] = total[:, y * LANES : (y + 1) * LANES]
    sends = begin(
        sending,
        [
            (result.at[y], out.at[y * count_z + z, 0 : 2 * TILE, :])
            for y in range(count_y)
            for z in range(count_z)
        ],
    )
    for copy in sends:
        copy.wait()


def sum_kernel(exchange_grad, arrived, out, result, sending):
    depth = exchange_grad.shape[1]
    group = arrived.shape[0]
    sends = []

    def send(c):
        sends.append(pltpu.make_async_copy(result.at[c], out.at[c], sending.at[c]))
        sends[-1].start()

    def top(c):
        return arrived[:, c * TILE : (c + 1) * TILE, :].reshape(group * TILE, LANES)

    def side(c):
        rows = slice(2 * TILE + c * depth, 2 * TILE + (c + 1) * depth)
        total = arrived[0, rows, :]
        for p in range(1, group):
            total = total + arrived[p, rows, :]
        return total

    image = top(0)
    for z in range(depth):
        result[0, z] = exchange_grad[0, z] + image
    send(0)
    column = side(1)
    for z in range(depth):
        result[2, z] = exchange_grad[2, z] + column[z : z + 1]
    send(2)
    image, column = top(1), side(0)
    for z in range(depth):
        result[1, z] = exchange_grad[1, z] + image + column[z : z + 1]
    send(1)
    for copy in sends:
        copy.wait()


def residual_blocks(residual_top, residual_side, copies, share, quads):
    block_x, block_y = residual_top.shape
    top_rows = block_y // 2

    def body(at_x, top, side, out):
        piece = jnp.concatenate([top[0:top_rows, :], top[top_rows:, :]], axis=1)
        part = side[pl.ds(at_x[0] * share, share), :]
        if not quads:
            part = jnp.concatenate([part, jnp.zeros((TILE - share, LANES), f32)], axis=0)
        for copy in range(copies):
            if quads:
                for j in range(top_rows // QUAD):
                    out[copy, j] = piece[j * QUAD : (j + 1) * QUAD]
                out[copy, top_rows // QUAD] = part
            else:
                out[copy, 0:top_rows, :] = piece
                out[copy, top_rows:, :] = part

    shape = (top_rows // QUAD + 1, QUAD) if quads else (top_rows + TILE,)
    return call(
        body,
        "pack",
        (copies, *shape, LANES),
        60,
        0.8,
        (lax.axis_index("gx").reshape(1), residual_top.T, residual_side.T),
    )


def fast_on_device(magnetization, stiffness, residual_top, residual_side, top_kernel, side_kernel):
    counts = tuple(lax.axis_size(axis) for axis in ALL)
    count_x, count_y, count_z = counts
    group = count_y * count_z
    devices = count_x * group
    block_x, block_y = residual_top.shape
    depth_block = stiffness.shape[0]
    top_rows = block_y // 2
    kys, size = top_kernel.shape[2:]
    kzs = side_kernel.shape[2]
    extent = count_x * block_x
    here = [lax.axis_index(axis) for axis in ALL]
    plane_index = here[1] * count_z + here[2]
    index = (here[0] * group + plane_index).reshape(1)
    plane_index = plane_index.reshape(1)
    back, turns = (jnp.asarray(table) for table in spread_tables(extent, size))
    tiles, table = (jnp.asarray(values) for values in narrow_tables(extent, size))

    parities = [range(parity, devices, 2) for parity in range(2)]
    sent = residual_blocks(
        residual_top, residual_side, devices // 2, depth_block // count_x, True
    )
    gathered = lax.all_to_all(
        sent, ALL, 0, 0, tiled=True, axis_index_groups=[list(each) for each in parities]
    )
    z_first, z_last, x_first, x_last, y_faces = faces_of(magnetization, stiffness)
    top_spectra, side_spectra = call(
        narrow_kernel,
        "narrow",
        [(2, 2, kys, 2 * extent), (2, 2, kzs, 2 * extent)],
        16,
        2.5,
        (top_kernel, side_kernel, tiles),
    )
    gathered, x_first, x_last, y_faces, top_spectra, side_spectra = lax.optimization_barrier(
        (gathered, x_first, x_last, y_faces, top_spectra, side_spectra)
    )
    swapped = lax.ppermute(gathered, "gz", [(i, i ^ 1) for i in range(count_z)])
    zy = halos_zy(z_first, z_last, y_faces)

    lines = call(
        functools.partial(lines_kernel, counts),
        "lines",
        (devices, 2 * TILE, LANES),
        16,
        2.2,
        (index, gathered, swapped, table, top_spectra),
        scratch=[pltpu.VMEM((count_x, LANES, LANES), f32)],
    )
    arrived = lax.all_to_all(lines, ALL, 0, 0, tiled=True)
    lines, x_first, x_last = lax.optimization_barrier((lines, x_first, x_last))
    x = halos_x(x_first, x_last)
    side = call(
        functools.partial(side_kernel_body, counts),
        "side",
        (group, 2 * TILE + 2 * depth_block, LANES),
        8,
        2.0,
        (plane_index, gathered, swapped, table, side_spectra),
        in_hbm=(0,),
        scratch=[pltpu.VMEM((count_y, count_x * count_z * QUAD, LANES), f32)],
    )
    arrived, side = lax.optimization_barrier((arrived, side))
    rows = call(
        functools.partial(rows_kernel, counts),
        "rows",
        (group, 2 * TILE + 2 * depth_block, LANES),
        8,
        1.4,
        (arrived, from_hbm(side), back, turns),
        in_hbm=(0,),
        refs=(1,),
        scratch=[
            pltpu.VMEM((count_y, 2 * TILE, LANES), f32),
            pltpu.SemaphoreType.DMA((group,)),
        ],
        out_refs=(0,),
        aliases={1: 0},
    )
    rows, zy, x = lax.optimization_barrier((rows, zy, x))
    arrived = lax.all_to_all(rows, ("gy", "gz"), 0, 0, tiled=True)
    exchange_grad = exchange_of(counts, index, magnetization, stiffness, zy, x)
    return call(
        sum_kernel,
        "gradient",
        magnetization.shape,
        16,
        1.2,
        (exchange_grad, arrived),
        out_refs=(0,),
        scratch=[pltpu.VMEM(magnetization.shape, f32), pltpu.SemaphoreType.DMA((3,))],
    )


def fits(counts, stiffness, residual_top, residual_side, top_kernel, side_kernel):
    count_x, count_y, count_z = counts
    block_x, block_y = residual_top.shape
    group = count_y * count_z
    return (
        2 * block_x == LANES
        and 2 * top_kernel.shape[2] == LANES
        and stiffness.shape[2] == LANES
        and block_x == group * TILE
        and block_y * group == count_x * block_x == INNER
        and count_y * LANES == INNER
        and block_y % 16 == 0
        and count_x % 2 == 0
        and count_z % 2 == 0
        and (count_x * group) % (2 * top_kernel.shape[3] // INNER) == 0
        and INNER == top_kernel.shape[2] * count_z
        and top_kernel.shape[3] == TILE * INNER == side_kernel.shape[3]
        and INNER == 2 * LANES
        and stiffness.shape[0] % 16 == 0
        and stiffness.shape[0] == count_x * QUAD
        and side_kernel.shape[2] % 16 == 0
        and all(
            count & (count - 1) == 0
            for count in (group, count_x, count_z, top_kernel.shape[3], side_kernel.shape[2])
        )
    )


def on_device(magnetization, stiffness, residual_top, residual_side, top_kernel, side_kernel):
    counts = tuple(lax.axis_size(axis) for axis in ALL)
    count_x, count_y, count_z = counts
    if fits(counts, stiffness, residual_top, residual_side, top_kernel, side_kernel):
        return fast_on_device(
            magnetization, stiffness, residual_top, residual_side, top_kernel, side_kernel
        )
    devices = count_x * count_y * count_z
    depth_block = stiffness.shape[0]
    block_x, block_y = residual_top.shape
    top_rows = block_y // 2
    share = depth_block // count_x

    sent = residual_blocks(residual_top, residual_side, devices, share, False)
    rows = sent.shape[1]
    gathered = lax.all_to_all(sent, ALL, 0, 0, tiled=True)
    index = (
        (lax.axis_index("gx") * count_y + lax.axis_index("gy")) * count_z + lax.axis_index("gz")
    ).reshape(1)
    z_first, z_last, x_first, x_last, y_faces = faces_of(magnetization, stiffness)
    exchange_grad = exchange_of(
        counts,
        index,
        magnetization,
        stiffness,
        halos_zy(z_first, z_last, y_faces),
        halos_x(x_first, x_last),
    )

    parts = image_parts(
        gathered, top_kernel, side_kernel, counts, block_x, top_rows, depth_block
    )
    rows = parts.shape[1]
    arrived = lax.all_to_all(parts.reshape(devices * rows, LANES), ALL, 0, 0, tiled=True)
    arrived = arrived.reshape(devices, rows, LANES)
    top_sum = jnp.sum(arrived[:, : rows - TILE], axis=0)
    side_sum = jnp.sum(
        arrived[:, rows - TILE :].reshape(count_x, count_y * count_z, TILE, LANES), axis=1
    )
    side = side_sum[:, : 2 * share].reshape(count_x, 2, share, LANES)
    side = jnp.swapaxes(side, 0, 1).reshape(2, depth_block, 1, LANES)
    top = lax.all_gather(top_sum, "gz", axis=0)
    top = jnp.swapaxes(top.reshape(count_z, 2, block_x // count_z, LANES), 0, 1)
    top = top.reshape(2, 1, block_x, LANES)
    return jnp.stack(
        [
            exchange_grad[0] + top[0],
            exchange_grad[1] + top[1] + side[0],
            exchange_grad[2] + side[1],
        ]
    )


def solution(mesh):
    placed = (
        P(None, "gz", "gx", "gy"),
        P("gz", "gx", "gy"),
        P("gx", ("gy", "gz")),
        P("gy", "gz"),
        P(None, None, ("gx", "gy", "gz"), None),
        P(None, None, ("gy", "gz"), None),
    )
    return jax.shard_map(
        on_device, mesh=mesh, in_specs=placed, out_specs=P(None, "gz", "gx", "gy"), check_vma=False
    )
```

```python
import functools
import math

import jax
import jax.numpy as jnp
import ml_dtypes
import numpy as np
from jax import lax
from jax.experimental import pallas as pl
from jax.experimental.pallas import tpu as pltpu
from jax.sharding import PartitionSpec as P

LANES = 128
TILE = 8
INNER = 256
ALL = ("gx", "gy", "gz")
f32 = jnp.float32
bf16 = jnp.bfloat16
MIB = 1024 * 1024
QUAD = 4
SMEM = pl.BlockSpec(memory_space=pltpu.SMEM)
VMEM = pl.BlockSpec(memory_space=pltpu.VMEM)
HBM = pl.BlockSpec(memory_space=pltpu.HBM)


def whole_log(count):
    return count.bit_length() - 1


def split(values):
    high = values.astype(bf16)
    return high, (values - high.astype(f32)).astype(bf16)


def dot3(left, right):
    high, low = split(left)
    def one(a, b):
        return lax.dot_general(a, b, (((1,), (0,)), ((), ())), preferred_element_type=f32)
    return one(high, right[0]) + one(low, right[0]) + one(high, right[1])


def from_hbm(values):
    return pltpu.with_memory_space_constraint(values, pltpu.HBM)


def call(
    body,
    name,
    shape,
    limit,
    microseconds,
    operands,
    in_hbm=(),
    in_vmem=(),
    scratch=(),
    refs=(),
    out_refs=(),
    aliases=(),
):
    shapes = shape if isinstance(shape, list) else [shape]
    moved = sum(4 * math.prod(each) for each in shapes)
    moved += sum(x.size * x.dtype.itemsize for x in operands)
    results = pl.pallas_call(
        body,
        out_shape=[
            pltpu.HBM(each, f32)
            if i in in_hbm
            else pltpu.VMEM(each, bf16)
            if i in in_vmem
            else jax.ShapeDtypeStruct(each, f32)
            for i, each in enumerate(shapes)
        ],
        in_specs=[
            SMEM if x.shape == (1,) else HBM if i in refs else VMEM
            for i, x in enumerate(operands)
        ],
        out_specs=[HBM if i in out_refs else VMEM for i in range(len(shapes))],
        input_output_aliases=dict(aliases),
        scratch_shapes=list(scratch),
        compiler_params=pltpu.CompilerParams(vmem_limit_bytes=limit * MIB),
        cost_estimate=pl.CostEstimate(
            flops=int(microseconds * 1e9), bytes_accessed=moved, transcendentals=0
        ),
        name=name,
    )(*operands)
    return results if isinstance(shape, list) else results[0]


def transform_tables(extent, size):
    x = np.arange(extent)
    angle = (np.outer(x, np.arange(INNER)) % size) * (2.0 * math.pi / size)
    forward = np.concatenate([np.cos(angle), np.sin(angle)], 0).astype(np.float32)
    backward = np.concatenate([np.cos(angle).T, np.sin(angle).T], 0).astype(np.float32)

    def parts(table):
        high = table.astype(ml_dtypes.bfloat16)
        return high, (table - high.astype(np.float32)).astype(ml_dtypes.bfloat16)

    outer = size // INNER
    turn = (np.outer(np.arange(outer), x) % outer) * (2.0 * math.pi / outer)
    turns = np.stack([np.cos(turn), np.sin(turn)]).astype(np.float32)
    return parts(forward), parts(backward), turns


def phases(first, second, size):
    angle = (first * second % size).astype(f32) * (2.0 * math.pi / size)
    return jnp.cos(angle), jnp.sin(angle)


def image_kernel(
    counts, gathered, y_table, z_table, fh, fl, bh, bl, turns, top, side, y_back, z_back, out
):
    count_x, count_y, count_z, top_rows = counts
    group = count_y * count_z
    half = LANES // 2
    kys = top.shape[2]
    kzs = side.shape[2]
    forward = (fh[...], fl[...])
    backward = (bh[...], bl[...])

    blocks = [
        gathered[g * group : (g + 1) * group, 0:top_rows, :].reshape(group * top_rows, LANES)
        for g in range(count_x)
    ]
    mixed = dot3(y_table[...], split(jnp.concatenate(blocks, axis=1)))
    low_half, high_half = mixed[: 2 * kys], mixed[2 * kys :]
    lane = lax.broadcasted_iota(jnp.int32, (2 * kys, LANES), 1)
    pieces = []
    for g in range(0, count_x, 2):
        a = slice(g * LANES, (g + 1) * LANES)
        b = slice((g + 1) * LANES, (g + 2) * LANES)
        pieces.append(
            jnp.where(
                lane < half,
                low_half[:, a] + pltpu.roll(high_half[:, a], half, 1),
                pltpu.roll(low_half[:, b], half, 1) + high_half[:, b],
            )
        )
    top_lines = jnp.concatenate(pieces, axis=1)

    side_blocks = []
    for y in range(count_y):
        rows = [
            gathered[(x * count_y + y) * count_z + z, top_rows : top_rows + TILE, :]
            for x in range(count_x)
            for z in range(count_z)
        ]
        side_blocks.append(jnp.concatenate(rows, axis=0))
    side_lines = dot3(z_table[...], split(jnp.concatenate(side_blocks, axis=1)))

    real = jnp.concatenate([top_lines[:kys], side_lines[:kzs]], axis=0)
    imag = jnp.concatenate([top_lines[kys:], side_lines[kzs:]], axis=0)
    rows = kys + kzs
    total_real = total_imag = None
    for b in range(turns.shape[1]):
        cosine, sine = turns[0, b : b + 1, :], turns[1, b : b + 1, :]
        turned_real = real * cosine + imag * sine
        turned_imag = imag * cosine - real * sine
        waves = dot3(
            jnp.concatenate(
                [
                    jnp.concatenate([turned_real, turned_imag], axis=1),
                    jnp.concatenate([turned_imag, -turned_real], axis=1),
                ],
                axis=0,
            ),
            forward,
        )
        wave_real, wave_imag = waves[:rows], waves[rows:]
        columns = slice(b * INNER, (b + 1) * INNER)
        weighted_real, weighted_imag = [], []
        for c in range(2):
            for kernel, part in ((top, slice(0, kys)), (side, slice(kys, rows))):
                kernel_real, kernel_imag = kernel[c, 0, :, columns], kernel[c, 1, :, columns]
                weighted_real.append(
                    kernel_real * wave_real[part] + kernel_imag * wave_imag[part]
                )
                weighted_imag.append(
                    kernel_real * wave_imag[part] - kernel_imag * wave_real[part]
                )
        weighted_real = jnp.concatenate(weighted_real, axis=0)
        weighted_imag = jnp.concatenate(weighted_imag, axis=0)
        back = dot3(
            jnp.concatenate(
                [
                    jnp.concatenate([weighted_real, -weighted_imag], axis=1),
                    jnp.concatenate([weighted_imag, weighted_real], axis=1),
                ],
                axis=0,
            ),
            backward,
        )
        back_real, back_imag = back[: 2 * rows], back[2 * rows :]
        if b == 0:
            total_real, total_imag = back_real, back_imag
        else:
            total_real = total_real + (back_real * cosine - back_imag * sine)
            total_imag = total_imag + (back_real * sine + back_imag * cosine)

    y_parts = split(y_back[...])
    depth_rows = []
    quarter = (out.shape[1] - TILE) // 2
    block_x = quarter * count_z
    for c in range(2):
        start = c * rows
        lines = jnp.concatenate(
            [total_real[start : start + kys], total_imag[start : start + kys]], axis=0
        )
        image = dot3(lines.T, y_parts)
        for x in range(count_x):
            for y in range(count_y):
                for z in range(count_z):
                    first = x * block_x + z * quarter
                    out[
                        (x * count_y + y) * count_z + z, c * quarter : (c + 1) * quarter, :
                    ] = image[first : first + quarter, y * LANES : (y + 1) * LANES]
        depth_rows.append(total_real[start + kys : start + rows])
        depth_rows.append(total_imag[start + kys : start + rows])
    side_image = dot3(z_back[...], split(jnp.concatenate(depth_rows, axis=0)))
    for y in range(count_y):
        for z in range(count_z):
            block = side_image[z * TILE : (z + 1) * TILE, y * LANES : (y + 1) * LANES]
            for x in range(count_x):
                out[(x * count_y + y) * count_z + z, 2 * quarter :, :] = block


def image_parts(gathered, top_kernel, side_kernel, counts, block_x, top_rows, depth_block):
    count_x, count_y, count_z = counts
    group = count_y * count_z
    here = [lax.axis_index(axis) for axis in ALL]
    kys, size = top_kernel.shape[2:]
    kzs = side_kernel.shape[2]
    depth_size = kzs * group
    extent = count_y * LANES
    share = depth_block // count_x
    block_y = top_rows * 2

    ky = ((here[0] * count_y + here[1]) * count_z + here[2]) * kys + lax.iota(jnp.int32, kys)
    kz = (here[1] * count_z + here[2]) * kzs + lax.iota(jnp.int32, kzs)

    row = lax.iota(jnp.int32, group * top_rows)
    y_tables = []
    for h in range(2):
        y = row // top_rows * block_y + h * top_rows + row % top_rows
        cosine, sine = phases(ky[:, None], y[None, :], size)
        y_tables += [cosine, -sine]
    y_table = jnp.concatenate(y_tables, axis=0)

    row = lax.iota(jnp.int32, count_x * count_z * TILE)
    inside = row % TILE
    z = row // TILE % count_z * depth_block + row // (TILE * count_z) * share + inside
    cosine, sine = phases(kz[:, None], z[None, :], depth_size)
    z_table = jnp.where((inside < share)[None, :], jnp.concatenate([cosine, -sine], axis=0), 0.0)

    cosine, sine = phases(ky[:, None], lax.iota(jnp.int32, extent)[None, :], size)
    y_back = jnp.concatenate([cosine, -sine], axis=0) * (1.0 / (size * size))

    row = lax.iota(jnp.int32, count_z * TILE)
    z = row // TILE * depth_block + here[0] * share + row % TILE % share
    cosine, sine = phases(z[:, None], kz[None, :], depth_size)
    both = jnp.concatenate([cosine, -sine], axis=1) * (1.0 / (size * depth_size))
    component = (row % TILE // share)[:, None]
    z_back = jnp.concatenate(
        [jnp.where(component == 0, both, 0.0), jnp.where(component == 1, both, 0.0)], axis=1
    )

    forward, backward, turns = transform_tables(extent, size)
    out_rows = 2 * (block_x // count_z) + TILE
    return pl.pallas_call(
        functools.partial(image_kernel, counts + (top_rows,)),
        out_shape=jax.ShapeDtypeStruct((count_x * group, out_rows, LANES), f32),
        compiler_params=pltpu.CompilerParams(vmem_limit_bytes=56 * 1024 * 1024),
        name="images",
    )(
        gathered,
        y_table,
        z_table,
        *(jnp.asarray(t) for t in forward + backward),
        jnp.asarray(turns),
        top_kernel,
        side_kernel,
        y_back,
        z_back,
    )


def begin(semaphores, pairs):
    started = [
        pltpu.make_async_copy(source, target, semaphores.at[i])
        for i, (source, target) in enumerate(pairs)
    ]
    for copy in started:
        copy.start()
    return started


def faces_kernel(
    magnetization, stiffness, z_first, z_last, x_first, x_last, y_faces, m, s, loading
):
    depth, across = stiffness.shape[:2]
    loads = begin(
        loading, [(stiffness, s)] + [(magnetization.at[c], m.at[c]) for c in range(3)]
    )
    lane = lax.broadcasted_iota(jnp.int32, (across, LANES), 1)
    pair = (lane + 1 & (LANES - 1)) >> 1
    sides = jnp.zeros((across, LANES), f32)
    for field in (3, 0, 1, 2):
        loads[(field + 1) % 4].wait()
        ref = s if field == 3 else m.at[field]
        z_first[field] = ref[0]
        z_last[field] = ref[depth - 1]
        x_first[field] = ref[:, 0, :]
        x_last[field] = ref[:, across - 1, :]
        for z in range(depth):
            column = field * depth + z
            turned = pltpu.roll(ref[z], 2 * column, 1) if column else ref[z]
            sides = jnp.where(pair == column, turned, sides)
    y_faces[...] = sides


def twice_weight(a, b):
    total = a + b
    inverse = pl.reciprocal(total, approx=True)
    return 4.0 * a * b * (inverse * (2.0 - total * inverse))


def exchange_kernel(
    counts,
    here,
    magnetization_from,
    stiffness_from,
    y_faces_from,
    z_next,
    z_before,
    x_next,
    x_before,
    y_next,
    y_before,
    out,
    m,
    s,
    y_faces,
    loading,
):
    depth, across = s.shape[:2]
    chunk = depth // 4
    pairs = [(y_faces_from, y_faces)]
    for k in range(4):
        layers = pl.ds(k * chunk, chunk)
        pairs.append((stiffness_from.at[layers], s.at[layers]))
        pairs.append((magnetization_from.at[:, layers], m.at[:, layers]))
    loads = begin(loading, pairs)

    count_x, count_y, count_z = counts
    at_z = here[0] % count_z
    at_y = here[0] // count_z % count_y
    at_x = here[0] // (count_z * count_y)

    def inside(condition, values):
        return jnp.where(condition, values, 0.0)

    lane = lax.broadcasted_iota(jnp.int32, (across, LANES), 1)
    row = lax.broadcasted_iota(jnp.int32, (across, LANES), 0)
    first_lane, last_lane, last_row = lane == 0, lane == LANES - 1, row == across - 1

    loads[0].wait()
    own = y_faces[...]
    even = (lane & 1) == 0
    field = (lane + 1 & (LANES - 1)) >> whole_log(2 * depth)
    halo = jnp.where(
        even, pltpu.roll(y_before[...], 1, 1), pltpu.roll(y_next[...], LANES - 1, 1)
    )
    present = jnp.where(even, at_y, count_y - 1 - at_y) > 0
    weight = twice_weight(
        jnp.where(field == 3, own, 1.0),
        jnp.where(field == 3, jnp.where(present, halo, 0.0), 1.0),
    )
    spread = pltpu.roll(weight, LANES - 6 * depth, 1)
    for c in (1, 2):
        spread = jnp.where(
            field == c, pltpu.roll(weight, LANES - (3 - c) * 2 * depth, 1), spread
        )
    sides = spread * (own - halo)
    outer = first_lane | last_lane

    for copy in loads[1:3]:
        copy.wait()
    below_weight = twice_weight(inside(at_z > 0, z_before[3]), s[0])
    below = [below_weight * (z_before[c] - m[c, 0]) for c in range(3)]
    for z in range(depth):
        if z % chunk == chunk - 1:
            k = 1 + 2 * (z // chunk + 1)
            for copy in loads[k : k + 2]:
                copy.wait()
        centre = s[z]
        above = s[z + 1] if z + 1 < depth else inside(at_z < count_z - 1, z_next[3])
        weight_z = twice_weight(centre, above)
        weight_x = jnp.where(
            last_row, 0.0, twice_weight(centre, pltpu.roll(centre, across - 1, 0))
        )
        weight_y = jnp.where(
            last_lane, 0.0, twice_weight(centre, pltpu.roll(centre, LANES - 1, 1))
        )
        for c in range(3):
            column = c * depth + z
            values = m[c, z]
            upper = m[c, z + 1] if z + 1 < depth else z_next[c]
            up = weight_z * (values - upper)
            flux_x = weight_x * (values - pltpu.roll(values, across - 1, 0))
            flux_y = weight_y * (values - pltpu.roll(values, LANES - 1, 1))
            total = (up - below[c]) + (flux_x - pltpu.roll(flux_x, 1, 0))
            total = total + (flux_y - pltpu.roll(flux_y, 1, 1))
            both = pltpu.roll(sides, LANES - 2 * column, 1) if column else sides
            out[c, z] = jnp.where(outer, total + both, total)
            below[c] = up
    for edge_row, halo, present in (
        (across - 1, x_next, at_x < count_x - 1),
        (0, x_before, at_x > 0),
    ):
        weight = twice_weight(s[:, edge_row, :], inside(present, halo[3]))
        for c in range(3):
            out[c, :, edge_row, :] += weight * (m[c, :, edge_row, :] - halo[c])


def ring(block, axis, distance):
    count = lax.axis_size(axis)
    return lax.ppermute(block, axis, [(i, (i + distance) % count) for i in range(count)])


def faces_of(magnetization, stiffness):
    depth, across, along = stiffness.shape
    return call(
        faces_kernel,
        "faces",
        [
            (4, across, along),
            (4, across, along),
            (4, depth, along),
            (4, depth, along),
            (across, LANES),
        ],
        8,
        2.0,
        (from_hbm(magnetization), from_hbm(stiffness)),
        in_hbm=(4,),
        refs=(0, 1),
        scratch=[
            pltpu.VMEM(magnetization.shape, f32),
            pltpu.VMEM(stiffness.shape, f32),
            pltpu.SemaphoreType.DMA((4,)),
        ],
    )


def halos_zy(z_first, z_last, y_faces):
    y_next = ring(y_faces, "gy", -1)
    y_before = y_next if lax.axis_size("gy") == 2 else ring(y_faces, "gy", 1)
    return ring(z_first, "gz", -1), ring(z_last, "gz", 1), y_next, y_before, y_faces


def halos_x(x_first, x_last):
    return ring(x_first, "gx", -1), ring(x_last, "gx", 1)


def exchange_of(counts, index, magnetization, stiffness, zy, x):
    z_next, z_before, y_next, y_before, y_faces = zy
    fetched = (magnetization, stiffness, y_faces)
    return call(
        functools.partial(exchange_kernel, counts),
        "exchange",
        magnetization.shape,
        8,
        5.0,
        (
            index,
            *(from_hbm(array) for array in fetched),
            z_next,
            z_before,
            *x,
            y_next,
            y_before,
        ),
        refs=(1, 2, 3),
        scratch=[pltpu.VMEM(array.shape, f32) for array in fetched]
        + [pltpu.SemaphoreType.DMA((9,))],
    )


def cos_sin(steps, size):
    quarter = steps >> whole_log(size // 4)
    angle = ((steps & (size // 4 - 1)) - size // 8).astype(f32) * (2.0 * math.pi / size)
    square = angle * angle
    sine = cosine = 0.0
    for k in range(5, -1, -1):
        sine = sine * square + (-1) ** k / math.factorial(2 * k + 1)
        cosine = cosine * square + (-1) ** k / math.factorial(2 * k)
    sine = sine * angle
    first, second = (cosine - sine) * math.sqrt(0.5), (cosine + sine) * math.sqrt(0.5)
    odd = (quarter & 1) == 1
    real = jnp.where(odd, -second, first)
    imag = jnp.where(odd, first, second)
    back = quarter >= 2
    return jnp.where(back, -real, real), jnp.where(back, -imag, imag)


def halves_of(table):
    table = table.astype(np.float32)
    high = table.astype(ml_dtypes.bfloat16)
    return high, (table - high.astype(np.float32)).astype(ml_dtypes.bfloat16)


def narrow_tables(extent, size):
    length = 2 * extent
    ratio = size // length
    m = np.arange(size)
    lags = np.arange(1, extent)
    window = 1.0 + 2.0 * np.cos(np.outer(m, lags) % size * (2.0 * math.pi / size)).sum(axis=1)
    i = np.arange(INNER)
    place = np.arange(0, size, INNER)[:, None, None] + i[:, None] - ratio * i[None, :]
    high, low = halves_of(window[place % size] / length)
    tiles = np.stack([high, low], axis=1)
    return tiles, transform_table(length)


def transform_table(size):
    i = np.arange(INNER)
    angle = np.outer(i, i) * (2.0 * math.pi / size)
    return np.stack(halves_of(np.concatenate([np.cos(angle), np.sin(angle)], axis=0)))


def y_table_of(counts, here, kys, size):
    group = counts[1] * counts[2]
    top_rows = LANES // group
    ky = here[0] * kys + lax.broadcasted_iota(jnp.int32, (kys, LANES), 0)
    lane = lax.broadcasted_iota(jnp.int32, (kys, LANES), 1)
    odd = (lane >> whole_log(LANES // 2)) ^ (here[0] & 1)
    pair = lane >> whole_log(top_rows) & (group // 2 - 1)
    phases_of = []
    for h in range(2):
        y = (2 * pair + odd) * (2 * top_rows) + h * top_rows + (lane & (top_rows - 1))
        cosine, sine = cos_sin(ky * y & (size - 1), size)
        phases_of += [cosine, -sine]
    high, low = split(jnp.concatenate(phases_of, axis=0))
    return jnp.concatenate([high, low, high], axis=1)


def narrow_kernel(top, side, tiles, top_out, side_out):
    count = tiles.shape[0]
    parts = top_out.shape[3] // INNER
    step = count // parts
    top_rows, side_rows = top.shape[2], side.shape[2]
    totals = [None] * parts
    for k in range(count):
        columns = slice(k * INNER, (k + 1) * INNER)
        lines = jnp.concatenate(
            [
                top[:, :, :, columns].reshape(4 * top_rows, INNER),
                side[:, :, :, columns].reshape(4 * side_rows, INNER),
            ],
            axis=0,
        )
        high, low = split(lines)
        lines = jnp.concatenate([high, low, high], axis=1)
        for part in range(parts):
            tile = tiles[(k - part * step) % count]
            term = product(lines, jnp.concatenate([tile[0], tile[0], tile[1]], axis=0))
            totals[part] = term if k == 0 else totals[part] + term
    for part in range(parts):
        columns = slice(part * INNER, (part + 1) * INNER)
        top_out[:, :, :, columns] = totals[part][: 4 * top_rows].reshape(2, 2, top_rows, INNER)
        side_out[:, :, :, columns] = totals[part][4 * top_rows :].reshape(2, 2, side_rows, INNER)


def product(left, right, contracted=0):
    return lax.dot_general(
        left, right, (((1,), (contracted,)), ((), ())), preferred_element_type=f32
    )


def dot3_with(values, table):
    high, low = split(values)
    lines = jnp.concatenate([high, low, high], axis=1)
    return product(lines, jnp.concatenate([table[0], table[0], table[1]], axis=0))


def there_and_back(real, imag, kernel, table):
    rows, extent = real.shape
    sign = jnp.where(lax.broadcasted_iota(jnp.int32, (1, extent), 1) & 1 == 0, 1.0, -1.0)
    lines = jnp.concatenate(
        [jnp.concatenate([real, imag], axis=1), jnp.concatenate([imag, -real], axis=1)], axis=0
    )
    signs = jnp.concatenate([sign, sign], axis=1)
    waves = dot3_with(jnp.concatenate([lines, lines * signs], axis=0), table)
    totals = []
    for b in range(2):
        wave_real, wave_imag = (
            waves[(2 * b + k) * rows : (2 * b + k + 1) * rows] for k in range(2)
        )
        columns = slice(b * INNER, (b + 1) * INNER)
        weighted = ([], [])
        for c in range(2):
            kernel_real, kernel_imag = kernel[c, 0, :, columns], kernel[c, 1, :, columns]
            weighted[0].append(kernel_real * wave_real + kernel_imag * wave_imag)
            weighted[1].append(kernel_real * wave_imag - kernel_imag * wave_real)
        a, b = (jnp.concatenate(part, axis=0) for part in weighted)
        lines = jnp.concatenate(
            [jnp.concatenate([a, -b], axis=1), jnp.concatenate([b, a], axis=1)], axis=0
        )
        totals.append(dot3_with(lines, table))
    total = totals[0] + totals[1] * sign
    return total[: 2 * rows], total[2 * rows :]


def lines_kernel(counts, here, gathered, swapped, table, kernel, out, received):
    count_x, count_y, count_z = counts
    group = count_y * count_z
    top_rows = LANES // group
    half = LANES // 2
    kys = kernel.shape[2]
    y_table = y_table_of(counts, here, kys, INNER * TILE)
    for k, part in enumerate((gathered, swapped)):
        for member in range(part.shape[0]):
            g, place = divmod(member, group // 2)
            for j in range(top_rows // QUAD):
                row = (k * group // 2 + place) * top_rows + j * QUAD
                received[g, row : row + QUAD, :] = part[member, j]
    blocks = [received[g] for g in range(count_x)]
    high, low = split(jnp.concatenate(blocks, axis=1))
    mixed = product(y_table, jnp.concatenate([high, high, low], axis=0))
    low_half, high_half = mixed[: 2 * kys], mixed[2 * kys :]
    lane = lax.broadcasted_iota(jnp.int32, (2 * kys, LANES), 1)
    pieces = []
    for g in range(0, count_x, 2):
        a = slice(g * LANES, (g + 1) * LANES)
        b = slice((g + 1) * LANES, (g + 2) * LANES)
        pieces.append(
            jnp.where(
                lane < half,
                low_half[:, a] + pltpu.roll(high_half[:, a], half, 1),
                pltpu.roll(low_half[:, b], half, 1) + high_half[:, b],
            )
        )
    lines = jnp.concatenate(pieces, axis=1)
    for k, part in enumerate(there_and_back(lines[:kys], lines[kys:], kernel, table)):
        out[:, k * TILE : (k + 1) * TILE, :] = part.T.reshape(count_x * group, TILE, LANES)


def side_kernel_body(
    counts, here, gathered, swapped, spectrum, kernel, later_from, out, later, received, loading
):
    copies = begin(loading, [(later_from, later)])
    count_x, count_y, count_z = counts
    depth_block = (out.shape[1] - 2 * TILE) // 2
    last = gathered.shape[1] - 1
    kzs, length = kernel.shape[2], INNER * TILE
    size = kzs * count_y * count_z
    columns = count_x * count_z * QUAD
    kz = here[0] * kzs + lax.broadcasted_iota(jnp.int32, (kzs, columns), 0)
    column = lax.broadcasted_iota(jnp.int32, (kzs, columns), 1)
    pair = column >> whole_log(QUAD) & (count_z // 2 - 1)
    odd = (column >> whole_log(columns // 2)) ^ (here[0] & 1)
    z = (2 * pair + odd) * depth_block + (column & (QUAD - 1))
    z = z + (column >> whole_log(QUAD * count_z // 2) & (count_x - 1)) * QUAD
    cosine, sine = cos_sin(kz * z & (size - 1), size)
    table = jnp.concatenate([cosine, -sine], axis=0)
    for k, part in enumerate((gathered, swapped)):
        for x in range(count_x):
            for y in range(count_y):
                for pair in range(count_z // 2):
                    row = ((k * count_x + x) * count_z // 2 + pair) * QUAD
                    member = (x * count_y + y) * count_z // 2 + pair
                    received[y, row : row + QUAD, :] = part[member, last]
    blocks = [received[y] for y in range(count_y)]
    lines = dot3(table, split(jnp.concatenate(blocks, axis=1)))

    real, imag = there_and_back(lines[:kzs], lines[kzs:], kernel, spectrum)

    rows = depth_block * count_z
    z = lax.broadcasted_iota(jnp.int32, (rows, 2 * kzs), 0)
    column = lax.broadcasted_iota(jnp.int32, (rows, 2 * kzs), 1)
    cosine, sine = cos_sin((here[0] * kzs + (column & (kzs - 1))) * z & (size - 1), size)
    table = jnp.where(column < kzs, cosine, -sine) * (1.0 / (size * length))
    for c in range(2):
        part = slice(c * kzs, (c + 1) * kzs)
        image = dot3(table, split(jnp.concatenate([real[part], imag[part]], axis=0)))
        for y in range(count_y):
            for z in range(count_z):
                start = 2 * TILE + c * depth_block
                out[y * count_z + z, start : start + depth_block, :] = image[
                    z * depth_block : (z + 1) * depth_block, y * LANES : (y + 1) * LANES
                ]
    out[:, 0 : 2 * TILE, :] = jnp.zeros((out.shape[0], 2 * TILE, LANES), f32)
    copies[0].wait()


def rows_kernel(counts, arrived, side, table, out, result, sending):
    del side
    count_y, count_z = counts[1:]
    per_turn = INNER * 2 // LANES
    step = arrived.shape[0] // per_turn
    size = step * INNER
    half = LANES // 2
    lane = lax.broadcasted_iota(jnp.int32, (2 * TILE, LANES), 1)
    upper, lower = [], []
    for b in range(step):
        parts = ([], [])
        for pair in range(b * per_turn, (b + 1) * per_turn, 2):
            first, second = arrived[pair], arrived[pair + 1]
            spectra = (
                jnp.where(lane < half, first, pltpu.roll(second, half, 1)),
                jnp.where(lane < half, pltpu.roll(first, half, 1), second),
            )
            for k in range(2):
                parts[k].append(
                    jnp.concatenate(
                        [spectrum[k * TILE : (k + 1) * TILE] for spectrum in spectra], axis=0
                    )
                )
        real, imag = (jnp.concatenate(part, axis=1) for part in parts)
        upper.append(jnp.concatenate([real, -imag], axis=1))
        lower.append(jnp.concatenate([imag, real], axis=1))
    lines = dot3_with(jnp.concatenate(upper + lower, axis=0), table)
    y = lax.broadcasted_iota(jnp.int32, (1, INNER), 1) & (step - 1)
    total = None
    for b in range(step):
        cosine, sine = cos_sin(y * b & (step - 1), step)
        real, imag = (
            lines[(k * step + b) * 2 * TILE : (k * step + b + 1) * 2 * TILE] for k in range(2)
        )
        term = real * cosine - imag * sine if b else real
        total = term if b == 0 else total + term
    total = total * (1.0 / (size * size))
    for y in range(count_y):
        result[y] = total[:, y * LANES : (y + 1) * LANES]
    sends = begin(
        sending,
        [
            (result.at[y], out.at[y * count_z + z, 0 : 2 * TILE, :])
            for y in range(count_y)
            for z in range(count_z)
        ],
    )
    for copy in sends:
        copy.wait()


def sum_kernel(exchange_grad, arrived, out, result, sending):
    depth = exchange_grad.shape[1]
    group = arrived.shape[0]
    sends = []

    def send(c):
        sends.append(pltpu.make_async_copy(result.at[c], out.at[c], sending.at[c]))
        sends[-1].start()

    def top(c):
        return arrived[:, c * TILE : (c + 1) * TILE, :].reshape(group * TILE, LANES)

    def side(c):
        rows = slice(2 * TILE + c * depth, 2 * TILE + (c + 1) * depth)
        total = arrived[0, rows, :]
        for p in range(1, group):
            total = total + arrived[p, rows, :]
        return total

    image = top(0)
    for z in range(depth):
        result[0, z] = exchange_grad[0, z] + image
    send(0)
    column = side(1)
    for z in range(depth):
        result[2, z] = exchange_grad[2, z] + column[z : z + 1]
    send(2)
    image, column = top(1), side(0)
    for z in range(depth):
        result[1, z] = exchange_grad[1, z] + image + column[z : z + 1]
    send(1)
    for copy in sends:
        copy.wait()


def residual_blocks(residual_top, residual_side, copies, share, quads):
    block_x, block_y = residual_top.shape
    top_rows = block_y // 2

    def body(at_x, top, side, out):
        piece = jnp.concatenate([top[0:top_rows, :], top[top_rows:, :]], axis=1)
        part = side[pl.ds(at_x[0] * share, share), :]
        if not quads:
            part = jnp.concatenate([part, jnp.zeros((TILE - share, LANES), f32)], axis=0)
        for copy in range(copies):
            if quads:
                for j in range(top_rows // QUAD):
                    out[copy, j] = piece[j * QUAD : (j + 1) * QUAD]
                out[copy, top_rows // QUAD] = part
            else:
                out[copy, 0:top_rows, :] = piece
                out[copy, top_rows:, :] = part

    shape = (top_rows // QUAD + 1, QUAD) if quads else (top_rows + TILE,)
    return call(
        body,
        "pack",
        (copies, *shape, LANES),
        60,
        0.8,
        (lax.axis_index("gx").reshape(1), residual_top.T, residual_side.T),
    )


def fast_on_device(magnetization, stiffness, residual_top, residual_side, top_kernel, side_kernel):
    counts = tuple(lax.axis_size(axis) for axis in ALL)
    count_x, count_y, count_z = counts
    group = count_y * count_z
    devices = count_x * group
    block_x, block_y = residual_top.shape
    depth_block = stiffness.shape[0]
    top_rows = block_y // 2
    kys, size = top_kernel.shape[2:]
    kzs = side_kernel.shape[2]
    extent = count_x * block_x
    here = [lax.axis_index(axis) for axis in ALL]
    plane_index = here[1] * count_z + here[2]
    index = (here[0] * group + plane_index).reshape(1)
    plane_index = plane_index.reshape(1)
    tiles, table = (jnp.asarray(values) for values in narrow_tables(extent, size))
    rows_table = jnp.asarray(transform_table(size))

    parities = [range(parity, devices, 2) for parity in range(2)]
    sent = residual_blocks(
        residual_top, residual_side, devices // 2, depth_block // count_x, True
    )
    gathered = lax.all_to_all(
        sent, ALL, 0, 0, tiled=True, axis_index_groups=[list(each) for each in parities]
    )
    z_first, z_last, x_first, x_last, y_faces = faces_of(magnetization, stiffness)
    narrowed = call(
        narrow_kernel,
        "narrow",
        [(2, 2, kys, 2 * extent), (2, 2, kzs, 2 * extent)],
        16,
        2.5,
        (top_kernel, side_kernel, tiles),
    )
    gathered, x_first, x_last, y_faces, narrowed = lax.optimization_barrier(
        (gathered, x_first, x_last, y_faces, narrowed)
    )
    top_spectra, side_spectra = narrowed
    swapped = lax.ppermute(gathered, "gz", [(i, i ^ 1) for i in range(count_z)])
    zy = halos_zy(z_first, z_last, y_faces)

    lines = call(
        functools.partial(lines_kernel, counts),
        "lines",
        (devices, 2 * TILE, LANES),
        16,
        2.2,
        (index, gathered, swapped, table, top_spectra),
        scratch=[pltpu.VMEM((count_x, LANES, LANES), f32)],
    )
    arrived = lax.all_to_all(lines, ALL, 0, 0, tiled=True)
    lines, x_first, x_last = lax.optimization_barrier((lines, x_first, x_last))
    x = halos_x(x_first, x_last)
    side, rows_table = call(
        functools.partial(side_kernel_body, counts),
        "side",
        [(group, 2 * TILE + 2 * depth_block, LANES), rows_table.shape],
        8,
        2.0,
        (plane_index, gathered, swapped, table, side_spectra, from_hbm(rows_table)),
        in_hbm=(0,),
        in_vmem=(1,),
        refs=(5,),
        scratch=[
            pltpu.VMEM((count_y, count_x * count_z * QUAD, LANES), f32),
            pltpu.SemaphoreType.DMA((1,)),
        ],
    )
    arrived, side, rows_table = lax.optimization_barrier((arrived, side, rows_table))
    rows = call(
        functools.partial(rows_kernel, counts),
        "rows",
        (group, 2 * TILE + 2 * depth_block, LANES),
        8,
        1.4,
        (arrived, from_hbm(side), rows_table),
        in_hbm=(0,),
        refs=(1,),
        scratch=[
            pltpu.VMEM((count_y, 2 * TILE, LANES), f32),
            pltpu.SemaphoreType.DMA((group,)),
        ],
        out_refs=(0,),
        aliases={1: 0},
    )
    _, zy, x = lax.optimization_barrier((rows, zy, x))
    arrived = lax.all_to_all(rows, ("gy", "gz"), 0, 0, tiled=True)
    exchange_grad = exchange_of(counts, index, magnetization, stiffness, zy, x)
    return call(
        sum_kernel,
        "gradient",
        magnetization.shape,
        16,
        1.2,
        (exchange_grad, arrived),
        out_refs=(0,),
        scratch=[pltpu.VMEM(magnetization.shape, f32), pltpu.SemaphoreType.DMA((3,))],
    )


def fits(counts, stiffness, residual_top, residual_side, top_kernel, side_kernel):
    count_x, count_y, count_z = counts
    block_x, block_y = residual_top.shape
    group = count_y * count_z
    return (
        2 * block_x == LANES
        and 2 * top_kernel.shape[2] == LANES
        and stiffness.shape[2] == LANES
        and block_x == group * TILE
        and block_y * group == count_x * block_x == INNER
        and count_y * LANES == INNER
        and block_y % 16 == 0
        and count_x % 2 == 0
        and count_z % 2 == 0
        and (count_x * group) % (2 * top_kernel.shape[3] // INNER) == 0
        and INNER == top_kernel.shape[2] * count_z
        and top_kernel.shape[3] == TILE * INNER == side_kernel.shape[3]
        and INNER == 2 * LANES
        and stiffness.shape[0] % 16 == 0
        and stiffness.shape[0] == count_x * QUAD
        and side_kernel.shape[2] % 16 == 0
        and all(
            count & (count - 1) == 0
            for count in (group, count_x, count_z, top_kernel.shape[3], side_kernel.shape[2])
        )
    )


def on_device(magnetization, stiffness, residual_top, residual_side, top_kernel, side_kernel):
    counts = tuple(lax.axis_size(axis) for axis in ALL)
    count_x, count_y, count_z = counts
    if fits(counts, stiffness, residual_top, residual_side, top_kernel, side_kernel):
        return fast_on_device(
            magnetization, stiffness, residual_top, residual_side, top_kernel, side_kernel
        )
    devices = count_x * count_y * count_z
    depth_block = stiffness.shape[0]
    block_x, block_y = residual_top.shape
    top_rows = block_y // 2
    share = depth_block // count_x

    sent = residual_blocks(residual_top, residual_side, devices, share, False)
    rows = sent.shape[1]
    gathered = lax.all_to_all(sent, ALL, 0, 0, tiled=True)
    index = (
        (lax.axis_index("gx") * count_y + lax.axis_index("gy")) * count_z + lax.axis_index("gz")
    ).reshape(1)
    z_first, z_last, x_first, x_last, y_faces = faces_of(magnetization, stiffness)
    exchange_grad = exchange_of(
        counts,
        index,
        magnetization,
        stiffness,
        halos_zy(z_first, z_last, y_faces),
        halos_x(x_first, x_last),
    )

    parts = image_parts(
        gathered, top_kernel, side_kernel, counts, block_x, top_rows, depth_block
    )
    rows = parts.shape[1]
    arrived = lax.all_to_all(parts.reshape(devices * rows, LANES), ALL, 0, 0, tiled=True)
    arrived = arrived.reshape(devices, rows, LANES)
    top_sum = jnp.sum(arrived[:, : rows - TILE], axis=0)
    side_sum = jnp.sum(
        arrived[:, rows - TILE :].reshape(count_x, count_y * count_z, TILE, LANES), axis=1
    )
    side = side_sum[:, : 2 * share].reshape(count_x, 2, share, LANES)
    side = jnp.swapaxes(side, 0, 1).reshape(2, depth_block, 1, LANES)
    top = lax.all_gather(top_sum, "gz", axis=0)
    top = jnp.swapaxes(top.reshape(count_z, 2, block_x // count_z, LANES), 0, 1)
    top = top.reshape(2, 1, block_x, LANES)
    return jnp.stack(
        [
            exchange_grad[0] + top[0],
            exchange_grad[1] + top[1] + side[0],
            exchange_grad[2] + side[1],
        ]
    )


def solution(mesh):
    placed = (
        P(None, "gz", "gx", "gy"),
        P("gz", "gx", "gy"),
        P("gx", ("gy", "gz")),
        P("gy", "gz"),
        P(None, None, ("gx", "gy", "gz"), None),
        P(None, None, ("gy", "gz"), None),
    )
    return jax.shard_map(
        on_device, mesh=mesh, in_specs=placed, out_specs=P(None, "gz", "gx", "gy"), check_vma=False
    )
```

```python
import functools
import math

import jax
import jax.numpy as jnp
import ml_dtypes
import numpy as np
from jax import lax
from jax.experimental import pallas as pl
from jax.experimental.pallas import tpu as pltpu
from jax.sharding import PartitionSpec as P

LANES = 128
TILE = 8
INNER = 256
ALL = ("gx", "gy", "gz")
f32 = jnp.float32
bf16 = jnp.bfloat16
MIB = 1024 * 1024
QUAD = 4
SMEM = pl.BlockSpec(memory_space=pltpu.SMEM)
VMEM = pl.BlockSpec(memory_space=pltpu.VMEM)
HBM = pl.BlockSpec(memory_space=pltpu.HBM)


def whole_log(count):
    return count.bit_length() - 1


def split(values):
    high = values.astype(bf16)
    return high, (values - high.astype(f32)).astype(bf16)


def dot3(left, right):
    high, low = split(left)
    def one(a, b):
        return lax.dot_general(a, b, (((1,), (0,)), ((), ())), preferred_element_type=f32)
    return one(high, right[0]) + one(low, right[0]) + one(high, right[1])


def from_hbm(values):
    return pltpu.with_memory_space_constraint(values, pltpu.HBM)


def call(
    body,
    name,
    shape,
    limit,
    microseconds,
    operands,
    in_hbm=(),
    in_vmem=(),
    scratch=(),
    refs=(),
    out_refs=(),
    aliases=(),
):
    shapes = shape if isinstance(shape, list) else [shape]
    moved = sum(4 * math.prod(each) for each in shapes)
    moved += sum(x.size * x.dtype.itemsize for x in operands)
    results = pl.pallas_call(
        body,
        out_shape=[
            pltpu.HBM(each, f32)
            if i in in_hbm
            else pltpu.VMEM(each, bf16)
            if i in in_vmem
            else jax.ShapeDtypeStruct(each, f32)
            for i, each in enumerate(shapes)
        ],
        in_specs=[
            SMEM if x.shape == (1,) else HBM if i in refs else VMEM
            for i, x in enumerate(operands)
        ],
        out_specs=[HBM if i in out_refs else VMEM for i in range(len(shapes))],
        input_output_aliases=dict(aliases),
        scratch_shapes=list(scratch),
        compiler_params=pltpu.CompilerParams(vmem_limit_bytes=limit * MIB),
        cost_estimate=pl.CostEstimate(
            flops=int(microseconds * 1e9), bytes_accessed=moved, transcendentals=0
        ),
        name=name,
    )(*operands)
    return results if isinstance(shape, list) else results[0]


def transform_tables(extent, size):
    x = np.arange(extent)
    angle = (np.outer(x, np.arange(INNER)) % size) * (2.0 * math.pi / size)
    forward = np.concatenate([np.cos(angle), np.sin(angle)], 0).astype(np.float32)
    backward = np.concatenate([np.cos(angle).T, np.sin(angle).T], 0).astype(np.float32)

    def parts(table):
        high = table.astype(ml_dtypes.bfloat16)
        return high, (table - high.astype(np.float32)).astype(ml_dtypes.bfloat16)

    outer = size // INNER
    turn = (np.outer(np.arange(outer), x) % outer) * (2.0 * math.pi / outer)
    turns = np.stack([np.cos(turn), np.sin(turn)]).astype(np.float32)
    return parts(forward), parts(backward), turns


def phases(first, second, size):
    angle = (first * second % size).astype(f32) * (2.0 * math.pi / size)
    return jnp.cos(angle), jnp.sin(angle)


def image_kernel(
    counts, gathered, y_table, z_table, fh, fl, bh, bl, turns, top, side, y_back, z_back, out
):
    count_x, count_y, count_z, top_rows = counts
    group = count_y * count_z
    half = LANES // 2
    kys = top.shape[2]
    kzs = side.shape[2]
    forward = (fh[...], fl[...])
    backward = (bh[...], bl[...])

    blocks = [
        gathered[g * group : (g + 1) * group, 0:top_rows, :].reshape(group * top_rows, LANES)
        for g in range(count_x)
    ]
    mixed = dot3(y_table[...], split(jnp.concatenate(blocks, axis=1)))
    low_half, high_half = mixed[: 2 * kys], mixed[2 * kys :]
    lane = lax.broadcasted_iota(jnp.int32, (2 * kys, LANES), 1)
    pieces = []
    for g in range(0, count_x, 2):
        a = slice(g * LANES, (g + 1) * LANES)
        b = slice((g + 1) * LANES, (g + 2) * LANES)
        pieces.append(
            jnp.where(
                lane < half,
                low_half[:, a] + pltpu.roll(high_half[:, a], half, 1),
                pltpu.roll(low_half[:, b], half, 1) + high_half[:, b],
            )
        )
    top_lines = jnp.concatenate(pieces, axis=1)

    side_blocks = []
    for y in range(count_y):
        rows = [
            gathered[(x * count_y + y) * count_z + z, top_rows : top_rows + TILE, :]
            for x in range(count_x)
            for z in range(count_z)
        ]
        side_blocks.append(jnp.concatenate(rows, axis=0))
    side_lines = dot3(z_table[...], split(jnp.concatenate(side_blocks, axis=1)))

    real = jnp.concatenate([top_lines[:kys], side_lines[:kzs]], axis=0)
    imag = jnp.concatenate([top_lines[kys:], side_lines[kzs:]], axis=0)
    rows = kys + kzs
    total_real = total_imag = None
    for b in range(turns.shape[1]):
        cosine, sine = turns[0, b : b + 1, :], turns[1, b : b + 1, :]
        turned_real = real * cosine + imag * sine
        turned_imag = imag * cosine - real * sine
        waves = dot3(
            jnp.concatenate(
                [
                    jnp.concatenate([turned_real, turned_imag], axis=1),
                    jnp.concatenate([turned_imag, -turned_real], axis=1),
                ],
                axis=0,
            ),
            forward,
        )
        wave_real, wave_imag = waves[:rows], waves[rows:]
        columns = slice(b * INNER, (b + 1) * INNER)
        weighted_real, weighted_imag = [], []
        for c in range(2):
            for kernel, part in ((top, slice(0, kys)), (side, slice(kys, rows))):
                kernel_real, kernel_imag = kernel[c, 0, :, columns], kernel[c, 1, :, columns]
                weighted_real.append(
                    kernel_real * wave_real[part] + kernel_imag * wave_imag[part]
                )
                weighted_imag.append(
                    kernel_real * wave_imag[part] - kernel_imag * wave_real[part]
                )
        weighted_real = jnp.concatenate(weighted_real, axis=0)
        weighted_imag = jnp.concatenate(weighted_imag, axis=0)
        back = dot3(
            jnp.concatenate(
                [
                    jnp.concatenate([weighted_real, -weighted_imag], axis=1),
                    jnp.concatenate([weighted_imag, weighted_real], axis=1),
                ],
                axis=0,
            ),
            backward,
        )
        back_real, back_imag = back[: 2 * rows], back[2 * rows :]
        if b == 0:
            total_real, total_imag = back_real, back_imag
        else:
            total_real = total_real + (back_real * cosine - back_imag * sine)
            total_imag = total_imag + (back_real * sine + back_imag * cosine)

    y_parts = split(y_back[...])
    depth_rows = []
    quarter = (out.shape[1] - TILE) // 2
    block_x = quarter * count_z
    for c in range(2):
        start = c * rows
        lines = jnp.concatenate(
            [total_real[start : start + kys], total_imag[start : start + kys]], axis=0
        )
        image = dot3(lines.T, y_parts)
        for x in range(count_x):
            for y in range(count_y):
                for z in range(count_z):
                    first = x * block_x + z * quarter
                    out[
                        (x * count_y + y) * count_z + z, c * quarter : (c + 1) * quarter, :
                    ] = image[first : first + quarter, y * LANES : (y + 1) * LANES]
        depth_rows.append(total_real[start + kys : start + rows])
        depth_rows.append(total_imag[start + kys : start + rows])
    side_image = dot3(z_back[...], split(jnp.concatenate(depth_rows, axis=0)))
    for y in range(count_y):
        for z in range(count_z):
            block = side_image[z * TILE : (z + 1) * TILE, y * LANES : (y + 1) * LANES]
            for x in range(count_x):
                out[(x * count_y + y) * count_z + z, 2 * quarter :, :] = block


def image_parts(gathered, top_kernel, side_kernel, counts, block_x, top_rows, depth_block):
    count_x, count_y, count_z = counts
    group = count_y * count_z
    here = [lax.axis_index(axis) for axis in ALL]
    kys, size = top_kernel.shape[2:]
    kzs = side_kernel.shape[2]
    depth_size = kzs * group
    extent = count_y * LANES
    share = depth_block // count_x
    block_y = top_rows * 2

    ky = ((here[0] * count_y + here[1]) * count_z + here[2]) * kys + lax.iota(jnp.int32, kys)
    kz = (here[1] * count_z + here[2]) * kzs + lax.iota(jnp.int32, kzs)

    row = lax.iota(jnp.int32, group * top_rows)
    y_tables = []
    for h in range(2):
        y = row // top_rows * block_y + h * top_rows + row % top_rows
        cosine, sine = phases(ky[:, None], y[None, :], size)
        y_tables += [cosine, -sine]
    y_table = jnp.concatenate(y_tables, axis=0)

    row = lax.iota(jnp.int32, count_x * count_z * TILE)
    inside = row % TILE
    z = row // TILE % count_z * depth_block + row // (TILE * count_z) * share + inside
    cosine, sine = phases(kz[:, None], z[None, :], depth_size)
    z_table = jnp.where((inside < share)[None, :], jnp.concatenate([cosine, -sine], axis=0), 0.0)

    cosine, sine = phases(ky[:, None], lax.iota(jnp.int32, extent)[None, :], size)
    y_back = jnp.concatenate([cosine, -sine], axis=0) * (1.0 / (size * size))

    row = lax.iota(jnp.int32, count_z * TILE)
    z = row // TILE * depth_block + here[0] * share + row % TILE % share
    cosine, sine = phases(z[:, None], kz[None, :], depth_size)
    both = jnp.concatenate([cosine, -sine], axis=1) * (1.0 / (size * depth_size))
    component = (row % TILE // share)[:, None]
    z_back = jnp.concatenate(
        [jnp.where(component == 0, both, 0.0), jnp.where(component == 1, both, 0.0)], axis=1
    )

    forward, backward, turns = transform_tables(extent, size)
    out_rows = 2 * (block_x // count_z) + TILE
    return pl.pallas_call(
        functools.partial(image_kernel, counts + (top_rows,)),
        out_shape=jax.ShapeDtypeStruct((count_x * group, out_rows, LANES), f32),
        compiler_params=pltpu.CompilerParams(vmem_limit_bytes=56 * 1024 * 1024),
        name="images",
    )(
        gathered,
        y_table,
        z_table,
        *(jnp.asarray(t) for t in forward + backward),
        jnp.asarray(turns),
        top_kernel,
        side_kernel,
        y_back,
        z_back,
    )


def begin(semaphores, pairs):
    started = [
        pltpu.make_async_copy(source, target, semaphores.at[i])
        for i, (source, target) in enumerate(pairs)
    ]
    for copy in started:
        copy.start()
    return started


def faces_kernel(
    magnetization, stiffness, z_first, z_last, x_first, x_last, y_faces, m, s, loading
):
    depth, across = stiffness.shape[:2]
    loads = begin(
        loading, [(stiffness, s)] + [(magnetization.at[c], m.at[c]) for c in range(3)]
    )
    lane = lax.broadcasted_iota(jnp.int32, (across, LANES), 1)
    pair = (lane + 1 & (LANES - 1)) >> 1
    sides = jnp.zeros((across, LANES), f32)
    for field in (3, 0, 1, 2):
        loads[(field + 1) % 4].wait()
        ref = s if field == 3 else m.at[field]
        z_first[field] = ref[0]
        z_last[field] = ref[depth - 1]
        x_first[field] = ref[:, 0, :]
        x_last[field] = ref[:, across - 1, :]
        for z in range(depth):
            column = field * depth + z
            turned = pltpu.roll(ref[z], 2 * column, 1) if column else ref[z]
            sides = jnp.where(pair == column, turned, sides)
    y_faces[...] = sides


def twice_weight(a, b):
    total = a + b
    inverse = pl.reciprocal(total, approx=True)
    return 4.0 * a * b * (inverse * (2.0 - total * inverse))


def exchange_kernel(
    counts,
    here,
    magnetization_from,
    stiffness_from,
    y_faces_from,
    z_next,
    z_before,
    x_next,
    x_before,
    y_next,
    y_before,
    out,
    m,
    s,
    y_faces,
    loading,
):
    depth, across = s.shape[:2]
    chunk = depth // 4
    pairs = [(y_faces_from, y_faces)]
    for k in range(4):
        layers = pl.ds(k * chunk, chunk)
        pairs.append((stiffness_from.at[layers], s.at[layers]))
        pairs.append((magnetization_from.at[:, layers], m.at[:, layers]))
    loads = begin(loading, pairs)

    count_x, count_y, count_z = counts
    at_z = here[0] % count_z
    at_y = here[0] // count_z % count_y
    at_x = here[0] // (count_z * count_y)

    def inside(condition, values):
        return jnp.where(condition, values, 0.0)

    lane = lax.broadcasted_iota(jnp.int32, (across, LANES), 1)
    row = lax.broadcasted_iota(jnp.int32, (across, LANES), 0)
    first_lane, last_lane, last_row = lane == 0, lane == LANES - 1, row == across - 1

    loads[0].wait()
    own = y_faces[...]
    even = (lane & 1) == 0
    field = (lane + 1 & (LANES - 1)) >> whole_log(2 * depth)
    halo = jnp.where(
        even, pltpu.roll(y_before[...], 1, 1), pltpu.roll(y_next[...], LANES - 1, 1)
    )
    present = jnp.where(even, at_y, count_y - 1 - at_y) > 0
    weight = twice_weight(
        jnp.where(field == 3, own, 1.0),
        jnp.where(field == 3, jnp.where(present, halo, 0.0), 1.0),
    )
    spread = pltpu.roll(weight, LANES - 6 * depth, 1)
    for c in (1, 2):
        spread = jnp.where(
            field == c, pltpu.roll(weight, LANES - (3 - c) * 2 * depth, 1), spread
        )
    sides = spread * (own - halo)
    outer = first_lane | last_lane

    for copy in loads[1:3]:
        copy.wait()
    below_weight = twice_weight(inside(at_z > 0, z_before[3]), s[0])
    below = [below_weight * (z_before[c] - m[c, 0]) for c in range(3)]
    for z in range(depth):
        if z % chunk == chunk - 1:
            k = 1 + 2 * (z // chunk + 1)
            for copy in loads[k : k + 2]:
                copy.wait()
        centre = s[z]
        above = s[z + 1] if z + 1 < depth else inside(at_z < count_z - 1, z_next[3])
        weight_z = twice_weight(centre, above)
        weight_x = jnp.where(
            last_row, 0.0, twice_weight(centre, pltpu.roll(centre, across - 1, 0))
        )
        weight_y = jnp.where(
            last_lane, 0.0, twice_weight(centre, pltpu.roll(centre, LANES - 1, 1))
        )
        for c in range(3):
            column = c * depth + z
            values = m[c, z]
            upper = m[c, z + 1] if z + 1 < depth else z_next[c]
            up = weight_z * (values - upper)
            flux_x = weight_x * (values - pltpu.roll(values, across - 1, 0))
            flux_y = weight_y * (values - pltpu.roll(values, LANES - 1, 1))
            total = (up - below[c]) + (flux_x - pltpu.roll(flux_x, 1, 0))
            total = total + (flux_y - pltpu.roll(flux_y, 1, 1))
            both = pltpu.roll(sides, LANES - 2 * column, 1) if column else sides
            out[c, z] = jnp.where(outer, total + both, total)
            below[c] = up
    for edge_row, halo, present in (
        (across - 1, x_next, at_x < count_x - 1),
        (0, x_before, at_x > 0),
    ):
        weight = twice_weight(s[:, edge_row, :], inside(present, halo[3]))
        for c in range(3):
            out[c, :, edge_row, :] += weight * (m[c, :, edge_row, :] - halo[c])


def ring(block, axis, distance):
    count = lax.axis_size(axis)
    return lax.ppermute(block, axis, [(i, (i + distance) % count) for i in range(count)])


def faces_of(magnetization, stiffness):
    depth, across, along = stiffness.shape
    return call(
        faces_kernel,
        "faces",
        [
            (4, across, along),
            (4, across, along),
            (4, depth, along),
            (4, depth, along),
            (across, LANES),
        ],
        8,
        2.0,
        (from_hbm(magnetization), from_hbm(stiffness)),
        in_hbm=(4,),
        refs=(0, 1),
        scratch=[
            pltpu.VMEM(magnetization.shape, f32),
            pltpu.VMEM(stiffness.shape, f32),
            pltpu.SemaphoreType.DMA((4,)),
        ],
    )


def halos_zy(z_first, z_last, y_faces):
    y_next = ring(y_faces, "gy", -1)
    y_before = y_next if lax.axis_size("gy") == 2 else ring(y_faces, "gy", 1)
    return ring(z_first, "gz", -1), ring(z_last, "gz", 1), y_next, y_before, y_faces


def halos_x(x_first, x_last):
    return ring(x_first, "gx", -1), ring(x_last, "gx", 1)


def exchange_of(counts, index, magnetization, stiffness, zy, x):
    z_next, z_before, y_next, y_before, y_faces = zy
    fetched = (magnetization, stiffness, y_faces)
    return call(
        functools.partial(exchange_kernel, counts),
        "exchange",
        magnetization.shape,
        8,
        5.0,
        (
            index,
            *(from_hbm(array) for array in fetched),
            z_next,
            z_before,
            *x,
            y_next,
            y_before,
        ),
        refs=(1, 2, 3),
        scratch=[pltpu.VMEM(array.shape, f32) for array in fetched]
        + [pltpu.SemaphoreType.DMA((9,))],
    )


def cos_sin(steps, size):
    quarter = steps >> whole_log(size // 4)
    angle = ((steps & (size // 4 - 1)) - size // 8).astype(f32) * (2.0 * math.pi / size)
    square = angle * angle
    sine = cosine = 0.0
    for k in range(5, -1, -1):
        sine = sine * square + (-1) ** k / math.factorial(2 * k + 1)
        cosine = cosine * square + (-1) ** k / math.factorial(2 * k)
    sine = sine * angle
    first, second = (cosine - sine) * math.sqrt(0.5), (cosine + sine) * math.sqrt(0.5)
    odd = (quarter & 1) == 1
    real = jnp.where(odd, -second, first)
    imag = jnp.where(odd, first, second)
    back = quarter >= 2
    return jnp.where(back, -real, real), jnp.where(back, -imag, imag)


def halves_of(table):
    table = table.astype(np.float32)
    high = table.astype(ml_dtypes.bfloat16)
    return high, (table - high.astype(np.float32)).astype(ml_dtypes.bfloat16)


def narrow_tables(extent, size):
    length = 2 * extent
    ratio = size // length
    m = np.arange(size)
    lags = np.arange(1, extent)
    window = 1.0 + 2.0 * np.cos(np.outer(m, lags) % size * (2.0 * math.pi / size)).sum(axis=1)
    i = np.arange(INNER)
    place = np.arange(0, size, INNER)[:, None, None] + i[:, None] - ratio * i[None, :]
    high, low = halves_of(window[place % size] / length)
    tiles = np.stack([high, low], axis=1)
    return tiles, transform_table(length)


def transform_table(size):
    i = np.arange(INNER)
    angle = np.outer(i, i) * (2.0 * math.pi / size)
    return np.stack(halves_of(np.concatenate([np.cos(angle), np.sin(angle)], axis=0)))


def y_table_of(counts, here, kys, size):
    group = counts[1] * counts[2]
    top_rows = LANES // group
    ky = here[0] * kys + lax.broadcasted_iota(jnp.int32, (kys, LANES), 0)
    lane = lax.broadcasted_iota(jnp.int32, (kys, LANES), 1)
    odd = (lane >> whole_log(LANES // 2)) ^ (here[0] & 1)
    pair = lane >> whole_log(top_rows) & (group // 2 - 1)
    phases_of = []
    for h in range(2):
        y = (2 * pair + odd) * (2 * top_rows) + h * top_rows + (lane & (top_rows - 1))
        cosine, sine = cos_sin(ky * y & (size - 1), size)
        phases_of += [cosine, -sine]
    high, low = split(jnp.concatenate(phases_of, axis=0))
    return jnp.concatenate([high, low, high], axis=1)


def narrow_kernel(top, side, tiles, top_out, side_out):
    count = tiles.shape[0]
    parts = top_out.shape[3] // INNER
    step = count // parts
    top_rows, side_rows = top.shape[2], side.shape[2]
    totals = [None] * parts
    for k in range(count):
        columns = slice(k * INNER, (k + 1) * INNER)
        lines = jnp.concatenate(
            [
                top[:, :, :, columns].reshape(4 * top_rows, INNER),
                side[:, :, :, columns].reshape(4 * side_rows, INNER),
            ],
            axis=0,
        )
        high, low = split(lines)
        lines = jnp.concatenate([high, low, high], axis=1)
        for part in range(parts):
            tile = tiles[(k - part * step) % count]
            term = product(lines, jnp.concatenate([tile[0], tile[0], tile[1]], axis=0))
            totals[part] = term if k == 0 else totals[part] + term
    for part in range(parts):
        columns = slice(part * INNER, (part + 1) * INNER)
        top_out[:, :, :, columns] = totals[part][: 4 * top_rows].reshape(2, 2, top_rows, INNER)
        side_out[:, :, :, columns] = totals[part][4 * top_rows :].reshape(2, 2, side_rows, INNER)


def product(left, right, contracted=0):
    return lax.dot_general(
        left, right, (((1,), (contracted,)), ((), ())), preferred_element_type=f32
    )


def dot3_with(values, table):
    high, low = split(values)
    lines = jnp.concatenate([high, low, high], axis=1)
    return product(lines, jnp.concatenate([table[0], table[0], table[1]], axis=0))


def there_and_back(real, imag, kernel, table):
    rows, extent = real.shape
    sign = jnp.where(lax.broadcasted_iota(jnp.int32, (1, extent), 1) & 1 == 0, 1.0, -1.0)
    lines = jnp.concatenate(
        [jnp.concatenate([real, imag], axis=1), jnp.concatenate([imag, -real], axis=1)], axis=0
    )
    signs = jnp.concatenate([sign, sign], axis=1)
    waves = dot3_with(jnp.concatenate([lines, lines * signs], axis=0), table)
    totals = []
    for b in range(2):
        wave_real, wave_imag = (
            waves[(2 * b + k) * rows : (2 * b + k + 1) * rows] for k in range(2)
        )
        columns = slice(b * INNER, (b + 1) * INNER)
        weighted = ([], [])
        for c in range(2):
            kernel_real, kernel_imag = kernel[c, 0, :, columns], kernel[c, 1, :, columns]
            weighted[0].append(kernel_real * wave_real + kernel_imag * wave_imag)
            weighted[1].append(kernel_real * wave_imag - kernel_imag * wave_real)
        a, b = (jnp.concatenate(part, axis=0) for part in weighted)
        lines = jnp.concatenate(
            [jnp.concatenate([a, -b], axis=1), jnp.concatenate([b, a], axis=1)], axis=0
        )
        totals.append(dot3_with(lines, table))
    total = totals[0] + totals[1] * sign
    return total[: 2 * rows], total[2 * rows :]


def lines_kernel(counts, here, gathered, swapped, table, kernel, out, received):
    count_x, count_y, count_z = counts
    group = count_y * count_z
    top_rows = LANES // group
    half = LANES // 2
    kys = kernel.shape[2]
    y_table = y_table_of(counts, here, kys, INNER * TILE)
    for k, part in enumerate((gathered, swapped)):
        for member in range(part.shape[0]):
            g, place = divmod(member, group // 2)
            for j in range(top_rows // QUAD):
                row = (k * group // 2 + place) * top_rows + j * QUAD
                received[g, row : row + QUAD, :] = part[member, j]
    blocks = [received[g] for g in range(count_x)]
    high, low = split(jnp.concatenate(blocks, axis=1))
    mixed = product(y_table, jnp.concatenate([high, high, low], axis=0))
    low_half, high_half = mixed[: 2 * kys], mixed[2 * kys :]
    lane = lax.broadcasted_iota(jnp.int32, (2 * kys, LANES), 1)
    pieces = []
    for g in range(0, count_x, 2):
        a = slice(g * LANES, (g + 1) * LANES)
        b = slice((g + 1) * LANES, (g + 2) * LANES)
        pieces.append(
            jnp.where(
                lane < half,
                low_half[:, a] + pltpu.roll(high_half[:, a], half, 1),
                pltpu.roll(low_half[:, b], half, 1) + high_half[:, b],
            )
        )
    lines = jnp.concatenate(pieces, axis=1)
    for k, part in enumerate(there_and_back(lines[:kys], lines[kys:], kernel, table)):
        out[:, k * TILE : (k + 1) * TILE, :] = part.T.reshape(count_x * group, TILE, LANES)


def side_kernel_body(
    counts,
    here,
    gathered,
    swapped,
    spectrum,
    kernel,
    later_from,
    mine,
    other,
    later,
    received,
    loading,
):
    copies = begin(loading, [(later_from, later)])
    count_x, count_y, count_z = counts
    depth_block = mine.shape[1]
    last = gathered.shape[1] - 1
    kzs, length = kernel.shape[2], INNER * TILE
    size = kzs * count_y * count_z
    columns = count_x * count_z * QUAD
    kz = here[0] * kzs + lax.broadcasted_iota(jnp.int32, (kzs, columns), 0)
    column = lax.broadcasted_iota(jnp.int32, (kzs, columns), 1)
    pair = column >> whole_log(QUAD) & (count_z // 2 - 1)
    odd = (column >> whole_log(columns // 2)) ^ (here[0] & 1)
    z = (2 * pair + odd) * depth_block + (column & (QUAD - 1))
    z = z + (column >> whole_log(QUAD * count_z // 2) & (count_x - 1)) * QUAD
    cosine, sine = cos_sin(kz * z & (size - 1), size)
    table = jnp.concatenate([cosine, -sine], axis=0)
    for k, part in enumerate((gathered, swapped)):
        for x in range(count_x):
            for y in range(count_y):
                for pair in range(count_z // 2):
                    row = ((k * count_x + x) * count_z // 2 + pair) * QUAD
                    member = (x * count_y + y) * count_z // 2 + pair
                    received[y, row : row + QUAD, :] = part[member, last]
    blocks = [received[y] for y in range(count_y)]
    lines = dot3(table, split(jnp.concatenate(blocks, axis=1)))

    real, imag = there_and_back(lines[:kzs], lines[kzs:], kernel, spectrum)

    rows = depth_block * count_z
    z = lax.broadcasted_iota(jnp.int32, (rows, 2 * kzs), 0)
    column = lax.broadcasted_iota(jnp.int32, (rows, 2 * kzs), 1)
    cosine, sine = cos_sin((here[0] * kzs + (column & (kzs - 1))) * z & (size - 1), size)
    table = jnp.where(column < kzs, cosine, -sine) * (1.0 / (size * length))
    even = (here[0] & 1) == 0
    lines = [jnp.concatenate([part[:kzs] for part in (real, imag)], axis=0)]
    lines.append(jnp.concatenate([part[kzs:] for part in (real, imag)], axis=0))
    for out, (a, b) in ((mine, lines), (other, lines[::-1])):
        image = dot3(table, split(jnp.where(even, a, b)))
        for y in range(count_y):
            for z in range(count_z):
                out[y * count_z + z] = image[
                    z * depth_block : (z + 1) * depth_block, y * LANES : (y + 1) * LANES
                ]
    copies[0].wait()


def rows_kernel(counts, arrived, mine, other, table, out):
    count_y, count_z = counts[1:]
    out[:, 2 * TILE :, :] = mine[...] + other[...]
    per_turn = INNER * 2 // LANES
    step = arrived.shape[0] // per_turn
    size = step * INNER
    half = LANES // 2
    lane = lax.broadcasted_iota(jnp.int32, (2 * TILE, LANES), 1)
    upper, lower = [], []
    for b in range(step):
        parts = ([], [])
        for pair in range(b * per_turn, (b + 1) * per_turn, 2):
            first, second = arrived[pair], arrived[pair + 1]
            spectra = (
                jnp.where(lane < half, first, pltpu.roll(second, half, 1)),
                jnp.where(lane < half, pltpu.roll(first, half, 1), second),
            )
            for k in range(2):
                parts[k].append(
                    jnp.concatenate(
                        [spectrum[k * TILE : (k + 1) * TILE] for spectrum in spectra], axis=0
                    )
                )
        real, imag = (jnp.concatenate(part, axis=1) for part in parts)
        upper.append(jnp.concatenate([real, -imag], axis=1))
        lower.append(jnp.concatenate([imag, real], axis=1))
    lines = dot3_with(jnp.concatenate(upper + lower, axis=0), table)
    y = lax.broadcasted_iota(jnp.int32, (1, INNER), 1) & (step - 1)
    total = None
    for b in range(step):
        cosine, sine = cos_sin(y * b & (step - 1), step)
        real, imag = (
            lines[(k * step + b) * 2 * TILE : (k * step + b + 1) * 2 * TILE] for k in range(2)
        )
        term = real * cosine - imag * sine if b else real
        total = term if b == 0 else total + term
    total = total * (1.0 / (size * size))
    for y in range(count_y):
        for z in range(count_z):
            out[y * count_z + z, 0 : 2 * TILE, :] = total[:, y * LANES : (y + 1) * LANES]


def sum_kernel(exchange_grad, arrived, out, result, sending):
    depth = exchange_grad.shape[1]
    group = arrived.shape[0]
    sends = []

    def send(c):
        sends.append(pltpu.make_async_copy(result.at[c], out.at[c], sending.at[c]))
        sends[-1].start()

    def top(c):
        return arrived[:, c * TILE : (c + 1) * TILE, :].reshape(group * TILE, LANES)

    def side(c):
        total = arrived[c, 2 * TILE :, :]
        for p in range(c + 2, group, 2):
            total = total + arrived[p, 2 * TILE :, :]
        return total

    image = top(0)
    for z in range(depth):
        result[0, z] = exchange_grad[0, z] + image
    send(0)
    column = side(1)
    for z in range(depth):
        result[2, z] = exchange_grad[2, z] + column[z : z + 1]
    send(2)
    image, column = top(1), side(0)
    for z in range(depth):
        result[1, z] = exchange_grad[1, z] + image + column[z : z + 1]
    send(1)
    for copy in sends:
        copy.wait()


def residual_blocks(residual_top, residual_side, copies, share, quads):
    block_x, block_y = residual_top.shape
    top_rows = block_y // 2

    def body(at_x, top, side, out):
        piece = jnp.concatenate([top[0:top_rows, :], top[top_rows:, :]], axis=1)
        part = side[pl.ds(at_x[0] * share, share), :]
        if not quads:
            part = jnp.concatenate([part, jnp.zeros((TILE - share, LANES), f32)], axis=0)
        for copy in range(copies):
            if quads:
                for j in range(top_rows // QUAD):
                    out[copy, j] = piece[j * QUAD : (j + 1) * QUAD]
                out[copy, top_rows // QUAD] = part
            else:
                out[copy, 0:top_rows, :] = piece
                out[copy, top_rows:, :] = part

    shape = (top_rows // QUAD + 1, QUAD) if quads else (top_rows + TILE,)
    return call(
        body,
        "pack",
        (copies, *shape, LANES),
        60,
        0.8,
        (lax.axis_index("gx").reshape(1), residual_top.T, residual_side.T),
    )


def fast_on_device(magnetization, stiffness, residual_top, residual_side, top_kernel, side_kernel):
    counts = tuple(lax.axis_size(axis) for axis in ALL)
    count_x, count_y, count_z = counts
    group = count_y * count_z
    devices = count_x * group
    block_x, block_y = residual_top.shape
    depth_block = stiffness.shape[0]
    top_rows = block_y // 2
    kys, size = top_kernel.shape[2:]
    kzs = side_kernel.shape[2]
    extent = count_x * block_x
    here = [lax.axis_index(axis) for axis in ALL]
    plane_index = here[1] * count_z + here[2]
    index = (here[0] * group + plane_index).reshape(1)
    plane_index = plane_index.reshape(1)
    tiles, table = (jnp.asarray(values) for values in narrow_tables(extent, size))
    rows_table = jnp.asarray(transform_table(size))

    parities = [range(parity, devices, 2) for parity in range(2)]
    sent = residual_blocks(
        residual_top, residual_side, devices // 2, depth_block // count_x, True
    )
    gathered = lax.all_to_all(
        sent, ALL, 0, 0, tiled=True, axis_index_groups=[list(each) for each in parities]
    )
    z_first, z_last, x_first, x_last, y_faces = faces_of(magnetization, stiffness)
    narrowed = call(
        narrow_kernel,
        "narrow",
        [(2, 2, kys, 2 * extent), (2, 2, kzs, 2 * extent)],
        16,
        2.5,
        (top_kernel, side_kernel, tiles),
    )
    gathered, x_first, x_last, y_faces, narrowed = lax.optimization_barrier(
        (gathered, x_first, x_last, y_faces, narrowed)
    )
    top_spectra, side_spectra = narrowed
    swapped = lax.ppermute(gathered, "gz", [(i, i ^ 1) for i in range(count_z)])
    zy = halos_zy(z_first, z_last, y_faces)

    lines = call(
        functools.partial(lines_kernel, counts),
        "lines",
        (devices, 2 * TILE, LANES),
        16,
        2.2,
        (index, gathered, swapped, table, top_spectra),
        scratch=[pltpu.VMEM((count_x, LANES, LANES), f32)],
    )
    arrived = lax.all_to_all(lines, ALL, 0, 0, tiled=True)
    lines, x_first, x_last = lax.optimization_barrier((lines, x_first, x_last))
    x = halos_x(x_first, x_last)
    mine, other, rows_table = call(
        functools.partial(side_kernel_body, counts),
        "side",
        [(group, depth_block, LANES), (group, depth_block, LANES), rows_table.shape],
        8,
        2.0,
        (plane_index, gathered, swapped, table, side_spectra, from_hbm(rows_table)),
        in_vmem=(2,),
        refs=(5,),
        scratch=[
            pltpu.VMEM((count_y, count_x * count_z * QUAD, LANES), f32),
            pltpu.SemaphoreType.DMA((1,)),
        ],
    )
    other = lax.ppermute(other, "gz", [(i, i ^ 1) for i in range(count_z)])
    arrived, mine, other, rows_table = lax.optimization_barrier(
        (arrived, mine, other, rows_table)
    )
    rows = call(
        functools.partial(rows_kernel, counts),
        "rows",
        (group, 2 * TILE + depth_block, LANES),
        8,
        1.1,
        (arrived, mine, other, rows_table),
    )
    _, zy, x = lax.optimization_barrier((rows, zy, x))
    arrived = lax.all_to_all(rows, ("gy", "gz"), 0, 0, tiled=True)
    exchange_grad = exchange_of(counts, index, magnetization, stiffness, zy, x)
    return call(
        sum_kernel,
        "gradient",
        magnetization.shape,
        16,
        1.2,
        (exchange_grad, arrived),
        out_refs=(0,),
        scratch=[pltpu.VMEM(magnetization.shape, f32), pltpu.SemaphoreType.DMA((3,))],
    )


def fits(counts, stiffness, residual_top, residual_side, top_kernel, side_kernel):
    count_x, count_y, count_z = counts
    block_x, block_y = residual_top.shape
    group = count_y * count_z
    return (
        2 * block_x == LANES
        and 2 * top_kernel.shape[2] == LANES
        and stiffness.shape[2] == LANES
        and block_x == group * TILE
        and block_y * group == count_x * block_x == INNER
        and count_y * LANES == INNER
        and block_y % 16 == 0
        and count_x % 2 == 0
        and count_z % 2 == 0
        and (count_x * group) % (2 * top_kernel.shape[3] // INNER) == 0
        and INNER == top_kernel.shape[2] * count_z
        and top_kernel.shape[3] == TILE * INNER == side_kernel.shape[3]
        and INNER == 2 * LANES
        and stiffness.shape[0] % 16 == 0
        and stiffness.shape[0] == count_x * QUAD
        and side_kernel.shape[2] % 16 == 0
        and all(
            count & (count - 1) == 0
            for count in (group, count_x, count_z, top_kernel.shape[3], side_kernel.shape[2])
        )
    )


def on_device(magnetization, stiffness, residual_top, residual_side, top_kernel, side_kernel):
    counts = tuple(lax.axis_size(axis) for axis in ALL)
    count_x, count_y, count_z = counts
    if fits(counts, stiffness, residual_top, residual_side, top_kernel, side_kernel):
        return fast_on_device(
            magnetization, stiffness, residual_top, residual_side, top_kernel, side_kernel
        )
    devices = count_x * count_y * count_z
    depth_block = stiffness.shape[0]
    block_x, block_y = residual_top.shape
    top_rows = block_y // 2
    share = depth_block // count_x

    sent = residual_blocks(residual_top, residual_side, devices, share, False)
    rows = sent.shape[1]
    gathered = lax.all_to_all(sent, ALL, 0, 0, tiled=True)
    index = (
        (lax.axis_index("gx") * count_y + lax.axis_index("gy")) * count_z + lax.axis_index("gz")
    ).reshape(1)
    z_first, z_last, x_first, x_last, y_faces = faces_of(magnetization, stiffness)
    exchange_grad = exchange_of(
        counts,
        index,
        magnetization,
        stiffness,
        halos_zy(z_first, z_last, y_faces),
        halos_x(x_first, x_last),
    )

    parts = image_parts(
        gathered, top_kernel, side_kernel, counts, block_x, top_rows, depth_block
    )
    rows = parts.shape[1]
    arrived = lax.all_to_all(parts.reshape(devices * rows, LANES), ALL, 0, 0, tiled=True)
    arrived = arrived.reshape(devices, rows, LANES)
    top_sum = jnp.sum(arrived[:, : rows - TILE], axis=0)
    side_sum = jnp.sum(
        arrived[:, rows - TILE :].reshape(count_x, count_y * count_z, TILE, LANES), axis=1
    )
    side = side_sum[:, : 2 * share].reshape(count_x, 2, share, LANES)
    side = jnp.swapaxes(side, 0, 1).reshape(2, depth_block, 1, LANES)
    top = lax.all_gather(top_sum, "gz", axis=0)
    top = jnp.swapaxes(top.reshape(count_z, 2, block_x // count_z, LANES), 0, 1)
    top = top.reshape(2, 1, block_x, LANES)
    return jnp.stack(
        [
            exchange_grad[0] + top[0],
            exchange_grad[1] + top[1] + side[0],
            exchange_grad[2] + side[1],
        ]
    )


def solution(mesh):
    placed = (
        P(None, "gz", "gx", "gy"),
        P("gz", "gx", "gy"),
        P("gx", ("gy", "gz")),
        P("gy", "gz"),
        P(None, None, ("gx", "gy", "gz"), None),
        P(None, None, ("gy", "gz"), None),
    )
    return jax.shard_map(
        on_device, mesh=mesh, in_specs=placed, out_specs=P(None, "gz", "gx", "gy"), check_vma=False
    )
```

```python
import functools
import math

import jax
import jax.numpy as jnp
import ml_dtypes
import numpy as np
from jax import lax
from jax.experimental import pallas as pl
from jax.experimental.pallas import tpu as pltpu
from jax.sharding import PartitionSpec as P

LANES = 128
TILE = 8
INNER = 256
ALL = ("gx", "gy", "gz")
f32 = jnp.float32
bf16 = jnp.bfloat16
MIB = 1024 * 1024
QUAD = 4
SMEM = pl.BlockSpec(memory_space=pltpu.SMEM)
VMEM = pl.BlockSpec(memory_space=pltpu.VMEM)
HBM = pl.BlockSpec(memory_space=pltpu.HBM)


def whole_log(count):
    return count.bit_length() - 1


def split(values):
    high = values.astype(bf16)
    return high, (values - high.astype(f32)).astype(bf16)


def dot3(left, right):
    high, low = split(left)
    def one(a, b):
        return lax.dot_general(a, b, (((1,), (0,)), ((), ())), preferred_element_type=f32)
    return one(high, right[0]) + one(low, right[0]) + one(high, right[1])


def from_hbm(values):
    return pltpu.with_memory_space_constraint(values, pltpu.HBM)


def call(
    body,
    name,
    shape,
    limit,
    microseconds,
    operands,
    in_hbm=(),
    in_vmem=(),
    scratch=(),
    refs=(),
    out_refs=(),
    aliases=(),
):
    shapes = shape if isinstance(shape, list) else [shape]
    moved = sum(4 * math.prod(each) for each in shapes)
    moved += sum(x.size * x.dtype.itemsize for x in operands)
    results = pl.pallas_call(
        body,
        out_shape=[
            pltpu.HBM(each, f32)
            if i in in_hbm
            else pltpu.VMEM(each, bf16)
            if i in in_vmem
            else jax.ShapeDtypeStruct(each, f32)
            for i, each in enumerate(shapes)
        ],
        in_specs=[
            SMEM if x.shape == (1,) else HBM if i in refs else VMEM
            for i, x in enumerate(operands)
        ],
        out_specs=[HBM if i in out_refs else VMEM for i in range(len(shapes))],
        input_output_aliases=dict(aliases),
        scratch_shapes=list(scratch),
        compiler_params=pltpu.CompilerParams(vmem_limit_bytes=limit * MIB),
        cost_estimate=pl.CostEstimate(
            flops=int(microseconds * 1e9), bytes_accessed=moved, transcendentals=0
        ),
        name=name,
    )(*operands)
    return results if isinstance(shape, list) else results[0]


def transform_tables(extent, size):
    x = np.arange(extent)
    angle = (np.outer(x, np.arange(INNER)) % size) * (2.0 * math.pi / size)
    forward = np.concatenate([np.cos(angle), np.sin(angle)], 0).astype(np.float32)
    backward = np.concatenate([np.cos(angle).T, np.sin(angle).T], 0).astype(np.float32)

    def parts(table):
        high = table.astype(ml_dtypes.bfloat16)
        return high, (table - high.astype(np.float32)).astype(ml_dtypes.bfloat16)

    outer = size // INNER
    turn = (np.outer(np.arange(outer), x) % outer) * (2.0 * math.pi / outer)
    turns = np.stack([np.cos(turn), np.sin(turn)]).astype(np.float32)
    return parts(forward), parts(backward), turns


def phases(first, second, size):
    angle = (first * second % size).astype(f32) * (2.0 * math.pi / size)
    return jnp.cos(angle), jnp.sin(angle)


def image_kernel(
    counts, gathered, y_table, z_table, fh, fl, bh, bl, turns, top, side, y_back, z_back, out
):
    count_x, count_y, count_z, top_rows = counts
    group = count_y * count_z
    half = LANES // 2
    kys = top.shape[2]
    kzs = side.shape[2]
    forward = (fh[...], fl[...])
    backward = (bh[...], bl[...])

    blocks = [
        gathered[g * group : (g + 1) * group, 0:top_rows, :].reshape(group * top_rows, LANES)
        for g in range(count_x)
    ]
    mixed = dot3(y_table[...], split(jnp.concatenate(blocks, axis=1)))
    low_half, high_half = mixed[: 2 * kys], mixed[2 * kys :]
    lane = lax.broadcasted_iota(jnp.int32, (2 * kys, LANES), 1)
    pieces = []
    for g in range(0, count_x, 2):
        a = slice(g * LANES, (g + 1) * LANES)
        b = slice((g + 1) * LANES, (g + 2) * LANES)
        pieces.append(
            jnp.where(
                lane < half,
                low_half[:, a] + pltpu.roll(high_half[:, a], half, 1),
                pltpu.roll(low_half[:, b], half, 1) + high_half[:, b],
            )
        )
    top_lines = jnp.concatenate(pieces, axis=1)

    side_blocks = []
    for y in range(count_y):
        rows = [
            gathered[(x * count_y + y) * count_z + z, top_rows : top_rows + TILE, :]
            for x in range(count_x)
            for z in range(count_z)
        ]
        side_blocks.append(jnp.concatenate(rows, axis=0))
    side_lines = dot3(z_table[...], split(jnp.concatenate(side_blocks, axis=1)))

    real = jnp.concatenate([top_lines[:kys], side_lines[:kzs]], axis=0)
    imag = jnp.concatenate([top_lines[kys:], side_lines[kzs:]], axis=0)
    rows = kys + kzs
    total_real = total_imag = None
    for b in range(turns.shape[1]):
        cosine, sine = turns[0, b : b + 1, :], turns[1, b : b + 1, :]
        turned_real = real * cosine + imag * sine
        turned_imag = imag * cosine - real * sine
        waves = dot3(
            jnp.concatenate(
                [
                    jnp.concatenate([turned_real, turned_imag], axis=1),
                    jnp.concatenate([turned_imag, -turned_real], axis=1),
                ],
                axis=0,
            ),
            forward,
        )
        wave_real, wave_imag = waves[:rows], waves[rows:]
        columns = slice(b * INNER, (b + 1) * INNER)
        weighted_real, weighted_imag = [], []
        for c in range(2):
            for kernel, part in ((top, slice(0, kys)), (side, slice(kys, rows))):
                kernel_real, kernel_imag = kernel[c, 0, :, columns], kernel[c, 1, :, columns]
                weighted_real.append(
                    kernel_real * wave_real[part] + kernel_imag * wave_imag[part]
                )
                weighted_imag.append(
                    kernel_real * wave_imag[part] - kernel_imag * wave_real[part]
                )
        weighted_real = jnp.concatenate(weighted_real, axis=0)
        weighted_imag = jnp.concatenate(weighted_imag, axis=0)
        back = dot3(
            jnp.concatenate(
                [
                    jnp.concatenate([weighted_real, -weighted_imag], axis=1),
                    jnp.concatenate([weighted_imag, weighted_real], axis=1),
                ],
                axis=0,
            ),
            backward,
        )
        back_real, back_imag = back[: 2 * rows], back[2 * rows :]
        if b == 0:
            total_real, total_imag = back_real, back_imag
        else:
            total_real = total_real + (back_real * cosine - back_imag * sine)
            total_imag = total_imag + (back_real * sine + back_imag * cosine)

    y_parts = split(y_back[...])
    depth_rows = []
    quarter = (out.shape[1] - TILE) // 2
    block_x = quarter * count_z
    for c in range(2):
        start = c * rows
        lines = jnp.concatenate(
            [total_real[start : start + kys], total_imag[start : start + kys]], axis=0
        )
        image = dot3(lines.T, y_parts)
        for x in range(count_x):
            for y in range(count_y):
                for z in range(count_z):
                    first = x * block_x + z * quarter
                    out[
                        (x * count_y + y) * count_z + z, c * quarter : (c + 1) * quarter, :
                    ] = image[first : first + quarter, y * LANES : (y + 1) * LANES]
        depth_rows.append(total_real[start + kys : start + rows])
        depth_rows.append(total_imag[start + kys : start + rows])
    side_image = dot3(z_back[...], split(jnp.concatenate(depth_rows, axis=0)))
    for y in range(count_y):
        for z in range(count_z):
            block = side_image[z * TILE : (z + 1) * TILE, y * LANES : (y + 1) * LANES]
            for x in range(count_x):
                out[(x * count_y + y) * count_z + z, 2 * quarter :, :] = block


def image_parts(gathered, top_kernel, side_kernel, counts, block_x, top_rows, depth_block):
    count_x, count_y, count_z = counts
    group = count_y * count_z
    here = [lax.axis_index(axis) for axis in ALL]
    kys, size = top_kernel.shape[2:]
    kzs = side_kernel.shape[2]
    depth_size = kzs * group
    extent = count_y * LANES
    share = depth_block // count_x
    block_y = top_rows * 2

    ky = ((here[0] * count_y + here[1]) * count_z + here[2]) * kys + lax.iota(jnp.int32, kys)
    kz = (here[1] * count_z + here[2]) * kzs + lax.iota(jnp.int32, kzs)

    row = lax.iota(jnp.int32, group * top_rows)
    y_tables = []
    for h in range(2):
        y = row // top_rows * block_y + h * top_rows + row % top_rows
        cosine, sine = phases(ky[:, None], y[None, :], size)
        y_tables += [cosine, -sine]
    y_table = jnp.concatenate(y_tables, axis=0)

    row = lax.iota(jnp.int32, count_x * count_z * TILE)
    inside = row % TILE
    z = row // TILE % count_z * depth_block + row // (TILE * count_z) * share + inside
    cosine, sine = phases(kz[:, None], z[None, :], depth_size)
    z_table = jnp.where((inside < share)[None, :], jnp.concatenate([cosine, -sine], axis=0), 0.0)

    cosine, sine = phases(ky[:, None], lax.iota(jnp.int32, extent)[None, :], size)
    y_back = jnp.concatenate([cosine, -sine], axis=0) * (1.0 / (size * size))

    row = lax.iota(jnp.int32, count_z * TILE)
    z = row // TILE * depth_block + here[0] * share + row % TILE % share
    cosine, sine = phases(z[:, None], kz[None, :], depth_size)
    both = jnp.concatenate([cosine, -sine], axis=1) * (1.0 / (size * depth_size))
    component = (row % TILE // share)[:, None]
    z_back = jnp.concatenate(
        [jnp.where(component == 0, both, 0.0), jnp.where(component == 1, both, 0.0)], axis=1
    )

    forward, backward, turns = transform_tables(extent, size)
    out_rows = 2 * (block_x // count_z) + TILE
    return pl.pallas_call(
        functools.partial(image_kernel, counts + (top_rows,)),
        out_shape=jax.ShapeDtypeStruct((count_x * group, out_rows, LANES), f32),
        compiler_params=pltpu.CompilerParams(vmem_limit_bytes=56 * 1024 * 1024),
        name="images",
    )(
        gathered,
        y_table,
        z_table,
        *(jnp.asarray(t) for t in forward + backward),
        jnp.asarray(turns),
        top_kernel,
        side_kernel,
        y_back,
        z_back,
    )


def begin(semaphores, pairs):
    started = [
        pltpu.make_async_copy(source, target, semaphores.at[i])
        for i, (source, target) in enumerate(pairs)
    ]
    for copy in started:
        copy.start()
    return started


def faces_kernel(
    magnetization, stiffness, z_first, z_last, x_first, x_last, y_faces, m, s, loading
):
    depth, across = stiffness.shape[:2]
    loads = begin(
        loading, [(stiffness, s)] + [(magnetization.at[c], m.at[c]) for c in range(3)]
    )
    lane = lax.broadcasted_iota(jnp.int32, (across, LANES), 1)
    pair = (lane + 1 & (LANES - 1)) >> 1
    sides = jnp.zeros((across, LANES), f32)
    for field in (3, 0, 1, 2):
        loads[(field + 1) % 4].wait()
        ref = s if field == 3 else m.at[field]
        z_first[field] = ref[0]
        z_last[field] = ref[depth - 1]
        x_first[field] = ref[:, 0, :]
        x_last[field] = ref[:, across - 1, :]
        for z in range(depth):
            column = field * depth + z
            turned = pltpu.roll(ref[z], 2 * column, 1) if column else ref[z]
            sides = jnp.where(pair == column, turned, sides)
    y_faces[...] = sides


def twice_weight(a, b):
    total = a + b
    inverse = pl.reciprocal(total, approx=True)
    return 4.0 * a * b * (inverse * (2.0 - total * inverse))


def exchange_kernel(
    counts,
    here,
    magnetization_from,
    stiffness_from,
    y_faces_from,
    z_next,
    z_before,
    x_next,
    x_before,
    y_next,
    y_before,
    out,
    m,
    s,
    y_faces,
    loading,
):
    depth, across = s.shape[:2]
    chunk = depth // 4
    pairs = [(y_faces_from, y_faces)]
    for k in range(4):
        layers = pl.ds(k * chunk, chunk)
        pairs.append((stiffness_from.at[layers], s.at[layers]))
        pairs.append((magnetization_from.at[:, layers], m.at[:, layers]))
    loads = begin(loading, pairs)

    count_x, count_y, count_z = counts
    at_z = here[0] % count_z
    at_y = here[0] // count_z % count_y
    at_x = here[0] // (count_z * count_y)

    def inside(condition, values):
        return jnp.where(condition, values, 0.0)

    lane = lax.broadcasted_iota(jnp.int32, (across, LANES), 1)
    row = lax.broadcasted_iota(jnp.int32, (across, LANES), 0)
    first_lane, last_lane, last_row = lane == 0, lane == LANES - 1, row == across - 1

    loads[0].wait()
    own = y_faces[...]
    even = (lane & 1) == 0
    field = (lane + 1 & (LANES - 1)) >> whole_log(2 * depth)
    halo = jnp.where(
        even, pltpu.roll(y_before[...], 1, 1), pltpu.roll(y_next[...], LANES - 1, 1)
    )
    present = jnp.where(even, at_y, count_y - 1 - at_y) > 0
    weight = twice_weight(
        jnp.where(field == 3, own, 1.0),
        jnp.where(field == 3, jnp.where(present, halo, 0.0), 1.0),
    )
    spread = pltpu.roll(weight, LANES - 6 * depth, 1)
    for c in (1, 2):
        spread = jnp.where(
            field == c, pltpu.roll(weight, LANES - (3 - c) * 2 * depth, 1), spread
        )
    sides = spread * (own - halo)
    outer = first_lane | last_lane

    for copy in loads[1:3]:
        copy.wait()
    below_weight = twice_weight(inside(at_z > 0, z_before[3]), s[0])
    below = [below_weight * (z_before[c] - m[c, 0]) for c in range(3)]
    for z in range(depth):
        if z % chunk == chunk - 1:
            k = 1 + 2 * (z // chunk + 1)
            for copy in loads[k : k + 2]:
                copy.wait()
        centre = s[z]
        above = s[z + 1] if z + 1 < depth else inside(at_z < count_z - 1, z_next[3])
        weight_z = twice_weight(centre, above)
        weight_x = jnp.where(
            last_row, 0.0, twice_weight(centre, pltpu.roll(centre, across - 1, 0))
        )
        weight_y = jnp.where(
            last_lane, 0.0, twice_weight(centre, pltpu.roll(centre, LANES - 1, 1))
        )
        for c in range(3):
            column = c * depth + z
            values = m[c, z]
            upper = m[c, z + 1] if z + 1 < depth else z_next[c]
            up = weight_z * (values - upper)
            flux_x = weight_x * (values - pltpu.roll(values, across - 1, 0))
            flux_y = weight_y * (values - pltpu.roll(values, LANES - 1, 1))
            total = (up - below[c]) + (flux_x - pltpu.roll(flux_x, 1, 0))
            total = total + (flux_y - pltpu.roll(flux_y, 1, 1))
            both = pltpu.roll(sides, LANES - 2 * column, 1) if column else sides
            out[c, z] = jnp.where(outer, total + both, total)
            below[c] = up
    for edge_row, halo, present in (
        (across - 1, x_next, at_x < count_x - 1),
        (0, x_before, at_x > 0),
    ):
        weight = twice_weight(s[:, edge_row, :], inside(present, halo[3]))
        for c in range(3):
            out[c, :, edge_row, :] += weight * (m[c, :, edge_row, :] - halo[c])


def ring(block, axis, distance):
    count = lax.axis_size(axis)
    return lax.ppermute(block, axis, [(i, (i + distance) % count) for i in range(count)])


def faces_of(magnetization, stiffness):
    depth, across, along = stiffness.shape
    return call(
        faces_kernel,
        "faces",
        [
            (4, across, along),
            (4, across, along),
            (4, depth, along),
            (4, depth, along),
            (across, LANES),
        ],
        8,
        2.0,
        (from_hbm(magnetization), from_hbm(stiffness)),
        in_hbm=(4,),
        refs=(0, 1),
        scratch=[
            pltpu.VMEM(magnetization.shape, f32),
            pltpu.VMEM(stiffness.shape, f32),
            pltpu.SemaphoreType.DMA((4,)),
        ],
    )


def halos_zy(z_first, z_last, y_faces):
    y_next = ring(y_faces, "gy", -1)
    y_before = y_next if lax.axis_size("gy") == 2 else ring(y_faces, "gy", 1)
    return ring(z_first, "gz", -1), ring(z_last, "gz", 1), y_next, y_before, y_faces


def halos_x(x_first, x_last):
    return ring(x_first, "gx", -1), ring(x_last, "gx", 1)


def exchange_of(counts, index, magnetization, stiffness, zy, x):
    z_next, z_before, y_next, y_before, y_faces = zy
    fetched = (magnetization, stiffness, y_faces)
    return call(
        functools.partial(exchange_kernel, counts),
        "exchange",
        magnetization.shape,
        8,
        5.0,
        (
            index,
            *(from_hbm(array) for array in fetched),
            z_next,
            z_before,
            *x,
            y_next,
            y_before,
        ),
        refs=(1, 2, 3),
        scratch=[pltpu.VMEM(array.shape, f32) for array in fetched]
        + [pltpu.SemaphoreType.DMA((9,))],
    )


def cos_sin(steps, size):
    quarter = steps >> whole_log(size // 4)
    angle = ((steps & (size // 4 - 1)) - size // 8).astype(f32) * (2.0 * math.pi / size)
    square = angle * angle
    sine = cosine = 0.0
    for k in range(5, -1, -1):
        sine = sine * square + (-1) ** k / math.factorial(2 * k + 1)
        cosine = cosine * square + (-1) ** k / math.factorial(2 * k)
    sine = sine * angle
    first, second = (cosine - sine) * math.sqrt(0.5), (cosine + sine) * math.sqrt(0.5)
    odd = (quarter & 1) == 1
    real = jnp.where(odd, -second, first)
    imag = jnp.where(odd, first, second)
    back = quarter >= 2
    return jnp.where(back, -real, real), jnp.where(back, -imag, imag)


def halves_of(table):
    table = table.astype(np.float32)
    high = table.astype(ml_dtypes.bfloat16)
    return high, (table - high.astype(np.float32)).astype(ml_dtypes.bfloat16)


def narrow_tables(extent, size):
    length = 2 * extent
    ratio = size // length
    m = np.arange(size)
    lags = np.arange(1, extent)
    window = 1.0 + 2.0 * np.cos(np.outer(m, lags) % size * (2.0 * math.pi / size)).sum(axis=1)
    i = np.arange(INNER)
    place = np.arange(0, size, INNER)[:, None, None] + i[:, None] - ratio * i[None, :]
    high, low = halves_of(window[place % size] / length)
    tiles = np.stack([high, low], axis=1)
    return tiles, transform_table(length)


def transform_table(size):
    i = np.arange(INNER)
    angle = np.outer(i, i) * (2.0 * math.pi / size)
    return np.stack(halves_of(np.concatenate([np.cos(angle), np.sin(angle)], axis=0)))


def pair_order(planes, per_plane):
    return [plane * per_plane + p for p in range(per_plane) for plane in reversed(range(planes))]


def y_table_of(counts, here, kys, size):
    group = counts[1] * counts[2]
    top_rows = LANES // group
    ky = here[0] * kys + lax.broadcasted_iota(jnp.int32, (kys, LANES), 0)
    lane = lax.broadcasted_iota(jnp.int32, (kys, LANES), 1)
    odd = (lane >> whole_log(LANES // 2)) ^ (here[0] & 1)
    pair = lane >> whole_log(top_rows) & (group // 2 - 1)
    phases_of = []
    for h in range(2):
        y = (2 * pair + odd) * (2 * top_rows) + h * top_rows + (lane & (top_rows - 1))
        cosine, sine = cos_sin(ky * y & (size - 1), size)
        phases_of += [cosine, -sine]
    high, low = split(jnp.concatenate(phases_of, axis=0))
    return jnp.concatenate([high, low, high], axis=1)


def narrow_kernel(top, side, tiles, top_out, side_out):
    count = tiles.shape[0]
    parts = top_out.shape[3] // INNER
    step = count // parts
    top_rows, side_rows = top.shape[2], side.shape[2]
    totals = [None] * parts
    for k in range(count):
        columns = slice(k * INNER, (k + 1) * INNER)
        lines = jnp.concatenate(
            [
                top[:, :, :, columns].reshape(4 * top_rows, INNER),
                side[:, :, :, columns].reshape(4 * side_rows, INNER),
            ],
            axis=0,
        )
        high, low = split(lines)
        lines = jnp.concatenate([high, low, high], axis=1)
        for part in range(parts):
            tile = tiles[(k - part * step) % count]
            term = product(lines, jnp.concatenate([tile[0], tile[0], tile[1]], axis=0))
            totals[part] = term if k == 0 else totals[part] + term
    for part in range(parts):
        columns = slice(part * INNER, (part + 1) * INNER)
        top_out[:, :, :, columns] = totals[part][: 4 * top_rows].reshape(2, 2, top_rows, INNER)
        side_out[:, :, :, columns] = totals[part][4 * top_rows :].reshape(2, 2, side_rows, INNER)


def product(left, right, contracted=0):
    return lax.dot_general(
        left, right, (((1,), (contracted,)), ((), ())), preferred_element_type=f32
    )


def dot3_with(values, table):
    high, low = split(values)
    lines = jnp.concatenate([high, low, high], axis=1)
    return product(lines, jnp.concatenate([table[0], table[0], table[1]], axis=0))


def there_and_back(real, imag, kernel, table):
    rows, extent = real.shape
    sign = jnp.where(lax.broadcasted_iota(jnp.int32, (1, extent), 1) & 1 == 0, 1.0, -1.0)
    lines = jnp.concatenate(
        [jnp.concatenate([real, imag], axis=1), jnp.concatenate([imag, -real], axis=1)], axis=0
    )
    signs = jnp.concatenate([sign, sign], axis=1)
    waves = dot3_with(jnp.concatenate([lines, lines * signs], axis=0), table)
    totals = []
    for b in range(2):
        wave_real, wave_imag = (
            waves[(2 * b + k) * rows : (2 * b + k + 1) * rows] for k in range(2)
        )
        columns = slice(b * INNER, (b + 1) * INNER)
        weighted = ([], [])
        for c in range(2):
            kernel_real, kernel_imag = kernel[c, 0, :, columns], kernel[c, 1, :, columns]
            weighted[0].append(kernel_real * wave_real + kernel_imag * wave_imag)
            weighted[1].append(kernel_real * wave_imag - kernel_imag * wave_real)
        a, b = (jnp.concatenate(part, axis=0) for part in weighted)
        lines = jnp.concatenate(
            [jnp.concatenate([a, -b], axis=1), jnp.concatenate([b, a], axis=1)], axis=0
        )
        totals.append(dot3_with(lines, table))
    total = totals[0] + totals[1] * sign
    return total[: 2 * rows], total[2 * rows :]


def lines_kernel(counts, here, gathered, swapped, table, kernel, out, received):
    count_x, count_y, count_z = counts
    group = count_y * count_z
    top_rows = LANES // group
    half = LANES // 2
    kys = kernel.shape[2]
    y_table = y_table_of(counts, here, kys, INNER * TILE)
    pairs = pair_order(count_x, group // 2)
    for k, part in enumerate((gathered, swapped)):
        for member in range(part.shape[0]):
            g, place = divmod(member, group // 2)
            for j in range(top_rows // QUAD):
                row = (k * group // 2 + place) * top_rows + j * QUAD
                received[g, row : row + QUAD, :] = part[pairs.index(member), j]
    blocks = [received[g] for g in range(count_x)]
    high, low = split(jnp.concatenate(blocks, axis=1))
    mixed = product(y_table, jnp.concatenate([high, high, low], axis=0))
    low_half, high_half = mixed[: 2 * kys], mixed[2 * kys :]
    lane = lax.broadcasted_iota(jnp.int32, (2 * kys, LANES), 1)
    pieces = []
    for g in range(0, count_x, 2):
        a = slice(g * LANES, (g + 1) * LANES)
        b = slice((g + 1) * LANES, (g + 2) * LANES)
        pieces.append(
            jnp.where(
                lane < half,
                low_half[:, a] + pltpu.roll(high_half[:, a], half, 1),
                pltpu.roll(low_half[:, b], half, 1) + high_half[:, b],
            )
        )
    lines = jnp.concatenate(pieces, axis=1)
    for k, part in enumerate(there_and_back(lines[:kys], lines[kys:], kernel, table)):
        out[:, k * TILE : (k + 1) * TILE, :] = part.T.reshape(count_x * group, TILE, LANES)


def side_kernel_body(
    counts,
    here,
    gathered,
    swapped,
    spectrum,
    kernel,
    later_from,
    mine,
    other,
    later,
    received,
    loading,
):
    copies = begin(loading, [(later_from, later)])
    count_x, count_y, count_z = counts
    depth_block = mine.shape[1]
    last = gathered.shape[1] - 1
    kzs, length = kernel.shape[2], INNER * TILE
    size = kzs * count_y * count_z
    columns = count_x * count_z * QUAD
    kz = here[0] * kzs + lax.broadcasted_iota(jnp.int32, (kzs, columns), 0)
    column = lax.broadcasted_iota(jnp.int32, (kzs, columns), 1)
    pair = column >> whole_log(QUAD) & (count_z // 2 - 1)
    odd = (column >> whole_log(columns // 2)) ^ (here[0] & 1)
    z = (2 * pair + odd) * depth_block + (column & (QUAD - 1))
    z = z + (column >> whole_log(QUAD * count_z // 2) & (count_x - 1)) * QUAD
    cosine, sine = cos_sin(kz * z & (size - 1), size)
    table = jnp.concatenate([cosine, -sine], axis=0)
    pairs = pair_order(count_x, count_y * count_z // 2)
    for k, part in enumerate((gathered, swapped)):
        for x in range(count_x):
            for y in range(count_y):
                for pair in range(count_z // 2):
                    row = ((k * count_x + x) * count_z // 2 + pair) * QUAD
                    member = (x * count_y + y) * count_z // 2 + pair
                    received[y, row : row + QUAD, :] = part[pairs.index(member), last]
    blocks = [received[y] for y in range(count_y)]
    lines = dot3(table, split(jnp.concatenate(blocks, axis=1)))

    real, imag = there_and_back(lines[:kzs], lines[kzs:], kernel, spectrum)

    rows = depth_block * count_z
    z = lax.broadcasted_iota(jnp.int32, (rows, 2 * kzs), 0)
    column = lax.broadcasted_iota(jnp.int32, (rows, 2 * kzs), 1)
    cosine, sine = cos_sin((here[0] * kzs + (column & (kzs - 1))) * z & (size - 1), size)
    table = jnp.where(column < kzs, cosine, -sine) * (1.0 / (size * length))
    even = (here[0] & 1) == 0
    lines = [jnp.concatenate([part[:kzs] for part in (real, imag)], axis=0)]
    lines.append(jnp.concatenate([part[kzs:] for part in (real, imag)], axis=0))
    for out, (a, b) in ((mine, lines), (other, lines[::-1])):
        image = dot3(table, split(jnp.where(even, a, b)))
        for y in range(count_y):
            for z in range(count_z):
                out[y * count_z + z] = image[
                    z * depth_block : (z + 1) * depth_block, y * LANES : (y + 1) * LANES
                ]
    copies[0].wait()


def rows_kernel(counts, arrived, mine, other, table, out):
    count_y, count_z = counts[1:]
    out[:, 2 * TILE :, :] = mine[...] + other[...]
    per_turn = INNER * 2 // LANES
    step = arrived.shape[0] // per_turn
    size = step * INNER
    half = LANES // 2
    lane = lax.broadcasted_iota(jnp.int32, (2 * TILE, LANES), 1)
    upper, lower = [], []
    for b in range(step):
        parts = ([], [])
        for pair in range(b * per_turn, (b + 1) * per_turn, 2):
            first, second = arrived[pair], arrived[pair + 1]
            spectra = (
                jnp.where(lane < half, first, pltpu.roll(second, half, 1)),
                jnp.where(lane < half, pltpu.roll(first, half, 1), second),
            )
            for k in range(2):
                parts[k].append(
                    jnp.concatenate(
                        [spectrum[k * TILE : (k + 1) * TILE] for spectrum in spectra], axis=0
                    )
                )
        real, imag = (jnp.concatenate(part, axis=1) for part in parts)
        upper.append(jnp.concatenate([real, -imag], axis=1))
        lower.append(jnp.concatenate([imag, real], axis=1))
    lines = dot3_with(jnp.concatenate(upper + lower, axis=0), table)
    y = lax.broadcasted_iota(jnp.int32, (1, INNER), 1) & (step - 1)
    total = None
    for b in range(step):
        cosine, sine = cos_sin(y * b & (step - 1), step)
        real, imag = (
            lines[(k * step + b) * 2 * TILE : (k * step + b + 1) * 2 * TILE] for k in range(2)
        )
        term = real * cosine - imag * sine if b else real
        total = term if b == 0 else total + term
    total = total * (1.0 / (size * size))
    for y in range(count_y):
        for z in range(count_z):
            out[y * count_z + z, 0 : 2 * TILE, :] = total[:, y * LANES : (y + 1) * LANES]


def sum_kernel(exchange_grad, arrived, out, result, sending):
    depth = exchange_grad.shape[1]
    group = arrived.shape[0]
    sends = []

    def send(c):
        sends.append(pltpu.make_async_copy(result.at[c], out.at[c], sending.at[c]))
        sends[-1].start()

    def top(c):
        return arrived[:, c * TILE : (c + 1) * TILE, :].reshape(group * TILE, LANES)

    def side(c):
        total = arrived[c, 2 * TILE :, :]
        for p in range(c + 2, group, 2):
            total = total + arrived[p, 2 * TILE :, :]
        return total

    image = top(0)
    for z in range(depth):
        result[0, z] = exchange_grad[0, z] + image
    send(0)
    column = side(1)
    for z in range(depth):
        result[2, z] = exchange_grad[2, z] + column[z : z + 1]
    send(2)
    image, column = top(1), side(0)
    for z in range(depth):
        result[1, z] = exchange_grad[1, z] + image + column[z : z + 1]
    send(1)
    for copy in sends:
        copy.wait()


def residual_blocks(residual_top, residual_side, copies, share, quads):
    block_x, block_y = residual_top.shape
    top_rows = block_y // 2

    def body(at_x, top, side, out):
        piece = jnp.concatenate([top[0:top_rows, :], top[top_rows:, :]], axis=1)
        part = side[pl.ds(at_x[0] * share, share), :]
        if not quads:
            part = jnp.concatenate([part, jnp.zeros((TILE - share, LANES), f32)], axis=0)
        for copy in range(copies):
            if quads:
                for j in range(top_rows // QUAD):
                    out[copy, j] = piece[j * QUAD : (j + 1) * QUAD]
                out[copy, top_rows // QUAD] = part
            else:
                out[copy, 0:top_rows, :] = piece
                out[copy, top_rows:, :] = part

    shape = (top_rows // QUAD + 1, QUAD) if quads else (top_rows + TILE,)
    return call(
        body,
        "pack",
        (copies, *shape, LANES),
        60,
        0.8,
        (lax.axis_index("gx").reshape(1), residual_top.T, residual_side.T),
    )


def fast_on_device(magnetization, stiffness, residual_top, residual_side, top_kernel, side_kernel):
    counts = tuple(lax.axis_size(axis) for axis in ALL)
    count_x, count_y, count_z = counts
    group = count_y * count_z
    devices = count_x * group
    block_x, block_y = residual_top.shape
    depth_block = stiffness.shape[0]
    top_rows = block_y // 2
    kys, size = top_kernel.shape[2:]
    kzs = side_kernel.shape[2]
    extent = count_x * block_x
    here = [lax.axis_index(axis) for axis in ALL]
    plane_index = here[1] * count_z + here[2]
    index = (here[0] * group + plane_index).reshape(1)
    plane_index = plane_index.reshape(1)
    tiles, table = (jnp.asarray(values) for values in narrow_tables(extent, size))
    rows_table = jnp.asarray(transform_table(size))

    pairs = pair_order(count_x, group // 2)
    parities = [[2 * pair + parity for pair in pairs] for parity in range(2)]
    sent = residual_blocks(
        residual_top, residual_side, devices // 2, depth_block // count_x, True
    )
    gathered = lax.all_to_all(
        sent, ALL, 0, 0, tiled=True, axis_index_groups=parities
    )
    z_first, z_last, x_first, x_last, y_faces = faces_of(magnetization, stiffness)
    narrowed = call(
        narrow_kernel,
        "narrow",
        [(2, 2, kys, 2 * extent), (2, 2, kzs, 2 * extent)],
        16,
        2.5,
        (top_kernel, side_kernel, tiles),
    )
    gathered, x_first, x_last, y_faces, narrowed = lax.optimization_barrier(
        (gathered, x_first, x_last, y_faces, narrowed)
    )
    top_spectra, side_spectra = narrowed
    swapped = lax.ppermute(gathered, "gz", [(i, i ^ 1) for i in range(count_z)])
    zy = halos_zy(z_first, z_last, y_faces)

    lines = call(
        functools.partial(lines_kernel, counts),
        "lines",
        (devices, 2 * TILE, LANES),
        16,
        2.2,
        (index, gathered, swapped, table, top_spectra),
        scratch=[pltpu.VMEM((count_x, LANES, LANES), f32)],
    )
    arrived = lax.all_to_all(lines, ALL, 0, 0, tiled=True)
    lines, x_first, x_last = lax.optimization_barrier((lines, x_first, x_last))
    x = halos_x(x_first, x_last)
    mine, other, rows_table = call(
        functools.partial(side_kernel_body, counts),
        "side",
        [(group, depth_block, LANES), (group, depth_block, LANES), rows_table.shape],
        8,
        2.0,
        (plane_index, gathered, swapped, table, side_spectra, from_hbm(rows_table)),
        in_vmem=(2,),
        refs=(5,),
        scratch=[
            pltpu.VMEM((count_y, count_x * count_z * QUAD, LANES), f32),
            pltpu.SemaphoreType.DMA((1,)),
        ],
    )
    other = lax.ppermute(other, "gz", [(i, i ^ 1) for i in range(count_z)])
    arrived, mine, other, rows_table = lax.optimization_barrier(
        (arrived, mine, other, rows_table)
    )
    rows = call(
        functools.partial(rows_kernel, counts),
        "rows",
        (group, 2 * TILE + depth_block, LANES),
        8,
        1.1,
        (arrived, mine, other, rows_table),
    )
    _, zy, x = lax.optimization_barrier((rows, zy, x))
    arrived = lax.all_to_all(rows, ("gy", "gz"), 0, 0, tiled=True)
    exchange_grad = exchange_of(counts, index, magnetization, stiffness, zy, x)
    return call(
        sum_kernel,
        "gradient",
        magnetization.shape,
        16,
        1.2,
        (exchange_grad, arrived),
        out_refs=(0,),
        scratch=[pltpu.VMEM(magnetization.shape, f32), pltpu.SemaphoreType.DMA((3,))],
    )


def fits(counts, stiffness, residual_top, residual_side, top_kernel, side_kernel):
    count_x, count_y, count_z = counts
    block_x, block_y = residual_top.shape
    group = count_y * count_z
    return (
        2 * block_x == LANES
        and 2 * top_kernel.shape[2] == LANES
        and stiffness.shape[2] == LANES
        and block_x == group * TILE
        and block_y * group == count_x * block_x == INNER
        and count_y * LANES == INNER
        and block_y % 16 == 0
        and count_x % 2 == 0
        and count_z % 2 == 0
        and (count_x * group) % (2 * top_kernel.shape[3] // INNER) == 0
        and INNER == top_kernel.shape[2] * count_z
        and top_kernel.shape[3] == TILE * INNER == side_kernel.shape[3]
        and INNER == 2 * LANES
        and stiffness.shape[0] % 16 == 0
        and stiffness.shape[0] == count_x * QUAD
        and side_kernel.shape[2] % 16 == 0
        and all(
            count & (count - 1) == 0
            for count in (group, count_x, count_z, top_kernel.shape[3], side_kernel.shape[2])
        )
    )


def on_device(magnetization, stiffness, residual_top, residual_side, top_kernel, side_kernel):
    counts = tuple(lax.axis_size(axis) for axis in ALL)
    count_x, count_y, count_z = counts
    if fits(counts, stiffness, residual_top, residual_side, top_kernel, side_kernel):
        return fast_on_device(
            magnetization, stiffness, residual_top, residual_side, top_kernel, side_kernel
        )
    devices = count_x * count_y * count_z
    depth_block = stiffness.shape[0]
    block_x, block_y = residual_top.shape
    top_rows = block_y // 2
    share = depth_block // count_x

    sent = residual_blocks(residual_top, residual_side, devices, share, False)
    rows = sent.shape[1]
    gathered = lax.all_to_all(sent, ALL, 0, 0, tiled=True)
    index = (
        (lax.axis_index("gx") * count_y + lax.axis_index("gy")) * count_z + lax.axis_index("gz")
    ).reshape(1)
    z_first, z_last, x_first, x_last, y_faces = faces_of(magnetization, stiffness)
    exchange_grad = exchange_of(
        counts,
        index,
        magnetization,
        stiffness,
        halos_zy(z_first, z_last, y_faces),
        halos_x(x_first, x_last),
    )

    parts = image_parts(
        gathered, top_kernel, side_kernel, counts, block_x, top_rows, depth_block
    )
    rows = parts.shape[1]
    arrived = lax.all_to_all(parts.reshape(devices * rows, LANES), ALL, 0, 0, tiled=True)
    arrived = arrived.reshape(devices, rows, LANES)
    top_sum = jnp.sum(arrived[:, : rows - TILE], axis=0)
    side_sum = jnp.sum(
        arrived[:, rows - TILE :].reshape(count_x, count_y * count_z, TILE, LANES), axis=1
    )
    side = side_sum[:, : 2 * share].reshape(count_x, 2, share, LANES)
    side = jnp.swapaxes(side, 0, 1).reshape(2, depth_block, 1, LANES)
    top = lax.all_gather(top_sum, "gz", axis=0)
    top = jnp.swapaxes(top.reshape(count_z, 2, block_x // count_z, LANES), 0, 1)
    top = top.reshape(2, 1, block_x, LANES)
    return jnp.stack(
        [
            exchange_grad[0] + top[0],
            exchange_grad[1] + top[1] + side[0],
            exchange_grad[2] + side[1],
        ]
    )


def solution(mesh):
    placed = (
        P(None, "gz", "gx", "gy"),
        P("gz", "gx", "gy"),
        P("gx", ("gy", "gz")),
        P("gy", "gz"),
        P(None, None, ("gx", "gy", "gz"), None),
        P(None, None, ("gy", "gz"), None),
    )
    return jax.shard_map(
        on_device, mesh=mesh, in_specs=placed, out_specs=P(None, "gz", "gx", "gy"), check_vma=False
    )
```

```python
import functools
import math

import jax
import jax.numpy as jnp
import ml_dtypes
import numpy as np
from jax import lax
from jax.experimental import pallas as pl
from jax.experimental.pallas import tpu as pltpu
from jax.sharding import PartitionSpec as P

LANES = 128
TILE = 8
INNER = 256
ALL = ("gx", "gy", "gz")
f32 = jnp.float32
bf16 = jnp.bfloat16
MIB = 1024 * 1024
QUAD = 4
SMEM = pl.BlockSpec(memory_space=pltpu.SMEM)
VMEM = pl.BlockSpec(memory_space=pltpu.VMEM)
HBM = pl.BlockSpec(memory_space=pltpu.HBM)


def whole_log(count):
    return count.bit_length() - 1


def split(values):
    high = values.astype(bf16)
    return high, (values - high.astype(f32)).astype(bf16)


def dot3(left, right):
    high, low = split(left)
    def one(a, b):
        return lax.dot_general(a, b, (((1,), (0,)), ((), ())), preferred_element_type=f32)
    return one(high, right[0]) + one(low, right[0]) + one(high, right[1])


def from_hbm(values):
    return pltpu.with_memory_space_constraint(values, pltpu.HBM)


def call(
    body,
    name,
    shape,
    limit,
    microseconds,
    operands,
    in_hbm=(),
    in_vmem=(),
    scratch=(),
    refs=(),
    out_refs=(),
    aliases=(),
):
    shapes = shape if isinstance(shape, list) else [shape]
    moved = sum(4 * math.prod(each) for each in shapes)
    moved += sum(x.size * x.dtype.itemsize for x in operands)
    results = pl.pallas_call(
        body,
        out_shape=[
            pltpu.HBM(each, f32)
            if i in in_hbm
            else pltpu.VMEM(each, bf16)
            if i in in_vmem
            else jax.ShapeDtypeStruct(each, f32)
            for i, each in enumerate(shapes)
        ],
        in_specs=[
            SMEM if x.shape == (1,) else HBM if i in refs else VMEM
            for i, x in enumerate(operands)
        ],
        out_specs=[HBM if i in out_refs else VMEM for i in range(len(shapes))],
        input_output_aliases=dict(aliases),
        scratch_shapes=list(scratch),
        compiler_params=pltpu.CompilerParams(vmem_limit_bytes=limit * MIB),
        cost_estimate=pl.CostEstimate(
            flops=int(microseconds * 1e9), bytes_accessed=moved, transcendentals=0
        ),
        name=name,
    )(*operands)
    return results if isinstance(shape, list) else results[0]


def transform_tables(extent, size):
    x = np.arange(extent)
    angle = (np.outer(x, np.arange(INNER)) % size) * (2.0 * math.pi / size)
    forward = np.concatenate([np.cos(angle), np.sin(angle)], 0).astype(np.float32)
    backward = np.concatenate([np.cos(angle).T, np.sin(angle).T], 0).astype(np.float32)

    def parts(table):
        high = table.astype(ml_dtypes.bfloat16)
        return high, (table - high.astype(np.float32)).astype(ml_dtypes.bfloat16)

    outer = size // INNER
    turn = (np.outer(np.arange(outer), x) % outer) * (2.0 * math.pi / outer)
    turns = np.stack([np.cos(turn), np.sin(turn)]).astype(np.float32)
    return parts(forward), parts(backward), turns


def phases(first, second, size):
    angle = (first * second % size).astype(f32) * (2.0 * math.pi / size)
    return jnp.cos(angle), jnp.sin(angle)


def image_kernel(
    counts, gathered, y_table, z_table, fh, fl, bh, bl, turns, top, side, y_back, z_back, out
):
    count_x, count_y, count_z, top_rows = counts
    group = count_y * count_z
    half = LANES // 2
    kys = top.shape[2]
    kzs = side.shape[2]
    forward = (fh[...], fl[...])
    backward = (bh[...], bl[...])

    blocks = [
        gathered[g * group : (g + 1) * group, 0:top_rows, :].reshape(group * top_rows, LANES)
        for g in range(count_x)
    ]
    mixed = dot3(y_table[...], split(jnp.concatenate(blocks, axis=1)))
    low_half, high_half = mixed[: 2 * kys], mixed[2 * kys :]
    lane = lax.broadcasted_iota(jnp.int32, (2 * kys, LANES), 1)
    pieces = []
    for g in range(0, count_x, 2):
        a = slice(g * LANES, (g + 1) * LANES)
        b = slice((g + 1) * LANES, (g + 2) * LANES)
        pieces.append(
            jnp.where(
                lane < half,
                low_half[:, a] + pltpu.roll(high_half[:, a], half, 1),
                pltpu.roll(low_half[:, b], half, 1) + high_half[:, b],
            )
        )
    top_lines = jnp.concatenate(pieces, axis=1)

    side_blocks = []
    for y in range(count_y):
        rows = [
            gathered[(x * count_y + y) * count_z + z, top_rows : top_rows + TILE, :]
            for x in range(count_x)
            for z in range(count_z)
        ]
        side_blocks.append(jnp.concatenate(rows, axis=0))
    side_lines = dot3(z_table[...], split(jnp.concatenate(side_blocks, axis=1)))

    real = jnp.concatenate([top_lines[:kys], side_lines[:kzs]], axis=0)
    imag = jnp.concatenate([top_lines[kys:], side_lines[kzs:]], axis=0)
    rows = kys + kzs
    total_real = total_imag = None
    for b in range(turns.shape[1]):
        cosine, sine = turns[0, b : b + 1, :], turns[1, b : b + 1, :]
        turned_real = real * cosine + imag * sine
        turned_imag = imag * cosine - real * sine
        waves = dot3(
            jnp.concatenate(
                [
                    jnp.concatenate([turned_real, turned_imag], axis=1),
                    jnp.concatenate([turned_imag, -turned_real], axis=1),
                ],
                axis=0,
            ),
            forward,
        )
        wave_real, wave_imag = waves[:rows], waves[rows:]
        columns = slice(b * INNER, (b + 1) * INNER)
        weighted_real, weighted_imag = [], []
        for c in range(2):
            for kernel, part in ((top, slice(0, kys)), (side, slice(kys, rows))):
                kernel_real, kernel_imag = kernel[c, 0, :, columns], kernel[c, 1, :, columns]
                weighted_real.append(
                    kernel_real * wave_real[part] + kernel_imag * wave_imag[part]
                )
                weighted_imag.append(
                    kernel_real * wave_imag[part] - kernel_imag * wave_real[part]
                )
        weighted_real = jnp.concatenate(weighted_real, axis=0)
        weighted_imag = jnp.concatenate(weighted_imag, axis=0)
        back = dot3(
            jnp.concatenate(
                [
                    jnp.concatenate([weighted_real, -weighted_imag], axis=1),
                    jnp.concatenate([weighted_imag, weighted_real], axis=1),
                ],
                axis=0,
            ),
            backward,
        )
        back_real, back_imag = back[: 2 * rows], back[2 * rows :]
        if b == 0:
            total_real, total_imag = back_real, back_imag
        else:
            total_real = total_real + (back_real * cosine - back_imag * sine)
            total_imag = total_imag + (back_real * sine + back_imag * cosine)

    y_parts = split(y_back[...])
    depth_rows = []
    quarter = (out.shape[1] - TILE) // 2
    block_x = quarter * count_z
    for c in range(2):
        start = c * rows
        lines = jnp.concatenate(
            [total_real[start : start + kys], total_imag[start : start + kys]], axis=0
        )
        image = dot3(lines.T, y_parts)
        for x in range(count_x):
            for y in range(count_y):
                for z in range(count_z):
                    first = x * block_x + z * quarter
                    out[
                        (x * count_y + y) * count_z + z, c * quarter : (c + 1) * quarter, :
                    ] = image[first : first + quarter, y * LANES : (y + 1) * LANES]
        depth_rows.append(total_real[start + kys : start + rows])
        depth_rows.append(total_imag[start + kys : start + rows])
    side_image = dot3(z_back[...], split(jnp.concatenate(depth_rows, axis=0)))
    for y in range(count_y):
        for z in range(count_z):
            block = side_image[z * TILE : (z + 1) * TILE, y * LANES : (y + 1) * LANES]
            for x in range(count_x):
                out[(x * count_y + y) * count_z + z, 2 * quarter :, :] = block


def image_parts(gathered, top_kernel, side_kernel, counts, block_x, top_rows, depth_block):
    count_x, count_y, count_z = counts
    group = count_y * count_z
    here = [lax.axis_index(axis) for axis in ALL]
    kys, size = top_kernel.shape[2:]
    kzs = side_kernel.shape[2]
    depth_size = kzs * group
    extent = count_y * LANES
    share = depth_block // count_x
    block_y = top_rows * 2

    ky = ((here[0] * count_y + here[1]) * count_z + here[2]) * kys + lax.iota(jnp.int32, kys)
    kz = (here[1] * count_z + here[2]) * kzs + lax.iota(jnp.int32, kzs)

    row = lax.iota(jnp.int32, group * top_rows)
    y_tables = []
    for h in range(2):
        y = row // top_rows * block_y + h * top_rows + row % top_rows
        cosine, sine = phases(ky[:, None], y[None, :], size)
        y_tables += [cosine, -sine]
    y_table = jnp.concatenate(y_tables, axis=0)

    row = lax.iota(jnp.int32, count_x * count_z * TILE)
    inside = row % TILE
    z = row // TILE % count_z * depth_block + row // (TILE * count_z) * share + inside
    cosine, sine = phases(kz[:, None], z[None, :], depth_size)
    z_table = jnp.where((inside < share)[None, :], jnp.concatenate([cosine, -sine], axis=0), 0.0)

    cosine, sine = phases(ky[:, None], lax.iota(jnp.int32, extent)[None, :], size)
    y_back = jnp.concatenate([cosine, -sine], axis=0) * (1.0 / (size * size))

    row = lax.iota(jnp.int32, count_z * TILE)
    z = row // TILE * depth_block + here[0] * share + row % TILE % share
    cosine, sine = phases(z[:, None], kz[None, :], depth_size)
    both = jnp.concatenate([cosine, -sine], axis=1) * (1.0 / (size * depth_size))
    component = (row % TILE // share)[:, None]
    z_back = jnp.concatenate(
        [jnp.where(component == 0, both, 0.0), jnp.where(component == 1, both, 0.0)], axis=1
    )

    forward, backward, turns = transform_tables(extent, size)
    out_rows = 2 * (block_x // count_z) + TILE
    return pl.pallas_call(
        functools.partial(image_kernel, counts + (top_rows,)),
        out_shape=jax.ShapeDtypeStruct((count_x * group, out_rows, LANES), f32),
        compiler_params=pltpu.CompilerParams(vmem_limit_bytes=56 * 1024 * 1024),
        name="images",
    )(
        gathered,
        y_table,
        z_table,
        *(jnp.asarray(t) for t in forward + backward),
        jnp.asarray(turns),
        top_kernel,
        side_kernel,
        y_back,
        z_back,
    )


def begin(semaphores, pairs):
    started = [
        pltpu.make_async_copy(source, target, semaphores.at[i])
        for i, (source, target) in enumerate(pairs)
    ]
    for copy in started:
        copy.start()
    return started


def faces_kernel(
    magnetization, stiffness, z_first, z_last, x_first, x_last, y_faces, m, s, loading
):
    depth, across = stiffness.shape[:2]
    loads = begin(
        loading, [(stiffness, s)] + [(magnetization.at[c], m.at[c]) for c in range(3)]
    )
    lane = lax.broadcasted_iota(jnp.int32, (across, LANES), 1)
    pair = (lane + 1 & (LANES - 1)) >> 1
    sides = jnp.zeros((across, LANES), f32)
    for field in (3, 0, 1, 2):
        loads[(field + 1) % 4].wait()
        ref = s if field == 3 else m.at[field]
        z_first[field] = ref[0]
        z_last[field] = ref[depth - 1]
        x_first[field] = ref[:, 0, :]
        x_last[field] = ref[:, across - 1, :]
        for z in range(depth):
            column = field * depth + z
            turned = pltpu.roll(ref[z], 2 * column, 1) if column else ref[z]
            sides = jnp.where(pair == column, turned, sides)
    y_faces[...] = sides


def twice_weight(a, b):
    total = a + b
    inverse = pl.reciprocal(total, approx=True)
    return 4.0 * a * b * (inverse * (2.0 - total * inverse))


def exchange_kernel(
    counts,
    here,
    magnetization_from,
    stiffness_from,
    y_faces_from,
    z_next,
    z_before,
    x_next,
    x_before,
    y_next,
    y_before,
    out,
    m,
    s,
    y_faces,
    loading,
):
    depth, across = s.shape[:2]
    chunk = depth // 4
    pairs = [(y_faces_from, y_faces)]
    for k in range(4):
        layers = pl.ds(k * chunk, chunk)
        pairs.append((stiffness_from.at[layers], s.at[layers]))
        pairs.append((magnetization_from.at[:, layers], m.at[:, layers]))
    loads = begin(loading, pairs)

    count_x, count_y, count_z = counts
    at_z = here[0] % count_z
    at_y = here[0] // count_z % count_y
    at_x = here[0] // (count_z * count_y)

    def inside(condition, values):
        return jnp.where(condition, values, 0.0)

    lane = lax.broadcasted_iota(jnp.int32, (across, LANES), 1)
    row = lax.broadcasted_iota(jnp.int32, (across, LANES), 0)
    first_lane, last_lane, last_row = lane == 0, lane == LANES - 1, row == across - 1

    loads[0].wait()
    own = y_faces[...]
    even = (lane & 1) == 0
    field = (lane + 1 & (LANES - 1)) >> whole_log(2 * depth)
    halo = jnp.where(
        even, pltpu.roll(y_before[...], 1, 1), pltpu.roll(y_next[...], LANES - 1, 1)
    )
    present = jnp.where(even, at_y, count_y - 1 - at_y) > 0
    weight = twice_weight(
        jnp.where(field == 3, own, 1.0),
        jnp.where(field == 3, jnp.where(present, halo, 0.0), 1.0),
    )
    spread = pltpu.roll(weight, LANES - 6 * depth, 1)
    for c in (1, 2):
        spread = jnp.where(
            field == c, pltpu.roll(weight, LANES - (3 - c) * 2 * depth, 1), spread
        )
    sides = spread * (own - halo)
    outer = first_lane | last_lane

    for copy in loads[1:3]:
        copy.wait()
    below_weight = twice_weight(inside(at_z > 0, z_before[3]), s[0])
    below = [below_weight * (z_before[c] - m[c, 0]) for c in range(3)]
    for z in range(depth):
        if z % chunk == chunk - 1:
            k = 1 + 2 * (z // chunk + 1)
            for copy in loads[k : k + 2]:
                copy.wait()
        centre = s[z]
        above = s[z + 1] if z + 1 < depth else inside(at_z < count_z - 1, z_next[3])
        weight_z = twice_weight(centre, above)
        weight_x = jnp.where(
            last_row, 0.0, twice_weight(centre, pltpu.roll(centre, across - 1, 0))
        )
        weight_y = jnp.where(
            last_lane, 0.0, twice_weight(centre, pltpu.roll(centre, LANES - 1, 1))
        )
        for c in range(3):
            column = c * depth + z
            values = m[c, z]
            upper = m[c, z + 1] if z + 1 < depth else z_next[c]
            up = weight_z * (values - upper)
            flux_x = weight_x * (values - pltpu.roll(values, across - 1, 0))
            flux_y = weight_y * (values - pltpu.roll(values, LANES - 1, 1))
            total = (up - below[c]) + (flux_x - pltpu.roll(flux_x, 1, 0))
            total = total + (flux_y - pltpu.roll(flux_y, 1, 1))
            both = pltpu.roll(sides, LANES - 2 * column, 1) if column else sides
            out[c, z] = jnp.where(outer, total + both, total)
            below[c] = up
    for edge_row, halo, present in (
        (across - 1, x_next, at_x < count_x - 1),
        (0, x_before, at_x > 0),
    ):
        weight = twice_weight(s[:, edge_row, :], inside(present, halo[3]))
        for c in range(3):
            out[c, :, edge_row, :] += weight * (m[c, :, edge_row, :] - halo[c])


def ring(block, axis, distance):
    count = lax.axis_size(axis)
    return lax.ppermute(block, axis, [(i, (i + distance) % count) for i in range(count)])


def faces_of(magnetization, stiffness):
    depth, across, along = stiffness.shape
    return call(
        faces_kernel,
        "faces",
        [
            (4, across, along),
            (4, across, along),
            (4, depth, along),
            (4, depth, along),
            (across, LANES),
        ],
        8,
        2.0,
        (from_hbm(magnetization), from_hbm(stiffness)),
        refs=(0, 1),
        scratch=[
            pltpu.VMEM(magnetization.shape, f32),
            pltpu.VMEM(stiffness.shape, f32),
            pltpu.SemaphoreType.DMA((4,)),
        ],
    )


def halos_zy(z_first, z_last, y_faces):
    y_next = ring(y_faces, "gy", -1)
    y_before = y_next if lax.axis_size("gy") == 2 else ring(y_faces, "gy", 1)
    return ring(z_first, "gz", -1), ring(z_last, "gz", 1), y_next, y_before, y_faces


def halos_x(x_first, x_last):
    return ring(x_first, "gx", -1), ring(x_last, "gx", 1)


def exchange_of(counts, index, magnetization, stiffness, zy, x):
    z_next, z_before, y_next, y_before, y_faces = zy
    fetched = (magnetization, stiffness, y_faces)
    return call(
        functools.partial(exchange_kernel, counts),
        "exchange",
        magnetization.shape,
        8,
        5.0,
        (
            index,
            *(from_hbm(array) for array in fetched),
            z_next,
            z_before,
            *x,
            y_next,
            y_before,
        ),
        refs=(1, 2, 3),
        scratch=[pltpu.VMEM(array.shape, f32) for array in fetched]
        + [pltpu.SemaphoreType.DMA((9,))],
    )


def cos_sin(steps, size):
    quarter = steps >> whole_log(size // 4)
    angle = ((steps & (size // 4 - 1)) - size // 8).astype(f32) * (2.0 * math.pi / size)
    square = angle * angle
    sine = cosine = 0.0
    for k in range(5, -1, -1):
        sine = sine * square + (-1) ** k / math.factorial(2 * k + 1)
        cosine = cosine * square + (-1) ** k / math.factorial(2 * k)
    sine = sine * angle
    first, second = (cosine - sine) * math.sqrt(0.5), (cosine + sine) * math.sqrt(0.5)
    odd = (quarter & 1) == 1
    real = jnp.where(odd, -second, first)
    imag = jnp.where(odd, first, second)
    back = quarter >= 2
    return jnp.where(back, -real, real), jnp.where(back, -imag, imag)


def halves_of(table):
    table = table.astype(np.float32)
    high = table.astype(ml_dtypes.bfloat16)
    return high, (table - high.astype(np.float32)).astype(ml_dtypes.bfloat16)


def narrow_tables(extent, size):
    length = 2 * extent
    ratio = size // length
    m = np.arange(size)
    lags = np.arange(1, extent)
    window = 1.0 + 2.0 * np.cos(np.outer(m, lags) % size * (2.0 * math.pi / size)).sum(axis=1)
    i = np.arange(INNER)
    place = np.array([0, INNER])[:, None, None] + i[:, None] - ratio * np.arange(length)[None, :]
    tiles = np.stack(halves_of(window[place % size] / length), axis=1)
    return tiles, transform_table(length)


def transform_table(size):
    i = np.arange(INNER)
    angle = np.outer(i, i) * (2.0 * math.pi / size)
    return np.stack(halves_of(np.concatenate([np.cos(angle), np.sin(angle)], axis=0)))


def pair_order(planes, per_plane):
    return [plane * per_plane + p for p in range(per_plane) for plane in reversed(range(planes))]


def y_table_of(counts, here, kys, size):
    group = counts[1] * counts[2]
    top_rows = LANES // group
    ky = here[0] * kys + lax.broadcasted_iota(jnp.int32, (kys, LANES), 0)
    lane = lax.broadcasted_iota(jnp.int32, (kys, LANES), 1)
    odd = (lane >> whole_log(LANES // 2)) ^ (here[0] & 1)
    pair = lane >> whole_log(top_rows) & (group // 2 - 1)
    phases_of = []
    for h in range(2):
        y = (2 * pair + odd) * (2 * top_rows) + h * top_rows + (lane & (top_rows - 1))
        cosine, sine = cos_sin(ky * y & (size - 1), size)
        phases_of += [cosine, -sine]
    high, low = split(jnp.concatenate(phases_of, axis=0))
    return jnp.concatenate([high, low, high], axis=1)


def narrow_kernel(top, side, tiles, top_out, side_out):
    count = top.shape[3] // INNER
    parts = top_out.shape[3] // INNER
    step = count // parts
    columns_of = tiles.shape[3] // LANES
    ratio = top.shape[3] // top_out.shape[3]

    def tile_of(place, k):
        first = -(place // 2) * (2 * INNER // ratio // LANES)
        columns = [(first + i) % columns_of * LANES for i in range(INNER // LANES)]
        return jnp.concatenate(
            [tiles[place % 2, k, :, column : column + LANES] for column in columns], axis=1
        )

    top_rows, side_rows = top.shape[2], side.shape[2]
    totals = [None] * parts
    for k in range(count):
        columns = slice(k * INNER, (k + 1) * INNER)
        lines = jnp.concatenate(
            [
                top[:, :, :, columns].reshape(4 * top_rows, INNER),
                side[:, :, :, columns].reshape(4 * side_rows, INNER),
            ],
            axis=0,
        )
        high, low = split(lines)
        lines = jnp.concatenate([high, low, high], axis=1)
        for part in range(parts):
            high, low = (tile_of((k - part * step) % count, i) for i in range(2))
            term = product(lines, jnp.concatenate([high, high, low], axis=0))
            totals[part] = term if k == 0 else totals[part] + term
    for part in range(parts):
        columns = slice(part * INNER, (part + 1) * INNER)
        top_out[:, :, :, columns] = totals[part][: 4 * top_rows].reshape(2, 2, top_rows, INNER)
        side_out[:, :, :, columns] = totals[part][4 * top_rows :].reshape(2, 2, side_rows, INNER)


def product(left, right, contracted=0):
    return lax.dot_general(
        left, right, (((1,), (contracted,)), ((), ())), preferred_element_type=f32
    )


def dot3_with(values, table):
    high, low = split(values)
    first = product(
        jnp.concatenate([high, low], axis=1), jnp.concatenate([table[0], table[0]], axis=0)
    )
    return first + product(high, table[1])


def there_and_back(real, imag, kernel, table):
    rows, extent = real.shape
    sign = jnp.where(lax.broadcasted_iota(jnp.int32, (1, extent), 1) & 1 == 0, 1.0, -1.0)
    lines = jnp.concatenate(
        [jnp.concatenate([real, imag], axis=1), jnp.concatenate([imag, -real], axis=1)], axis=0
    )
    signs = jnp.concatenate([sign, sign], axis=1)
    waves = dot3_with(jnp.concatenate([lines, lines * signs], axis=0), table)
    totals = []
    for b in range(2):
        wave_real, wave_imag = (
            waves[(2 * b + k) * rows : (2 * b + k + 1) * rows] for k in range(2)
        )
        columns = slice(b * INNER, (b + 1) * INNER)
        weighted = ([], [])
        for c in range(2):
            kernel_real, kernel_imag = kernel[c, 0, :, columns], kernel[c, 1, :, columns]
            weighted[0].append(kernel_real * wave_real + kernel_imag * wave_imag)
            weighted[1].append(kernel_real * wave_imag - kernel_imag * wave_real)
        a, b = (jnp.concatenate(part, axis=0) for part in weighted)
        lines = jnp.concatenate(
            [jnp.concatenate([a, -b], axis=1), jnp.concatenate([b, a], axis=1)], axis=0
        )
        totals.append(dot3_with(lines, table))
    total = totals[0] + totals[1] * sign
    return total[: 2 * rows], total[2 * rows :]


def lines_kernel(counts, here, gathered, swapped, table, kernel, out, received):
    count_x, count_y, count_z = counts
    group = count_y * count_z
    top_rows = LANES // group
    half = LANES // 2
    kys = kernel.shape[2]
    y_table = y_table_of(counts, here, kys, INNER * TILE)
    pairs = pair_order(count_x, group // 2)
    for k, part in enumerate((gathered, swapped)):
        for member in range(part.shape[0]):
            g, place = divmod(member, group // 2)
            for j in range(top_rows // QUAD):
                row = (k * group // 2 + place) * top_rows + j * QUAD
                received[g, row : row + QUAD, :] = part[pairs.index(member), j]
    blocks = [received[g] for g in range(count_x)]
    high, low = split(jnp.concatenate(blocks, axis=1))
    mixed = product(y_table, jnp.concatenate([high, high, low], axis=0))
    low_half, high_half = mixed[: 2 * kys], mixed[2 * kys :]
    lane = lax.broadcasted_iota(jnp.int32, (2 * kys, LANES), 1)
    pieces = []
    for g in range(0, count_x, 2):
        a = slice(g * LANES, (g + 1) * LANES)
        b = slice((g + 1) * LANES, (g + 2) * LANES)
        pieces.append(
            jnp.where(
                lane < half,
                low_half[:, a] + pltpu.roll(high_half[:, a], half, 1),
                pltpu.roll(low_half[:, b], half, 1) + high_half[:, b],
            )
        )
    lines = jnp.concatenate(pieces, axis=1)
    for k, part in enumerate(there_and_back(lines[:kys], lines[kys:], kernel, table)):
        out[:, k * TILE : (k + 1) * TILE, :] = part.T.reshape(count_x * group, TILE, LANES)


def side_kernel_body(
    counts,
    here,
    gathered,
    swapped,
    spectrum,
    kernel,
    later_from,
    mine,
    other,
    later,
    received,
    loading,
):
    copies = begin(loading, [(later_from, later)])
    count_x, count_y, count_z = counts
    depth_block = mine.shape[1]
    last = gathered.shape[1] - 1
    kzs, length = kernel.shape[2], INNER * TILE
    size = kzs * count_y * count_z
    columns = count_x * count_z * QUAD
    kz = here[0] * kzs + lax.broadcasted_iota(jnp.int32, (kzs, columns), 0)
    column = lax.broadcasted_iota(jnp.int32, (kzs, columns), 1)
    pair = column >> whole_log(QUAD) & (count_z // 2 - 1)
    odd = (column >> whole_log(columns // 2)) ^ (here[0] & 1)
    z = (2 * pair + odd) * depth_block + (column & (QUAD - 1))
    z = z + (column >> whole_log(QUAD * count_z // 2) & (count_x - 1)) * QUAD
    cosine, sine = cos_sin(kz * z & (size - 1), size)
    table = jnp.concatenate([cosine, -sine], axis=0)
    pairs = pair_order(count_x, count_y * count_z // 2)
    for k, part in enumerate((gathered, swapped)):
        for x in range(count_x):
            for y in range(count_y):
                for pair in range(count_z // 2):
                    row = ((k * count_x + x) * count_z // 2 + pair) * QUAD
                    member = (x * count_y + y) * count_z // 2 + pair
                    received[y, row : row + QUAD, :] = part[pairs.index(member), last]
    blocks = [received[y] for y in range(count_y)]
    lines = dot3(table, split(jnp.concatenate(blocks, axis=1)))

    real, imag = there_and_back(lines[:kzs], lines[kzs:], kernel, spectrum)

    rows = depth_block * count_z
    z = lax.broadcasted_iota(jnp.int32, (rows, 2 * kzs), 0)
    column = lax.broadcasted_iota(jnp.int32, (rows, 2 * kzs), 1)
    cosine, sine = cos_sin((here[0] * kzs + (column & (kzs - 1))) * z & (size - 1), size)
    table = jnp.where(column < kzs, cosine, -sine) * (1.0 / (size * length))
    even = (here[0] & 1) == 0
    lines = [jnp.concatenate([part[:kzs] for part in (real, imag)], axis=0)]
    lines.append(jnp.concatenate([part[kzs:] for part in (real, imag)], axis=0))
    for out, (a, b) in ((mine, lines), (other, lines[::-1])):
        image = dot3(table, split(jnp.where(even, a, b)))
        for y in range(count_y):
            for z in range(count_z):
                out[y * count_z + z] = image[
                    z * depth_block : (z + 1) * depth_block, y * LANES : (y + 1) * LANES
                ]
    copies[0].wait()


def rows_kernel(counts, arrived, mine, other, table, out):
    count_y, count_z = counts[1:]
    out[:, 2 * TILE :, :] = mine[...] + other[...]
    per_turn = INNER * 2 // LANES
    step = arrived.shape[0] // per_turn
    size = step * INNER
    half = LANES // 2
    lane = lax.broadcasted_iota(jnp.int32, (2 * TILE, LANES), 1)
    upper, lower = [], []
    for b in range(step):
        parts = ([], [])
        for pair in range(b * per_turn, (b + 1) * per_turn, 2):
            first, second = arrived[pair], arrived[pair + 1]
            spectra = (
                jnp.where(lane < half, first, pltpu.roll(second, half, 1)),
                jnp.where(lane < half, pltpu.roll(first, half, 1), second),
            )
            for k in range(2):
                parts[k].append(
                    jnp.concatenate(
                        [spectrum[k * TILE : (k + 1) * TILE] for spectrum in spectra], axis=0
                    )
                )
        real, imag = (jnp.concatenate(part, axis=1) for part in parts)
        upper.append(jnp.concatenate([real, -imag], axis=1))
        lower.append(jnp.concatenate([imag, real], axis=1))
    lines = dot3_with(jnp.concatenate(upper + lower, axis=0), table)
    y = lax.broadcasted_iota(jnp.int32, (1, INNER), 1) & (step - 1)
    total = None
    for b in range(step):
        cosine, sine = cos_sin(y * b & (step - 1), step)
        real, imag = (
            lines[(k * step + b) * 2 * TILE : (k * step + b + 1) * 2 * TILE] for k in range(2)
        )
        term = real * cosine - imag * sine if b else real
        total = term if b == 0 else total + term
    total = total * (1.0 / (size * size))
    for y in range(count_y):
        for z in range(count_z):
            out[y * count_z + z, 0 : 2 * TILE, :] = total[:, y * LANES : (y + 1) * LANES]


def sum_kernel(exchange_grad, arrived, out, result, sending):
    depth = exchange_grad.shape[1]
    group = arrived.shape[0]
    sends = []

    def send(c):
        sends.append(pltpu.make_async_copy(result.at[c], out.at[c], sending.at[c]))
        sends[-1].start()

    def top(c):
        return arrived[:, c * TILE : (c + 1) * TILE, :].reshape(group * TILE, LANES)

    def side(c):
        total = arrived[c, 2 * TILE :, :]
        for p in range(c + 2, group, 2):
            total = total + arrived[p, 2 * TILE :, :]
        return total

    image = top(0)
    for z in range(depth):
        result[0, z] = exchange_grad[0, z] + image
    send(0)
    column = side(1)
    for z in range(depth):
        result[2, z] = exchange_grad[2, z] + column[z : z + 1]
    send(2)
    image, column = top(1), side(0)
    for z in range(depth):
        result[1, z] = exchange_grad[1, z] + image + column[z : z + 1]
    send(1)
    for copy in sends:
        copy.wait()


def residual_blocks(residual_top, residual_side, copies, share, quads):
    block_x, block_y = residual_top.shape
    top_rows = block_y // 2

    def body(at_x, top, side, out):
        piece = jnp.concatenate([top[0:top_rows, :], top[top_rows:, :]], axis=1)
        part = side[pl.ds(at_x[0] * share, share), :]
        if not quads:
            part = jnp.concatenate([part, jnp.zeros((TILE - share, LANES), f32)], axis=0)
        for copy in range(copies):
            if quads:
                for j in range(top_rows // QUAD):
                    out[copy, j] = piece[j * QUAD : (j + 1) * QUAD]
                out[copy, top_rows // QUAD] = part
            else:
                out[copy, 0:top_rows, :] = piece
                out[copy, top_rows:, :] = part

    shape = (top_rows // QUAD + 1, QUAD) if quads else (top_rows + TILE,)
    return call(
        body,
        "pack",
        (copies, *shape, LANES),
        60,
        0.8,
        (lax.axis_index("gx").reshape(1), residual_top.T, residual_side.T),
    )


def fast_on_device(magnetization, stiffness, residual_top, residual_side, top_kernel, side_kernel):
    counts = tuple(lax.axis_size(axis) for axis in ALL)
    count_x, count_y, count_z = counts
    group = count_y * count_z
    devices = count_x * group
    block_x, block_y = residual_top.shape
    depth_block = stiffness.shape[0]
    top_rows = block_y // 2
    kys, size = top_kernel.shape[2:]
    kzs = side_kernel.shape[2]
    extent = count_x * block_x
    here = [lax.axis_index(axis) for axis in ALL]
    plane_index = here[1] * count_z + here[2]
    index = (here[0] * group + plane_index).reshape(1)
    plane_index = plane_index.reshape(1)
    tiles, table = (jnp.asarray(values) for values in narrow_tables(extent, size))
    rows_table = jnp.asarray(transform_table(size))

    pairs = pair_order(count_x, group // 2)
    parities = [[2 * pair + parity for pair in pairs] for parity in range(2)]
    sent = residual_blocks(
        residual_top, residual_side, devices // 2, depth_block // count_x, True
    )
    gathered = lax.all_to_all(
        sent, ALL, 0, 0, tiled=True, axis_index_groups=parities
    )
    z_first, z_last, x_first, x_last, y_faces = faces_of(magnetization, stiffness)
    narrowed = call(
        narrow_kernel,
        "narrow",
        [(2, 2, kys, 2 * extent), (2, 2, kzs, 2 * extent)],
        16,
        2.5,
        (top_kernel, side_kernel, tiles),
    )
    gathered, x_first, x_last, y_faces, narrowed = lax.optimization_barrier(
        (gathered, x_first, x_last, y_faces, narrowed)
    )
    top_spectra, side_spectra = narrowed
    swapped = lax.ppermute(gathered, "gz", [(i, i ^ 1) for i in range(count_z)])
    zy = halos_zy(z_first, z_last, y_faces)

    lines = call(
        functools.partial(lines_kernel, counts),
        "lines",
        (devices, 2 * TILE, LANES),
        16,
        2.2,
        (index, gathered, swapped, table, top_spectra),
        scratch=[pltpu.VMEM((count_x, LANES, LANES), f32)],
    )
    arrived = lax.all_to_all(lines, ALL, 0, 0, tiled=True)
    lines, x_first, x_last = lax.optimization_barrier((lines, x_first, x_last))
    x = halos_x(x_first, x_last)
    mine, other, rows_table = call(
        functools.partial(side_kernel_body, counts),
        "side",
        [(group, depth_block, LANES), (group, depth_block, LANES), rows_table.shape],
        8,
        2.0,
        (plane_index, gathered, swapped, table, side_spectra, from_hbm(rows_table)),
        in_vmem=(2,),
        refs=(5,),
        scratch=[
            pltpu.VMEM((count_y, count_x * count_z * QUAD, LANES), f32),
            pltpu.SemaphoreType.DMA((1,)),
        ],
    )
    other = lax.ppermute(other, "gz", [(i, i ^ 1) for i in range(count_z)])
    arrived, mine, other, rows_table = lax.optimization_barrier(
        (arrived, mine, other, rows_table)
    )
    rows = call(
        functools.partial(rows_kernel, counts),
        "rows",
        (group, 2 * TILE + depth_block, LANES),
        8,
        1.1,
        (arrived, mine, other, rows_table),
    )
    _, zy, x = lax.optimization_barrier((rows, zy, x))
    arrived = lax.all_to_all(rows, ("gy", "gz"), 0, 0, tiled=True)
    exchange_grad = exchange_of(counts, index, magnetization, stiffness, zy, x)
    return call(
        sum_kernel,
        "gradient",
        magnetization.shape,
        16,
        1.2,
        (exchange_grad, arrived),
        out_refs=(0,),
        scratch=[pltpu.VMEM(magnetization.shape, f32), pltpu.SemaphoreType.DMA((3,))],
    )


def fits(counts, stiffness, residual_top, residual_side, top_kernel, side_kernel):
    count_x, count_y, count_z = counts
    block_x, block_y = residual_top.shape
    group = count_y * count_z
    return (
        2 * block_x == LANES
        and 2 * top_kernel.shape[2] == LANES
        and stiffness.shape[2] == LANES
        and block_x == group * TILE
        and block_y * group == count_x * block_x == INNER
        and count_y * LANES == INNER
        and block_y % 16 == 0
        and count_x % 2 == 0
        and count_z % 2 == 0
        and (count_x * group) % (2 * top_kernel.shape[3] // INNER) == 0
        and INNER == top_kernel.shape[2] * count_z
        and top_kernel.shape[3] == TILE * INNER == side_kernel.shape[3]
        and INNER == 2 * LANES
        and stiffness.shape[0] % 16 == 0
        and stiffness.shape[0] == count_x * QUAD
        and side_kernel.shape[2] % 16 == 0
        and all(
            count & (count - 1) == 0
            for count in (group, count_x, count_z, top_kernel.shape[3], side_kernel.shape[2])
        )
    )


def on_device(magnetization, stiffness, residual_top, residual_side, top_kernel, side_kernel):
    counts = tuple(lax.axis_size(axis) for axis in ALL)
    count_x, count_y, count_z = counts
    if fits(counts, stiffness, residual_top, residual_side, top_kernel, side_kernel):
        return fast_on_device(
            magnetization, stiffness, residual_top, residual_side, top_kernel, side_kernel
        )
    devices = count_x * count_y * count_z
    depth_block = stiffness.shape[0]
    block_x, block_y = residual_top.shape
    top_rows = block_y // 2
    share = depth_block // count_x

    sent = residual_blocks(residual_top, residual_side, devices, share, False)
    rows = sent.shape[1]
    gathered = lax.all_to_all(sent, ALL, 0, 0, tiled=True)
    index = (
        (lax.axis_index("gx") * count_y + lax.axis_index("gy")) * count_z + lax.axis_index("gz")
    ).reshape(1)
    z_first, z_last, x_first, x_last, y_faces = faces_of(magnetization, stiffness)
    exchange_grad = exchange_of(
        counts,
        index,
        magnetization,
        stiffness,
        halos_zy(z_first, z_last, y_faces),
        halos_x(x_first, x_last),
    )

    parts = image_parts(
        gathered, top_kernel, side_kernel, counts, block_x, top_rows, depth_block
    )
    rows = parts.shape[1]
    arrived = lax.all_to_all(parts.reshape(devices * rows, LANES), ALL, 0, 0, tiled=True)
    arrived = arrived.reshape(devices, rows, LANES)
    top_sum = jnp.sum(arrived[:, : rows - TILE], axis=0)
    side_sum = jnp.sum(
        arrived[:, rows - TILE :].reshape(count_x, count_y * count_z, TILE, LANES), axis=1
    )
    side = side_sum[:, : 2 * share].reshape(count_x, 2, share, LANES)
    side = jnp.swapaxes(side, 0, 1).reshape(2, depth_block, 1, LANES)
    top = lax.all_gather(top_sum, "gz", axis=0)
    top = jnp.swapaxes(top.reshape(count_z, 2, block_x // count_z, LANES), 0, 1)
    top = top.reshape(2, 1, block_x, LANES)
    return jnp.stack(
        [
            exchange_grad[0] + top[0],
            exchange_grad[1] + top[1] + side[0],
            exchange_grad[2] + side[1],
        ]
    )


def solution(mesh):
    placed = (
        P(None, "gz", "gx", "gy"),
        P("gz", "gx", "gy"),
        P("gx", ("gy", "gz")),
        P("gy", "gz"),
        P(None, None, ("gx", "gy", "gz"), None),
        P(None, None, ("gy", "gz"), None),
    )
    return jax.shard_map(
        on_device, mesh=mesh, in_specs=placed, out_specs=P(None, "gz", "gx", "gy"), check_vma=False
    )
```

```python
import functools
import math

import jax
import jax.numpy as jnp
import ml_dtypes
import numpy as np
from jax import lax
from jax.experimental import pallas as pl
from jax.experimental.pallas import tpu as pltpu
from jax.sharding import PartitionSpec as P

LANES = 128
TILE = 8
INNER = 256
ALL = ("gx", "gy", "gz")
f32 = jnp.float32
bf16 = jnp.bfloat16
MIB = 1024 * 1024
QUAD = 4
SMEM = pl.BlockSpec(memory_space=pltpu.SMEM)
VMEM = pl.BlockSpec(memory_space=pltpu.VMEM)
HBM = pl.BlockSpec(memory_space=pltpu.HBM)


def whole_log(count):
    return count.bit_length() - 1


def split(values):
    high = values.astype(bf16)
    return high, (values - high.astype(f32)).astype(bf16)


def dot3(left, right):
    high, low = split(left)
    def one(a, b):
        return lax.dot_general(a, b, (((1,), (0,)), ((), ())), preferred_element_type=f32)
    return one(high, right[0]) + one(low, right[0]) + one(high, right[1])


def from_hbm(values):
    return pltpu.with_memory_space_constraint(values, pltpu.HBM)


def call(
    body,
    name,
    shape,
    limit,
    microseconds,
    operands,
    in_hbm=(),
    in_vmem=(),
    scratch=(),
    refs=(),
    out_refs=(),
    aliases=(),
):
    shapes = shape if isinstance(shape, list) else [shape]
    moved = sum(4 * math.prod(each) for each in shapes)
    moved += sum(x.size * x.dtype.itemsize for x in operands)
    results = pl.pallas_call(
        body,
        out_shape=[
            pltpu.HBM(each, f32)
            if i in in_hbm
            else pltpu.VMEM(each, bf16)
            if i in in_vmem
            else jax.ShapeDtypeStruct(each, f32)
            for i, each in enumerate(shapes)
        ],
        in_specs=[
            SMEM if x.shape == (1,) else HBM if i in refs else VMEM
            for i, x in enumerate(operands)
        ],
        out_specs=[HBM if i in out_refs else VMEM for i in range(len(shapes))],
        input_output_aliases=dict(aliases),
        scratch_shapes=list(scratch),
        compiler_params=pltpu.CompilerParams(vmem_limit_bytes=limit * MIB),
        cost_estimate=pl.CostEstimate(
            flops=int(microseconds * 1e9), bytes_accessed=moved, transcendentals=0
        ),
        name=name,
    )(*operands)
    return results if isinstance(shape, list) else results[0]


def transform_tables(extent, size):
    x = np.arange(extent)
    angle = (np.outer(x, np.arange(INNER)) % size) * (2.0 * math.pi / size)
    forward = np.concatenate([np.cos(angle), np.sin(angle)], 0).astype(np.float32)
    backward = np.concatenate([np.cos(angle).T, np.sin(angle).T], 0).astype(np.float32)

    def parts(table):
        high = table.astype(ml_dtypes.bfloat16)
        return high, (table - high.astype(np.float32)).astype(ml_dtypes.bfloat16)

    outer = size // INNER
    turn = (np.outer(np.arange(outer), x) % outer) * (2.0 * math.pi / outer)
    turns = np.stack([np.cos(turn), np.sin(turn)]).astype(np.float32)
    return parts(forward), parts(backward), turns


def phases(first, second, size):
    angle = (first * second % size).astype(f32) * (2.0 * math.pi / size)
    return jnp.cos(angle), jnp.sin(angle)


def image_kernel(
    counts, gathered, y_table, z_table, fh, fl, bh, bl, turns, top, side, y_back, z_back, out
):
    count_x, count_y, count_z, top_rows = counts
    group = count_y * count_z
    half = LANES // 2
    kys = top.shape[2]
    kzs = side.shape[2]
    forward = (fh[...], fl[...])
    backward = (bh[...], bl[...])

    blocks = [
        gathered[g * group : (g + 1) * group, 0:top_rows, :].reshape(group * top_rows, LANES)
        for g in range(count_x)
    ]
    mixed = dot3(y_table[...], split(jnp.concatenate(blocks, axis=1)))
    low_half, high_half = mixed[: 2 * kys], mixed[2 * kys :]
    lane = lax.broadcasted_iota(jnp.int32, (2 * kys, LANES), 1)
    pieces = []
    for g in range(0, count_x, 2):
        a = slice(g * LANES, (g + 1) * LANES)
        b = slice((g + 1) * LANES, (g + 2) * LANES)
        pieces.append(
            jnp.where(
                lane < half,
                low_half[:, a] + pltpu.roll(high_half[:, a], half, 1),
                pltpu.roll(low_half[:, b], half, 1) + high_half[:, b],
            )
        )
    top_lines = jnp.concatenate(pieces, axis=1)

    side_blocks = []
    for y in range(count_y):
        rows = [
            gathered[(x * count_y + y) * count_z + z, top_rows : top_rows + TILE, :]
            for x in range(count_x)
            for z in range(count_z)
        ]
        side_blocks.append(jnp.concatenate(rows, axis=0))
    side_lines = dot3(z_table[...], split(jnp.concatenate(side_blocks, axis=1)))

    real = jnp.concatenate([top_lines[:kys], side_lines[:kzs]], axis=0)
    imag = jnp.concatenate([top_lines[kys:], side_lines[kzs:]], axis=0)
    rows = kys + kzs
    total_real = total_imag = None
    for b in range(turns.shape[1]):
        cosine, sine = turns[0, b : b + 1, :], turns[1, b : b + 1, :]
        turned_real = real * cosine + imag * sine
        turned_imag = imag * cosine - real * sine
        waves = dot3(
            jnp.concatenate(
                [
                    jnp.concatenate([turned_real, turned_imag], axis=1),
                    jnp.concatenate([turned_imag, -turned_real], axis=1),
                ],
                axis=0,
            ),
            forward,
        )
        wave_real, wave_imag = waves[:rows], waves[rows:]
        columns = slice(b * INNER, (b + 1) * INNER)
        weighted_real, weighted_imag = [], []
        for c in range(2):
            for kernel, part in ((top, slice(0, kys)), (side, slice(kys, rows))):
                kernel_real, kernel_imag = kernel[c, 0, :, columns], kernel[c, 1, :, columns]
                weighted_real.append(
                    kernel_real * wave_real[part] + kernel_imag * wave_imag[part]
                )
                weighted_imag.append(
                    kernel_real * wave_imag[part] - kernel_imag * wave_real[part]
                )
        weighted_real = jnp.concatenate(weighted_real, axis=0)
        weighted_imag = jnp.concatenate(weighted_imag, axis=0)
        back = dot3(
            jnp.concatenate(
                [
                    jnp.concatenate([weighted_real, -weighted_imag], axis=1),
                    jnp.concatenate([weighted_imag, weighted_real], axis=1),
                ],
                axis=0,
            ),
            backward,
        )
        back_real, back_imag = back[: 2 * rows], back[2 * rows :]
        if b == 0:
            total_real, total_imag = back_real, back_imag
        else:
            total_real = total_real + (back_real * cosine - back_imag * sine)
            total_imag = total_imag + (back_real * sine + back_imag * cosine)

    y_parts = split(y_back[...])
    depth_rows = []
    quarter = (out.shape[1] - TILE) // 2
    block_x = quarter * count_z
    for c in range(2):
        start = c * rows
        lines = jnp.concatenate(
            [total_real[start : start + kys], total_imag[start : start + kys]], axis=0
        )
        image = dot3(lines.T, y_parts)
        for x in range(count_x):
            for y in range(count_y):
                for z in range(count_z):
                    first = x * block_x + z * quarter
                    out[
                        (x * count_y + y) * count_z + z, c * quarter : (c + 1) * quarter, :
                    ] = image[first : first + quarter, y * LANES : (y + 1) * LANES]
        depth_rows.append(total_real[start + kys : start + rows])
        depth_rows.append(total_imag[start + kys : start + rows])
    side_image = dot3(z_back[...], split(jnp.concatenate(depth_rows, axis=0)))
    for y in range(count_y):
        for z in range(count_z):
            block = side_image[z * TILE : (z + 1) * TILE, y * LANES : (y + 1) * LANES]
            for x in range(count_x):
                out[(x * count_y + y) * count_z + z, 2 * quarter :, :] = block


def image_parts(gathered, top_kernel, side_kernel, counts, block_x, top_rows, depth_block):
    count_x, count_y, count_z = counts
    group = count_y * count_z
    here = [lax.axis_index(axis) for axis in ALL]
    kys, size = top_kernel.shape[2:]
    kzs = side_kernel.shape[2]
    depth_size = kzs * group
    extent = count_y * LANES
    share = depth_block // count_x
    block_y = top_rows * 2

    ky = ((here[0] * count_y + here[1]) * count_z + here[2]) * kys + lax.iota(jnp.int32, kys)
    kz = (here[1] * count_z + here[2]) * kzs + lax.iota(jnp.int32, kzs)

    row = lax.iota(jnp.int32, group * top_rows)
    y_tables = []
    for h in range(2):
        y = row // top_rows * block_y + h * top_rows + row % top_rows
        cosine, sine = phases(ky[:, None], y[None, :], size)
        y_tables += [cosine, -sine]
    y_table = jnp.concatenate(y_tables, axis=0)

    row = lax.iota(jnp.int32, count_x * count_z * TILE)
    inside = row % TILE
    z = row // TILE % count_z * depth_block + row // (TILE * count_z) * share + inside
    cosine, sine = phases(kz[:, None], z[None, :], depth_size)
    z_table = jnp.where((inside < share)[None, :], jnp.concatenate([cosine, -sine], axis=0), 0.0)

    cosine, sine = phases(ky[:, None], lax.iota(jnp.int32, extent)[None, :], size)
    y_back = jnp.concatenate([cosine, -sine], axis=0) * (1.0 / (size * size))

    row = lax.iota(jnp.int32, count_z * TILE)
    z = row // TILE * depth_block + here[0] * share + row % TILE % share
    cosine, sine = phases(z[:, None], kz[None, :], depth_size)
    both = jnp.concatenate([cosine, -sine], axis=1) * (1.0 / (size * depth_size))
    component = (row % TILE // share)[:, None]
    z_back = jnp.concatenate(
        [jnp.where(component == 0, both, 0.0), jnp.where(component == 1, both, 0.0)], axis=1
    )

    forward, backward, turns = transform_tables(extent, size)
    out_rows = 2 * (block_x // count_z) + TILE
    return pl.pallas_call(
        functools.partial(image_kernel, counts + (top_rows,)),
        out_shape=jax.ShapeDtypeStruct((count_x * group, out_rows, LANES), f32),
        compiler_params=pltpu.CompilerParams(vmem_limit_bytes=56 * 1024 * 1024),
        name="images",
    )(
        gathered,
        y_table,
        z_table,
        *(jnp.asarray(t) for t in forward + backward),
        jnp.asarray(turns),
        top_kernel,
        side_kernel,
        y_back,
        z_back,
    )


def begin(semaphores, pairs):
    started = [
        pltpu.make_async_copy(source, target, semaphores.at[i])
        for i, (source, target) in enumerate(pairs)
    ]
    for copy in started:
        copy.start()
    return started


def faces_kernel(
    magnetization, stiffness, z_first, z_last, x_first, x_last, y_faces, m, s, loading
):
    depth, across = stiffness.shape[:2]
    loads = begin(
        loading, [(stiffness, s)] + [(magnetization.at[c], m.at[c]) for c in range(3)]
    )
    lane = lax.broadcasted_iota(jnp.int32, (across, LANES), 1)
    pair = (lane + 1 & (LANES - 1)) >> 1
    sides = jnp.zeros((across, LANES), f32)
    for field in (3, 0, 1, 2):
        loads[(field + 1) % 4].wait()
        ref = s if field == 3 else m.at[field]
        z_first[field] = ref[0]
        z_last[field] = ref[depth - 1]
        x_first[field] = ref[:, 0, :]
        x_last[field] = ref[:, across - 1, :]
        for z in range(depth):
            column = field * depth + z
            turned = pltpu.roll(ref[z], 2 * column, 1) if column else ref[z]
            sides = jnp.where(pair == column, turned, sides)
    y_faces[...] = sides


def twice_weight(a, b):
    total = a + b
    inverse = pl.reciprocal(total, approx=True)
    return 4.0 * a * b * (inverse * (2.0 - total * inverse))


def exchange_kernel(
    counts,
    here,
    magnetization_from,
    stiffness_from,
    y_faces_from,
    z_next,
    z_before,
    x_next,
    x_before,
    y_next,
    y_before,
    out,
    m,
    s,
    y_faces,
    loading,
):
    depth, across = s.shape[:2]
    chunk = depth // 4
    pairs = [(y_faces_from, y_faces)]
    for k in range(4):
        layers = pl.ds(k * chunk, chunk)
        pairs.append((stiffness_from.at[layers], s.at[layers]))
        pairs.append((magnetization_from.at[:, layers], m.at[:, layers]))
    loads = begin(loading, pairs)

    count_x, count_y, count_z = counts
    at_z = here[0] % count_z
    at_y = here[0] // count_z % count_y
    at_x = here[0] // (count_z * count_y)

    def inside(condition, values):
        return jnp.where(condition, values, 0.0)

    lane = lax.broadcasted_iota(jnp.int32, (across, LANES), 1)
    row = lax.broadcasted_iota(jnp.int32, (across, LANES), 0)
    first_lane, last_lane, last_row = lane == 0, lane == LANES - 1, row == across - 1

    loads[0].wait()
    own = y_faces[...]
    even = (lane & 1) == 0
    field = (lane + 1 & (LANES - 1)) >> whole_log(2 * depth)
    halo = jnp.where(
        even, pltpu.roll(y_before[...], 1, 1), pltpu.roll(y_next[...], LANES - 1, 1)
    )
    present = jnp.where(even, at_y, count_y - 1 - at_y) > 0
    weight = twice_weight(
        jnp.where(field == 3, own, 1.0),
        jnp.where(field == 3, jnp.where(present, halo, 0.0), 1.0),
    )
    spread = pltpu.roll(weight, LANES - 6 * depth, 1)
    for c in (1, 2):
        spread = jnp.where(
            field == c, pltpu.roll(weight, LANES - (3 - c) * 2 * depth, 1), spread
        )
    sides = spread * (own - halo)
    outer = first_lane | last_lane

    for copy in loads[1:3]:
        copy.wait()
    below_weight = twice_weight(inside(at_z > 0, z_before[3]), s[0])
    below = [below_weight * (z_before[c] - m[c, 0]) for c in range(3)]
    for z in range(depth):
        if z % chunk == chunk - 1:
            k = 1 + 2 * (z // chunk + 1)
            for copy in loads[k : k + 2]:
                copy.wait()
        centre = s[z]
        above = s[z + 1] if z + 1 < depth else inside(at_z < count_z - 1, z_next[3])
        weight_z = twice_weight(centre, above)
        weight_x = jnp.where(
            last_row, 0.0, twice_weight(centre, pltpu.roll(centre, across - 1, 0))
        )
        weight_y = jnp.where(
            last_lane, 0.0, twice_weight(centre, pltpu.roll(centre, LANES - 1, 1))
        )
        for c in range(3):
            column = c * depth + z
            values = m[c, z]
            upper = m[c, z + 1] if z + 1 < depth else z_next[c]
            up = weight_z * (values - upper)
            flux_x = weight_x * (values - pltpu.roll(values, across - 1, 0))
            flux_y = weight_y * (values - pltpu.roll(values, LANES - 1, 1))
            total = (up - below[c]) + (flux_x - pltpu.roll(flux_x, 1, 0))
            total = total + (flux_y - pltpu.roll(flux_y, 1, 1))
            both = pltpu.roll(sides, LANES - 2 * column, 1) if column else sides
            out[c, z] = jnp.where(outer, total + both, total)
            below[c] = up
    for edge_row, halo, present in (
        (across - 1, x_next, at_x < count_x - 1),
        (0, x_before, at_x > 0),
    ):
        weight = twice_weight(s[:, edge_row, :], inside(present, halo[3]))
        for c in range(3):
            out[c, :, edge_row, :] += weight * (m[c, :, edge_row, :] - halo[c])


def ring(block, axis, distance):
    count = lax.axis_size(axis)
    return lax.ppermute(block, axis, [(i, (i + distance) % count) for i in range(count)])


def faces_of(magnetization, stiffness):
    depth, across, along = stiffness.shape
    return call(
        faces_kernel,
        "faces",
        [
            (4, across, along),
            (4, across, along),
            (4, depth, along),
            (4, depth, along),
            (across, LANES),
        ],
        8,
        2.0,
        (from_hbm(magnetization), from_hbm(stiffness)),
        in_hbm=(4,),
        refs=(0, 1),
        scratch=[
            pltpu.VMEM(magnetization.shape, f32),
            pltpu.VMEM(stiffness.shape, f32),
            pltpu.SemaphoreType.DMA((4,)),
        ],
    )


def halos_zy(z_first, z_last, y_faces):
    y_next = ring(y_faces, "gy", -1)
    y_before = y_next if lax.axis_size("gy") == 2 else ring(y_faces, "gy", 1)
    return ring(z_first, "gz", -1), ring(z_last, "gz", 1), y_next, y_before, y_faces


def halos_x(x_first, x_last):
    return ring(x_first, "gx", -1), ring(x_last, "gx", 1)


def exchange_of(counts, index, magnetization, stiffness, zy, x):
    z_next, z_before, y_next, y_before, y_faces = zy
    fetched = (magnetization, stiffness, y_faces)
    return call(
        functools.partial(exchange_kernel, counts),
        "exchange",
        magnetization.shape,
        8,
        5.0,
        (
            index,
            *(from_hbm(array) for array in fetched),
            z_next,
            z_before,
            *x,
            y_next,
            y_before,
        ),
        refs=(1, 2, 3),
        scratch=[pltpu.VMEM(array.shape, f32) for array in fetched]
        + [pltpu.SemaphoreType.DMA((9,))],
    )


def cos_sin(steps, size):
    quarter = steps >> whole_log(size // 4)
    angle = ((steps & (size // 4 - 1)) - size // 8).astype(f32) * (2.0 * math.pi / size)
    square = angle * angle
    sine = cosine = 0.0
    for k in range(5, -1, -1):
        sine = sine * square + (-1) ** k / math.factorial(2 * k + 1)
        cosine = cosine * square + (-1) ** k / math.factorial(2 * k)
    sine = sine * angle
    first, second = (cosine - sine) * math.sqrt(0.5), (cosine + sine) * math.sqrt(0.5)
    odd = (quarter & 1) == 1
    real = jnp.where(odd, -second, first)
    imag = jnp.where(odd, first, second)
    back = quarter >= 2
    return jnp.where(back, -real, real), jnp.where(back, -imag, imag)


def halves_of(table):
    table = table.astype(np.float32)
    high = table.astype(ml_dtypes.bfloat16)
    return high, (table - high.astype(np.float32)).astype(ml_dtypes.bfloat16)


def narrow_tables(extent, size):
    length = 2 * extent
    ratio = size // length
    m = np.arange(size)
    lags = np.arange(1, extent)
    window = 1.0 + 2.0 * np.cos(np.outer(m, lags) % size * (2.0 * math.pi / size)).sum(axis=1)
    i = np.arange(INNER)
    place = np.arange(0, size, INNER)[:, None, None] + i[:, None] - ratio * i[None, :]
    high, low = halves_of(window[place % size] / length)
    tiles = np.stack([high, low], axis=1)
    return tiles, transform_table(length)


def transform_table(size):
    i = np.arange(INNER)
    angle = np.outer(i, i) * (2.0 * math.pi / size)
    return np.stack(halves_of(np.concatenate([np.cos(angle), np.sin(angle)], axis=0)))


def pair_order(planes, per_plane):
    return [plane * per_plane + p for p in range(per_plane) for plane in reversed(range(planes))]


def y_table_of(counts, here, kys, size):
    group = counts[1] * counts[2]
    top_rows = LANES // group
    ky = here[0] * kys + lax.broadcasted_iota(jnp.int32, (kys, LANES), 0)
    lane = lax.broadcasted_iota(jnp.int32, (kys, LANES), 1)
    odd = (lane >> whole_log(LANES // 2)) ^ (here[0] & 1)
    pair = lane >> whole_log(top_rows) & (group // 2 - 1)
    phases_of = []
    for h in range(2):
        y = (2 * pair + odd) * (2 * top_rows) + h * top_rows + (lane & (top_rows - 1))
        cosine, sine = cos_sin(ky * y & (size - 1), size)
        phases_of += [cosine, -sine]
    high, low = split(jnp.concatenate(phases_of, axis=0))
    return jnp.concatenate([high, low, high], axis=1)


def narrow_kernel(top, side, tiles, top_out, side_out):
    count = tiles.shape[0]
    parts = top_out.shape[3] // INNER
    step = count // parts
    top_rows, side_rows = top.shape[2], side.shape[2]
    totals = [None] * parts
    for k in range(count):
        columns = slice(k * INNER, (k + 1) * INNER)
        lines = jnp.concatenate(
            [
                top[:, :, :, columns].reshape(4 * top_rows, INNER),
                side[:, :, :, columns].reshape(4 * side_rows, INNER),
            ],
            axis=0,
        )
        high, low = split(lines)
        lines = jnp.concatenate([high, low, high], axis=1)
        for part in range(parts):
            tile = tiles[(k - part * step) % count]
            term = product(lines, jnp.concatenate([tile[0], tile[0], tile[1]], axis=0))
            totals[part] = term if k == 0 else totals[part] + term
    for part in range(parts):
        columns = slice(part * INNER, (part + 1) * INNER)
        top_out[:, :, :, columns] = totals[part][: 4 * top_rows].reshape(2, 2, top_rows, INNER)
        side_out[:, :, :, columns] = totals[part][4 * top_rows :].reshape(2, 2, side_rows, INNER)


def product(left, right, contracted=0):
    return lax.dot_general(
        left, right, (((1,), (contracted,)), ((), ())), preferred_element_type=f32
    )


def dot3_with(values, table):
    high, low = split(values)
    lines = jnp.concatenate([high, low, high], axis=1)
    return product(lines, jnp.concatenate([table[0], table[0], table[1]], axis=0))


def there_and_back(real, imag, kernel, table):
    rows, extent = real.shape
    sign = jnp.where(lax.broadcasted_iota(jnp.int32, (1, extent), 1) & 1 == 0, 1.0, -1.0)
    lines = jnp.concatenate(
        [jnp.concatenate([real, imag], axis=1), jnp.concatenate([imag, -real], axis=1)], axis=0
    )
    signs = jnp.concatenate([sign, sign], axis=1)
    waves = dot3_with(jnp.concatenate([lines, lines * signs], axis=0), table)
    totals = []
    for b in range(2):
        wave_real, wave_imag = (
            waves[(2 * b + k) * rows : (2 * b + k + 1) * rows] for k in range(2)
        )
        columns = slice(b * INNER, (b + 1) * INNER)
        weighted = ([], [])
        for c in range(2):
            kernel_real, kernel_imag = kernel[c, 0, :, columns], kernel[c, 1, :, columns]
            weighted[0].append(kernel_real * wave_real + kernel_imag * wave_imag)
            weighted[1].append(kernel_real * wave_imag - kernel_imag * wave_real)
        a, b = (jnp.concatenate(part, axis=0) for part in weighted)
        lines = jnp.concatenate(
            [jnp.concatenate([a, -b], axis=1), jnp.concatenate([b, a], axis=1)], axis=0
        )
        totals.append(dot3_with(lines, table))
    total = totals[0] + totals[1] * sign
    return total[: 2 * rows], total[2 * rows :]


def lines_kernel(
    counts, here, gathered, swapped, table, kernel, out, received, result, sending
):
    count_x, count_y, count_z = counts
    group = count_y * count_z
    top_rows = LANES // group
    half = LANES // 2
    kys = kernel.shape[2]
    y_table = y_table_of(counts, here, kys, INNER * TILE)
    pairs = pair_order(count_x, group // 2)
    for k, part in enumerate((gathered, swapped)):
        for member in range(part.shape[0]):
            g, place = divmod(member, group // 2)
            for j in range(top_rows // QUAD):
                row = (k * group // 2 + place) * top_rows + j * QUAD
                received[g, row : row + QUAD, :] = part[pairs.index(member), j]
    blocks = [received[g] for g in range(count_x)]
    high, low = split(jnp.concatenate(blocks, axis=1))
    mixed = product(y_table, jnp.concatenate([high, high, low], axis=0))
    low_half, high_half = mixed[: 2 * kys], mixed[2 * kys :]
    lane = lax.broadcasted_iota(jnp.int32, (2 * kys, LANES), 1)
    pieces = []
    for g in range(0, count_x, 2):
        a = slice(g * LANES, (g + 1) * LANES)
        b = slice((g + 1) * LANES, (g + 2) * LANES)
        pieces.append(
            jnp.where(
                lane < half,
                low_half[:, a] + pltpu.roll(high_half[:, a], half, 1),
                pltpu.roll(low_half[:, b], half, 1) + high_half[:, b],
            )
        )
    lines = jnp.concatenate(pieces, axis=1)
    sends = []
    for k, part in enumerate(there_and_back(lines[:kys], lines[kys:], kernel, table)):
        rows = slice(k * TILE, (k + 1) * TILE)
        result[:, rows, :] = part.T.reshape(count_x * group, TILE, LANES)
        sends.append(pltpu.make_async_copy(result.at[:, rows], out.at[:, rows], sending.at[k]))
        sends[-1].start()
    for copy in sends:
        copy.wait()


def side_kernel_body(
    counts,
    here,
    gathered,
    swapped,
    spectrum,
    kernel,
    later_from,
    mine,
    other,
    later,
    received,
    loading,
):
    copies = begin(loading, [(later_from, later)])
    count_x, count_y, count_z = counts
    depth_block = mine.shape[1]
    last = gathered.shape[1] - 1
    kzs, length = kernel.shape[2], INNER * TILE
    size = kzs * count_y * count_z
    columns = count_x * count_z * QUAD
    kz = here[0] * kzs + lax.broadcasted_iota(jnp.int32, (kzs, columns), 0)
    column = lax.broadcasted_iota(jnp.int32, (kzs, columns), 1)
    pair = column >> whole_log(QUAD) & (count_z // 2 - 1)
    odd = (column >> whole_log(columns // 2)) ^ (here[0] & 1)
    z = (2 * pair + odd) * depth_block + (column & (QUAD - 1))
    z = z + (column >> whole_log(QUAD * count_z // 2) & (count_x - 1)) * QUAD
    cosine, sine = cos_sin(kz * z & (size - 1), size)
    table = jnp.concatenate([cosine, -sine], axis=0)
    pairs = pair_order(count_x, count_y * count_z // 2)
    for k, part in enumerate((gathered, swapped)):
        for x in range(count_x):
            for y in range(count_y):
                for pair in range(count_z // 2):
                    row = ((k * count_x + x) * count_z // 2 + pair) * QUAD
                    member = (x * count_y + y) * count_z // 2 + pair
                    received[y, row : row + QUAD, :] = part[pairs.index(member), last]
    blocks = [received[y] for y in range(count_y)]
    lines = dot3(table, split(jnp.concatenate(blocks, axis=1)))

    real, imag = there_and_back(lines[:kzs], lines[kzs:], kernel, spectrum)

    rows = depth_block * count_z
    z = lax.broadcasted_iota(jnp.int32, (rows, 2 * kzs), 0)
    column = lax.broadcasted_iota(jnp.int32, (rows, 2 * kzs), 1)
    cosine, sine = cos_sin((here[0] * kzs + (column & (kzs - 1))) * z & (size - 1), size)
    table = jnp.where(column < kzs, cosine, -sine) * (1.0 / (size * length))
    even = (here[0] & 1) == 0
    lines = [jnp.concatenate([part[:kzs] for part in (real, imag)], axis=0)]
    lines.append(jnp.concatenate([part[kzs:] for part in (real, imag)], axis=0))
    for out, (a, b) in ((mine, lines), (other, lines[::-1])):
        image = dot3(table, split(jnp.where(even, a, b)))
        for y in range(count_y):
            for z in range(count_z):
                out[y * count_z + z] = image[
                    z * depth_block : (z + 1) * depth_block, y * LANES : (y + 1) * LANES
                ]
    copies[0].wait()


def rows_kernel(counts, arrived, mine, other, table, out):
    count_y, count_z = counts[1:]
    out[:, 2 * TILE :, :] = mine[...] + other[...]
    per_turn = INNER * 2 // LANES
    step = arrived.shape[0] // per_turn
    size = step * INNER
    half = LANES // 2
    lane = lax.broadcasted_iota(jnp.int32, (2 * TILE, LANES), 1)
    upper, lower = [], []
    for b in range(step):
        parts = ([], [])
        for pair in range(b * per_turn, (b + 1) * per_turn, 2):
            first, second = arrived[pair], arrived[pair + 1]
            spectra = (
                jnp.where(lane < half, first, pltpu.roll(second, half, 1)),
                jnp.where(lane < half, pltpu.roll(first, half, 1), second),
            )
            for k in range(2):
                parts[k].append(
                    jnp.concatenate(
                        [spectrum[k * TILE : (k + 1) * TILE] for spectrum in spectra], axis=0
                    )
                )
        real, imag = (jnp.concatenate(part, axis=1) for part in parts)
        upper.append(jnp.concatenate([real, -imag], axis=1))
        lower.append(jnp.concatenate([imag, real], axis=1))
    lines = dot3_with(jnp.concatenate(upper + lower, axis=0), table)
    y = lax.broadcasted_iota(jnp.int32, (1, INNER), 1) & (step - 1)
    total = None
    for b in range(step):
        cosine, sine = cos_sin(y * b & (step - 1), step)
        real, imag = (
            lines[(k * step + b) * 2 * TILE : (k * step + b + 1) * 2 * TILE] for k in range(2)
        )
        term = real * cosine - imag * sine if b else real
        total = term if b == 0 else total + term
    total = total * (1.0 / (size * size))
    for y in range(count_y):
        for z in range(count_z):
            out[y * count_z + z, 0 : 2 * TILE, :] = total[:, y * LANES : (y + 1) * LANES]


def sum_kernel(exchange_grad, arrived, out, result, sending):
    depth = exchange_grad.shape[1]
    group = arrived.shape[0]
    sends = []

    def send(c):
        sends.append(pltpu.make_async_copy(result.at[c], out.at[c], sending.at[c]))
        sends[-1].start()

    def top(c):
        return arrived[:, c * TILE : (c + 1) * TILE, :].reshape(group * TILE, LANES)

    def side(c):
        total = arrived[c, 2 * TILE :, :]
        for p in range(c + 2, group, 2):
            total = total + arrived[p, 2 * TILE :, :]
        return total

    image = top(0)
    for z in range(depth):
        result[0, z] = exchange_grad[0, z] + image
    send(0)
    column = side(1)
    for z in range(depth):
        result[2, z] = exchange_grad[2, z] + column[z : z + 1]
    send(2)
    image, column = top(1), side(0)
    for z in range(depth):
        result[1, z] = exchange_grad[1, z] + image + column[z : z + 1]
    send(1)
    for copy in sends:
        copy.wait()


def residual_blocks(residual_top, residual_side, copies, share, quads):
    block_x, block_y = residual_top.shape
    top_rows = block_y // 2

    def body(at_x, top, side, out):
        piece = jnp.concatenate([top[0:top_rows, :], top[top_rows:, :]], axis=1)
        part = side[pl.ds(at_x[0] * share, share), :]
        if not quads:
            part = jnp.concatenate([part, jnp.zeros((TILE - share, LANES), f32)], axis=0)
        for copy in range(copies):
            if quads:
                for j in range(top_rows // QUAD):
                    out[copy, j] = piece[j * QUAD : (j + 1) * QUAD]
                out[copy, top_rows // QUAD] = part
            else:
                out[copy, 0:top_rows, :] = piece
                out[copy, top_rows:, :] = part

    shape = (top_rows // QUAD + 1, QUAD) if quads else (top_rows + TILE,)
    return call(
        body,
        "pack",
        (copies, *shape, LANES),
        60,
        0.8,
        (lax.axis_index("gx").reshape(1), residual_top.T, residual_side.T),
    )


def fast_on_device(magnetization, stiffness, residual_top, residual_side, top_kernel, side_kernel):
    counts = tuple(lax.axis_size(axis) for axis in ALL)
    count_x, count_y, count_z = counts
    group = count_y * count_z
    devices = count_x * group
    block_x, block_y = residual_top.shape
    depth_block = stiffness.shape[0]
    top_rows = block_y // 2
    kys, size = top_kernel.shape[2:]
    kzs = side_kernel.shape[2]
    extent = count_x * block_x
    here = [lax.axis_index(axis) for axis in ALL]
    plane_index = here[1] * count_z + here[2]
    index = (here[0] * group + plane_index).reshape(1)
    plane_index = plane_index.reshape(1)
    tiles, table = (jnp.asarray(values) for values in narrow_tables(extent, size))
    rows_table = jnp.asarray(transform_table(size))

    pairs = pair_order(count_x, group // 2)
    parities = [[2 * pair + parity for pair in pairs] for parity in range(2)]
    sent = residual_blocks(
        residual_top, residual_side, devices // 2, depth_block // count_x, True
    )
    gathered = lax.all_to_all(
        sent, ALL, 0, 0, tiled=True, axis_index_groups=parities
    )
    z_first, z_last, x_first, x_last, y_faces = faces_of(magnetization, stiffness)
    narrowed = call(
        narrow_kernel,
        "narrow",
        [(2, 2, kys, 2 * extent), (2, 2, kzs, 2 * extent)],
        16,
        2.5,
        (top_kernel, side_kernel, tiles),
    )
    gathered, x_first, x_last, y_faces, narrowed = lax.optimization_barrier(
        (gathered, x_first, x_last, y_faces, narrowed)
    )
    top_spectra, side_spectra = narrowed
    swapped = lax.ppermute(gathered, "gz", [(i, i ^ 1) for i in range(count_z)])
    zy = halos_zy(z_first, z_last, y_faces)

    lines = call(
        functools.partial(lines_kernel, counts),
        "lines",
        (devices, 2 * TILE, LANES),
        16,
        2.2,
        (index, gathered, swapped, table, top_spectra),
        in_hbm=(0,),
        out_refs=(0,),
        scratch=[
            pltpu.VMEM((count_x, LANES, LANES), f32),
            pltpu.VMEM((devices, 2 * TILE, LANES), f32),
            pltpu.SemaphoreType.DMA((2,)),
        ],
    )
    arrived = lax.all_to_all(lines, ALL, 0, 0, tiled=True)
    lines, x_first, x_last = lax.optimization_barrier((lines, x_first, x_last))
    x = halos_x(x_first, x_last)
    mine, other, rows_table = call(
        functools.partial(side_kernel_body, counts),
        "side",
        [(group, depth_block, LANES), (group, depth_block, LANES), rows_table.shape],
        8,
        2.0,
        (plane_index, gathered, swapped, table, side_spectra, from_hbm(rows_table)),
        in_vmem=(2,),
        refs=(5,),
        scratch=[
            pltpu.VMEM((count_y, count_x * count_z * QUAD, LANES), f32),
            pltpu.SemaphoreType.DMA((1,)),
        ],
    )
    other = lax.ppermute(other, "gz", [(i, i ^ 1) for i in range(count_z)])
    arrived, mine, other, rows_table = lax.optimization_barrier(
        (arrived, mine, other, rows_table)
    )
    rows = call(
        functools.partial(rows_kernel, counts),
        "rows",
        (group, 2 * TILE + depth_block, LANES),
        8,
        1.1,
        (arrived, mine, other, rows_table),
    )
    _, zy, x = lax.optimization_barrier((rows, zy, x))
    arrived = lax.all_to_all(rows, ("gy", "gz"), 0, 0, tiled=True)
    exchange_grad = exchange_of(counts, index, magnetization, stiffness, zy, x)
    return call(
        sum_kernel,
        "gradient",
        magnetization.shape,
        16,
        1.2,
        (exchange_grad, arrived),
        out_refs=(0,),
        scratch=[pltpu.VMEM(magnetization.shape, f32), pltpu.SemaphoreType.DMA((3,))],
    )


def fits(counts, stiffness, residual_top, residual_side, top_kernel, side_kernel):
    count_x, count_y, count_z = counts
    block_x, block_y = residual_top.shape
    group = count_y * count_z
    return (
        2 * block_x == LANES
        and 2 * top_kernel.shape[2] == LANES
        and stiffness.shape[2] == LANES
        and block_x == group * TILE
        and block_y * group == count_x * block_x == INNER
        and count_y * LANES == INNER
        and block_y % 16 == 0
        and count_x % 2 == 0
        and count_z % 2 == 0
        and (count_x * group) % (2 * top_kernel.shape[3] // INNER) == 0
        and INNER == top_kernel.shape[2] * count_z
        and top_kernel.shape[3] == TILE * INNER == side_kernel.shape[3]
        and INNER == 2 * LANES
        and stiffness.shape[0] % 16 == 0
        and stiffness.shape[0] == count_x * QUAD
        and side_kernel.shape[2] % 16 == 0
        and all(
            count & (count - 1) == 0
            for count in (group, count_x, count_z, top_kernel.shape[3], side_kernel.shape[2])
        )
    )


def on_device(magnetization, stiffness, residual_top, residual_side, top_kernel, side_kernel):
    counts = tuple(lax.axis_size(axis) for axis in ALL)
    count_x, count_y, count_z = counts
    if fits(counts, stiffness, residual_top, residual_side, top_kernel, side_kernel):
        return fast_on_device(
            magnetization, stiffness, residual_top, residual_side, top_kernel, side_kernel
        )
    devices = count_x * count_y * count_z
    depth_block = stiffness.shape[0]
    block_x, block_y = residual_top.shape
    top_rows = block_y // 2
    share = depth_block // count_x

    sent = residual_blocks(residual_top, residual_side, devices, share, False)
    rows = sent.shape[1]
    gathered = lax.all_to_all(sent, ALL, 0, 0, tiled=True)
    index = (
        (lax.axis_index("gx") * count_y + lax.axis_index("gy")) * count_z + lax.axis_index("gz")
    ).reshape(1)
    z_first, z_last, x_first, x_last, y_faces = faces_of(magnetization, stiffness)
    exchange_grad = exchange_of(
        counts,
        index,
        magnetization,
        stiffness,
        halos_zy(z_first, z_last, y_faces),
        halos_x(x_first, x_last),
    )

    parts = image_parts(
        gathered, top_kernel, side_kernel, counts, block_x, top_rows, depth_block
    )
    rows = parts.shape[1]
    arrived = lax.all_to_all(parts.reshape(devices * rows, LANES), ALL, 0, 0, tiled=True)
    arrived = arrived.reshape(devices, rows, LANES)
    top_sum = jnp.sum(arrived[:, : rows - TILE], axis=0)
    side_sum = jnp.sum(
        arrived[:, rows - TILE :].reshape(count_x, count_y * count_z, TILE, LANES), axis=1
    )
    side = side_sum[:, : 2 * share].reshape(count_x, 2, share, LANES)
    side = jnp.swapaxes(side, 0, 1).reshape(2, depth_block, 1, LANES)
    top = lax.all_gather(top_sum, "gz", axis=0)
    top = jnp.swapaxes(top.reshape(count_z, 2, block_x // count_z, LANES), 0, 1)
    top = top.reshape(2, 1, block_x, LANES)
    return jnp.stack(
        [
            exchange_grad[0] + top[0],
            exchange_grad[1] + top[1] + side[0],
            exchange_grad[2] + side[1],
        ]
    )


def solution(mesh):
    placed = (
        P(None, "gz", "gx", "gy"),
        P("gz", "gx", "gy"),
        P("gx", ("gy", "gz")),
        P("gy", "gz"),
        P(None, None, ("gx", "gy", "gz"), None),
        P(None, None, ("gy", "gz"), None),
    )
    return jax.shard_map(
        on_device, mesh=mesh, in_specs=placed, out_specs=P(None, "gz", "gx", "gy"), check_vma=False
    )
```
